32 devices in a mesh: stream: 2 (over core), clip: 4 (over z), tm: 4 (over y, x).
Axes of the slice: x: 2, y: 2, z: 4, core: 2. Of those that a mesh axis runs over, the one named last changes fastest.
Arguments:
- features: bfloat16 [8, 8, 14, 14, 528], P(('stream', 'clip'), 'tm'), parts along dimension 0, may hold values from -135 to 135
- w_in_4f: bfloat16 [1056, 448], P('stream'), parts along dimension 0, may hold values from -0.25 to 0.25
- w_pool_4f: bfloat16 [1056, 128], P('stream'), parts along dimension 0, may hold values from -0.25 to 0.25
- w_mid_4f: bfloat16 [54, 160, 320], P('stream'), parts along dimension 0, may hold values from -0.09375 to 0.09375
- w_small_4f: bfloat16 [54, 32, 128], P('stream'), parts along dimension 0, may hold values from -0.21875 to 0.21875
- offsets_4f: float32 [2048], P('stream'), parts along dimension 0, may hold values from -3 to 3
- w_in_5b: bfloat16 [1664, 448], P('stream'), parts along dimension 0, may hold values from -0.21875 to 0.21875
- w_pool_5b: bfloat16 [1664, 128], P('stream'), parts along dimension 0, may hold values from -0.21875 to 0.21875
- w_mid_5b: bfloat16 [54, 160, 320], P('stream'), parts along dimension 0, may hold values from -0.09375 to 0.09375
- w_small_5b: bfloat16 [54, 32, 128], P('stream'), parts along dimension 0, may hold values from -0.21875 to 0.21875
- offsets_5b: float32 [2048], P('stream'), parts along dimension 0, may hold values from -3 to 3
- cotangent: bfloat16 [8, 4, 7, 7, 832], P(('stream', 'clip'), 'tm'), parts along dimension 0, may hold values from -135 to 135
Outputs:
- output: bfloat16 [8, 4, 7, 7, 832], P(('stream', 'clip'), 'tm'), parts along dimension 0
- grad_features: float32 [8, 8, 14, 14, 528], P(('stream', 'clip'), 'tm'), parts along dimension 0
- grad_w_in_4f: float32 [1056, 448], P('stream', 'tm'), parts along dimension 0
- grad_w_pool_4f: float32 [1056, 128], P('stream', 'tm'), parts along dimension 0
- grad_w_mid_4f: float32 [54, 160, 320], P('stream', None, 'tm'), parts along dimension 0
- grad_w_small_4f: float32 [54, 32, 128], P('stream', None, 'tm'), parts along dimension 0
- grad_offsets_4f: float32 [2048], P('stream'), parts along dimension 0
- grad_w_in_5b: float32 [1664, 448], P('stream', 'tm'), parts along dimension 0
- grad_w_pool_5b: float32 [1664, 128], P('stream', 'tm'), parts along dimension 0
- grad_w_mid_5b: float32 [54, 160, 320], P('stream', None, 'tm'), parts along dimension 0
- grad_w_small_5b: float32 [54, 32, 128], P('stream', None, 'tm'), parts along dimension 0
- grad_offsets_5b: float32 [2048], P('stream'), parts along dimension 0
The draws below stay inside these ranges and needn't reach their ends.
There are 2 independent parts, one for each index of `stream`. The reference program is written for one: setup_inputs(seed, part) draws one part's arguments, and reference() takes and returns one part's arrays. A program takes and returns all parts, laid end to end along the dimension named above; each array names one. Nothing has to cross between parts.
All inputs are finite; a program needn't handle non-finite values.
Results may differ from the reference program's by a relative error of at most 0.023.
Values may be sent and summed in bfloat16 or wider, within the bound.
No kernel may reach another device: no remote copies, remote signals or barrier semaphores. Data moves between devices by JAX's collectives and lax.ppermute only.
A program may use at most 192 MiB of HBM per device.

```python
import jax
import jax.numpy as jnp
from jax import lax

HW = 14
C_4E = 528
C0 = 256
C1A = 160
C1B = 320
C2A = 32
C2B = 128
C3 = 128
C_IN = 832
IN_OUT = 448
SECTION_A = 576
NOFF = 1024
CLIPS = 4
FRAMES = 8


def ramp_field(key, clips, frames, side, channels):
    key_base = jax.random.fold_in(key, 0)
    normal_part = jnp.clip(jax.random.normal(key_base, (clips, frames, side, side, channels), jnp.float32), -4.0, 4.0)
    clip_ramp = 1.0 + 2.0 * jnp.arange(clips, dtype=jnp.float32) / max(clips - 1, 1)
    frame_ramp = 1.0 + 2.0 * jnp.arange(frames, dtype=jnp.float32) / max(frames - 1, 1)
    scale = clip_ramp[:, None, None, None, None] * frame_ramp[None, :, None, None, None]
    return scale * normal_part


def draw_features(key, part):
    key = jax.random.fold_in(key, 11)
    field = ramp_field(key, CLIPS, FRAMES, HW, C_4E)
    return field.astype(jnp.bfloat16)


def draw_cotangent(key, part):
    key = jax.random.fold_in(key, 12)
    field = ramp_field(key, CLIPS, FRAMES // 2, HW // 2, C_IN)
    return field.astype(jnp.bfloat16)


def centred(stream_key, extent, scale, limit, kind=jnp.bfloat16):
    return jnp.clip(scale * jax.random.normal(stream_key, extent, jnp.float32), -limit, limit).astype(kind)


def setup_inputs(seed: int = 0, part: int = 0) -> dict:
    splits = jax.random.split(jax.random.key(seed), 13)
    part_splits = jax.random.split(jax.random.fold_in(splits[12], part), 13)
    features = draw_features(jax.random.fold_in(jax.random.fold_in(splits[12], part), 71), part)
    w_in_4f = centred(part_splits[1], (C_4E, IN_OUT), C_4E ** -0.5, 0.25)
    w_pool_4f = centred(part_splits[2], (C_4E, C3), C_4E ** -0.5, 0.25)
    w_mid_4f = centred(part_splits[3], (27, C1A, C1B), (27 * C1A) ** -0.5, 0.09375)
    w_small_4f = centred(part_splits[4], (27, C2A, C2B), (27 * C2A) ** -0.5, 0.21875)
    offsets_4f = centred(part_splits[5], (NOFF,), 0.5, 3.0, jnp.float32)
    w_in_5b = centred(part_splits[6], (C_IN, IN_OUT), C_IN ** -0.5, 0.21875)
    w_pool_5b = centred(part_splits[7], (C_IN, C3), C_IN ** -0.5, 0.21875)
    w_mid_5b = centred(part_splits[8], (27, C1A, C1B), (27 * C1A) ** -0.5, 0.09375)
    w_small_5b = centred(part_splits[9], (27, C2A, C2B), (27 * C2A) ** -0.5, 0.21875)
    offsets_5b = centred(part_splits[10], (NOFF,), 0.5, 3.0, jnp.float32)
    cotangent = draw_cotangent(jax.random.fold_in(jax.random.fold_in(splits[12], part), 71), part)
    return dict(features=features, w_in_4f=w_in_4f, w_pool_4f=w_pool_4f, w_mid_4f=w_mid_4f, w_small_4f=w_small_4f, offsets_4f=offsets_4f, w_in_5b=w_in_5b, w_pool_5b=w_pool_5b, w_mid_5b=w_mid_5b, w_small_5b=w_small_5b, offsets_5b=offsets_5b, cotangent=cotangent)


EPSILON = 0.001
HIGHEST_PRECISION = lax.Precision.HIGHEST

@jax.custom_vjp
def low(v):
    return lax.optimization_barrier(v.astype(jnp.bfloat16)).astype(jnp.float32)

@jax.custom_vjp
def low_back(v):
    return v

def low_keep(v):
    return (low(v), None)

def low_pass(kept, grad):
    return (grad,)

def back_keep(v):
    return (v, None)

def back_low(kept, grad):
    return (low(grad),)
low.defvjp(low_keep, low_pass)
low_back.defvjp(back_keep, back_low)

def project(values, weight):
    return jnp.einsum('nfhwc,cd->nfhwd', values, weight, precision=HIGHEST_PRECISION)

def box_mean(values):
    padded = jnp.pad(values, ((0, 0), (1, 1), (1, 1), (1, 1), (0, 0)))
    summed = padded[:, :-2] + padded[:, 1:-1] + padded[:, 2:]
    summed = summed[:, :, :-2] + summed[:, :, 1:-1] + summed[:, :, 2:]
    summed = summed[:, :, :, :-2] + summed[:, :, :, 1:-1] + summed[:, :, :, 2:]
    return summed / 27.0

def volume(values, weight):
    kernel = weight.reshape(3, 3, 3, weight.shape[1], weight.shape[2])
    return lax.conv_general_dilated(values, kernel, (1, 1, 1), ((1, 1), (1, 1), (1, 1)), dimension_numbers=('NDHWC', 'DHWIO', 'NDHWC'), precision=HIGHEST_PRECISION)

def normalize(pre_act, offsets):
    center = lax.optimization_barrier(jnp.mean(pre_act, axis=(0, 1, 2, 3)))
    variance = lax.optimization_barrier(jnp.mean(jnp.square(pre_act - center), axis=(0, 1, 2, 3)))
    return jax.nn.silu((pre_act - center) * lax.rsqrt(variance + EPSILON) + offsets)

def mixed_block(features, w_in, w_pool, w_mid, w_small, offsets):
    proj_in = low_back(project(features, w_in))
    pooled = low(box_mean(features))
    proj_pool = low_back(project(pooled, w_pool))
    hidden_a = normalize(jnp.concatenate([proj_in, proj_pool], axis=-1), offsets[:SECTION_A])
    middle = low(hidden_a[..., C0:IN_OUT])
    conv_one = low_back(volume(middle[..., :C1A], w_mid))
    conv_two = low_back(volume(middle[..., C1A:], w_small))
    hidden_b = normalize(jnp.concatenate([conv_one, conv_two], axis=-1), offsets[SECTION_A:])
    return jnp.concatenate([hidden_a[..., :C0], hidden_b, hidden_a[..., IN_OUT:]], axis=-1)

def halve_grid(values):
    n, f, h, w, c = values.shape
    return lax.optimization_barrier(jnp.mean(values.reshape(n, f // 2, 2, h // 2, 2, w // 2, 2, c), axis=(2, 4, 6)))

def forward(features, w_in_4f, w_pool_4f, w_mid_4f, w_small_4f, offsets_4f, w_in_5b, w_pool_5b, w_mid_5b, w_small_5b, offsets_5b):
    first_out = mixed_block(features, w_in_4f, w_pool_4f, w_mid_4f, w_small_4f, offsets_4f)
    second_in = low(halve_grid(first_out))
    return mixed_block(second_in, w_in_5b, w_pool_5b, w_mid_5b, w_small_5b, offsets_5b)

def reference(features, w_in_4f, w_pool_4f, w_mid_4f, w_small_4f, offsets_4f, w_in_5b, w_pool_5b, w_mid_5b, w_small_5b, offsets_5b, cotangent):
    primals = [value.astype(jnp.float32) for value in (features, w_in_4f, w_pool_4f, w_mid_4f, w_small_4f, offsets_4f, w_in_5b, w_pool_5b, w_mid_5b, w_small_5b, offsets_5b)]
    result, pullback = jax.vjp(forward, *primals)
    grads = pullback(cotangent.astype(jnp.float32))
    return (result.astype(jnp.bfloat16), grads[0], grads[1], grads[2], grads[3], grads[4], grads[5], grads[6], grads[7], grads[8], grads[9], grads[10])
```

```python
import functools

import jax
import jax.numpy as jnp
from jax import lax
from jax.experimental import pallas as pl
from jax.experimental.pallas import tpu as pltpu
from jax.sharding import PartitionSpec as P

C0 = 256
C1A = 160
C1B = 320
C2A = 32
C2B = 128
IN_OUT = 448
SECTION_A = 576


EPSILON = 0.001
VOXEL_AXES = (0, 1, 2, 3)


def extended(value, sides, width):
    for axis, dim in sides:
        size, length = (lax.axis_size(axis), value.shape[dim])
        up = [(i, (i + 1) % size) for i in range(size - 1)]
        down = [(j, i) for i, j in up]
        last = lax.slice_in_dim(value, length - width, length, axis=dim)
        first = lax.slice_in_dim(value, 0, width, axis=dim)
        before = lax.ppermute(last, axis, up)
        after = lax.ppermute(first, axis, down)
        value = jnp.concatenate([before, value, after], axis=dim)
    return value


def as_sent(value):
    return jax.tree.map(lambda a: a.astype(jnp.bfloat16) if a.dtype == jnp.float32 else a, value)


def project(values, weight):
    return jnp.einsum("nfhwc,cd->nfhwd", values, weight, preferred_element_type=jnp.float32)


def pad_plane(values):
    return jnp.pad(values, ((0, 0), (0, 0), (1, 1), (1, 1), (0, 0)))


def box_sum(padded):
    summed = padded[:, :-2] + padded[:, 1:-1] + padded[:, 2:]
    summed = summed[:, :, :-2] + summed[:, :, 1:-1] + summed[:, :, 2:]
    return summed[:, :, :, :-2] + summed[:, :, :, 1:-1] + summed[:, :, :, 2:]


def unfold(padded, frames, height, width):
    slices = []
    for shift_f in range(3):
        for shift_h in range(3):
            for shift_w in range(3):
                slices.append(
                    padded[
                        :,
                        shift_f : shift_f + frames,
                        shift_h : shift_h + height,
                        shift_w : shift_w + width,
                    ]
                )
    return jnp.concatenate(slices, axis=-1)


def fold_back(patch_grad, channels):
    summed = None
    offset_index = 0
    for shift_f in range(3):
        for shift_h in range(3):
            for shift_w in range(3):
                segment = patch_grad[..., offset_index * channels : (offset_index + 1) * channels]
                placed = jnp.pad(
                    segment,
                    (
                        (0, 0),
                        (shift_f, 2 - shift_f),
                        (shift_h, 2 - shift_h),
                        (shift_w, 2 - shift_w),
                        (0, 0),
                    ),
                )
                summed = placed if summed is None else summed + placed
                offset_index += 1
    return summed


def return_input_rims(grad_padded):
    interior = grad_padded[:, 1:-1]
    rim_pair = jnp.concatenate([grad_padded[:, :1], grad_padded[:, -1:]], axis=1)
    arrived = extended(rim_pair.astype(jnp.bfloat16), (("tm", 1),), 1).astype(rim_pair.dtype)
    interior = interior.at[:, 0].add(arrived[:, 0])
    return interior.at[:, -1].add(arrived[:, 3])


def return_hidden_rims(grad_padded):
    interior = grad_padded[:, 1:-1]
    rim_pair = jnp.concatenate([grad_padded[:, :1], grad_padded[:, -1:]], axis=1)
    arrived = extended(rim_pair.astype(jnp.bfloat16), (("tm", 1),), 1).astype(rim_pair.dtype)
    interior = interior.at[:, 0].add(arrived[:, 0])
    return interior.at[:, -1].add(arrived[:, 3])


def section_first(features, w_in, w_pool):
    rimmed = extended(features, (("tm", 1),), 1)
    padded = pad_plane(rimmed).astype(jnp.float32)
    pooled = (box_sum(padded) / 27.0).astype(jnp.bfloat16)
    pre_first = jnp.concatenate([project(features, w_in), project(pooled, w_pool)], axis=-1)
    return (pre_first, pooled)


def section_second(middle, w_mid, w_small):
    rimmed = extended(middle, (("tm", 1),), 1)
    padded = pad_plane(rimmed)
    frames, height, width = (middle.shape[1], middle.shape[2], middle.shape[3])
    patch_one = unfold(padded[..., :C1A], frames, height, width)
    patch_two = unfold(padded[..., C1A:], frames, height, width)
    pre_second = jnp.concatenate(
        [
            project(patch_one, w_mid.reshape(27 * C1A, C1B)),
            project(patch_two, w_small.reshape(27 * C2A, C2B)),
        ],
        axis=-1,
    )
    return (pre_second, patch_one, patch_two)


def moments(pre_act, voxel_count):
    first_sum = lax.psum(jnp.sum(pre_act, axis=VOXEL_AXES), ("clip", "tm"))
    center = first_sum / voxel_count
    spread = lax.psum(jnp.sum(jnp.square(pre_act - center), axis=VOXEL_AXES), ("clip", "tm"))
    variance = spread / voxel_count
    return (center, variance)


def standardize(pre_act, center, variance):
    return (pre_act - center) * lax.rsqrt(variance + EPSILON)


def silu_slope(act_in):
    sigmoid_value = jax.nn.sigmoid(act_in)
    return sigmoid_value + act_in * sigmoid_value * (1.0 - sigmoid_value)


def block_forward(features, params, voxel_count):
    w_in, w_pool, w_mid, w_small, offsets = params
    pre_first, pooled = section_first(features, w_in, w_pool)
    center_a, variance_a = moments(pre_first, voxel_count)
    hidden_a = jax.nn.silu(standardize(pre_first, center_a, variance_a) + offsets[:SECTION_A])
    middle = hidden_a[..., C0:IN_OUT].astype(jnp.bfloat16)
    pre_second, patch_one, patch_two = section_second(middle, w_mid, w_small)
    center_b, variance_b = moments(pre_second, voxel_count)
    hidden_b = jax.nn.silu(standardize(pre_second, center_b, variance_b) + offsets[SECTION_A:])
    block_out = jnp.concatenate([hidden_a[..., :C0], hidden_b, hidden_a[..., IN_OUT:]], axis=-1)
    return (block_out, (center_a, variance_a, center_b, variance_b))


def norm_back(slope_grad, normed, variance, voxel_count):
    sum_grad, sum_cross = lax.psum(
        (jnp.sum(slope_grad, axis=VOXEL_AXES), jnp.sum(slope_grad * normed, axis=VOXEL_AXES)),
        ("clip", "tm"),
    )
    scaled = lax.rsqrt(variance + EPSILON) * (
        slope_grad - sum_grad / voxel_count - normed * (sum_cross / voxel_count)
    )
    return (scaled.astype(jnp.bfloat16), sum_grad)


def block_backward(features, params, moment_pair, out_grad, voxel_count):
    w_in, w_pool, w_mid, w_small, offsets = params
    center_a, variance_a, center_b, variance_b = moment_pair
    pre_first, pooled = section_first(features, w_in, w_pool)
    normed_a = standardize(pre_first, center_a, variance_a)
    act_a = normed_a + offsets[:SECTION_A]
    middle = jax.nn.silu(act_a)[..., C0:IN_OUT].astype(jnp.bfloat16)
    pre_second, patch_one, patch_two = section_second(middle, w_mid, w_small)
    normed_b = standardize(pre_second, center_b, variance_b)
    act_b = normed_b + offsets[SECTION_A:]
    grad_b = out_grad[..., C0 : C0 + C1B + C2B] * silu_slope(act_b)
    error_b, offset_grad_b = norm_back(grad_b, normed_b, variance_b, voxel_count)
    error_one = error_b[..., :C1B]
    error_two = error_b[..., C1B:]
    grad_mid = jnp.einsum(
        "nfhwk,nfhwo->ko", patch_one, error_one, preferred_element_type=jnp.float32
    ).reshape(27, C1A, C1B)
    grad_small = jnp.einsum(
        "nfhwk,nfhwo->ko", patch_two, error_two, preferred_element_type=jnp.float32
    ).reshape(27, C2A, C2B)
    back_one = fold_back(
        jnp.einsum(
            "nfhwo,ko->nfhwk",
            error_one,
            w_mid.reshape(27 * C1A, C1B),
            preferred_element_type=jnp.float32,
        ),
        C1A,
    )
    back_two = fold_back(
        jnp.einsum(
            "nfhwo,ko->nfhwk",
            error_two,
            w_small.reshape(27 * C2A, C2B),
            preferred_element_type=jnp.float32,
        ),
        C2A,
    )
    middle_grad = return_hidden_rims(
        jnp.concatenate([back_one, back_two], axis=-1)[:, :, 1:-1, 1:-1]
    )
    grad_a = jnp.concatenate(
        [out_grad[..., :C0], middle_grad, out_grad[..., C0 + C1B + C2B :]], axis=-1
    ) * silu_slope(act_a)
    error_a, offset_grad_a = norm_back(grad_a, normed_a, variance_a, voxel_count)
    error_in = error_a[..., :IN_OUT]
    error_pool = error_a[..., IN_OUT:]
    grad_in = jnp.einsum("nfhwc,nfhwd->cd", features, error_in, preferred_element_type=jnp.float32)
    grad_pool = jnp.einsum(
        "nfhwc,nfhwd->cd", pooled, error_pool, preferred_element_type=jnp.float32
    )
    direct = jnp.einsum("nfhwd,cd->nfhwc", error_in, w_in, preferred_element_type=jnp.float32)
    pool_grad = jnp.einsum(
        "nfhwd,cd->nfhwc", error_pool, w_pool, preferred_element_type=jnp.float32
    )
    spread_pad = jnp.pad(pool_grad, ((0, 0), (2, 2), (2, 2), (2, 2), (0, 0)))
    padded_grad = (box_sum(spread_pad) / 27.0)[:, :, 1:-1, 1:-1]
    input_grad = direct + return_input_rims(padded_grad)
    return (
        input_grad,
        (grad_in, grad_pool, grad_mid, grad_small),
        jnp.concatenate([offset_grad_a, offset_grad_b]),
    )


def reduce_grads(weight_grads):
    summed = jax.tree.map(
        lambda part: part.astype(jnp.float32), lax.psum(as_sent(weight_grads), "clip")
    )
    reduced = (
        lax.psum_scatter(
            summed[0].astype(jnp.bfloat16), "tm", scatter_dimension=1, tiled=True
        ).astype(jnp.float32),
        lax.psum_scatter(
            summed[1].astype(jnp.bfloat16), "tm", scatter_dimension=1, tiled=True
        ).astype(jnp.float32),
        lax.psum_scatter(
            summed[2].astype(jnp.bfloat16), "tm", scatter_dimension=2, tiled=True
        ).astype(jnp.float32),
        lax.psum_scatter(
            summed[3].astype(jnp.bfloat16), "tm", scatter_dimension=2, tiled=True
        ).astype(jnp.float32),
    )
    return reduced


def halve_grid(values):
    n, f, h, w, c = values.shape
    return jnp.sum(values.reshape(n, f // 2, 2, h // 2, 2, w // 2, 2, c), axis=(2, 4, 6)) * 0.125


def spread_half(grad_small_grid):
    n, f, h, w, c = grad_small_grid.shape
    expanded = jnp.broadcast_to(
        (grad_small_grid * 0.125)[:, :, None, :, None, :, None, :], (n, f, 2, h, 2, w, 2, c)
    )
    return expanded.reshape(n, 2 * f, 2 * h, 2 * w, c)


def shards(
    features,
    w_in_4f,
    w_pool_4f,
    w_mid_4f,
    w_small_4f,
    offsets_4f,
    w_in_5b,
    w_pool_5b,
    w_mid_5b,
    w_small_5b,
    offsets_5b,
    cotangent,
):
    params_first = (w_in_4f, w_pool_4f, w_mid_4f, w_small_4f, offsets_4f)
    params_second = (w_in_5b, w_pool_5b, w_mid_5b, w_small_5b, offsets_5b)
    devices_used = lax.axis_size("clip") * lax.axis_size("tm")
    count_first = float(
        features.shape[0] * features.shape[1] * features.shape[2] * features.shape[3] * devices_used
    )
    count_second = count_first / 8.0
    out_first, moments_first = block_forward(features, params_first, count_first)
    input_second = halve_grid(out_first).astype(jnp.bfloat16)
    out_second, moments_second = block_forward(input_second, params_second, count_second)
    grad_second, weights_second, offsets_grad_second = block_backward(
        input_second, params_second, moments_second, cotangent.astype(jnp.float32), count_second
    )
    reduced_second = reduce_grads(weights_second)
    grad_first, weights_first, offsets_grad_first = block_backward(
        features, params_first, moments_first, spread_half(grad_second), count_first
    )
    reduced_first = reduce_grads(weights_first)
    final_out = out_second.astype(jnp.bfloat16)
    return (
        final_out,
        grad_first,
        reduced_first[0],
        reduced_first[1],
        reduced_first[2],
        reduced_first[3],
        offsets_grad_first,
        reduced_second[0],
        reduced_second[1],
        reduced_second[2],
        reduced_second[3],
        offsets_grad_second,
    )


F32 = jnp.float32
BF16 = jnp.bfloat16
MID = 192
BOUT = 448
POOL = 128
OUTC = 832
VMEM_LIMIT = 56 * 1024 * 1024


def dot_nn(a, b):
    return lax.dot_general(a, b, (((1,), (0,)), ((), ())), preferred_element_type=F32)


def dot_nt(a, b):
    return lax.dot_general(a, b, (((1,), (1,)), ((), ())), preferred_element_type=F32)


def roll_rows(value, shift):
    rows = value.shape[0]
    shift %= rows
    return value if shift == 0 else pltpu.roll(value, shift, 0)


def valid_first(rows):
    r = lax.broadcasted_iota(jnp.int32, (rows, 1), 0)
    return ((r & 255) < 224) & ((r & 15) < 14)


def valid_second(rows):
    r = lax.broadcasted_iota(jnp.int32, (rows, 1), 0)
    return ((r & 63) < 56) & ((r & 7) < 7)


def act(a):
    return a * jax.nn.sigmoid(a)


def slope(a):
    s = jax.nn.sigmoid(a)
    return s + a * s * (1.0 - s)


def pack_rows(vectors):
    pieces = []
    for v in vectors:
        width = v.shape[1]
        full = -(-width // 128) * 128
        if full != width:
            v = jnp.concatenate([v, jnp.zeros((1, full - width), F32)], axis=1)
        for i in range(full // 128):
            pieces.append(v[:, i * 128 : (i + 1) * 128])
    return jnp.concatenate(pieces, axis=0)


def unpack_rows(rows, start, width):
    count = -(-width // 128)
    return jnp.concatenate([rows[start + i : start + i + 1] for i in range(count)], axis=1)[
        :, :width
    ]


def store_copies(ref, rows):
    count, height = ref.shape[0], ref.shape[1]
    if rows.shape[0] < height:
        rows = jnp.concatenate([rows, jnp.zeros((height - rows.shape[0], 128), F32)], axis=0)
    for i in range(count):
        ref[i] = rows


def local_moments(value, mask, cells):
    total = jnp.sum(jnp.where(mask, value, 0.0), axis=0, keepdims=True)
    delta = jnp.where(mask, value - total * (1.0 / cells), 0.0)
    return total, jnp.sum(delta * delta, axis=0, keepdims=True)


def joint_moments(gathered, height, cells):
    devices = gathered.shape[0]
    sums, squares = gathered[:, :height], gathered[:, height : 2 * height]
    mean = jnp.sum(sums, axis=0) * (1.0 / (cells * devices))
    apart = sums * (1.0 / cells) - mean[None]
    spread = jnp.sum(squares, axis=0) + cells * jnp.sum(apart * apart, axis=0)
    return mean, lax.rsqrt(spread * (1.0 / (cells * devices)) + EPSILON)


def halve(total, scratch, dtype):
    width = total.shape[1]
    both = total[:256] + total[256:]
    pairs = jnp.sum(both.reshape(8, 2, 16, width), axis=1).reshape(128, width)
    pieces = []
    for i in range(-(-width // 128)):
        lanes = min(128, width - i * 128)
        scratch[i, :, :lanes] = pairs[:, i * 128 : i * 128 + lanes]
        piece = scratch[i, pl.ds(0, 64, 2), :] + scratch[i, pl.ds(1, 64, 2), :]
        pieces.append(piece[:, :lanes])
    halved = jnp.concatenate(pieces, axis=1)
    return (halved * 0.125).astype(dtype)


def box_plane(value, stride):
    value = value + roll_rows(value, stride) + roll_rows(value, -stride)
    return value + roll_rows(value, 1) + roll_rows(value, -1)


def first_project(x_ref, win_ref, wpool_ref, zin_ref, q_ref, st_ref, head_ref, tail_ref):
    for f in range(2):
        rows = pl.ds(f * 256, 256)
        x = x_ref[rows, :]
        zin_ref[rows, :] = dot_nn(x, win_ref[...])
        q_ref[rows, :] = dot_nn(x, wpool_ref[...])
    total, squares = local_moments(zin_ref[...], valid_first(512), 392)
    store_copies(st_ref, pack_rows([total, squares]))
    for f, ref in ((0, head_ref), (1, tail_ref)):
        rows = pl.ds(f * 256, 256)
        ref[:, :MID] = zin_ref[rows, C0:].astype(BF16)
        ref[:, MID:] = q_ref[rows, :].astype(BF16)


def first_hidden(
    flag_ref, st_ref, zin_ref, q_ref, before_ref, after_ref, wmid_ref, wsmall_ref, off_ref,
    zb_ref, zp_ref, st2_ref, x2_ref, um_ref, us_ref, head_ref, tail_ref, ma_ref,
    mid, half,
):
    mean_rows, scale_rows = joint_moments(st_ref[...], 4, 392.0)
    mean, scale = unpack_rows(mean_rows, 0, IN_OUT), unpack_rows(scale_rows, 0, IN_OUT)
    ma_ref[...] = jnp.concatenate([mean, scale], axis=0)
    off = off_ref[:, :IN_OUT]
    frame = valid_first(256)
    prev, after = flag_ref[1] > 0, flag_ref[2] > 0

    def middle(z, mask):
        return jnp.where(mask, act((z - mean[:, C0:]) * scale[:, C0:] + off[:, C0:]), 0.0)

    mid[0:256, :] = middle(before_ref[:, :MID].astype(F32), frame & prev)
    mid[256:512, :] = middle(zin_ref[0:256, C0:], frame)
    mid[512:768, :] = middle(zin_ref[256:512, C0:], frame)
    mid[768:1024, :] = middle(after_ref[:, :MID].astype(F32), frame & after)
    for ref in (um_ref, us_ref):
        edge = jnp.zeros((16, ref.shape[1]), BF16)
        ref[0:16, :] = edge
        ref[1040:1056, :] = edge

    for f in range(4):
        rows = slice(f * 256, (f + 1) * 256)
        shifted = [roll_rows(mid[rows, :], 1 - g) for g in range(3)]
        into = slice(16 + f * 256, 16 + (f + 1) * 256)
        um_ref[into, :] = jnp.concatenate([v[:, :C1A] for v in shifted], axis=1).astype(BF16)
        us_ref[into, :] = jnp.concatenate([v[:, C1A:] for v in shifted], axis=1).astype(BF16)

    def convolve(u_ref, w_ref, base):
        total = None
        for a in range(3):
            for e in range(3):
                start = base + 16 + a * 256 + (e - 1) * 16
                term = dot_nn(u_ref[start : start + 256, :], w_ref[3 * a + e])
                total = term if total is None else total + term
        return total

    for f in range(2):
        rows = pl.ds(f * 256, 256)
        zb_ref[rows, :C1B] = convolve(um_ref, wmid_ref, f * 256)
        zb_ref[rows, C1B:] = convolve(us_ref, wsmall_ref, f * 256)

    first, last = q_ref[0:256, :], q_ref[256:512, :]
    pair = first + last
    for f, value in (
        (0, pair + before_ref[:, MID:].astype(F32)),
        (1, pair + after_ref[:, MID:].astype(F32)),
    ):
        value = box_plane(value, 16) * (1.0 / 27.0)
        zp_ref[f * 256 : (f + 1) * 256, :] = jnp.where(frame, value, 0.0)

    both = valid_first(512)
    total_b, squares_b = local_moments(zb_ref[...], both, 392)
    total_p, squares_p = local_moments(zp_ref[...], both, 392)
    store_copies(st2_ref, pack_rows([total_b, total_p, squares_b, squares_p]))
    for f, ref in ((0, head_ref), (1, tail_ref)):
        rows = pl.ds(f * 256, 256)
        ref[:, :BOUT] = zb_ref[rows, :].astype(BF16)
        ref[:, BOUT:] = zp_ref[rows, :].astype(BF16)
    hidden = act((zin_ref[:, :C0] - mean[:, :C0]) * scale[:, :C0] + off[:, :C0])
    x2_ref[...] = halve(jnp.where(both, hidden, 0.0), half, BF16)


def first_output(st_ref, zb_ref, zp_ref, off_ref, x2_ref, mb_ref, half):
    mean_rows, scale_rows = joint_moments(st_ref[...], 5, 392.0)
    both = valid_first(512)
    moments = []
    for start, width, z_ref, offset in ((0, BOUT, zb_ref, SECTION_A), (4, POOL, zp_ref, IN_OUT)):
        mean, scale = unpack_rows(mean_rows, start, width), unpack_rows(scale_rows, start, width)
        hidden = act((z_ref[...] - mean) * scale + off_ref[:, offset : offset + width])
        into = slice(0, BOUT) if start == 0 else slice(BOUT, BOUT + POOL)
        x2_ref[:, into] = halve(jnp.where(both, hidden, 0.0), half, BF16)
        moments.append(jnp.concatenate([mean, scale], axis=0))
    mb_ref[...] = jnp.concatenate(moments, axis=1)


def second_layer(
    clips, frames, flag_ref, x0_ref, x1_ref, cot_ref, win_ref, wpool_ref, wmid_ref, wsmall_ref,
    off_ref,
    out_ref, dx_ref, gin_ref, gpool_ref, gmid_ref, gsmall_ref, goff_ref,
    xs, cs, za, zb, um, us, qs, eb, ea, et, eat, da,
):
    here = flag_ref[0]
    span = frames * 64
    slot = (frames + 1) * 64
    cells = clips * frames * 49.0
    wide = clips * slot
    part_mid, part_small = gmid_ref.shape[2], gsmall_ref.shape[2]
    part_in, part_pool = gin_ref.shape[0], gpool_ref.shape[0]
    mask = valid_second(span)

    for c in range(clips):
        for m in range(frames):
            frame = lax.rem(here + m, frames)
            rows = pl.ds(pl.multiple_of(c * span + frame * 64, 64), 64)
            xs[rows, :C0] = x0_ref[c * frames + m]
            xs[rows, C0:] = x1_ref[c * frames + m]
            cs[rows, :] = cot_ref[c * frames + m]
    for ref in (um, us, qs, eb, ea):
        blank = jnp.zeros((64, ref.shape[1]), ref.dtype)
        for c in range(clips + 1):
            ref[c * slot : c * slot + 64, :] = blank
        ref[wide + 64 : wide + 128, :] = blank

    def rows_of(c):
        return pl.ds(pl.multiple_of(c * span, 64), span)

    def slots_of(c, shift=1):
        return pl.ds(pl.multiple_of(c * slot + shift * 64, 64), span)

    def over_clips(body, init):
        return lax.fori_loop(0, clips, body, init)

    def box(c):
        value = qs[slots_of(c, 0), :] + qs[slots_of(c, 1), :] + qs[slots_of(c, 2), :]
        return jnp.where(mask, box_plane(value, 8) * (1.0 / 27.0), 0.0)

    def project_clip(c, total):
        x = xs[rows_of(c), :]
        z = dot_nn(x, win_ref[...])
        za[rows_of(c), :IN_OUT] = z
        qs[slots_of(c), :] = dot_nn(x, wpool_ref[...])
        p = box(c)
        za[rows_of(c), IN_OUT:] = p
        return total + jnp.concatenate(
            [jnp.sum(z, axis=0, keepdims=True), jnp.sum(p, axis=0, keepdims=True)], axis=1
        )

    total_a = over_clips(project_clip, jnp.zeros((1, SECTION_A), F32))
    mean_a = total_a * (1.0 / cells)

    def spread_clip(ref, mean):
        def body(c, total):
            delta = jnp.where(mask, ref[rows_of(c), :] - mean, 0.0)
            return total + jnp.sum(delta * delta, axis=0, keepdims=True)

        return body

    spread_a = over_clips(spread_clip(za, mean_a), jnp.zeros((1, SECTION_A), F32))
    scale_a = lax.rsqrt(spread_a * (1.0 / cells) + EPSILON)
    off_a, off_b = off_ref[:, :SECTION_A], off_ref[:, SECTION_A:]

    def normal_a(c, lo, hi):
        return (za[rows_of(c), lo:hi] - mean_a[:, lo:hi]) * scale_a[:, lo:hi]

    def unfold_clip(c, _):
        a = normal_a(c, C0, IN_OUT) + off_a[:, C0:IN_OUT]
        hidden = jnp.where(mask, act(a), 0.0)
        shifted = []
        for e in range(3):
            row = roll_rows(hidden, 8 * (1 - e))
            shifted += [roll_rows(row, 1 - g) for g in range(3)]
        um[slots_of(c), :] = jnp.concatenate([v[:, :C1A] for v in shifted], axis=1).astype(BF16)
        us[slots_of(c), :] = jnp.concatenate([v[:, C1A:] for v in shifted], axis=1).astype(BF16)
        return 0

    over_clips(unfold_clip, 0)

    def convolve_clip(c, total):
        mids, smalls = None, None
        for a in range(3):
            one = dot_nn(um[slots_of(c, a), :], wmid_ref[a])
            two = dot_nn(us[slots_of(c, a), :], wsmall_ref[a])
            mids = one if mids is None else mids + one
            smalls = two if smalls is None else smalls + two
        z = jnp.concatenate([mids, smalls], axis=1)
        zb[rows_of(c), :] = z
        return total + jnp.sum(jnp.where(mask, z, 0.0), axis=0, keepdims=True)

    total_b = over_clips(convolve_clip, jnp.zeros((1, BOUT), F32))
    mean_b = total_b * (1.0 / cells)
    spread_b = over_clips(spread_clip(zb, mean_b), jnp.zeros((1, BOUT), F32))
    scale_b = lax.rsqrt(spread_b * (1.0 / cells) + EPSILON)

    own = pl.ds(pl.multiple_of(here * 64, 64), 64)
    hidden_a = act((za[own, :] - mean_a) * scale_a + off_a)
    hidden_b = act((zb[own, :] - mean_b) * scale_b + off_b)
    out_ref[...] = jnp.concatenate(
        [hidden_a[:, :C0], hidden_b, hidden_a[:, IN_OUT:]], axis=1
    ).astype(BF16)

    def grad_b(c):
        y = (zb[rows_of(c), :] - mean_b) * scale_b
        d = cs[rows_of(c), C0 : C0 + BOUT].astype(F32) * slope(y + off_b)
        return d, y

    def sums_b(c, carry):
        d, y = grad_b(c)
        return (
            carry[0] + jnp.sum(d, axis=0, keepdims=True),
            carry[1] + jnp.sum(d * y, axis=0, keepdims=True),
        )

    zero_b = jnp.zeros((1, BOUT), F32)
    sum_b, cross_b = over_clips(sums_b, (zero_b, zero_b))

    def error_b(c, _):
        d, y = grad_b(c)
        e = scale_b * (d - sum_b * (1.0 / cells) - y * (cross_b * (1.0 / cells)))
        eb[slots_of(c), :] = jnp.where(mask, e, 0.0).astype(BF16)
        return 0

    over_clips(error_b, 0)

    def picker(rows, cut, part_one, part_two, columns, edge):
        r = lax.broadcasted_iota(jnp.int32, (rows, columns), 0)
        k = lax.broadcasted_iota(jnp.int32, (rows, columns), 1)
        want = jnp.where(r < cut, here * part_one + r, edge + here * part_two + r - cut)
        return jnp.where(k == want, 1.0, 0.0).astype(BF16)

    pick_b = picker(part_mid + part_small, part_mid, part_mid, part_small, BOUT, C1B)
    et[...] = dot_nt(pick_b, eb[64 : 64 + wide, :]).astype(BF16)
    for a in range(3):
        gm = dot_nn(et[:part_mid, :], um[a * 64 : a * 64 + wide, :])
        gmid_ref[9 * a : 9 * a + 9] = gm.T.reshape(9, C1A, part_mid)
        gs = dot_nn(et[part_mid:, :], us[a * 64 : a * 64 + wide, :])
        gsmall_ref[9 * a : 9 * a + 9] = gs.T.reshape(9, C2A, part_small)

    def grad_a(c, carry):
        mids, smalls = None, None
        for a in range(3):
            one = dot_nt(eb[slots_of(c, 2 - a), :C1B], wmid_ref[a])
            two = dot_nt(eb[slots_of(c, 2 - a), C1B:], wsmall_ref[a])
            mids = one if mids is None else mids + one
            smalls = two if smalls is None else smalls + two
        back = None
        for e in range(3):
            for g in range(3):
                k = 3 * e + g
                t = jnp.concatenate(
                    [mids[:, k * C1A : (k + 1) * C1A], smalls[:, k * C2A : (k + 1) * C2A]], axis=1
                )
                t = roll_rows(t, 8 * (e - 1) + g - 1)
                back = t if back is None else back + t
        y = normal_a(c, 0, SECTION_A)
        gain = slope(y + off_a)
        cot = cs[rows_of(c), :]
        d = jnp.concatenate([cot[:, :C0].astype(F32), back, cot[:, C0 + BOUT :].astype(F32)], axis=1)
        d = jnp.where(mask, d * gain, 0.0)
        da[rows_of(c), :] = d
        return (
            carry[0] + jnp.sum(d, axis=0, keepdims=True),
            carry[1] + jnp.sum(d * y, axis=0, keepdims=True),
        )

    zero_a = jnp.zeros((1, SECTION_A), F32)
    sum_a, cross_a = over_clips(grad_a, (zero_a, zero_a))
    goff_ref[...] = jnp.concatenate([sum_a, sum_b], axis=1)

    def error_a(c, _):
        y = normal_a(c, 0, SECTION_A)
        e = scale_a * (da[rows_of(c), :] - sum_a * (1.0 / cells) - y * (cross_a * (1.0 / cells)))
        e = jnp.where(mask, e, 0.0)
        ea[slots_of(c), :IN_OUT] = e[:, :IN_OUT].astype(BF16)
        qs[slots_of(c), :] = e[:, IN_OUT:].astype(BF16).astype(F32)
        ea[slots_of(c), IN_OUT:] = box(c).astype(BF16)
        return 0

    over_clips(error_a, 0)

    around = pl.ds(pl.multiple_of(here * 64, 64), 192)
    dx_ref[...] = dot_nt(ea[around, :IN_OUT], win_ref[...]) + dot_nt(
        ea[around, IN_OUT:], wpool_ref[...]
    )
    pick_a = picker(part_in + part_pool, part_in, part_in, part_pool, SECTION_A, IN_OUT)
    for c in range(clips):
        errors = ea[c * slot + 64 : c * slot + 64 + span, :]
        eat[:, c * span : (c + 1) * span] = dot_nt(pick_a, errors).astype(BF16)
    gin_ref[...] = dot_nn(eat[:part_in, :], xs[...])
    gpool_ref[...] = dot_nn(eat[part_in:, :], xs[...])


def first_errors(
    flag_ref, dx_ref, zb_ref, zp_ref, zin_ref, before_ref, after_ref, ma_ref, mb_ref, off_ref,
    db_ref, yb_ref, dp_ref, yp_ref, dc_ref, st_ref,
):
    r = lax.broadcasted_iota(jnp.int32, (256, 64), 0)
    k = lax.broadcasted_iota(jnp.int32, (256, 64), 1)
    spread = jnp.where(k == ((r >> 5) << 3) + ((r & 15) >> 1), 1.0, 0.0).astype(BF16)

    def frame_grad(f):
        d = dx_ref[f * 64 : (f + 1) * 64, :] * 0.125
        high = d.astype(BF16)
        low = (d - high.astype(F32)).astype(BF16)
        return dot_nn(spread, high) + dot_nn(spread, low)

    mean_b, scale_b = mb_ref[0:1, :], mb_ref[1:2, :]
    off_b, off_p = off_ref[:, SECTION_A:], off_ref[:, IN_OUT:SECTION_A]
    zero_b, zero_p = jnp.zeros((1, BOUT), F32), jnp.zeros((1, POOL), F32)
    sums = [zero_b, zero_p, jnp.zeros((1, C0), F32)]
    crosses = list(sums)

    def add(i, d, y):
        sums[i] = sums[i] + jnp.sum(d, axis=0, keepdims=True)
        crosses[i] = crosses[i] + jnp.sum(d * y, axis=0, keepdims=True)

    grads = [frame_grad(f) for f in range(3)]
    for s in range(4):
        rows = slice(s * 256, (s + 1) * 256)
        if s == 0:
            z_b, z_p = before_ref[:, :BOUT].astype(F32), before_ref[:, BOUT:].astype(F32)
        elif s == 3:
            z_b, z_p = after_ref[:, :BOUT].astype(F32), after_ref[:, BOUT:].astype(F32)
        else:
            inner = slice((s - 1) * 256, s * 256)
            z_b, z_p = zb_ref[inner, :], zp_ref[inner, :]
        g = grads[(s + 1) // 2]
        y_b = (z_b - mean_b[:, :BOUT]) * scale_b[:, :BOUT]
        d_b = g[:, C0 : C0 + BOUT] * slope(y_b + off_b)
        y_p = (z_p - mean_b[:, BOUT:]) * scale_b[:, BOUT:]
        d_p = g[:, C0 + BOUT :] * slope(y_p + off_p)
        db_ref[rows, :], yb_ref[rows, :] = d_b, y_b
        dp_ref[rows, :], yp_ref[rows, :] = d_p, y_p
        if s in (1, 2):
            add(0, d_b, y_b)
            add(1, d_p, y_p)
            y_c = (zin_ref[inner, :C0] - ma_ref[0:1, :C0]) * ma_ref[1:2, :C0]
            d_c = g[:, :C0] * slope(y_c + off_ref[:, :C0])
            dc_ref[inner, :] = d_c
            add(2, d_c, y_c)
    store_copies(st_ref, pack_rows(sums + crosses))


def first_hidden_back(
    cells, flag_ref, st_ref, db_ref, yb_ref, zin_ref, ma_ref, mb_ref, off_ref, um_ref, us_ref,
    wmid_ref, wsmall_ref,
    dm_ref, st2_ref, sum_ref, gmid_ref, gsmall_ref,
    eb, etm, ets,
):
    here = flag_ref[0]
    parts = gmid_ref.shape[0]
    part_mid, part_small = gmid_ref.shape[2], gsmall_ref.shape[2]
    totals = jnp.sum(st_ref[...], axis=0)
    sum_ref[...] = totals
    sum_b, cross_b = unpack_rows(totals, 0, BOUT), unpack_rows(totals, 7, BOUT)
    scale_b = mb_ref[1:2, :BOUT]
    frame = valid_first(256)
    edge = jnp.zeros((16, BOUT), BF16)
    eb[0:16, :] = edge
    eb[1040:1056, :] = edge
    for s in range(4):
        rows = slice(s * 256, (s + 1) * 256)
        e = scale_b * (
            db_ref[rows, :] - sum_b * (1.0 / cells) - yb_ref[rows, :] * (cross_b * (1.0 / cells))
        )
        mask = frame
        if s == 0:
            mask = frame & (flag_ref[1] > 0)
        elif s == 3:
            mask = frame & (flag_ref[2] > 0)
        eb[16 + s * 256 : 16 + (s + 1) * 256, :] = jnp.where(mask, e, 0.0).astype(BF16)

    sums, crosses = jnp.zeros((1, MID), F32), jnp.zeros((1, MID), F32)
    for f in range(2):
        mids, smalls = None, None
        for a in range(3):
            for e in range(3):
                start = 16 + 256 * (f + 1) - (a - 1) * 256 - (e - 1) * 16
                one = dot_nt(eb[start : start + 256, :C1B], wmid_ref[3 * a + e])
                two = dot_nt(eb[start : start + 256, C1B:], wsmall_ref[3 * a + e])
                mids = one if mids is None else mids + one
                smalls = two if smalls is None else smalls + two
        back = None
        for g in range(3):
            t = jnp.concatenate(
                [mids[:, g * C1A : (g + 1) * C1A], smalls[:, g * C2A : (g + 1) * C2A]], axis=1
            )
            t = roll_rows(t, g - 1)
            back = t if back is None else back + t
        rows = slice(f * 256, (f + 1) * 256)
        y = (zin_ref[rows, C0:] - ma_ref[0:1, C0:]) * ma_ref[1:2, C0:]
        d = jnp.where(frame, back * slope(y + off_ref[:, C0:IN_OUT]), 0.0)
        dm_ref[rows, :] = d
        sums = sums + jnp.sum(d, axis=0, keepdims=True)
        crosses = crosses + jnp.sum(d * y, axis=0, keepdims=True)
    store_copies(st2_ref, pack_rows([sums, crosses]))

    def eye(n):
        r = lax.broadcasted_iota(jnp.int32, (n, n), 0)
        k = lax.broadcasted_iota(jnp.int32, (n, n), 1)
        return jnp.where(r == k, 1.0, 0.0).astype(BF16)

    etm[...] = dot_nt(eye(C1B), eb[272:784, :C1B]).astype(BF16)
    ets[...] = dot_nt(eye(C2B), eb[272:784, C1B:]).astype(BF16)
    for a in range(3):
        for e in range(3):
            start = 16 + a * 256 + (e - 1) * 16
            gm = dot_nn(etm[...], um_ref[start : start + 512, :]).astype(BF16)
            gs = dot_nn(ets[...], us_ref[start : start + 512, :]).astype(BF16)
            for p in range(parts):
                to = lax.rem(p - here + parts, parts)
                gmid_ref[to, 3 * a + e] = gm[p * part_mid : (p + 1) * part_mid]
                gsmall_ref[to, 3 * a + e] = gs[p * part_small : (p + 1) * part_small]


def first_input_back(
    cells, flag_ref, st_ref, sum_ref, dm_ref, dc_ref, dp_ref, yp_ref, zin_ref, ma_ref, mb_ref,
    x_ref, win_ref, wpool_ref,
    dx_ref, g_ref, goff_ref,
    ea,
):
    here = flag_ref[0]
    parts = g_ref.shape[0]
    part_in, part_pool = IN_OUT // parts, POOL // parts
    totals = jnp.sum(st_ref[...], axis=0)
    before = sum_ref[...]
    sum_m, cross_m = unpack_rows(totals, 0, MID), unpack_rows(totals, 2, MID)
    sum_b = unpack_rows(before, 0, BOUT)
    sum_p, sum_c = unpack_rows(before, 4, POOL), unpack_rows(before, 5, C0)
    cross_p, cross_c = unpack_rows(before, 11, POOL), unpack_rows(before, 12, C0)
    goff_ref[...] = jnp.concatenate([sum_c, sum_m, sum_p, sum_b], axis=1)
    share = 1.0 / cells
    frame = valid_first(256)
    pools = []
    for s in range(4):
        rows = slice(s * 256, (s + 1) * 256)
        e = mb_ref[1:2, BOUT:] * (
            dp_ref[rows, :] - sum_p * share - yp_ref[rows, :] * (cross_p * share)
        )
        mask = frame
        if s == 0:
            mask = frame & (flag_ref[1] > 0)
        elif s == 3:
            mask = frame & (flag_ref[2] > 0)
        pools.append(jnp.where(mask, e, 0.0).astype(BF16).astype(F32))
    for f in range(2):
        rows = slice(f * 256, (f + 1) * 256)
        value = box_plane(pools[f] + pools[f + 1] + pools[f + 2], 16) * (1.0 / 27.0)
        ea[rows, IN_OUT:] = jnp.where(frame, value, 0.0).astype(BF16)
        y = (zin_ref[rows, :] - ma_ref[0:1, :]) * ma_ref[1:2, :]
        e = ma_ref[1:2, :C0] * (dc_ref[rows, :] - sum_c * share - y[:, :C0] * (cross_c * share))
        ea[rows, :C0] = jnp.where(frame, e, 0.0).astype(BF16)
        e = ma_ref[1:2, C0:] * (dm_ref[rows, :] - sum_m * share - y[:, C0:] * (cross_m * share))
        ea[rows, C0:IN_OUT] = jnp.where(frame, e, 0.0).astype(BF16)
        dx_ref[rows, :] = dot_nt(ea[rows, :IN_OUT], win_ref[...]) + dot_nt(
            ea[rows, IN_OUT:], wpool_ref[...]
        )
    r = lax.broadcasted_iota(jnp.int32, (SECTION_A, SECTION_A), 0)
    k = lax.broadcasted_iota(jnp.int32, (SECTION_A, SECTION_A), 1)
    eye = jnp.where(r == k, 1.0, 0.0).astype(BF16)
    turned = dot_nt(eye, ea[...]).astype(BF16)
    g = dot_nn(turned, x_ref[...]).astype(BF16)
    for p in range(parts):
        to = lax.rem(p - here + parts, parts)
        g_ref[to, :part_in] = g[p * part_in : (p + 1) * part_in]
        g_ref[to, part_in:] = g[IN_OUT + p * part_pool : IN_OUT + (p + 1) * part_pool]


def call(body, outs, scratch, *args, scalars=1):
    in_specs = [pl.BlockSpec(memory_space=pltpu.SMEM)] * scalars
    in_specs += [pl.BlockSpec(memory_space=pltpu.VMEM)] * (len(args) - scalars)
    return pl.pallas_call(
        body,
        out_shape=[jax.ShapeDtypeStruct(s, d) for s, d in outs],
        in_specs=in_specs,
        out_specs=[pl.BlockSpec(memory_space=pltpu.VMEM)] * len(outs),
        scratch_shapes=[pltpu.VMEM(s, d) for s, d in scratch],
        compiler_params=pltpu.CompilerParams(vmem_limit_bytes=VMEM_LIMIT),
    )(*args)


def exchange(copies):
    return lax.all_to_all(copies, ("clip", "tm"), 0, 0)


def neighbours(head, tail):
    size = lax.axis_size("tm")
    up = [(i, i + 1) for i in range(size - 1)]
    down = [(i + 1, i) for i in range(size - 1)]
    return lax.ppermute(tail, "tm", up), lax.ppermute(head, "tm", down)


def gather_from(value, axis):
    size = lax.axis_size(axis)
    blocks = [value]
    for m in range(1, size):
        blocks.append(lax.ppermute(value, axis, [((i + m) % size, i) for i in range(size)]))
    return jnp.stack(blocks)


def gather_stream(value):
    by_clip = gather_from(value, "clip")
    both = gather_from(by_clip, "tm")
    return jnp.swapaxes(both, 0, 1).reshape((-1,) + value.shape)


def scatter_sum(chunks):
    size = lax.axis_size("tm")
    total = chunks[0].astype(F32)
    for m in range(1, size):
        sent = lax.ppermute(chunks[m], "tm", [(i, (i + m) % size) for i in range(size)])
        total = total + sent.astype(F32)
    return lax.psum(total.astype(BF16), "clip").astype(F32)


def small_group(
    features, w_in_4f, w_pool_4f, w_mid_4f, w_small_4f, offsets_4f,
    w_in_5b, w_pool_5b, w_mid_5b, w_small_5b, offsets_5b, cotangent,
):
    clips, frames = lax.axis_size("clip"), lax.axis_size("tm")
    group = clips * frames
    cells = 392.0 * group
    here = lax.axis_index("tm")
    flags = jnp.stack([here, here > 0, here < frames - 1]).astype(jnp.int32)
    offsets_4f, offsets_5b = offsets_4f[None], offsets_5b[None]
    x = jnp.pad(features[0], ((0, 0), (0, 2), (0, 2), (0, 0))).reshape(512, features.shape[-1])
    cot = jnp.pad(cotangent[0, 0], ((0, 1), (0, 1), (0, 0))).reshape(64, OUTC)
    mid_4f, small_4f = w_mid_4f.reshape(9, 3 * C1A, C1B), w_small_4f.reshape(9, 3 * C2A, C2B)
    mid_5b, small_5b = w_mid_5b.reshape(3, 9 * C1A, C1B), w_small_5b.reshape(3, 9 * C2A, C2B)

    z_in, q, stats, head, tail = call(
        first_project,
        [((512, IN_OUT), F32), ((512, POOL), F32), ((group, 8, 128), F32),
         ((256, MID + POOL), BF16), ((256, MID + POOL), BF16)],
        [], x, w_in_4f, w_pool_4f, scalars=0,
    )
    before, after = neighbours(head, tail)
    stats = exchange(stats)
    z_b, z_p, stats, x2_c, u_mid, u_small, head, tail, moments_a = call(
        first_hidden,
        [((512, BOUT), F32), ((512, POOL), F32), ((group, 16, 128), F32), ((64, C0), BF16),
         ((1056, 3 * C1A), BF16), ((1056, 3 * C2A), BF16),
         ((256, BOUT + POOL), BF16), ((256, BOUT + POOL), BF16), ((2, IN_OUT), F32)],
        [((1024, MID), F32), ((4, 128, 128), F32)],
        flags, stats, z_in, q, before, after, mid_4f, small_4f, offsets_4f,
    )
    before, after = neighbours(head, tail)
    x2_c = gather_stream(x2_c)
    stats = exchange(stats)
    x2_b, moments_b = call(
        first_output,
        [((64, BOUT + POOL), BF16), ((2, BOUT + POOL), F32)],
        [((4, 128, 128), F32)],
        stats, z_b, z_p, offsets_4f, scalars=0,
    )
    x2_b = gather_stream(x2_b)
    cot = gather_stream(cot)
    rows, slots = group * 64, (clips * (frames + 1) + 2) * 64
    wide = clips * (frames + 1) * 64
    part = (C1B // frames, C2B // frames, IN_OUT // frames, POOL // frames)
    out, dx2, g_in_5b, g_pool_5b, g_mid_5b, g_small_5b, g_off_5b = call(
        functools.partial(second_layer, clips, frames),
        [((64, OUTC), BF16), ((192, OUTC), F32), ((part[2], OUTC), F32), ((part[3], OUTC), F32),
         ((27, C1A, part[0]), F32), ((27, C2A, part[1]), F32), ((1, 1024), F32)],
        [((rows, OUTC), BF16), ((rows, OUTC), BF16), ((rows, SECTION_A), F32), ((rows, BOUT), F32),
         ((slots, 9 * C1A), BF16), ((slots, 9 * C2A), BF16), ((slots, POOL), F32),
         ((slots, BOUT), BF16), ((slots, SECTION_A), BF16), ((part[0] + part[1], wide), BF16),
         ((part[2] + part[3], rows), BF16), ((rows, SECTION_A), F32)],
        flags, x2_c, x2_b, cot, w_in_5b, w_pool_5b, mid_5b, small_5b, offsets_5b,
    )
    d_b, y_b, d_p, y_p, d_c, stats = call(
        first_errors,
        [((1024, BOUT), F32), ((1024, BOUT), F32), ((1024, POOL), F32), ((1024, POOL), F32),
         ((512, C0), F32), ((group, 16, 128), F32)],
        [], flags, dx2, z_b, z_p, z_in, before, after, moments_a, moments_b, offsets_4f,
    )
    stats = exchange(stats)
    d_m, stats, sums, g_mid, g_small = call(
        functools.partial(first_hidden_back, cells),
        [((512, MID), F32), ((group, 8, 128), F32), ((16, 128), F32),
         ((frames, 9, part[0], 3 * C1A), BF16), ((frames, 9, part[1], 3 * C2A), BF16)],
        [((1056, BOUT), BF16), ((C1B, 512), BF16), ((C2B, 512), BF16)],
        flags, stats, d_b, y_b, z_in, moments_a, moments_b, offsets_4f, u_mid, u_small,
        mid_4f, small_4f,
    )
    g_mid, g_small = scatter_sum(g_mid), scatter_sum(g_small)
    stats = exchange(stats)
    d_x, g_a, g_off = call(
        functools.partial(first_input_back, cells),
        [((512, features.shape[-1]), F32), ((frames, part[2] + part[3], features.shape[-1]), BF16),
         ((1, 1024), F32)],
        [((512, SECTION_A), BF16)],
        flags, stats, sums, d_m, d_c, d_p, y_p, z_in, moments_a, moments_b, x, w_in_4f, w_pool_4f,
    )
    g_a = scatter_sum(g_a)

    def offsets_first(g, inner, outer):
        return jnp.transpose(g.reshape(9, outer, 3, inner), (0, 2, 3, 1)).reshape(27, inner, outer)

    return (
        out.reshape(1, 1, 8, 8, OUTC)[:, :, :7, :7],
        d_x.reshape(1, 2, 16, 16, -1)[:, :, :14, :14],
        g_a[: part[2]].T,
        g_a[part[2] :].T,
        offsets_first(g_mid, C1A, part[0]),
        offsets_first(g_small, C2A, part[1]),
        g_off[0],
        g_in_5b.T,
        g_pool_5b.T,
        g_mid_5b,
        g_small_5b,
        g_off_5b[0],
    )


def solution(mesh):
    placed = (
        P(("stream", "clip"), "tm", None, None, None),
        P("stream", None),
        P("stream", None),
        P("stream", None, None),
        P("stream", None, None),
        P("stream"),
        P("stream", None),
        P("stream", None),
        P("stream", None, None),
        P("stream", None, None),
        P("stream"),
        P(("stream", "clip"), "tm", None, None, None),
    )
    group = mesh.shape["clip"] * mesh.shape["tm"]
    return jax.shard_map(
        small_group if group <= 16 else shards,
        mesh=mesh,
        in_specs=placed,
        out_specs=(
            P(("stream", "clip"), "tm", None, None, None),
            P(("stream", "clip"), "tm", None, None, None),
            P("stream", "tm"),
            P("stream", "tm"),
            P("stream", None, "tm"),
            P("stream", None, "tm"),
            P("stream"),
            P("stream", "tm"),
            P("stream", "tm"),
            P("stream", None, "tm"),
            P("stream", None, "tm"),
            P("stream"),
        ),
        check_vma=False,
    )
```

```python
import functools

import jax
import jax.numpy as jnp
from jax import lax
from jax.experimental import pallas as pl
from jax.experimental.pallas import tpu as pltpu
from jax.sharding import PartitionSpec as P

C0 = 256
C1A = 160
C1B = 320
C2A = 32
C2B = 128
IN_OUT = 448
SECTION_A = 576


EPSILON = 0.001
VOXEL_AXES = (0, 1, 2, 3)


def extended(value, sides, width):
    for axis, dim in sides:
        size, length = (lax.axis_size(axis), value.shape[dim])
        up = [(i, (i + 1) % size) for i in range(size - 1)]
        down = [(j, i) for i, j in up]
        last = lax.slice_in_dim(value, length - width, length, axis=dim)
        first = lax.slice_in_dim(value, 0, width, axis=dim)
        before = lax.ppermute(last, axis, up)
        after = lax.ppermute(first, axis, down)
        value = jnp.concatenate([before, value, after], axis=dim)
    return value


def as_sent(value):
    return jax.tree.map(lambda a: a.astype(jnp.bfloat16) if a.dtype == jnp.float32 else a, value)


def project(values, weight):
    return jnp.einsum("nfhwc,cd->nfhwd", values, weight, preferred_element_type=jnp.float32)


def pad_plane(values):
    return jnp.pad(values, ((0, 0), (0, 0), (1, 1), (1, 1), (0, 0)))


def box_sum(padded):
    summed = padded[:, :-2] + padded[:, 1:-1] + padded[:, 2:]
    summed = summed[:, :, :-2] + summed[:, :, 1:-1] + summed[:, :, 2:]
    return summed[:, :, :, :-2] + summed[:, :, :, 1:-1] + summed[:, :, :, 2:]


def unfold(padded, frames, height, width):
    slices = []
    for shift_f in range(3):
        for shift_h in range(3):
            for shift_w in range(3):
                slices.append(
                    padded[
                        :,
                        shift_f : shift_f + frames,
                        shift_h : shift_h + height,
                        shift_w : shift_w + width,
                    ]
                )
    return jnp.concatenate(slices, axis=-1)


def fold_back(patch_grad, channels):
    summed = None
    offset_index = 0
    for shift_f in range(3):
        for shift_h in range(3):
            for shift_w in range(3):
                segment = patch_grad[..., offset_index * channels : (offset_index + 1) * channels]
                placed = jnp.pad(
                    segment,
                    (
                        (0, 0),
                        (shift_f, 2 - shift_f),
                        (shift_h, 2 - shift_h),
                        (shift_w, 2 - shift_w),
                        (0, 0),
                    ),
                )
                summed = placed if summed is None else summed + placed
                offset_index += 1
    return summed


def return_input_rims(grad_padded):
    interior = grad_padded[:, 1:-1]
    rim_pair = jnp.concatenate([grad_padded[:, :1], grad_padded[:, -1:]], axis=1)
    arrived = extended(rim_pair.astype(jnp.bfloat16), (("tm", 1),), 1).astype(rim_pair.dtype)
    interior = interior.at[:, 0].add(arrived[:, 0])
    return interior.at[:, -1].add(arrived[:, 3])


def return_hidden_rims(grad_padded):
    interior = grad_padded[:, 1:-1]
    rim_pair = jnp.concatenate([grad_padded[:, :1], grad_padded[:, -1:]], axis=1)
    arrived = extended(rim_pair.astype(jnp.bfloat16), (("tm", 1),), 1).astype(rim_pair.dtype)
    interior = interior.at[:, 0].add(arrived[:, 0])
    return interior.at[:, -1].add(arrived[:, 3])


def section_first(features, w_in, w_pool):
    rimmed = extended(features, (("tm", 1),), 1)
    padded = pad_plane(rimmed).astype(jnp.float32)
    pooled = (box_sum(padded) / 27.0).astype(jnp.bfloat16)
    pre_first = jnp.concatenate([project(features, w_in), project(pooled, w_pool)], axis=-1)
    return (pre_first, pooled)


def section_second(middle, w_mid, w_small):
    rimmed = extended(middle, (("tm", 1),), 1)
    padded = pad_plane(rimmed)
    frames, height, width = (middle.shape[1], middle.shape[2], middle.shape[3])
    patch_one = unfold(padded[..., :C1A], frames, height, width)
    patch_two = unfold(padded[..., C1A:], frames, height, width)
    pre_second = jnp.concatenate(
        [
            project(patch_one, w_mid.reshape(27 * C1A, C1B)),
            project(patch_two, w_small.reshape(27 * C2A, C2B)),
        ],
        axis=-1,
    )
    return (pre_second, patch_one, patch_two)


def moments(pre_act, voxel_count):
    first_sum = lax.psum(jnp.sum(pre_act, axis=VOXEL_AXES), ("clip", "tm"))
    center = first_sum / voxel_count
    spread = lax.psum(jnp.sum(jnp.square(pre_act - center), axis=VOXEL_AXES), ("clip", "tm"))
    variance = spread / voxel_count
    return (center, variance)


def standardize(pre_act, center, variance):
    return (pre_act - center) * lax.rsqrt(variance + EPSILON)


def silu_slope(act_in):
    sigmoid_value = jax.nn.sigmoid(act_in)
    return sigmoid_value + act_in * sigmoid_value * (1.0 - sigmoid_value)


def block_forward(features, params, voxel_count):
    w_in, w_pool, w_mid, w_small, offsets = params
    pre_first, pooled = section_first(features, w_in, w_pool)
    center_a, variance_a = moments(pre_first, voxel_count)
    hidden_a = jax.nn.silu(standardize(pre_first, center_a, variance_a) + offsets[:SECTION_A])
    middle = hidden_a[..., C0:IN_OUT].astype(jnp.bfloat16)
    pre_second, patch_one, patch_two = section_second(middle, w_mid, w_small)
    center_b, variance_b = moments(pre_second, voxel_count)
    hidden_b = jax.nn.silu(standardize(pre_second, center_b, variance_b) + offsets[SECTION_A:])
    block_out = jnp.concatenate([hidden_a[..., :C0], hidden_b, hidden_a[..., IN_OUT:]], axis=-1)
    return (block_out, (center_a, variance_a, center_b, variance_b))


def norm_back(slope_grad, normed, variance, voxel_count):
    sum_grad, sum_cross = lax.psum(
        (jnp.sum(slope_grad, axis=VOXEL_AXES), jnp.sum(slope_grad * normed, axis=VOXEL_AXES)),
        ("clip", "tm"),
    )
    scaled = lax.rsqrt(variance + EPSILON) * (
        slope_grad - sum_grad / voxel_count - normed * (sum_cross / voxel_count)
    )
    return (scaled.astype(jnp.bfloat16), sum_grad)


def block_backward(features, params, moment_pair, out_grad, voxel_count):
    w_in, w_pool, w_mid, w_small, offsets = params
    center_a, variance_a, center_b, variance_b = moment_pair
    pre_first, pooled = section_first(features, w_in, w_pool)
    normed_a = standardize(pre_first, center_a, variance_a)
    act_a = normed_a + offsets[:SECTION_A]
    middle = jax.nn.silu(act_a)[..., C0:IN_OUT].astype(jnp.bfloat16)
    pre_second, patch_one, patch_two = section_second(middle, w_mid, w_small)
    normed_b = standardize(pre_second, center_b, variance_b)
    act_b = normed_b + offsets[SECTION_A:]
    grad_b = out_grad[..., C0 : C0 + C1B + C2B] * silu_slope(act_b)
    error_b, offset_grad_b = norm_back(grad_b, normed_b, variance_b, voxel_count)
    error_one = error_b[..., :C1B]
    error_two = error_b[..., C1B:]
    grad_mid = jnp.einsum(
        "nfhwk,nfhwo->ko", patch_one, error_one, preferred_element_type=jnp.float32
    ).reshape(27, C1A, C1B)
    grad_small = jnp.einsum(
        "nfhwk,nfhwo->ko", patch_two, error_two, preferred_element_type=jnp.float32
    ).reshape(27, C2A, C2B)
    back_one = fold_back(
        jnp.einsum(
            "nfhwo,ko->nfhwk",
            error_one,
            w_mid.reshape(27 * C1A, C1B),
            preferred_element_type=jnp.float32,
        ),
        C1A,
    )
    back_two = fold_back(
        jnp.einsum(
            "nfhwo,ko->nfhwk",
            error_two,
            w_small.reshape(27 * C2A, C2B),
            preferred_element_type=jnp.float32,
        ),
        C2A,
    )
    middle_grad = return_hidden_rims(
        jnp.concatenate([back_one, back_two], axis=-1)[:, :, 1:-1, 1:-1]
    )
    grad_a = jnp.concatenate(
        [out_grad[..., :C0], middle_grad, out_grad[..., C0 + C1B + C2B :]], axis=-1
    ) * silu_slope(act_a)
    error_a, offset_grad_a = norm_back(grad_a, normed_a, variance_a, voxel_count)
    error_in = error_a[..., :IN_OUT]
    error_pool = error_a[..., IN_OUT:]
    grad_in = jnp.einsum("nfhwc,nfhwd->cd", features, error_in, preferred_element_type=jnp.float32)
    grad_pool = jnp.einsum(
        "nfhwc,nfhwd->cd", pooled, error_pool, preferred_element_type=jnp.float32
    )
    direct = jnp.einsum("nfhwd,cd->nfhwc", error_in, w_in, preferred_element_type=jnp.float32)
    pool_grad = jnp.einsum(
        "nfhwd,cd->nfhwc", error_pool, w_pool, preferred_element_type=jnp.float32
    )
    spread_pad = jnp.pad(pool_grad, ((0, 0), (2, 2), (2, 2), (2, 2), (0, 0)))
    padded_grad = (box_sum(spread_pad) / 27.0)[:, :, 1:-1, 1:-1]
    input_grad = direct + return_input_rims(padded_grad)
    return (
        input_grad,
        (grad_in, grad_pool, grad_mid, grad_small),
        jnp.concatenate([offset_grad_a, offset_grad_b]),
    )


def reduce_grads(weight_grads):
    summed = jax.tree.map(
        lambda part: part.astype(jnp.float32), lax.psum(as_sent(weight_grads), "clip")
    )
    reduced = (
        lax.psum_scatter(
            summed[0].astype(jnp.bfloat16), "tm", scatter_dimension=1, tiled=True
        ).astype(jnp.float32),
        lax.psum_scatter(
            summed[1].astype(jnp.bfloat16), "tm", scatter_dimension=1, tiled=True
        ).astype(jnp.float32),
        lax.psum_scatter(
            summed[2].astype(jnp.bfloat16), "tm", scatter_dimension=2, tiled=True
        ).astype(jnp.float32),
        lax.psum_scatter(
            summed[3].astype(jnp.bfloat16), "tm", scatter_dimension=2, tiled=True
        ).astype(jnp.float32),
    )
    return reduced


def halve_grid(values):
    n, f, h, w, c = values.shape
    return jnp.sum(values.reshape(n, f // 2, 2, h // 2, 2, w // 2, 2, c), axis=(2, 4, 6)) * 0.125


def spread_half(grad_small_grid):
    n, f, h, w, c = grad_small_grid.shape
    expanded = jnp.broadcast_to(
        (grad_small_grid * 0.125)[:, :, None, :, None, :, None, :], (n, f, 2, h, 2, w, 2, c)
    )
    return expanded.reshape(n, 2 * f, 2 * h, 2 * w, c)


def shards(
    features,
    w_in_4f,
    w_pool_4f,
    w_mid_4f,
    w_small_4f,
    offsets_4f,
    w_in_5b,
    w_pool_5b,
    w_mid_5b,
    w_small_5b,
    offsets_5b,
    cotangent,
):
    params_first = (w_in_4f, w_pool_4f, w_mid_4f, w_small_4f, offsets_4f)
    params_second = (w_in_5b, w_pool_5b, w_mid_5b, w_small_5b, offsets_5b)
    devices_used = lax.axis_size("clip") * lax.axis_size("tm")
    count_first = float(
        features.shape[0] * features.shape[1] * features.shape[2] * features.shape[3] * devices_used
    )
    count_second = count_first / 8.0
    out_first, moments_first = block_forward(features, params_first, count_first)
    input_second = halve_grid(out_first).astype(jnp.bfloat16)
    out_second, moments_second = block_forward(input_second, params_second, count_second)
    grad_second, weights_second, offsets_grad_second = block_backward(
        input_second, params_second, moments_second, cotangent.astype(jnp.float32), count_second
    )
    reduced_second = reduce_grads(weights_second)
    grad_first, weights_first, offsets_grad_first = block_backward(
        features, params_first, moments_first, spread_half(grad_second), count_first
    )
    reduced_first = reduce_grads(weights_first)
    final_out = out_second.astype(jnp.bfloat16)
    return (
        final_out,
        grad_first,
        reduced_first[0],
        reduced_first[1],
        reduced_first[2],
        reduced_first[3],
        offsets_grad_first,
        reduced_second[0],
        reduced_second[1],
        reduced_second[2],
        reduced_second[3],
        offsets_grad_second,
    )


F32 = jnp.float32
BF16 = jnp.bfloat16
MID = 192
BOUT = 448
POOL = 128
OUTC = 832
VMEM_LIMIT = 60 * 1024 * 1024


def dot_nn(a, b):
    return lax.dot_general(a, b, (((1,), (0,)), ((), ())), preferred_element_type=F32)


def dot_nt(a, b):
    return lax.dot_general(a, b, (((1,), (1,)), ((), ())), preferred_element_type=F32)


def roll_rows(value, shift):
    rows = value.shape[0]
    shift %= rows
    return value if shift == 0 else pltpu.roll(value, shift, 0)


def eye(n):
    r = lax.broadcasted_iota(jnp.int32, (n, n), 0)
    k = lax.broadcasted_iota(jnp.int32, (n, n), 1)
    return jnp.where(r == k, 1.0, 0.0).astype(BF16)


def valid_first(rows):
    r = lax.broadcasted_iota(jnp.int32, (rows, 1), 0)
    return ((r & 255) < 224) & ((r & 15) < 14)


def valid_second(rows):
    r = lax.broadcasted_iota(jnp.int32, (rows, 1), 0)
    return ((r & 63) < 56) & ((r & 7) < 7)


def act(a):
    return a * jax.nn.sigmoid(a)


def slope(a):
    s = jax.nn.sigmoid(a)
    return s + a * s * (1.0 - s)


def pack_rows(vectors):
    pieces = []
    for v in vectors:
        width = v.shape[1]
        full = -(-width // 128) * 128
        if full != width:
            v = jnp.concatenate([v, jnp.zeros((1, full - width), F32)], axis=1)
        for i in range(full // 128):
            pieces.append(v[:, i * 128 : (i + 1) * 128])
    return jnp.concatenate(pieces, axis=0)


def unpack_rows(rows, start, width):
    count = -(-width // 128)
    return jnp.concatenate([rows[start + i : start + i + 1] for i in range(count)], axis=1)[
        :, :width
    ]


def store_copies(ref, rows):
    count, height = ref.shape[0], ref.shape[1]
    if rows.shape[0] < height:
        rows = jnp.concatenate([rows, jnp.zeros((height - rows.shape[0], 128), F32)], axis=0)
    for i in range(count):
        ref[i] = rows


def local_moments(value, mask, cells):
    total = jnp.sum(jnp.where(mask, value, 0.0), axis=0, keepdims=True)
    delta = jnp.where(mask, value - total * (1.0 / cells), 0.0)
    return total, jnp.sum(delta * delta, axis=0, keepdims=True)


def joint_moments(gathered, height, cells):
    devices = gathered.shape[0]
    sums, squares = gathered[:, :height], gathered[:, height : 2 * height]
    mean = jnp.sum(sums, axis=0) * (1.0 / (cells * devices))
    apart = sums * (1.0 / cells) - mean[None]
    spread = jnp.sum(squares, axis=0) + cells * jnp.sum(apart * apart, axis=0)
    return mean, lax.rsqrt(spread * (1.0 / (cells * devices)) + EPSILON)


def halve(total, scratch, dtype):
    width = total.shape[1]
    both = total[:256] + total[256:]
    pairs = jnp.sum(both.reshape(8, 2, 16, width), axis=1).reshape(128, width)
    pieces = []
    for i in range(-(-width // 128)):
        lanes = min(128, width - i * 128)
        scratch[i, :, :lanes] = pairs[:, i * 128 : i * 128 + lanes]
        piece = scratch[i, pl.ds(0, 64, 2), :] + scratch[i, pl.ds(1, 64, 2), :]
        pieces.append(piece[:, :lanes])
    halved = jnp.concatenate(pieces, axis=1)
    return (halved * 0.125).astype(dtype)


def box_plane(value, stride):
    value = value + roll_rows(value, stride) + roll_rows(value, -stride)
    return value + roll_rows(value, 1) + roll_rows(value, -1)


def first_project(x_ref, win_ref, wpool_ref, zin_ref, q_ref, st_ref):
    for f in range(2):
        rows = pl.ds(f * 256, 256)
        x = x_ref[rows, :]
        zin_ref[rows, :] = dot_nn(x, win_ref[...])
        q_ref[rows, :] = dot_nn(x, wpool_ref[...])
    total, squares = local_moments(zin_ref[...], valid_first(512), 392)
    store_copies(st_ref, pack_rows([total, squares]))


def first_hidden(
    flag_ref, st_ref, zin_ref, q_ref, before_ref, after_ref, win_ref, wpool_ref, wmid_ref,
    wsmall_ref, off_ref,
    zb_ref, zp_ref, st2_ref, x2_ref, mt_ref, head_ref, tail_ref, ma_ref,
    mid, um_ref, us_ref, half,
):
    mean_rows, scale_rows = joint_moments(st_ref[...], 4, 392.0)
    mean, scale = unpack_rows(mean_rows, 0, IN_OUT), unpack_rows(scale_rows, 0, IN_OUT)
    ma_ref[...] = jnp.concatenate([mean, scale], axis=0)
    off = off_ref[:, :IN_OUT]
    frame = valid_first(256)
    prev, after = flag_ref[1] > 0, flag_ref[2] > 0

    def middle(z, mask):
        return jnp.where(mask, act((z - mean[:, C0:]) * scale[:, C0:] + off[:, C0:]), 0.0)

    blank = jnp.zeros((32, MID), F32)
    for start, ref, mask in ((0, before_ref, prev), (768, after_ref, after)):
        z = jnp.concatenate([dot_nn(ref[...], win_ref[:, C0:]), blank], axis=0)
        mid[start : start + 256, :] = middle(z, frame & mask)
    mid[256:512, :] = middle(zin_ref[0:256, C0:], frame)
    mid[512:768, :] = middle(zin_ref[256:512, C0:], frame)
    for ref in (um_ref, us_ref):
        edge = jnp.zeros((16, ref.shape[1]), BF16)
        ref[0:16, :] = edge
        ref[1040:1056, :] = edge

    for f in range(4):
        rows = slice(f * 256, (f + 1) * 256)
        shifted = [roll_rows(mid[rows, :], 1 - g) for g in range(3)]
        into = slice(16 + f * 256, 16 + (f + 1) * 256)
        um_ref[into, :] = jnp.concatenate([v[:, :C1A] for v in shifted], axis=1).astype(BF16)
        us_ref[into, :] = jnp.concatenate([v[:, C1A:] for v in shifted], axis=1).astype(BF16)

    def convolve(u_ref, w_ref, base):
        total = None
        for a in range(3):
            for e in range(3):
                start = base + 16 + a * 256 + (e - 1) * 16
                term = dot_nn(u_ref[start : start + 256, :], w_ref[3 * a + e])
                total = term if total is None else total + term
        return total

    for f in range(2):
        rows = pl.ds(f * 256, 256)
        zb_ref[rows, :C1B] = convolve(um_ref, wmid_ref, f * 256)
        zb_ref[rows, C1B:] = convolve(us_ref, wsmall_ref, f * 256)

    first, last = q_ref[0:256, :], q_ref[256:512, :]
    pair = first + last
    for f, ref in ((0, before_ref), (1, after_ref)):
        beside = jnp.concatenate([dot_nn(ref[...], wpool_ref[...]), blank[:, :POOL]], axis=0)
        value = pair + beside
        value = box_plane(value, 16) * (1.0 / 27.0)
        zp_ref[f * 256 : (f + 1) * 256, :] = jnp.where(frame, value, 0.0)

    both = valid_first(512)
    total_b, squares_b = local_moments(zb_ref[...], both, 392)
    total_p, squares_p = local_moments(zp_ref[...], both, 392)
    store_copies(st2_ref, pack_rows([total_b, total_p, squares_b, squares_p]))
    for f, ref in ((0, head_ref), (1, tail_ref)):
        rows = pl.ds(f * 256, 224)
        ref[:, :BOUT] = zb_ref[rows, :].astype(BF16)
        ref[:, BOUT:] = zp_ref[rows, :].astype(BF16)
    hidden = act((zin_ref[:, :C0] - mean[:, :C0]) * scale[:, :C0] + off[:, :C0])
    x2_ref[...] = halve(jnp.where(both, hidden, 0.0), half, BF16)
    mt_ref[...] = dot_nt(eye(MID), mid[256:768, :].astype(BF16)).astype(BF16)


def first_output(st_ref, zb_ref, zp_ref, x2c_ref, off_ref, x2_ref, mb_ref, half):
    mean_rows, scale_rows = joint_moments(st_ref[...], 5, 392.0)
    both = valid_first(512)
    moments = []
    for start, width, z_ref, offset in ((0, BOUT, zb_ref, SECTION_A), (4, POOL, zp_ref, IN_OUT)):
        mean, scale = unpack_rows(mean_rows, start, width), unpack_rows(scale_rows, start, width)
        hidden = act((z_ref[...] - mean) * scale + off_ref[:, offset : offset + width])
        into = slice(C0, C0 + BOUT) if start == 0 else slice(C0 + BOUT, OUTC)
        x2_ref[:, into] = halve(jnp.where(both, hidden, 0.0), half, BF16)
        moments.append(jnp.concatenate([mean, scale], axis=0))
    x2_ref[:, :C0] = x2c_ref[...]
    mb_ref[...] = jnp.concatenate(moments, axis=1)


def second_layer(
    clips, frames, flag_ref, *refs,
):
    x_refs, refs = refs[:frames], refs[frames:]
    cot_refs, refs = refs[:frames], refs[frames:]
    second_layer_body(clips, frames, flag_ref, x_refs, cot_refs, *refs)


def second_layer_body(
    clips, frames, flag_ref, x_refs, cot_refs, win_ref, wpool_ref, wmid_ref, wsmall_ref,
    off_ref,
    out_ref, dx_ref, gin_ref, gpool_ref, gmid_ref, gsmall_ref, goff_ref,
    xs, cs, za, zb, um, us, qs, eb, ea, et, eat, da,
):
    here = flag_ref[0]
    span = frames * 64
    slot = (frames + 1) * 64
    cells = clips * frames * 49.0
    wide = clips * slot
    part_mid, part_small = gmid_ref.shape[2], gsmall_ref.shape[2]
    part_in, part_pool = gin_ref.shape[0], gpool_ref.shape[0]
    mask = valid_second(span)

    for c in range(clips):
        for m in range(frames):
            frame = lax.rem(here + m, frames)
            rows = pl.ds(pl.multiple_of(c * span + frame * 64, 64), 64)
            xs[rows, :] = x_refs[m][c]
            cs[rows, :] = cot_refs[m][c]
    for ref in (um, us, qs, eb, ea):
        blank = jnp.zeros((64, ref.shape[1]), ref.dtype)
        for c in range(clips + 1):
            ref[c * slot : c * slot + 64, :] = blank
        ref[wide + 64 : wide + 128, :] = blank

    def rows_of(c):
        return pl.ds(pl.multiple_of(c * span, 64), span)

    def slots_of(c, shift=1):
        return pl.ds(pl.multiple_of(c * slot + shift * 64, 64), span)

    def over_clips(body, init):
        return lax.fori_loop(0, clips, body, init)

    def box(c):
        value = qs[slots_of(c, 0), :] + qs[slots_of(c, 1), :] + qs[slots_of(c, 2), :]
        return jnp.where(mask, box_plane(value, 8) * (1.0 / 27.0), 0.0)

    def project_clip(c, total):
        x = xs[rows_of(c), :]
        z = dot_nn(x, win_ref[...])
        za[rows_of(c), :IN_OUT] = z
        qs[slots_of(c), :] = dot_nn(x, wpool_ref[...])
        p = box(c)
        za[rows_of(c), IN_OUT:] = p
        return total + jnp.concatenate(
            [jnp.sum(z, axis=0, keepdims=True), jnp.sum(p, axis=0, keepdims=True)], axis=1
        )

    total_a = over_clips(project_clip, jnp.zeros((1, SECTION_A), F32))
    mean_a = total_a * (1.0 / cells)

    def spread_clip(ref, mean):
        def body(c, total):
            delta = jnp.where(mask, ref[rows_of(c), :] - mean, 0.0)
            return total + jnp.sum(delta * delta, axis=0, keepdims=True)

        return body

    spread_a = over_clips(spread_clip(za, mean_a), jnp.zeros((1, SECTION_A), F32))
    scale_a = lax.rsqrt(spread_a * (1.0 / cells) + EPSILON)
    off_a, off_b = off_ref[:, :SECTION_A], off_ref[:, SECTION_A:]

    def normal_a(c, lo, hi):
        return (za[rows_of(c), lo:hi] - mean_a[:, lo:hi]) * scale_a[:, lo:hi]

    def unfold_clip(c, _):
        a = normal_a(c, C0, IN_OUT) + off_a[:, C0:IN_OUT]
        hidden = jnp.where(mask, act(a), 0.0)
        shifted = []
        for e in range(3):
            row = roll_rows(hidden, 8 * (1 - e))
            shifted += [roll_rows(row, 1 - g) for g in range(3)]
        um[slots_of(c), :] = jnp.concatenate([v[:, :C1A] for v in shifted], axis=1).astype(BF16)
        us[slots_of(c), :] = jnp.concatenate([v[:, C1A:] for v in shifted], axis=1).astype(BF16)
        return 0

    over_clips(unfold_clip, 0)

    def convolve_clip(c, total):
        mids, smalls = None, None
        for a in range(3):
            one = dot_nn(um[slots_of(c, a), :], wmid_ref[a])
            two = dot_nn(us[slots_of(c, a), :], wsmall_ref[a])
            mids = one if mids is None else mids + one
            smalls = two if smalls is None else smalls + two
        z = jnp.concatenate([mids, smalls], axis=1)
        zb[rows_of(c), :] = z
        return total + jnp.sum(jnp.where(mask, z, 0.0), axis=0, keepdims=True)

    total_b = over_clips(convolve_clip, jnp.zeros((1, BOUT), F32))
    mean_b = total_b * (1.0 / cells)
    spread_b = over_clips(spread_clip(zb, mean_b), jnp.zeros((1, BOUT), F32))
    scale_b = lax.rsqrt(spread_b * (1.0 / cells) + EPSILON)

    own = pl.ds(pl.multiple_of(here * 64, 64), 64)
    hidden_a = act((za[own, :] - mean_a) * scale_a + off_a)
    hidden_b = act((zb[own, :] - mean_b) * scale_b + off_b)
    out_ref[...] = jnp.concatenate(
        [hidden_a[:, :C0], hidden_b, hidden_a[:, IN_OUT:]], axis=1
    ).astype(BF16)

    def grad_b(c):
        y = (zb[rows_of(c), :] - mean_b) * scale_b
        d = cs[rows_of(c), C0 : C0 + BOUT].astype(F32) * slope(y + off_b)
        return d, y

    def sums_b(c, carry):
        d, y = grad_b(c)
        return (
            carry[0] + jnp.sum(d, axis=0, keepdims=True),
            carry[1] + jnp.sum(d * y, axis=0, keepdims=True),
        )

    zero_b = jnp.zeros((1, BOUT), F32)
    sum_b, cross_b = over_clips(sums_b, (zero_b, zero_b))

    def error_b(c, _):
        d, y = grad_b(c)
        e = scale_b * (d - sum_b * (1.0 / cells) - y * (cross_b * (1.0 / cells)))
        eb[slots_of(c), :] = jnp.where(mask, e, 0.0).astype(BF16)
        return 0

    over_clips(error_b, 0)

    def picker(rows, cut, part_one, part_two, columns, edge):
        r = lax.broadcasted_iota(jnp.int32, (rows, columns), 0)
        k = lax.broadcasted_iota(jnp.int32, (rows, columns), 1)
        want = jnp.where(r < cut, here * part_one + r, edge + here * part_two + r - cut)
        return jnp.where(k == want, 1.0, 0.0).astype(BF16)

    pick_b = picker(part_mid + part_small, part_mid, part_mid, part_small, BOUT, C1B)
    et[...] = dot_nt(pick_b, eb[64 : 64 + wide, :]).astype(BF16)
    for a in range(3):
        gm = dot_nn(et[:part_mid, :], um[a * 64 : a * 64 + wide, :])
        gmid_ref[9 * a : 9 * a + 9] = gm.T.reshape(9, C1A, part_mid)
        gs = dot_nn(et[part_mid:, :], us[a * 64 : a * 64 + wide, :])
        gsmall_ref[9 * a : 9 * a + 9] = gs.T.reshape(9, C2A, part_small)

    def grad_a(c, carry):
        mids, smalls = None, None
        for a in range(3):
            one = dot_nt(eb[slots_of(c, 2 - a), :C1B], wmid_ref[a])
            two = dot_nt(eb[slots_of(c, 2 - a), C1B:], wsmall_ref[a])
            mids = one if mids is None else mids + one
            smalls = two if smalls is None else smalls + two
        back = None
        for e in range(3):
            for g in range(3):
                k = 3 * e + g
                t = jnp.concatenate(
                    [mids[:, k * C1A : (k + 1) * C1A], smalls[:, k * C2A : (k + 1) * C2A]], axis=1
                )
                t = roll_rows(t, 8 * (e - 1) + g - 1)
                back = t if back is None else back + t
        y = normal_a(c, 0, SECTION_A)
        gain = slope(y + off_a)
        cot = cs[rows_of(c), :]
        d = jnp.concatenate([cot[:, :C0].astype(F32), back, cot[:, C0 + BOUT :].astype(F32)], axis=1)
        d = jnp.where(mask, d * gain, 0.0)
        da[rows_of(c), :] = d
        return (
            carry[0] + jnp.sum(d, axis=0, keepdims=True),
            carry[1] + jnp.sum(d * y, axis=0, keepdims=True),
        )

    zero_a = jnp.zeros((1, SECTION_A), F32)
    sum_a, cross_a = over_clips(grad_a, (zero_a, zero_a))
    goff_ref[...] = jnp.concatenate([sum_a, sum_b], axis=1)

    def error_a(c, _):
        y = normal_a(c, 0, SECTION_A)
        e = scale_a * (da[rows_of(c), :] - sum_a * (1.0 / cells) - y * (cross_a * (1.0 / cells)))
        e = jnp.where(mask, e, 0.0)
        ea[slots_of(c), :IN_OUT] = e[:, :IN_OUT].astype(BF16)
        qs[slots_of(c), :] = e[:, IN_OUT:].astype(BF16).astype(F32)
        ea[slots_of(c), IN_OUT:] = box(c).astype(BF16)
        return 0

    over_clips(error_a, 0)

    around = pl.ds(pl.multiple_of(here * 64, 64), 192)
    dx_ref[...] = dot_nt(ea[around, :IN_OUT], win_ref[...]) + dot_nt(
        ea[around, IN_OUT:], wpool_ref[...]
    )
    pick_a = picker(part_in + part_pool, part_in, part_in, part_pool, SECTION_A, IN_OUT)
    for c in range(clips):
        errors = ea[c * slot + 64 : c * slot + 64 + span, :]
        eat[:, c * span : (c + 1) * span] = dot_nt(pick_a, errors).astype(BF16)
    gin_ref[...] = dot_nn(eat[:part_in, :], xs[...])
    gpool_ref[...] = dot_nn(eat[part_in:, :], xs[...])


def first_errors(
    flag_ref, dx_ref, zb_ref, zp_ref, zin_ref, before_ref, after_ref, ma_ref, mb_ref, off_ref,
    db_ref, yb_ref, dp_ref, yp_ref, dc_ref, st_ref,
):
    r = lax.broadcasted_iota(jnp.int32, (256, 64), 0)
    k = lax.broadcasted_iota(jnp.int32, (256, 64), 1)
    spread = jnp.where(k == ((r >> 5) << 3) + ((r & 15) >> 1), 1.0, 0.0).astype(BF16)

    def frame_grad(f):
        d = dx_ref[f * 64 : (f + 1) * 64, :] * 0.125
        high = d.astype(BF16)
        low = (d - high.astype(F32)).astype(BF16)
        return dot_nn(spread, high) + dot_nn(spread, low)

    mean_b, scale_b = mb_ref[0:1, :], mb_ref[1:2, :]
    off_b, off_p = off_ref[:, SECTION_A:], off_ref[:, IN_OUT:SECTION_A]
    zero_b, zero_p = jnp.zeros((1, BOUT), F32), jnp.zeros((1, POOL), F32)
    sums = [zero_b, zero_p, jnp.zeros((1, C0), F32)]
    crosses = list(sums)

    def framed(ref, lanes):
        value = ref[:, lanes].astype(F32)
        return jnp.concatenate([value, jnp.zeros((32, value.shape[1]), F32)], axis=0)

    def add(i, d, y):
        sums[i] = sums[i] + jnp.sum(d, axis=0, keepdims=True)
        crosses[i] = crosses[i] + jnp.sum(d * y, axis=0, keepdims=True)

    grads = [frame_grad(f) for f in range(3)]
    for s in range(4):
        rows = slice(s * 256, (s + 1) * 256)
        if s == 0:
            z_b, z_p = framed(before_ref, slice(0, BOUT)), framed(before_ref, slice(BOUT, None))
        elif s == 3:
            z_b, z_p = framed(after_ref, slice(0, BOUT)), framed(after_ref, slice(BOUT, None))
        else:
            inner = slice((s - 1) * 256, s * 256)
            z_b, z_p = zb_ref[inner, :], zp_ref[inner, :]
        g = grads[(s + 1) // 2]
        y_b = (z_b - mean_b[:, :BOUT]) * scale_b[:, :BOUT]
        d_b = g[:, C0 : C0 + BOUT] * slope(y_b + off_b)
        y_p = (z_p - mean_b[:, BOUT:]) * scale_b[:, BOUT:]
        d_p = g[:, C0 + BOUT :] * slope(y_p + off_p)
        db_ref[rows, :], yb_ref[rows, :] = d_b.astype(BF16), y_b.astype(BF16)
        dp_ref[rows, :], yp_ref[rows, :] = d_p.astype(BF16), y_p.astype(BF16)
        if s in (1, 2):
            add(0, d_b, y_b)
            add(1, d_p, y_p)
            y_c = (zin_ref[inner, :C0] - ma_ref[0:1, :C0]) * ma_ref[1:2, :C0]
            d_c = g[:, :C0] * slope(y_c + off_ref[:, :C0])
            dc_ref[inner, :] = d_c.astype(BF16)
            add(2, d_c, y_c)
    store_copies(st_ref, pack_rows(sums + crosses))


def first_hidden_back(
    cells, flag_ref, st_ref, db_ref, yb_ref, zin_ref, ma_ref, mb_ref, off_ref, wmid_ref, wsmall_ref,
    dm_ref, st2_ref, sum_ref, ec_ref,
    eb,
):
    parts = ec_ref.shape[0]
    part_mid, part_small = C1B // parts, C2B // parts
    here = flag_ref[0]
    totals = jnp.sum(st_ref[...], axis=0)
    sum_ref[...] = totals
    sum_b, cross_b = unpack_rows(totals, 0, BOUT), unpack_rows(totals, 7, BOUT)
    scale_b = mb_ref[1:2, :BOUT]
    frame = valid_first(256)
    edge = jnp.zeros((16, BOUT), BF16)
    eb[0:16, :] = edge
    eb[1040:1056, :] = edge
    for s in range(4):
        rows = slice(s * 256, (s + 1) * 256)
        e = scale_b * (
            db_ref[rows, :].astype(F32)
            - sum_b * (1.0 / cells)
            - yb_ref[rows, :].astype(F32) * (cross_b * (1.0 / cells))
        )
        mask = frame
        if s == 0:
            mask = frame & (flag_ref[1] > 0)
        elif s == 3:
            mask = frame & (flag_ref[2] > 0)
        e = jnp.where(mask, e, 0.0)
        eb[16 + s * 256 : 16 + (s + 1) * 256, :] = e.astype(BF16)
        if s in (1, 2):
            for p in range(parts):
                one = e[:224, p * part_mid : (p + 1) * part_mid]
                two = e[:224, C1B + p * part_small : C1B + (p + 1) * part_small]
                into = slice((s - 1) * 224, s * 224)
                ec_ref[lax.rem(p - here + parts, parts), into, :] = jnp.concatenate([one, two], axis=1).astype(BF16)

    sums, crosses = jnp.zeros((1, MID), F32), jnp.zeros((1, MID), F32)
    for f in range(2):
        mids, smalls = None, None
        for a in range(3):
            for e in range(3):
                start = 16 + 256 * (f + 1) - (a - 1) * 256 - (e - 1) * 16
                one = dot_nt(eb[start : start + 256, :C1B], wmid_ref[3 * a + e])
                two = dot_nt(eb[start : start + 256, C1B:], wsmall_ref[3 * a + e])
                mids = one if mids is None else mids + one
                smalls = two if smalls is None else smalls + two
        back = None
        for g in range(3):
            t = jnp.concatenate(
                [mids[:, g * C1A : (g + 1) * C1A], smalls[:, g * C2A : (g + 1) * C2A]], axis=1
            )
            t = roll_rows(t, g - 1)
            back = t if back is None else back + t
        rows = slice(f * 256, (f + 1) * 256)
        y = (zin_ref[rows, C0:] - ma_ref[0:1, C0:]) * ma_ref[1:2, C0:]
        d = jnp.where(frame, back * slope(y + off_ref[:, C0:IN_OUT]), 0.0)
        dm_ref[rows, :] = d
        sums = sums + jnp.sum(d, axis=0, keepdims=True)
        crosses = crosses + jnp.sum(d * y, axis=0, keepdims=True)
    store_copies(st2_ref, pack_rows([sums, crosses]))


def first_kernel_grad(
    flag_ref, own_ref, *refs,
):
    parts = own_ref.shape[0]
    errors = [own_ref.at[0]] + list(refs[: parts - 1])
    hidden = refs[parts - 1 : 2 * parts - 1]
    part_ref, em, es, turned = refs[2 * parts - 1 :]
    frames = 2 * parts
    chunks = part_ref.shape[0]
    part_mid = em.shape[1] // 9
    here, clip = flag_ref[0], flag_ref[3]
    for m in range(parts):
        source = lax.rem(here - m + parts, parts)
        turned[:, pl.ds(pl.multiple_of(source * 512, 512), 512)] = hidden[m][...]
        for f in range(2):
            e = errors[m][f * 224 : f * 224 + 224, :].astype(F32)
            e = jnp.concatenate([e, jnp.zeros((32, e.shape[1]), F32)], axis=0)
            moved = []
            for i in range(3):
                row = roll_rows(e, 16 * (i - 1))
                moved += [roll_rows(row, g - 1) for g in range(3)]
            rows = pl.ds(pl.multiple_of(source * 512 + f * 256, 256), 256)
            em[rows, :] = jnp.concatenate([v[:, :part_mid] for v in moved], axis=1).astype(BF16)
            es[rows, :] = jnp.concatenate([v[:, part_mid:] for v in moved], axis=1).astype(BF16)
    mids, smalls = [], []
    for a in range(3):
        shift = 256 * (a - 1)
        lo, hi = max(0, shift), min(frames * 256, frames * 256 + shift)
        lanes, rows = slice(lo, hi), slice(lo - shift, hi - shift)
        mids.append(dot_nn(turned[:C1A, lanes], em[rows, :]))
        smalls.append(dot_nn(turned[C1A:, lanes], es[rows, :]))
    mids, smalls = jnp.concatenate(mids, axis=1), jnp.concatenate(smalls, axis=1)
    high, low = C1A // chunks, C2A // chunks
    wide = smalls.shape[1] // chunks
    for i in range(chunks):
        tail = [smalls[i * low : (i + 1) * low, q * wide : (q + 1) * wide] for q in range(chunks)]
        tail = jnp.concatenate(tail + [jnp.zeros((high - C2A, wide), F32)], axis=0)
        value = jnp.concatenate([mids[i * high : (i + 1) * high], tail], axis=1).astype(BF16)
        part_ref[lax.rem(i - clip + chunks, chunks)] = value


def first_kernel_join(flag_ref, *refs):
    chunks = len(refs) - 2
    gmid_ref, gsmall_ref = refs[chunks:]
    high, low = C1A // chunks, C2A // chunks
    part_mid, part_small = gmid_ref.shape[2], gsmall_ref.shape[2]
    for m in range(chunks):
        at = lax.rem(flag_ref[3] + m, chunks)
        value = refs[m][...].astype(F32)
        rows = pl.ds(pl.multiple_of(at * high, 8), high)
        for k in range(27):
            gmid_ref[k, rows, :] = value[:, k * part_mid : (k + 1) * part_mid]
        small = [value[q * low : (q + 1) * low, 27 * part_mid :] for q in range(chunks)]
        small = jnp.concatenate(small, axis=1)
        rows = pl.ds(pl.multiple_of(at * low, 8), low)
        for k in range(27):
            gsmall_ref[k, rows, :] = small[:, k * part_small : (k + 1) * part_small]


def first_input_back(
    cells, parts, flag_ref, st_ref, sum_ref, dm_ref, dc_ref, dp_ref, yp_ref, zin_ref, ma_ref, mb_ref,
    x_ref, win_ref, wpool_ref,
    dx_ref, g_ref, goff_ref,
    ea,
):
    part_in, part_pool = IN_OUT // parts, POOL // parts
    totals = jnp.sum(st_ref[...], axis=0)
    before = sum_ref[...]
    sum_m, cross_m = unpack_rows(totals, 0, MID), unpack_rows(totals, 2, MID)
    sum_b = unpack_rows(before, 0, BOUT)
    sum_p, sum_c = unpack_rows(before, 4, POOL), unpack_rows(before, 5, C0)
    cross_p, cross_c = unpack_rows(before, 11, POOL), unpack_rows(before, 12, C0)
    goff_ref[...] = jnp.concatenate([sum_c, sum_m, sum_p, sum_b], axis=1)
    share = 1.0 / cells
    frame = valid_first(256)
    pools = []
    for s in range(4):
        rows = slice(s * 256, (s + 1) * 256)
        e = mb_ref[1:2, BOUT:] * (
            dp_ref[rows, :].astype(F32)
            - sum_p * share
            - yp_ref[rows, :].astype(F32) * (cross_p * share)
        )
        mask = frame
        if s == 0:
            mask = frame & (flag_ref[1] > 0)
        elif s == 3:
            mask = frame & (flag_ref[2] > 0)
        pools.append(jnp.where(mask, e, 0.0).astype(BF16).astype(F32))
    for f in range(2):
        rows = slice(f * 256, (f + 1) * 256)
        value = box_plane(pools[f] + pools[f + 1] + pools[f + 2], 16) * (1.0 / 27.0)
        ea[rows, IN_OUT:] = jnp.where(frame, value, 0.0).astype(BF16)
        y = (zin_ref[rows, :] - ma_ref[0:1, :]) * ma_ref[1:2, :]
        e = dc_ref[rows, :].astype(F32) - sum_c * share - y[:, :C0] * (cross_c * share)
        e = ma_ref[1:2, :C0] * e
        ea[rows, :C0] = jnp.where(frame, e, 0.0).astype(BF16)
        e = ma_ref[1:2, C0:] * (dm_ref[rows, :] - sum_m * share - y[:, C0:] * (cross_m * share))
        ea[rows, C0:IN_OUT] = jnp.where(frame, e, 0.0).astype(BF16)
        dx_ref[rows, :] = dot_nt(ea[rows, :IN_OUT], win_ref[...]) + dot_nt(
            ea[rows, IN_OUT:], wpool_ref[...]
        )
    turned = dot_nt(eye(SECTION_A), ea[...]).astype(BF16)
    g = dot_nn(turned, x_ref[...]).astype(BF16)
    for p in range(parts):
        g_ref[p, :part_in] = g[p * part_in : (p + 1) * part_in]
        g_ref[p, part_in:] = g[IN_OUT + p * part_pool : IN_OUT + (p + 1) * part_pool]


def call(body, outs, scratch, *args, scalars=1, limit=VMEM_LIMIT, us=1):
    in_specs = [pl.BlockSpec(memory_space=pltpu.SMEM)] * scalars
    in_specs += [pl.BlockSpec(memory_space=pltpu.VMEM)] * (len(args) - scalars)
    return pl.pallas_call(
        body,
        out_shape=[jax.ShapeDtypeStruct(s, d) for s, d in outs],
        in_specs=in_specs,
        out_specs=[pl.BlockSpec(memory_space=pltpu.VMEM)] * len(outs),
        scratch_shapes=[pltpu.VMEM(s, d) for s, d in scratch],
        compiler_params=pltpu.CompilerParams(vmem_limit_bytes=limit),
        cost_estimate=pl.CostEstimate(
            flops=int(us * 1.1e9),
            bytes_accessed=sum(a.size * a.dtype.itemsize for a in args),
            transcendentals=0,
        ),
    )(*args)


def exchange(copies):
    return lax.all_to_all(copies, ("clip", "tm"), 0, 0)


def neighbours(head, tail):
    size = lax.axis_size("tm")
    up = [(i, i + 1) for i in range(size - 1)]
    down = [(i + 1, i) for i in range(size - 1)]
    return lax.ppermute(tail, "tm", up), lax.ppermute(head, "tm", down)


def gather_from(value, axis, back=False):
    size = lax.axis_size(axis)
    blocks = [value]
    for m in range(1, size):
        step = -m if back else m
        blocks.append(lax.ppermute(value, axis, [((i + step) % size, i) for i in range(size)]))
    return blocks


def hand_on(chunks, axis):
    size = lax.axis_size(axis)
    blocks = [chunks[0]]
    for m in range(1, size):
        blocks.append(lax.ppermute(chunks[m], axis, [(i, (i + m) % size) for i in range(size)]))
    return blocks


def to_all(value, axis):
    size = lax.axis_size(axis)
    return lax.all_to_all(jnp.broadcast_to(value[None], (size,) + value.shape), axis, 0, 0)


def summed(parts):
    total = parts[0].astype(F32)
    for i in range(1, len(parts)):
        total = total + parts[i].astype(F32)
    return total.astype(BF16)


def after(value, *others):
    return lax.optimization_barrier((value,) + others)[0]


def small_group(
    features, w_in_4f, w_pool_4f, w_mid_4f, w_small_4f, offsets_4f,
    w_in_5b, w_pool_5b, w_mid_5b, w_small_5b, offsets_5b, cotangent,
):
    clips, frames = lax.axis_size("clip"), lax.axis_size("tm")
    group = clips * frames
    cells = 392.0 * group
    here = lax.axis_index("tm")
    flags = jnp.stack([here, here > 0, here < frames - 1, lax.axis_index("clip")]).astype(jnp.int32)
    offsets_4f, offsets_5b = offsets_4f[None], offsets_5b[None]
    x = jnp.pad(features[0], ((0, 0), (0, 2), (0, 2), (0, 0))).reshape(512, features.shape[-1])
    cot = jnp.pad(cotangent[0, 0], ((0, 1), (0, 1), (0, 0))).reshape(64, OUTC)
    mid_4f, small_4f = w_mid_4f.reshape(9, 3 * C1A, C1B), w_small_4f.reshape(9, 3 * C2A, C2B)
    mid_5b, small_5b = w_mid_5b.reshape(3, 9 * C1A, C1B), w_small_5b.reshape(3, 9 * C2A, C2B)
    before, behind = neighbours(x[:224], x[256:480])
    cot = jnp.stack(gather_from(cot, "clip"))

    z_in, q, stats = call(
        first_project,
        [((512, IN_OUT), F32), ((512, POOL), F32), ((group, 8, 128), F32)],
        [], x, w_in_4f, w_pool_4f, scalars=0, us=4,
    )
    stats = exchange(stats)
    z_b, z_p, stats, x2, m_turned, head, tail, moments_a = call(
        first_hidden,
        [((512, BOUT), F32), ((512, POOL), F32), ((group, 16, 128), F32), ((64, C0), BF16),
         ((MID, 512), BF16),
         ((224, BOUT + POOL), BF16), ((224, BOUT + POOL), BF16), ((2, IN_OUT), F32)],
        [((1024, MID), F32), ((1056, 3 * C1A), BF16), ((1056, 3 * C2A), BF16),
         ((4, 128, 128), F32)],
        flags, stats, z_in, q, before, behind, w_in_4f, w_pool_4f, mid_4f, small_4f, offsets_4f,
        us=8,
    )
    cot = gather_from(after(cot, z_b), "tm")
    stats = exchange(stats)
    x2, moments_b = call(
        first_output,
        [((64, OUTC), BF16), ((2, BOUT + POOL), F32)],
        [((4, 128, 128), F32)],
        stats, z_b, z_p, x2, offsets_4f, scalars=0, us=3,
    )
    x2 = jnp.stack(gather_from(x2, "clip"))
    head, tail, m_turned = lax.optimization_barrier((head, tail, m_turned, x2))[:3]
    before, behind = neighbours(head, tail)
    m_turned = gather_from(m_turned, "tm", back=True)
    x2 = gather_from(after(x2, *cot), "tm")
    rows, slots = group * 64, (clips * (frames + 1) + 2) * 64
    wide = clips * (frames + 1) * 64
    part = (C1B // frames, C2B // frames, IN_OUT // frames, POOL // frames)
    out, dx2, g_in_5b, g_pool_5b, g_mid_5b, g_small_5b, g_off_5b = call(
        functools.partial(second_layer, clips, frames),
        [((64, OUTC), BF16), ((192, OUTC), F32), ((part[2], OUTC), F32), ((part[3], OUTC), F32),
         ((27, C1A, part[0]), F32), ((27, C2A, part[1]), F32), ((1, 1024), F32)],
        [((rows, OUTC), BF16), ((rows, OUTC), BF16), ((rows, SECTION_A), F32), ((rows, BOUT), F32),
         ((slots, 9 * C1A), BF16), ((slots, 9 * C2A), BF16), ((slots, POOL), F32),
         ((slots, BOUT), BF16), ((slots, SECTION_A), BF16), ((part[0] + part[1], wide), BF16),
         ((part[2] + part[3], rows), BF16), ((rows, SECTION_A), F32)],
        flags, *x2, *cot, w_in_5b, w_pool_5b, mid_5b, small_5b,
        offsets_5b, us=35,
    )
    d_b, y_b, d_p, y_p, d_c, stats = call(
        first_errors,
        [((1024, BOUT), BF16), ((1024, BOUT), BF16), ((1024, POOL), BF16), ((1024, POOL), BF16),
         ((512, C0), BF16), ((group, 16, 128), F32)],
        [], flags, dx2, z_b, z_p, z_in, before, behind, moments_a, moments_b, offsets_4f,
        us=5,
    )
    stats = exchange(stats)
    d_m, stats, sums, errors = call(
        functools.partial(first_hidden_back, cells),
        [((512, MID), F32), ((group, 8, 128), F32), ((16, 128), F32),
         ((frames, 448, part[0] + part[1]), BF16)],
        [((1056, BOUT), BF16)],
        flags, stats, d_b, y_b, z_in, moments_a, moments_b, offsets_4f, mid_4f, small_4f,
        us=8,
    )
    received = hand_on(errors, "tm")
    stats = exchange(stats)
    (g_conv,) = call(
        first_kernel_grad,
        [((clips, C1A // clips, 27 * part[0] + 27 * part[1] // clips), BF16)],
        [((frames * 512, 9 * part[0]), BF16), ((frames * 512, 9 * part[1]), BF16),
         ((MID, frames * 512), BF16)],
        flags, errors, *received[1:], *m_turned, us=6,
    )
    stats = after(stats, g_conv)
    g_conv = hand_on(g_conv, "clip")
    d_x, g_a, g_off = call(
        functools.partial(first_input_back, cells, frames),
        [((512, features.shape[-1]), F32),
         ((frames, part[2] + part[3], features.shape[-1]), BF16), ((1, 1024), F32)],
        [((512, SECTION_A), BF16)],
        flags, stats, sums, d_m, d_c, d_p, y_p, z_in, moments_a, moments_b, x, w_in_4f, w_pool_4f,
        us=6,
    )
    g_a = summed(lax.all_to_all(g_a, "tm", 0, 0))
    g_a = g_a.reshape(clips, (part[2] + part[3]) // clips, -1)
    g_conv = gather_from(summed(g_conv), "clip")
    g_a = summed(lax.all_to_all(g_a, "clip", 0, 0))
    g_a = to_all(g_a, "clip").astype(F32).reshape(part[2] + part[3], -1)
    g_mid, g_small = call(
        first_kernel_join,
        [((27, C1A, part[0]), F32), ((27, C2A, part[1]), F32)],
        [], flags, *g_conv, us=4,
    )

    return (
        out.reshape(1, 1, 8, 8, OUTC)[:, :, :7, :7],
        d_x.reshape(1, 2, 16, 16, -1)[:, :, :14, :14],
        g_a[: part[2]].T,
        g_a[part[2] :].T,
        g_mid,
        g_small,
        g_off[0],
        g_in_5b.T,
        g_pool_5b.T,
        g_mid_5b,
        g_small_5b,
        g_off_5b[0],
    )


def solution(mesh):
    placed = (
        P(("stream", "clip"), "tm", None, None, None),
        P("stream", None),
        P("stream", None),
        P("stream", None, None),
        P("stream", None, None),
        P("stream"),
        P("stream", None),
        P("stream", None),
        P("stream", None, None),
        P("stream", None, None),
        P("stream"),
        P(("stream", "clip"), "tm", None, None, None),
    )
    group = mesh.shape["clip"] * mesh.shape["tm"]
    return jax.shard_map(
        small_group if group <= 16 else shards,
        mesh=mesh,
        in_specs=placed,
        out_specs=(
            P(("stream", "clip"), "tm", None, None, None),
            P(("stream", "clip"), "tm", None, None, None),
            P("stream", "tm"),
            P("stream", "tm"),
            P("stream", None, "tm"),
            P("stream", None, "tm"),
            P("stream"),
            P("stream", "tm"),
            P("stream", "tm"),
            P("stream", None, "tm"),
            P("stream", None, "tm"),
            P("stream"),
        ),
        check_vma=False,
    )
```

```python
import functools

import jax
import jax.numpy as jnp
from jax import lax
from jax.experimental import pallas as pl
from jax.experimental.pallas import tpu as pltpu
from jax.sharding import PartitionSpec as P

C0 = 256
C1A = 160
C1B = 320
C2A = 32
C2B = 128
IN_OUT = 448
SECTION_A = 576


EPSILON = 0.001
VOXEL_AXES = (0, 1, 2, 3)


def extended(value, sides, width):
    for axis, dim in sides:
        size, length = (lax.axis_size(axis), value.shape[dim])
        up = [(i, (i + 1) % size) for i in range(size - 1)]
        down = [(j, i) for i, j in up]
        last = lax.slice_in_dim(value, length - width, length, axis=dim)
        first = lax.slice_in_dim(value, 0, width, axis=dim)
        before = lax.ppermute(last, axis, up)
        after = lax.ppermute(first, axis, down)
        value = jnp.concatenate([before, value, after], axis=dim)
    return value


def as_sent(value):
    return jax.tree.map(lambda a: a.astype(jnp.bfloat16) if a.dtype == jnp.float32 else a, value)


def project(values, weight):
    return jnp.einsum("nfhwc,cd->nfhwd", values, weight, preferred_element_type=jnp.float32)


def pad_plane(values):
    return jnp.pad(values, ((0, 0), (0, 0), (1, 1), (1, 1), (0, 0)))


def box_sum(padded):
    summed = padded[:, :-2] + padded[:, 1:-1] + padded[:, 2:]
    summed = summed[:, :, :-2] + summed[:, :, 1:-1] + summed[:, :, 2:]
    return summed[:, :, :, :-2] + summed[:, :, :, 1:-1] + summed[:, :, :, 2:]


def unfold(padded, frames, height, width):
    slices = []
    for shift_f in range(3):
        for shift_h in range(3):
            for shift_w in range(3):
                slices.append(
                    padded[
                        :,
                        shift_f : shift_f + frames,
                        shift_h : shift_h + height,
                        shift_w : shift_w + width,
                    ]
                )
    return jnp.concatenate(slices, axis=-1)


def fold_back(patch_grad, channels):
    summed = None
    offset_index = 0
    for shift_f in range(3):
        for shift_h in range(3):
            for shift_w in range(3):
                segment = patch_grad[..., offset_index * channels : (offset_index + 1) * channels]
                placed = jnp.pad(
                    segment,
                    (
                        (0, 0),
                        (shift_f, 2 - shift_f),
                        (shift_h, 2 - shift_h),
                        (shift_w, 2 - shift_w),
                        (0, 0),
                    ),
                )
                summed = placed if summed is None else summed + placed
                offset_index += 1
    return summed


def return_input_rims(grad_padded):
    interior = grad_padded[:, 1:-1]
    rim_pair = jnp.concatenate([grad_padded[:, :1], grad_padded[:, -1:]], axis=1)
    arrived = extended(rim_pair.astype(jnp.bfloat16), (("tm", 1),), 1).astype(rim_pair.dtype)
    interior = interior.at[:, 0].add(arrived[:, 0])
    return interior.at[:, -1].add(arrived[:, 3])


def return_hidden_rims(grad_padded):
    interior = grad_padded[:, 1:-1]
    rim_pair = jnp.concatenate([grad_padded[:, :1], grad_padded[:, -1:]], axis=1)
    arrived = extended(rim_pair.astype(jnp.bfloat16), (("tm", 1),), 1).astype(rim_pair.dtype)
    interior = interior.at[:, 0].add(arrived[:, 0])
    return interior.at[:, -1].add(arrived[:, 3])


def section_first(features, w_in, w_pool):
    rimmed = extended(features, (("tm", 1),), 1)
    padded = pad_plane(rimmed).astype(jnp.float32)
    pooled = (box_sum(padded) / 27.0).astype(jnp.bfloat16)
    pre_first = jnp.concatenate([project(features, w_in), project(pooled, w_pool)], axis=-1)
    return (pre_first, pooled)


def section_second(middle, w_mid, w_small):
    rimmed = extended(middle, (("tm", 1),), 1)
    padded = pad_plane(rimmed)
    frames, height, width = (middle.shape[1], middle.shape[2], middle.shape[3])
    patch_one = unfold(padded[..., :C1A], frames, height, width)
    patch_two = unfold(padded[..., C1A:], frames, height, width)
    pre_second = jnp.concatenate(
        [
            project(patch_one, w_mid.reshape(27 * C1A, C1B)),
            project(patch_two, w_small.reshape(27 * C2A, C2B)),
        ],
        axis=-1,
    )
    return (pre_second, patch_one, patch_two)


def moments(pre_act, voxel_count):
    first_sum = lax.psum(jnp.sum(pre_act, axis=VOXEL_AXES), ("clip", "tm"))
    center = first_sum / voxel_count
    spread = lax.psum(jnp.sum(jnp.square(pre_act - center), axis=VOXEL_AXES), ("clip", "tm"))
    variance = spread / voxel_count
    return (center, variance)


def standardize(pre_act, center, variance):
    return (pre_act - center) * lax.rsqrt(variance + EPSILON)


def silu_slope(act_in):
    sigmoid_value = jax.nn.sigmoid(act_in)
    return sigmoid_value + act_in * sigmoid_value * (1.0 - sigmoid_value)


def block_forward(features, params, voxel_count):
    w_in, w_pool, w_mid, w_small, offsets = params
    pre_first, pooled = section_first(features, w_in, w_pool)
    center_a, variance_a = moments(pre_first, voxel_count)
    hidden_a = jax.nn.silu(standardize(pre_first, center_a, variance_a) + offsets[:SECTION_A])
    middle = hidden_a[..., C0:IN_OUT].astype(jnp.bfloat16)
    pre_second, patch_one, patch_two = section_second(middle, w_mid, w_small)
    center_b, variance_b = moments(pre_second, voxel_count)
    hidden_b = jax.nn.silu(standardize(pre_second, center_b, variance_b) + offsets[SECTION_A:])
    block_out = jnp.concatenate([hidden_a[..., :C0], hidden_b, hidden_a[..., IN_OUT:]], axis=-1)
    return (block_out, (center_a, variance_a, center_b, variance_b))


def norm_back(slope_grad, normed, variance, voxel_count):
    sum_grad, sum_cross = lax.psum(
        (jnp.sum(slope_grad, axis=VOXEL_AXES), jnp.sum(slope_grad * normed, axis=VOXEL_AXES)),
        ("clip", "tm"),
    )
    scaled = lax.rsqrt(variance + EPSILON) * (
        slope_grad - sum_grad / voxel_count - normed * (sum_cross / voxel_count)
    )
    return (scaled.astype(jnp.bfloat16), sum_grad)


def block_backward(features, params, moment_pair, out_grad, voxel_count):
    w_in, w_pool, w_mid, w_small, offsets = params
    center_a, variance_a, center_b, variance_b = moment_pair
    pre_first, pooled = section_first(features, w_in, w_pool)
    normed_a = standardize(pre_first, center_a, variance_a)
    act_a = normed_a + offsets[:SECTION_A]
    middle = jax.nn.silu(act_a)[..., C0:IN_OUT].astype(jnp.bfloat16)
    pre_second, patch_one, patch_two = section_second(middle, w_mid, w_small)
    normed_b = standardize(pre_second, center_b, variance_b)
    act_b = normed_b + offsets[SECTION_A:]
    grad_b = out_grad[..., C0 : C0 + C1B + C2B] * silu_slope(act_b)
    error_b, offset_grad_b = norm_back(grad_b, normed_b, variance_b, voxel_count)
    error_one = error_b[..., :C1B]
    error_two = error_b[..., C1B:]
    grad_mid = jnp.einsum(
        "nfhwk,nfhwo->ko", patch_one, error_one, preferred_element_type=jnp.float32
    ).reshape(27, C1A, C1B)
    grad_small = jnp.einsum(
        "nfhwk,nfhwo->ko", patch_two, error_two, preferred_element_type=jnp.float32
    ).reshape(27, C2A, C2B)
    back_one = fold_back(
        jnp.einsum(
            "nfhwo,ko->nfhwk",
            error_one,
            w_mid.reshape(27 * C1A, C1B),
            preferred_element_type=jnp.float32,
        ),
        C1A,
    )
    back_two = fold_back(
        jnp.einsum(
            "nfhwo,ko->nfhwk",
            error_two,
            w_small.reshape(27 * C2A, C2B),
            preferred_element_type=jnp.float32,
        ),
        C2A,
    )
    middle_grad = return_hidden_rims(
        jnp.concatenate([back_one, back_two], axis=-1)[:, :, 1:-1, 1:-1]
    )
    grad_a = jnp.concatenate(
        [out_grad[..., :C0], middle_grad, out_grad[..., C0 + C1B + C2B :]], axis=-1
    ) * silu_slope(act_a)
    error_a, offset_grad_a = norm_back(grad_a, normed_a, variance_a, voxel_count)
    error_in = error_a[..., :IN_OUT]
    error_pool = error_a[..., IN_OUT:]
    grad_in = jnp.einsum("nfhwc,nfhwd->cd", features, error_in, preferred_element_type=jnp.float32)
    grad_pool = jnp.einsum(
        "nfhwc,nfhwd->cd", pooled, error_pool, preferred_element_type=jnp.float32
    )
    direct = jnp.einsum("nfhwd,cd->nfhwc", error_in, w_in, preferred_element_type=jnp.float32)
    pool_grad = jnp.einsum(
        "nfhwd,cd->nfhwc", error_pool, w_pool, preferred_element_type=jnp.float32
    )
    spread_pad = jnp.pad(pool_grad, ((0, 0), (2, 2), (2, 2), (2, 2), (0, 0)))
    padded_grad = (box_sum(spread_pad) / 27.0)[:, :, 1:-1, 1:-1]
    input_grad = direct + return_input_rims(padded_grad)
    return (
        input_grad,
        (grad_in, grad_pool, grad_mid, grad_small),
        jnp.concatenate([offset_grad_a, offset_grad_b]),
    )


def reduce_grads(weight_grads):
    summed = jax.tree.map(
        lambda part: part.astype(jnp.float32), lax.psum(as_sent(weight_grads), "clip")
    )
    reduced = (
        lax.psum_scatter(
            summed[0].astype(jnp.bfloat16), "tm", scatter_dimension=1, tiled=True
        ).astype(jnp.float32),
        lax.psum_scatter(
            summed[1].astype(jnp.bfloat16), "tm", scatter_dimension=1, tiled=True
        ).astype(jnp.float32),
        lax.psum_scatter(
            summed[2].astype(jnp.bfloat16), "tm", scatter_dimension=2, tiled=True
        ).astype(jnp.float32),
        lax.psum_scatter(
            summed[3].astype(jnp.bfloat16), "tm", scatter_dimension=2, tiled=True
        ).astype(jnp.float32),
    )
    return reduced


def halve_grid(values):
    n, f, h, w, c = values.shape
    return jnp.sum(values.reshape(n, f // 2, 2, h // 2, 2, w // 2, 2, c), axis=(2, 4, 6)) * 0.125


def spread_half(grad_small_grid):
    n, f, h, w, c = grad_small_grid.shape
    expanded = jnp.broadcast_to(
        (grad_small_grid * 0.125)[:, :, None, :, None, :, None, :], (n, f, 2, h, 2, w, 2, c)
    )
    return expanded.reshape(n, 2 * f, 2 * h, 2 * w, c)


def shards(
    features,
    w_in_4f,
    w_pool_4f,
    w_mid_4f,
    w_small_4f,
    offsets_4f,
    w_in_5b,
    w_pool_5b,
    w_mid_5b,
    w_small_5b,
    offsets_5b,
    cotangent,
):
    params_first = (w_in_4f, w_pool_4f, w_mid_4f, w_small_4f, offsets_4f)
    params_second = (w_in_5b, w_pool_5b, w_mid_5b, w_small_5b, offsets_5b)
    devices_used = lax.axis_size("clip") * lax.axis_size("tm")
    count_first = float(
        features.shape[0] * features.shape[1] * features.shape[2] * features.shape[3] * devices_used
    )
    count_second = count_first / 8.0
    out_first, moments_first = block_forward(features, params_first, count_first)
    input_second = halve_grid(out_first).astype(jnp.bfloat16)
    out_second, moments_second = block_forward(input_second, params_second, count_second)
    grad_second, weights_second, offsets_grad_second = block_backward(
        input_second, params_second, moments_second, cotangent.astype(jnp.float32), count_second
    )
    reduced_second = reduce_grads(weights_second)
    grad_first, weights_first, offsets_grad_first = block_backward(
        features, params_first, moments_first, spread_half(grad_second), count_first
    )
    reduced_first = reduce_grads(weights_first)
    final_out = out_second.astype(jnp.bfloat16)
    return (
        final_out,
        grad_first,
        reduced_first[0],
        reduced_first[1],
        reduced_first[2],
        reduced_first[3],
        offsets_grad_first,
        reduced_second[0],
        reduced_second[1],
        reduced_second[2],
        reduced_second[3],
        offsets_grad_second,
    )


F32 = jnp.float32
BF16 = jnp.bfloat16
MID = 192
BOUT = 448
POOL = 128
OUTC = 832
VMEM_LIMIT = 60 * 1024 * 1024


def dot_nn(a, b):
    return lax.dot_general(a, b, (((1,), (0,)), ((), ())), preferred_element_type=F32)


def dot_nt(a, b):
    return lax.dot_general(a, b, (((1,), (1,)), ((), ())), preferred_element_type=F32)


def roll_rows(value, shift):
    rows = value.shape[0]
    shift %= rows
    return value if shift == 0 else pltpu.roll(value, shift, 0)


def eye(n):
    r = lax.broadcasted_iota(jnp.int32, (n, n), 0)
    k = lax.broadcasted_iota(jnp.int32, (n, n), 1)
    return jnp.where(r == k, 1.0, 0.0).astype(BF16)


def valid_first(rows):
    r = lax.broadcasted_iota(jnp.int32, (rows, 1), 0)
    return ((r & 255) < 224) & ((r & 15) < 14)


def valid_second(rows):
    r = lax.broadcasted_iota(jnp.int32, (rows, 1), 0)
    return ((r & 63) < 56) & ((r & 7) < 7)


def sigmoid(a):
    return 0.5 * jnp.tanh(0.5 * a) + 0.5


def act(a):
    return a * sigmoid(a)


def slope(a):
    s = sigmoid(a)
    return s + a * s * (1.0 - s)


def pack_rows(vectors):
    pieces = []
    for v in vectors:
        width = v.shape[1]
        full = -(-width // 128) * 128
        if full != width:
            v = jnp.concatenate([v, jnp.zeros((1, full - width), F32)], axis=1)
        for i in range(full // 128):
            pieces.append(v[:, i * 128 : (i + 1) * 128])
    return jnp.concatenate(pieces, axis=0)


def unpack_rows(rows, start, width):
    count = -(-width // 128)
    return jnp.concatenate([rows[start + i : start + i + 1] for i in range(count)], axis=1)[
        :, :width
    ]


def store_copies(ref, rows):
    count, height = ref.shape[0], ref.shape[1]
    if rows.shape[0] < height:
        rows = jnp.concatenate([rows, jnp.zeros((height - rows.shape[0], 128), F32)], axis=0)
    for i in range(count):
        ref[i] = rows


def local_moments(value, mask, cells):
    total = jnp.sum(jnp.where(mask, value, 0.0), axis=0, keepdims=True)
    delta = jnp.where(mask, value - total * (1.0 / cells), 0.0)
    return total, jnp.sum(delta * delta, axis=0, keepdims=True)


def joint_moments(gathered, height, cells):
    devices = gathered.shape[0]
    sums, squares = gathered[:, :height], gathered[:, height : 2 * height]
    mean = jnp.sum(sums, axis=0) * (1.0 / (cells * devices))
    apart = sums * (1.0 / cells) - mean[None]
    spread = jnp.sum(squares, axis=0) + cells * jnp.sum(apart * apart, axis=0)
    return mean, lax.rsqrt(spread * (1.0 / (cells * devices)) + EPSILON)


def halve(total, scratch, dtype):
    width = total.shape[1]
    both = total[:256] + total[256:]
    pairs = jnp.sum(both.reshape(8, 2, 16, width), axis=1).reshape(128, width)
    pieces = []
    for i in range(-(-width // 128)):
        lanes = min(128, width - i * 128)
        scratch[i, :, :lanes] = pairs[:, i * 128 : i * 128 + lanes]
        piece = scratch[i, pl.ds(0, 64, 2), :] + scratch[i, pl.ds(1, 64, 2), :]
        pieces.append(piece[:, :lanes])
    halved = jnp.concatenate(pieces, axis=1)
    return (halved * 0.125).astype(dtype)


def box_plane(value, stride):
    value = value + roll_rows(value, stride) + roll_rows(value, -stride)
    return value + roll_rows(value, 1) + roll_rows(value, -1)


def first_project(x_ref, win_ref, wpool_ref, zc_ref, zm_ref, q_ref, st_ref):
    for f in range(2):
        rows = pl.ds(f * 256, 256)
        x = x_ref[rows, :]
        z = dot_nn(x, win_ref[...])
        zc_ref[rows, :], zm_ref[rows, :] = z[:, :C0], z[:, C0:]
        q_ref[rows, :] = dot_nn(x, wpool_ref[...])
    mask = valid_first(512)
    moments = [local_moments(ref[...], mask, 392) for ref in (zc_ref, zm_ref)]
    total, squares = [jnp.concatenate([m[i] for m in moments], axis=1) for i in range(2)]
    store_copies(st_ref, pack_rows([total, squares]))


def first_hidden(
    flag_ref, st_ref, zc_ref, zm_ref, q_ref, before_ref, after_ref, win_ref, wpool_ref, wmid_ref,
    wsmall_ref, off_ref,
    zb_ref, zp_ref, st2_ref, x2_ref, mt_ref, head_ref, tail_ref, ma_ref,
    mid, um_ref, us_ref, half,
):
    mean_rows, scale_rows = joint_moments(st_ref[...], 4, 392.0)
    mean, scale = unpack_rows(mean_rows, 0, IN_OUT), unpack_rows(scale_rows, 0, IN_OUT)
    ma_ref[...] = jnp.concatenate([mean, scale], axis=0)
    off = off_ref[:, :IN_OUT]
    frame = valid_first(256)
    prev, after = flag_ref[1] > 0, flag_ref[2] > 0

    def middle(z, mask):
        return jnp.where(mask, act((z - mean[:, C0:]) * scale[:, C0:] + off[:, C0:]), 0.0)

    blank = jnp.zeros((32, MID), F32)
    for start, ref, mask in ((0, before_ref, prev), (768, after_ref, after)):
        z = jnp.concatenate([dot_nn(ref[...], win_ref[:, C0:]), blank], axis=0)
        mid[start : start + 256, :] = middle(z, frame & mask)
    mid[256:512, :] = middle(zm_ref[0:256, :], frame)
    mid[512:768, :] = middle(zm_ref[256:512, :], frame)
    for ref in (um_ref, us_ref):
        edge = jnp.zeros((16, ref.shape[1]), BF16)
        ref[0:16, :] = edge
        ref[1040:1056, :] = edge

    for f in range(4):
        rows = slice(f * 256, (f + 1) * 256)
        shifted = [roll_rows(mid[rows, :], 1 - g) for g in range(3)]
        into = slice(16 + f * 256, 16 + (f + 1) * 256)
        um_ref[into, :] = jnp.concatenate([v[:, :C1A] for v in shifted], axis=1).astype(BF16)
        us_ref[into, :] = jnp.concatenate([v[:, C1A:] for v in shifted], axis=1).astype(BF16)

    def convolve(u_ref, w_ref):
        total = None
        for a in range(3):
            for e in range(3):
                start = 16 + a * 256 + (e - 1) * 16
                term = dot_nn(u_ref[start : start + 512, :], w_ref[3 * a + e])
                total = term if total is None else total + term
        return total

    zb_ref[:, :C1B] = convolve(um_ref, wmid_ref)
    zb_ref[:, C1B:] = convolve(us_ref, wsmall_ref)

    first, last = q_ref[0:256, :], q_ref[256:512, :]
    pair = first + last
    for f, ref in ((0, before_ref), (1, after_ref)):
        beside = jnp.concatenate([dot_nn(ref[...], wpool_ref[...]), blank[:, :POOL]], axis=0)
        value = pair + beside
        value = box_plane(value, 16) * (1.0 / 27.0)
        zp_ref[f * 256 : (f + 1) * 256, :] = jnp.where(frame, value, 0.0)

    both = valid_first(512)
    total_b, squares_b = local_moments(zb_ref[...], both, 392)
    total_p, squares_p = local_moments(zp_ref[...], both, 392)
    store_copies(st2_ref, pack_rows([total_b, total_p, squares_b, squares_p]))
    for f, ref in ((0, head_ref), (1, tail_ref)):
        rows = pl.ds(f * 256, 224)
        ref[:, :BOUT] = zb_ref[rows, :].astype(BF16)
        ref[:, BOUT:] = zp_ref[rows, :].astype(BF16)
    hidden = act((zc_ref[...] - mean[:, :C0]) * scale[:, :C0] + off[:, :C0])
    x2_ref[...] = halve(jnp.where(both, hidden, 0.0), half, BF16)[:56]
    mt_ref[...] = dot_nt(eye(MID), mid[256:768, :].astype(BF16)).astype(BF16)


def first_output(st_ref, zb_ref, zp_ref, x2c_ref, off_ref, x2_ref, mb_ref, half):
    mean_rows, scale_rows = joint_moments(st_ref[...], 5, 392.0)
    both = valid_first(512)
    moments = []
    for start, width, z_ref, offset in ((0, BOUT, zb_ref, SECTION_A), (4, POOL, zp_ref, IN_OUT)):
        mean, scale = unpack_rows(mean_rows, start, width), unpack_rows(scale_rows, start, width)
        hidden = act((z_ref[...] - mean) * scale + off_ref[:, offset : offset + width])
        into = slice(C0, C0 + BOUT) if start == 0 else slice(C0 + BOUT, OUTC)
        x2_ref[:, into] = halve(jnp.where(both, hidden, 0.0), half, BF16)[:56]
        moments.append(jnp.concatenate([mean, scale], axis=0))
    x2_ref[:, :C0] = x2c_ref[...]
    mb_ref[...] = jnp.concatenate(moments, axis=1)


def second_layer(clips, frames, flag_ref, *refs):
    x_refs, refs = refs[:frames], refs[frames:]
    win_ref, wpool_ref, wsmall_ref, off_ref = refs[:4]
    moment_refs, far_refs, refs = refs[4:7], refs[7 : 11 + frames], refs[11 + frames :]
    out_ref, gin_ref, gpool_ref, gmid_hbm, gsmall_hbm, goff_ref = refs[:6]
    dn_ref, error_refs, scratch = refs[6], refs[7:13], refs[13:]
    xs, cs, za, zb, um, us, qs, eb, es, ea, et, ets, eat, da, tmid_ref, tsmall_ref = scratch[:16]
    gmid_ref, gsmall_ref, near_refs, sems = *scratch[16:18], scratch[18:-1], scratch[-1]
    loads = [
        pltpu.make_async_copy(far, near, sems.at[i])
        for i, (far, near) in enumerate(zip(far_refs, near_refs))
    ]
    for load in loads:
        load.start()
    wmid_ref, cot_refs = near_refs[0], near_refs[1 : 1 + frames]
    here = flag_ref[0]
    step = clips * 64
    rows = frames * step
    cells = clips * frames * 49.0
    share = 1.0 / cells
    part_mid, part_small = gmid_ref.shape[2], gsmall_ref.shape[2]
    part_in, part_pool = gin_ref.shape[0], gpool_ref.shape[0]
    mask = valid_second(step)

    tail = jnp.zeros((16, OUTC), BF16)

    def assemble(into, blocks):
        for m in range(frames):
            for c in range(clips):
                base = lax.rem(here + m, frames) * step + c * 64
                into[pl.ds(pl.multiple_of(base + 48, 16), 16), :] = tail
                into[pl.ds(pl.multiple_of(base, 64), 56), :] = blocks[m][c]

    assemble(xs, x_refs)
    for ref in (um, us, qs, ea):
        blank = jnp.zeros((step, ref.shape[1]), ref.dtype)
        ref[:step, :] = blank
        ref[step + rows :, :] = blank

    def rows_of(f):
        return pl.ds(pl.multiple_of(f * step, 64), step)

    def inner(f, shift=1):
        return pl.ds(pl.multiple_of((f + shift) * step, 64), step)

    def window(a):
        return slice(a * step, a * step + rows)

    def over_frames(body, init):
        return lax.fori_loop(0, frames, body, init)

    def box(f):
        value = qs[inner(f, 0), :] + qs[inner(f, 1), :] + qs[inner(f, 2), :]
        return jnp.where(mask, box_plane(value, 8) * (1.0 / 27.0), 0.0)

    za[:, :IN_OUT] = dot_nn(xs[...], win_ref[...])
    qs[window(1), :] = dot_nn(xs[...], wpool_ref[...])

    def pool_frame(f, total):
        z, p = za[rows_of(f), :IN_OUT], box(f)
        za[rows_of(f), IN_OUT:] = p
        return total + jnp.concatenate(
            [jnp.sum(z, axis=0, keepdims=True), jnp.sum(p, axis=0, keepdims=True)], axis=1
        )

    total_a = over_frames(pool_frame, jnp.zeros((1, SECTION_A), F32))
    mean_a = total_a * share

    def spread_frame(ref, mean):
        def body(f, total):
            delta = jnp.where(mask, ref[rows_of(f), :] - mean, 0.0)
            return total + jnp.sum(delta * delta, axis=0, keepdims=True)

        return body

    spread_a = over_frames(spread_frame(za, mean_a), jnp.zeros((1, SECTION_A), F32))
    scale_a = lax.rsqrt(spread_a * share + EPSILON)
    off_a, off_b = off_ref[:, :SECTION_A], off_ref[:, SECTION_A:]

    def normal_a(f, lo, hi):
        return (za[rows_of(f), lo:hi] - mean_a[:, lo:hi]) * scale_a[:, lo:hi]

    def unfold_frame(f, _):
        a = normal_a(f, C0, IN_OUT) + off_a[:, C0:IN_OUT]
        hidden = jnp.where(mask, act(a), 0.0)
        shifted = []
        for e in range(3):
            row = roll_rows(hidden, 8 * (1 - e))
            shifted += [roll_rows(row, 1 - g) for g in range(3)]
        um[inner(f), :] = jnp.concatenate([v[:, :C1A] for v in shifted], axis=1).astype(BF16)
        us[inner(f), :] = jnp.concatenate([v[:, C1A:] for v in shifted], axis=1).astype(BF16)
        return 0

    over_frames(unfold_frame, 0)
    loads[0].wait()

    def convolve(u_ref, w_ref):
        total = dot_nn(u_ref[window(0), :], w_ref[0])
        for a in range(1, 3):
            total = total + dot_nn(u_ref[window(a), :], w_ref[a])
        return total

    zb[:, :C1B] = convolve(um, wmid_ref)
    zb[:, C1B:] = convolve(us, wsmall_ref)
    turn_kernels(wmid_ref, tmid_ref, (1, 0, 2))
    turn_kernels(wsmall_ref, tsmall_ref, (1, 0, 2))

    def total_frame(f, total):
        return total + jnp.sum(jnp.where(mask, zb[rows_of(f), :], 0.0), axis=0, keepdims=True)

    zero_b = jnp.zeros((1, BOUT), F32)
    mean_b = over_frames(total_frame, zero_b) * share
    spread_b = over_frames(spread_frame(zb, mean_b), zero_b)
    scale_b = lax.rsqrt(spread_b * share + EPSILON)

    own = pl.ds(pl.multiple_of(here * step, 64), 64)
    hidden_a = act((za[own, :] - mean_a) * scale_a + off_a)
    hidden_b = act((zb[own, :] - mean_b) * scale_b + off_b)
    out_ref[...] = jnp.concatenate(
        [hidden_a[:, :C0], hidden_b, hidden_a[:, IN_OUT:]], axis=1
    ).astype(BF16)

    for load in loads[1 : 1 + frames]:
        load.wait()
    assemble(cs, cot_refs)

    def sums_b(f, carry):
        y = (zb[rows_of(f), :] - mean_b) * scale_b
        d = cs[rows_of(f), C0 : C0 + BOUT].astype(F32) * slope(y + off_b)
        zb[rows_of(f), :] = y
        da[rows_of(f), :BOUT] = d
        return (
            carry[0] + jnp.sum(d, axis=0, keepdims=True),
            carry[1] + jnp.sum(d * y, axis=0, keepdims=True),
        )

    sum_b, cross_b = over_frames(sums_b, (zero_b, zero_b))

    for ref in (eb, es):
        width = ref.shape[1] // 3
        blank = jnp.zeros((step, width), BF16)
        ref[rows - step :, width : 2 * width] = blank
        ref[:step, 2 * width :] = blank

    for f in range(frames):
        at = slice(f * step, (f + 1) * step)
        e = da[at, :BOUT] - sum_b * share - zb[at, :] * (cross_b * share)
        e = jnp.where(mask, scale_b * e, 0.0).astype(BF16)
        for i, row in enumerate((f, f - 1, f + 1)):
            if 0 <= row < frames:
                at = slice(row * step, (row + 1) * step)
                eb[at, i * C1B : (i + 1) * C1B] = e[:, :C1B]
                es[at, i * C2B : (i + 1) * C2B] = e[:, C1B:]

    def picker(count, cut, part_one, part_two, columns, edge):
        r = lax.broadcasted_iota(jnp.int32, (count, columns), 0)
        k = lax.broadcasted_iota(jnp.int32, (count, columns), 1)
        want = jnp.where(r < cut, here * part_one + r, edge + here * part_two + r - cut)
        return jnp.where(k == want, 1.0, 0.0).astype(BF16)

    pick_mid = picker(part_mid, part_mid, part_mid, 0, C1B, 0)
    pick_small = picker(part_small, part_small, part_small, 0, C2B, 0)
    et[...] = dot_nt(pick_mid, eb[:, :C1B]).astype(BF16)
    ets[...] = dot_nt(pick_small, es[:, :C2B]).astype(BF16)
    for a in range(3):
        gm = dot_nn(et[...], um[window(a), :])
        gmid_ref[9 * a : 9 * a + 9] = gm.T.reshape(9, C1A, part_mid)
        gs = dot_nn(ets[...], us[window(a), :])
        gsmall_ref[9 * a : 9 * a + 9] = gs.T.reshape(9, C2A, part_small)
    stores = [
        pltpu.make_async_copy(gmid_ref, gmid_hbm, sems.at[4 + frames]),
        pltpu.make_async_copy(gsmall_ref, gsmall_hbm, sems.at[5 + frames]),
    ]
    for store in stores:
        store.start()

    small = dot_nt(es[...], tsmall_ref[...])
    for e in range(3):
        mid = dot_nt(eb[...], tmid_ref[e * 3 * C1A : (e + 1) * 3 * C1A, :])
        for t, width, lanes in (
            (mid, C1A, slice(0, C1A)),
            (small[:, e * 3 * C2A : (e + 1) * 3 * C2A], C2A, slice(C1A, MID)),
        ):
            back = roll_rows(t[:, :width], -1) + t[:, width : 2 * width]
            back = back + roll_rows(t[:, 2 * width :], 1)
            back = roll_rows(back, 8 * (e - 1))
            if e > 0:
                back = back + da[:, lanes]
            da[:, lanes] = back

    def grad_a(f, carry):
        y = normal_a(f, 0, SECTION_A)
        gain = slope(y + off_a)
        cot = cs[rows_of(f), :]
        d = jnp.concatenate(
            [cot[:, :C0].astype(F32), da[rows_of(f), :MID], cot[:, C0 + BOUT :].astype(F32)], axis=1
        )
        d = jnp.where(mask, d * gain, 0.0)
        da[rows_of(f), :] = d
        za[rows_of(f), :] = y
        return (
            carry[0] + jnp.sum(d, axis=0, keepdims=True),
            carry[1] + jnp.sum(d * y, axis=0, keepdims=True),
        )

    zero_a = jnp.zeros((1, SECTION_A), F32)
    sum_a, cross_a = over_frames(grad_a, (zero_a, zero_a))
    goff_ref[...] = jnp.concatenate([sum_a, sum_b], axis=1)

    def error_a(f, _):
        e = da[rows_of(f), :] - sum_a * share - za[rows_of(f), :] * (cross_a * share)
        e = jnp.where(mask, scale_a * e, 0.0)
        ea[inner(f), :IN_OUT] = e[:, :IN_OUT].astype(BF16)
        qs[inner(f), :] = e[:, IN_OUT:].astype(BF16).astype(F32)
        return 0

    over_frames(error_a, 0)

    def spread_pool(f, _):
        ea[inner(f), IN_OUT:] = box(f).astype(BF16)
        return 0

    over_frames(spread_pool, 0)

    near = [(here + f) * step for f in range(3)]
    near = jnp.concatenate([ea[pl.ds(pl.multiple_of(r, 64), 64), :] for r in near], axis=0)
    dx = dot_nt(near[:, :IN_OUT], win_ref[...]) + dot_nt(near[:, IN_OUT:], wpool_ref[...])
    for load in loads[1 + frames :]:
        load.wait()
    first_errors(dx[64:128], *near_refs[1 + frames :], *moment_refs, *error_refs)
    dn_ref[:64, :], dn_ref[64:, :] = dx[:64, C0:], dx[128:, C0:]
    pick_a = picker(part_in + part_pool, part_in, part_in, part_pool, SECTION_A, IN_OUT)
    eat[...] = dot_nt(pick_a, ea[window(1), :]).astype(BF16)
    gin_ref[...] = dot_nn(eat[:part_in, :], xs[...])
    gpool_ref[...] = dot_nn(eat[part_in:, :], xs[...])
    for store in stores:
        store.wait()


def second_scratch(rows, step, part, clips, frames):
    wide = rows + 2 * step
    return [
        ((rows, OUTC), BF16), ((rows, OUTC), BF16), ((rows, SECTION_A), F32), ((rows, BOUT), F32),
        ((wide, 9 * C1A), BF16), ((wide, 9 * C2A), BF16), ((wide, POOL), F32),
        ((rows, 3 * C1B), BF16), ((rows, 3 * C2B), BF16), ((wide, SECTION_A), BF16),
        ((part[0], rows), BF16), ((part[1], rows), BF16), ((part[2] + part[3], rows), BF16),
        ((rows, SECTION_A), F32), ((9 * C1A, 3 * C1B), BF16), ((9 * C2A, 3 * C2B), BF16),
        ((27, C1A, part[0]), F32), ((27, C2A, part[1]), F32), ((3, 9 * C1A, C1B), BF16),
        *[((clips, 56, OUTC), BF16)] * frames, ((512, BOUT), F32),
        ((512, POOL), F32), ((512, C0), F32), pltpu.SemaphoreType.DMA((6 + frames,)),
    ]


def turn_kernels(w_ref, t_ref, order):
    width = w_ref.shape[2]
    for i, k in enumerate(order):
        t_ref[:, i * width : (i + 1) * width] = w_ref[k]


def spread_grad(d):
    r = lax.broadcasted_iota(jnp.int32, (256, 64), 0)
    k = lax.broadcasted_iota(jnp.int32, (256, 64), 1)
    spread = jnp.where(k == ((r >> 5) << 3) + ((r & 15) >> 1), 1.0, 0.0).astype(BF16)
    d = d * 0.125
    high = d.astype(BF16)
    low = (d - high.astype(F32)).astype(BF16)
    return dot_nn(spread, high) + dot_nn(spread, low)


def first_errors(
    dx, zb_ref, zp_ref, zc_ref, ma_ref, mb_ref, off_ref,
    db_ref, yb_ref, dp_ref, yp_ref, dc_ref, st_ref,
):
    g = spread_grad(dx)
    sums, crosses = [], []
    for z_ref, m_ref, lanes, part, offset, d_ref, y_ref in (
        (zb_ref, mb_ref, slice(C0, C0 + BOUT), slice(0, BOUT), SECTION_A, db_ref, yb_ref),
        (zp_ref, mb_ref, slice(C0 + BOUT, OUTC), slice(BOUT, BOUT + POOL), IN_OUT, dp_ref, yp_ref),
        (zc_ref, ma_ref, slice(0, C0), slice(0, C0), 0, dc_ref, None),
    ):
        width = part.stop - part.start
        total, cross = jnp.zeros((1, width), F32), jnp.zeros((1, width), F32)
        for f in range(2):
            rows = slice(f * 256, (f + 1) * 256)
            y = (z_ref[rows, :] - m_ref[0:1, part]) * m_ref[1:2, part]
            d = g[:, lanes] * slope(y + off_ref[:, offset : offset + width])
            d_ref[rows, :] = d.astype(BF16)
            if y_ref is not None:
                y_ref[rows, :] = y.astype(BF16)
            total = total + jnp.sum(d, axis=0, keepdims=True)
            cross = cross + jnp.sum(d * y, axis=0, keepdims=True)
        sums.append(total)
        crosses.append(cross)
    store_copies(st_ref, pack_rows(sums + crosses))


def beside_errors(dn, z_ref, mb_ref, off_ref, lanes, offset):
    z = z_ref[:, lanes].astype(F32)
    z = jnp.concatenate([z, jnp.zeros((32, z.shape[1]), F32)], axis=0)
    y = (z - mb_ref[0:1, lanes]) * mb_ref[1:2, lanes]
    return spread_grad(dn) * slope(y + off_ref[:, offset : offset + z.shape[1]]), y


def first_hidden_errors(
    cells, parts, flag_ref, st_ref, db_ref, yb_ref, dn_ref, before_ref, after_ref, mb_ref, off_ref,
    eb_ref, sum_ref, *chunk_refs,
):
    part_mid, part_small = C1B // parts, C2B // parts
    totals = jnp.sum(st_ref[...], axis=0)
    sum_ref[...] = totals
    sum_b, cross_b = unpack_rows(totals, 0, BOUT), unpack_rows(totals, 7, BOUT)
    scale_b = mb_ref[1:2, :BOUT]
    frame = valid_first(256)
    edge = jnp.zeros((16, BOUT), BF16)
    eb_ref[0:16, :] = edge
    eb_ref[1040:1056, :] = edge
    r = lax.broadcasted_iota(jnp.int32, (BOUT, part_mid + part_small), 0)
    k = lax.broadcasted_iota(jnp.int32, (BOUT, part_mid + part_small), 1)
    picks = []
    for m in range(parts):
        p = lax.rem(flag_ref[0] + m, parts)
        want = jnp.where(k < part_mid, p * part_mid + k, C1B + p * part_small + k - part_mid)
        picks.append(jnp.where(r == want, 1.0, 0.0).astype(BF16))
    for s in range(4):
        mask = frame
        if s == 0:
            mask = frame & (flag_ref[1] > 0)
            d, y = beside_errors(
                dn_ref[:64, :BOUT], before_ref, mb_ref, off_ref, slice(0, BOUT), SECTION_A
            )
        elif s == 3:
            mask = frame & (flag_ref[2] > 0)
            d, y = beside_errors(
                dn_ref[64:, :BOUT], after_ref, mb_ref, off_ref, slice(0, BOUT), SECTION_A
            )
        else:
            rows = slice((s - 1) * 256, s * 256)
            d, y = db_ref[rows, :].astype(F32), yb_ref[rows, :].astype(F32)
        e = scale_b * (d - sum_b * (1.0 / cells) - y * (cross_b * (1.0 / cells)))
        e = jnp.where(mask, e, 0.0).astype(BF16)
        eb_ref[16 + s * 256 : 16 + (s + 1) * 256, :] = e
        if s in (1, 2):
            for ref, pick in zip(chunk_refs, picks):
                ref[(s - 1) * 224 : s * 224, :] = dot_nn(e[:224], pick).astype(BF16)


def first_hidden_back(
    eb, zm_ref, ma_ref, off_ref, wmid_ref, wsmall_ref,
    dm_ref, st_ref,
):
    mids, smalls = None, None
    for a in range(3):
        for e in range(3):
            start = 16 + 256 - (a - 1) * 256 - (e - 1) * 16
            one = dot_nt(eb[start : start + 512, :C1B], wmid_ref[3 * a + e])
            two = dot_nt(eb[start : start + 512, C1B:], wsmall_ref[3 * a + e])
            mids = one if mids is None else mids + one
            smalls = two if smalls is None else smalls + two
    back = None
    for g in range(3):
        t = jnp.concatenate(
            [mids[:, g * C1A : (g + 1) * C1A], smalls[:, g * C2A : (g + 1) * C2A]], axis=1
        )
        t = roll_rows(t, g - 1)
        back = t if back is None else back + t
    y = (zm_ref[...] - ma_ref[0:1, C0:]) * ma_ref[1:2, C0:]
    d = jnp.where(valid_first(512), back * slope(y + off_ref[:, C0:IN_OUT]), 0.0)
    dm_ref[...] = d
    sums = jnp.sum(d, axis=0, keepdims=True)
    crosses = jnp.sum(d * y, axis=0, keepdims=True)
    store_copies(st_ref, pack_rows([sums, crosses]))


def first_kernel_grad(
    parts, flag_ref, *refs,
):
    errors, hidden = refs[:parts], refs[parts : 2 * parts]
    chunk_refs, (em, turned, kept) = refs[2 * parts : -3], refs[-3:]
    frames = 2 * parts
    chunks = len(chunk_refs)
    part_small = C2B // parts
    part_mid = C1B // parts
    here, clip = flag_ref[0], flag_ref[3]
    blank = jnp.zeros((16, 128), BF16)
    for m in range(parts):
        source = lax.rem(here - m + parts, parts)
        turned[:, pl.ds(pl.multiple_of(source * 512, 512), 512)] = hidden[m][...]
        for f in range(2):
            base = source * 512 + f * 256
            e = errors[m][f * 224 : f * 224 + 224, :].astype(F32)
            e = jnp.concatenate([e, jnp.zeros((224, 128 - e.shape[1]), F32)], axis=1)
            e = jnp.concatenate([e, jnp.zeros((32, 128), F32)], axis=0)
            for g in range(3):
                moved = roll_rows(e, g - 1).astype(BF16)
                lanes = [slice((3 * i + g) * 128, (3 * i + g + 1) * 128) for i in range(3)]

                def at(start, size):
                    return pl.ds(pl.multiple_of(base + start, 16), size)

                em[at(0, 240), lanes[0]] = moved[16:]
                em[at(240, 16), lanes[0]] = blank
                em[at(0, 256), lanes[1]] = moved
                em[at(0, 16), lanes[2]] = blank
                em[at(16, 240), lanes[2]] = moved[:240]
    mids, smalls = [], []
    for a in range(3):
        shift = 256 * (a - 1)
        lo, hi = max(0, shift), min(frames * 256, frames * 256 + shift)
        both = dot_nn(turned[:, lo:hi], em[lo - shift : hi - shift, :])
        for k in range(9):
            mids.append(both[:C1A, k * 128 : k * 128 + part_mid])
            smalls.append(both[C1A:, k * 128 + part_mid : k * 128 + part_mid + part_small])
    mids, smalls = jnp.concatenate(mids, axis=1), jnp.concatenate(smalls, axis=1)
    high, low = C1A // chunks, C2A // chunks
    wide = smalls.shape[1] // chunks
    blank = jnp.zeros((high - C2A, wide), F32)
    for i in range(chunks):
        tail = [smalls[i * low : (i + 1) * low, q * wide : (q + 1) * wide] for q in range(chunks)]
        tail = jnp.concatenate(tail + [blank], axis=0)
        kept[i * high : (i + 1) * high, :] = jnp.concatenate(
            [mids[i * high : (i + 1) * high], tail], axis=1
        )
    for m, ref in enumerate(chunk_refs):
        at = lax.rem(clip + m, chunks) * high
        ref[...] = kept[pl.ds(pl.multiple_of(at, 8), high), :].astype(BF16)


def first_kernel_join(flag_ref, *refs):
    chunks = len(refs) - 2
    gmid_ref, gsmall_ref = refs[chunks:]
    high, low = C1A // chunks, C2A // chunks
    part_mid, part_small = gmid_ref.shape[2], gsmall_ref.shape[2]
    for m in range(chunks):
        at = lax.rem(flag_ref[3] + m, chunks)
        value = refs[m][...].astype(F32)
        rows = pl.ds(pl.multiple_of(at * high, 8), high)
        for k in range(27):
            gmid_ref[k, rows, :] = value[:, k * part_mid : (k + 1) * part_mid]
        small = [value[q * low : (q + 1) * low, 27 * part_mid :] for q in range(chunks)]
        small = jnp.concatenate(small, axis=1)
        rows = pl.ds(pl.multiple_of(at * low, 8), low)
        for k in range(27):
            gsmall_ref[k, rows, :] = small[:, k * part_small : (k + 1) * part_small]


def first_input_errors(
    cells, parts, flag_ref, st_ref, sum_ref, dm_ref, dc_ref, dp_ref, yp_ref, dn_ref, before_ref,
    after_ref, zc_ref, zm_ref, ma_ref, mb_ref, off_ref, x_ref,
    ea, goff_ref, *refs,
):
    part_in, part_pool = IN_OUT // parts, POOL // parts
    totals = jnp.sum(st_ref[...], axis=0)
    before = sum_ref[...]
    sum_m, cross_m = unpack_rows(totals, 0, MID), unpack_rows(totals, 2, MID)
    sum_b = unpack_rows(before, 0, BOUT)
    sum_p, sum_c = unpack_rows(before, 4, POOL), unpack_rows(before, 5, C0)
    cross_p, cross_c = unpack_rows(before, 11, POOL), unpack_rows(before, 12, C0)
    goff_ref[...] = jnp.concatenate([sum_c, sum_m, sum_p, sum_b], axis=1)
    share = 1.0 / cells
    frame = valid_first(256)
    pools = []
    lanes = slice(BOUT, BOUT + POOL)
    for s in range(4):
        mask = frame
        if s == 0:
            mask = frame & (flag_ref[1] > 0)
            d, y = beside_errors(dn_ref[:64, lanes], before_ref, mb_ref, off_ref, lanes, IN_OUT)
        elif s == 3:
            mask = frame & (flag_ref[2] > 0)
            d, y = beside_errors(dn_ref[64:, lanes], after_ref, mb_ref, off_ref, lanes, IN_OUT)
        else:
            rows = slice((s - 1) * 256, s * 256)
            d, y = dp_ref[rows, :].astype(F32), yp_ref[rows, :].astype(F32)
        e = mb_ref[1:2, BOUT:] * (d - sum_p * share - y * (cross_p * share))
        pools.append(jnp.where(mask, e, 0.0).astype(BF16).astype(F32))
    for f in range(2):
        rows = slice(f * 256, (f + 1) * 256)
        value = box_plane(pools[f] + pools[f + 1] + pools[f + 2], 16) * (1.0 / 27.0)
        ea[rows, IN_OUT:] = jnp.where(frame, value, 0.0).astype(BF16)
        y = (zc_ref[rows, :] - ma_ref[0:1, :C0]) * ma_ref[1:2, :C0]
        e = dc_ref[rows, :].astype(F32) - sum_c * share - y * (cross_c * share)
        ea[rows, :C0] = jnp.where(frame, ma_ref[1:2, :C0] * e, 0.0).astype(BF16)
        y = (zm_ref[rows, :] - ma_ref[0:1, C0:]) * ma_ref[1:2, C0:]
        e = dm_ref[rows, :] - sum_m * share - y * (cross_m * share)
        ea[rows, C0:IN_OUT] = jnp.where(frame, ma_ref[1:2, C0:] * e, 0.0).astype(BF16)
    turned = dot_nt(eye(SECTION_A), ea[...]).astype(BF16)
    chunk_refs, g_ref = refs[:-1], refs[-1]
    g_ref[...] = dot_nn(turned, x_ref[...])
    for m, ref in enumerate(chunk_refs):
        p = lax.rem(flag_ref[0] + m, parts)
        rows = pl.ds(pl.multiple_of(p * part_in, 8), part_in)
        ref[:part_in] = g_ref[rows, :].astype(BF16)
        rows = pl.ds(pl.multiple_of(IN_OUT + p * part_pool, 8), part_pool)
        ref[part_in:] = g_ref[rows, :].astype(BF16)


def first_input_back(ea, win_ref, wpool_ref, dx_ref):
    dx_ref[...] = dot_nt(ea[:, :IN_OUT], win_ref[...]) + dot_nt(ea[:, IN_OUT:], wpool_ref[...])


def call(body, outs, scratch, *args, scalars=1, us=1, in_hbm=(), out_hbm=()):
    in_specs = []
    for i in range(len(args)):
        space = pltpu.SMEM if i < scalars else pl.ANY if i in in_hbm else pltpu.VMEM
        in_specs.append(pl.BlockSpec(memory_space=space))
    out_specs = [
        pl.BlockSpec(memory_space=pl.ANY if i in out_hbm else pltpu.VMEM) for i in range(len(outs))
    ]
    return pl.pallas_call(
        body,
        out_shape=[jax.ShapeDtypeStruct(s, d) for s, d in outs],
        in_specs=in_specs,
        out_specs=out_specs,
        scratch_shapes=[pltpu.VMEM(*s) if isinstance(s, tuple) else s for s in scratch],
        compiler_params=pltpu.CompilerParams(vmem_limit_bytes=VMEM_LIMIT),
        cost_estimate=pl.CostEstimate(
            flops=int(us * 1.1e9),
            bytes_accessed=sum(a.size * a.dtype.itemsize for a in args),
            transcendentals=0,
        ),
    )(*args)


def exchange(copies):
    return lax.all_to_all(copies, ("clip", "tm"), 0, 0)


def neighbours(head, tail):
    size = lax.axis_size("tm")
    up = [(i, i + 1) for i in range(size - 1)]
    down = [(i + 1, i) for i in range(size - 1)]
    return lax.ppermute(tail, "tm", up), lax.ppermute(head, "tm", down)


def gather_from(value, axis, back=False):
    size = lax.axis_size(axis)
    blocks = [value]
    for m in range(1, size):
        step = -m if back else m
        blocks.append(lax.ppermute(value, axis, [((i + step) % size, i) for i in range(size)]))
    return blocks


def hand_on(chunks, axis):
    size = lax.axis_size(axis)
    blocks = [chunks[0]]
    for m in range(1, size):
        blocks.append(lax.ppermute(chunks[m], axis, [(i, (i + m) % size) for i in range(size)]))
    return blocks


def to_all(value, axis):
    size = lax.axis_size(axis)
    return lax.all_to_all(jnp.broadcast_to(value[None], (size,) + value.shape), axis, 0, 0)


def turned_to(blocks, first):
    return lax.dynamic_slice_in_dim(jnp.concatenate([blocks, blocks]), first, blocks.shape[0])


def summed(parts):
    total = parts[0].astype(F32)
    for i in range(1, len(parts)):
        total = total + parts[i].astype(F32)
    return total.astype(BF16)


def after(value, *others):
    return lax.optimization_barrier((value,) + others)[0]


def small_group(
    features, w_in_4f, w_pool_4f, w_mid_4f, w_small_4f, offsets_4f,
    w_in_5b, w_pool_5b, w_mid_5b, w_small_5b, offsets_5b, cotangent,
):
    clips, frames = lax.axis_size("clip"), lax.axis_size("tm")
    group = clips * frames
    cells = 392.0 * group
    here = lax.axis_index("tm")
    flags = jnp.stack([here, here > 0, here < frames - 1, lax.axis_index("clip")]).astype(jnp.int32)
    offsets_4f, offsets_5b = offsets_4f[None], offsets_5b[None]
    x = jnp.pad(features[0], ((0, 0), (0, 2), (0, 2), (0, 0))).reshape(512, features.shape[-1])
    cot = jnp.pad(cotangent[0, 0], ((0, 0), (0, 1), (0, 0))).reshape(56, OUTC)
    mid_4f, small_4f = w_mid_4f.reshape(9, 3 * C1A, C1B), w_small_4f.reshape(9, 3 * C2A, C2B)
    mid_5b, small_5b = w_mid_5b.reshape(3, 9 * C1A, C1B), w_small_5b.reshape(3, 9 * C2A, C2B)
    before, behind = neighbours(x[:224], x[256:480])
    cot = jnp.stack(gather_from(cot, "clip"))
    z_c, z_m, q, stats = call(
        first_project,
        [((512, C0), F32), ((512, MID), F32), ((512, POOL), F32), ((group, 8, 128), F32)],
        [], x, w_in_4f, w_pool_4f, scalars=0, us=4,
    )
    stats = exchange(stats)
    stats, cot = lax.optimization_barrier((stats, cot))
    z_b, z_p, stats, x2_c, m_turned, head, tail, moments_a = call(
        first_hidden,
        [((512, BOUT), F32), ((512, POOL), F32), ((group, 16, 128), F32), ((56, C0), BF16),
         ((MID, 512), BF16),
         ((224, BOUT + POOL), BF16), ((224, BOUT + POOL), BF16), ((2, IN_OUT), F32)],
        [((1024, MID), F32), ((1056, 3 * C1A), BF16), ((1056, 3 * C2A), BF16),
         ((4, 128, 128), F32)],
        flags, stats, z_c, z_m, q, before, behind, w_in_4f, w_pool_4f, mid_4f, small_4f,
        offsets_4f, us=8,
    )
    cot = gather_from(after(cot, z_b), "tm")
    stats = exchange(stats)
    x2, moments_b = call(
        first_output,
        [((56, OUTC), BF16), ((2, BOUT + POOL), F32)],
        [((4, 128, 128), F32)],
        stats, z_b, z_p, x2_c, offsets_4f, scalars=0, us=3,
    )
    x2 = jnp.stack(gather_from(x2, "clip"))
    before, behind = neighbours(head, tail)
    m_turned = gather_from(m_turned, "tm", back=True)
    x2 = gather_from(after(x2, *cot), "tm")
    part = (C1B // frames, C2B // frames, IN_OUT // frames, POOL // frames)
    near = frames + 8
    (out, g_in_5b, g_pool_5b, g_mid_5b, g_small_5b, g_off_5b, d_near,
     d_b, y_b, d_p, y_p, d_c, stats) = call(
        functools.partial(second_layer, clips, frames),
        [((64, OUTC), BF16), ((part[2], OUTC), F32), ((part[3], OUTC), F32),
         ((27, C1A, part[0]), F32), ((27, C2A, part[1]), F32), ((1, 1024), F32),
         ((128, BOUT + POOL), F32),
         ((512, BOUT), BF16), ((512, BOUT), BF16), ((512, POOL), BF16), ((512, POOL), BF16),
         ((512, C0), BF16), ((group, 16, 128), F32)],
        second_scratch(group * 64, clips * 64, part, clips, frames),
        flags, *x2, w_in_5b, w_pool_5b, small_5b, offsets_5b, moments_a, moments_b, offsets_4f,
        mid_5b, *cot, z_b, z_p, z_c,
        us=35, in_hbm=range(near, near + 4 + frames), out_hbm=(3, 4),
    )
    stats = exchange(stats)
    e_b, sums, *errors = call(
        functools.partial(first_hidden_errors, cells, frames),
        [((1056, BOUT), BF16), ((16, 128), F32)] + [((448, part[0] + part[1]), BF16)] * frames,
        [], flags, stats, d_b, y_b, d_near, before, behind, moments_b, offsets_4f, us=3,
    )
    errors = hand_on(errors, "tm")
    d_m, stats = call(
        first_hidden_back,
        [((512, MID), F32), ((group, 8, 128), F32)],
        [], e_b, z_m, moments_a, offsets_4f, mid_4f, small_4f, scalars=0, us=6,
    )
    stats = exchange(stats)
    wide = 27 * part[0] + 27 * part[1] // clips
    g_conv = call(
        functools.partial(first_kernel_grad, frames),
        [((C1A // clips, wide), BF16)] * clips,
        [((frames * 512, 9 * 128), BF16), ((MID, frames * 512), BF16), ((C1A, wide), F32)],
        after(flags, d_m), *errors, *m_turned, us=10,
    )
    stats = after(stats, *g_conv)
    g_conv = hand_on(g_conv, "clip")
    e_a, g_off, *g_a = call(
        functools.partial(first_input_errors, cells, frames),
        [((512, SECTION_A), BF16), ((1, 1024), F32)]
        + [((part[2] + part[3], features.shape[-1]), BF16)] * frames,
        [((SECTION_A, features.shape[-1]), F32)], flags, stats, sums, d_m, d_c, d_p, y_p, d_near, before, behind,
        z_c, z_m, moments_a, moments_b, offsets_4f, x, us=20,
    )
    (d_x,) = call(
        first_input_back,
        [((512, features.shape[-1]), F32)],
        [], e_a, w_in_4f, w_pool_4f, scalars=0, us=0,
    )
    g_a = hand_on(g_a, "tm")
    g_conv = summed(lax.optimization_barrier((*g_conv, d_x))[:clips])
    g_a = summed(lax.optimization_barrier((*g_a, g_conv))[:frames])
    g_conv = gather_from(g_conv, "clip")
    g_a = hand_on(turned_to(g_a.reshape(clips, -1, features.shape[-1]), flags[3]), "clip")
    g_a = after(summed(g_a), *g_conv)
    g_a = jnp.stack(gather_from(g_a, "clip")).astype(F32)
    g_a = turned_to(g_a, lax.rem(clips - flags[3], clips)).reshape(part[2] + part[3], -1)
    g_mid, g_small = call(
        first_kernel_join,
        [((27, C1A, part[0]), F32), ((27, C2A, part[1]), F32)],
        [], flags, *g_conv, us=4,
    )

    return (
        out.reshape(1, 1, 8, 8, OUTC)[:, :, :7, :7],
        d_x.reshape(1, 2, 16, 16, -1)[:, :, :14, :14],
        g_a[: part[2]].T,
        g_a[part[2] :].T,
        g_mid,
        g_small,
        g_off[0],
        g_in_5b.T,
        g_pool_5b.T,
        g_mid_5b,
        g_small_5b,
        g_off_5b[0],
    )


def solution(mesh):
    placed = (
        P(("stream", "clip"), "tm", None, None, None),
        P("stream", None),
        P("stream", None),
        P("stream", None, None),
        P("stream", None, None),
        P("stream"),
        P("stream", None),
        P("stream", None),
        P("stream", None, None),
        P("stream", None, None),
        P("stream"),
        P(("stream", "clip"), "tm", None, None, None),
    )
    group = mesh.shape["clip"] * mesh.shape["tm"]
    return jax.shard_map(
        small_group if group <= 16 else shards,
        mesh=mesh,
        in_specs=placed,
        out_specs=(
            P(("stream", "clip"), "tm", None, None, None),
            P(("stream", "clip"), "tm", None, None, None),
            P("stream", "tm"),
            P("stream", "tm"),
            P("stream", None, "tm"),
            P("stream", None, "tm"),
            P("stream"),
            P("stream", "tm"),
            P("stream", "tm"),
            P("stream", None, "tm"),
            P("stream", None, "tm"),
            P("stream"),
        ),
        check_vma=False,
    )
```

```python
import functools

import jax
import jax.numpy as jnp
from jax import lax
from jax.experimental import pallas as pl
from jax.experimental.pallas import tpu as pltpu
from jax.sharding import PartitionSpec as P

C0 = 256
C1A = 160
C1B = 320
C2A = 32
C2B = 128
IN_OUT = 448
SECTION_A = 576


EPSILON = 0.001
VOXEL_AXES = (0, 1, 2, 3)


def extended(value, sides, width):
    for axis, dim in sides:
        size, length = (lax.axis_size(axis), value.shape[dim])
        up = [(i, (i + 1) % size) for i in range(size - 1)]
        down = [(j, i) for i, j in up]
        last = lax.slice_in_dim(value, length - width, length, axis=dim)
        first = lax.slice_in_dim(value, 0, width, axis=dim)
        before = lax.ppermute(last, axis, up)
        after = lax.ppermute(first, axis, down)
        value = jnp.concatenate([before, value, after], axis=dim)
    return value


def as_sent(value):
    return jax.tree.map(lambda a: a.astype(jnp.bfloat16) if a.dtype == jnp.float32 else a, value)


def project(values, weight):
    return jnp.einsum("nfhwc,cd->nfhwd", values, weight, preferred_element_type=jnp.float32)


def pad_plane(values):
    return jnp.pad(values, ((0, 0), (0, 0), (1, 1), (1, 1), (0, 0)))


def box_sum(padded):
    summed = padded[:, :-2] + padded[:, 1:-1] + padded[:, 2:]
    summed = summed[:, :, :-2] + summed[:, :, 1:-1] + summed[:, :, 2:]
    return summed[:, :, :, :-2] + summed[:, :, :, 1:-1] + summed[:, :, :, 2:]


def unfold(padded, frames, height, width):
    slices = []
    for shift_f in range(3):
        for shift_h in range(3):
            for shift_w in range(3):
                slices.append(
                    padded[
                        :,
                        shift_f : shift_f + frames,
                        shift_h : shift_h + height,
                        shift_w : shift_w + width,
                    ]
                )
    return jnp.concatenate(slices, axis=-1)


def fold_back(patch_grad, channels):
    summed = None
    offset_index = 0
    for shift_f in range(3):
        for shift_h in range(3):
            for shift_w in range(3):
                segment = patch_grad[..., offset_index * channels : (offset_index + 1) * channels]
                placed = jnp.pad(
                    segment,
                    (
                        (0, 0),
                        (shift_f, 2 - shift_f),
                        (shift_h, 2 - shift_h),
                        (shift_w, 2 - shift_w),
                        (0, 0),
                    ),
                )
                summed = placed if summed is None else summed + placed
                offset_index += 1
    return summed


def return_input_rims(grad_padded):
    interior = grad_padded[:, 1:-1]
    rim_pair = jnp.concatenate([grad_padded[:, :1], grad_padded[:, -1:]], axis=1)
    arrived = extended(rim_pair.astype(jnp.bfloat16), (("tm", 1),), 1).astype(rim_pair.dtype)
    interior = interior.at[:, 0].add(arrived[:, 0])
    return interior.at[:, -1].add(arrived[:, 3])


def return_hidden_rims(grad_padded):
    interior = grad_padded[:, 1:-1]
    rim_pair = jnp.concatenate([grad_padded[:, :1], grad_padded[:, -1:]], axis=1)
    arrived = extended(rim_pair.astype(jnp.bfloat16), (("tm", 1),), 1).astype(rim_pair.dtype)
    interior = interior.at[:, 0].add(arrived[:, 0])
    return interior.at[:, -1].add(arrived[:, 3])


def section_first(features, w_in, w_pool):
    rimmed = extended(features, (("tm", 1),), 1)
    padded = pad_plane(rimmed).astype(jnp.float32)
    pooled = (box_sum(padded) / 27.0).astype(jnp.bfloat16)
    pre_first = jnp.concatenate([project(features, w_in), project(pooled, w_pool)], axis=-1)
    return (pre_first, pooled)


def section_second(middle, w_mid, w_small):
    rimmed = extended(middle, (("tm", 1),), 1)
    padded = pad_plane(rimmed)
    frames, height, width = (middle.shape[1], middle.shape[2], middle.shape[3])
    patch_one = unfold(padded[..., :C1A], frames, height, width)
    patch_two = unfold(padded[..., C1A:], frames, height, width)
    pre_second = jnp.concatenate(
        [
            project(patch_one, w_mid.reshape(27 * C1A, C1B)),
            project(patch_two, w_small.reshape(27 * C2A, C2B)),
        ],
        axis=-1,
    )
    return (pre_second, patch_one, patch_two)


def moments(pre_act, voxel_count):
    first_sum = lax.psum(jnp.sum(pre_act, axis=VOXEL_AXES), ("clip", "tm"))
    center = first_sum / voxel_count
    spread = lax.psum(jnp.sum(jnp.square(pre_act - center), axis=VOXEL_AXES), ("clip", "tm"))
    variance = spread / voxel_count
    return (center, variance)


def standardize(pre_act, center, variance):
    return (pre_act - center) * lax.rsqrt(variance + EPSILON)


def silu_slope(act_in):
    sigmoid_value = jax.nn.sigmoid(act_in)
    return sigmoid_value + act_in * sigmoid_value * (1.0 - sigmoid_value)


def block_forward(features, params, voxel_count):
    w_in, w_pool, w_mid, w_small, offsets = params
    pre_first, pooled = section_first(features, w_in, w_pool)
    center_a, variance_a = moments(pre_first, voxel_count)
    hidden_a = jax.nn.silu(standardize(pre_first, center_a, variance_a) + offsets[:SECTION_A])
    middle = hidden_a[..., C0:IN_OUT].astype(jnp.bfloat16)
    pre_second, patch_one, patch_two = section_second(middle, w_mid, w_small)
    center_b, variance_b = moments(pre_second, voxel_count)
    hidden_b = jax.nn.silu(standardize(pre_second, center_b, variance_b) + offsets[SECTION_A:])
    block_out = jnp.concatenate([hidden_a[..., :C0], hidden_b, hidden_a[..., IN_OUT:]], axis=-1)
    return (block_out, (center_a, variance_a, center_b, variance_b))


def norm_back(slope_grad, normed, variance, voxel_count):
    sum_grad, sum_cross = lax.psum(
        (jnp.sum(slope_grad, axis=VOXEL_AXES), jnp.sum(slope_grad * normed, axis=VOXEL_AXES)),
        ("clip", "tm"),
    )
    scaled = lax.rsqrt(variance + EPSILON) * (
        slope_grad - sum_grad / voxel_count - normed * (sum_cross / voxel_count)
    )
    return (scaled.astype(jnp.bfloat16), sum_grad)


def block_backward(features, params, moment_pair, out_grad, voxel_count):
    w_in, w_pool, w_mid, w_small, offsets = params
    center_a, variance_a, center_b, variance_b = moment_pair
    pre_first, pooled = section_first(features, w_in, w_pool)
    normed_a = standardize(pre_first, center_a, variance_a)
    act_a = normed_a + offsets[:SECTION_A]
    middle = jax.nn.silu(act_a)[..., C0:IN_OUT].astype(jnp.bfloat16)
    pre_second, patch_one, patch_two = section_second(middle, w_mid, w_small)
    normed_b = standardize(pre_second, center_b, variance_b)
    act_b = normed_b + offsets[SECTION_A:]
    grad_b = out_grad[..., C0 : C0 + C1B + C2B] * silu_slope(act_b)
    error_b, offset_grad_b = norm_back(grad_b, normed_b, variance_b, voxel_count)
    error_one = error_b[..., :C1B]
    error_two = error_b[..., C1B:]
    grad_mid = jnp.einsum(
        "nfhwk,nfhwo->ko", patch_one, error_one, preferred_element_type=jnp.float32
    ).reshape(27, C1A, C1B)
    grad_small = jnp.einsum(
        "nfhwk,nfhwo->ko", patch_two, error_two, preferred_element_type=jnp.float32
    ).reshape(27, C2A, C2B)
    back_one = fold_back(
        jnp.einsum(
            "nfhwo,ko->nfhwk",
            error_one,
            w_mid.reshape(27 * C1A, C1B),
            preferred_element_type=jnp.float32,
        ),
        C1A,
    )
    back_two = fold_back(
        jnp.einsum(
            "nfhwo,ko->nfhwk",
            error_two,
            w_small.reshape(27 * C2A, C2B),
            preferred_element_type=jnp.float32,
        ),
        C2A,
    )
    middle_grad = return_hidden_rims(
        jnp.concatenate([back_one, back_two], axis=-1)[:, :, 1:-1, 1:-1]
    )
    grad_a = jnp.concatenate(
        [out_grad[..., :C0], middle_grad, out_grad[..., C0 + C1B + C2B :]], axis=-1
    ) * silu_slope(act_a)
    error_a, offset_grad_a = norm_back(grad_a, normed_a, variance_a, voxel_count)
    error_in = error_a[..., :IN_OUT]
    error_pool = error_a[..., IN_OUT:]
    grad_in = jnp.einsum("nfhwc,nfhwd->cd", features, error_in, preferred_element_type=jnp.float32)
    grad_pool = jnp.einsum(
        "nfhwc,nfhwd->cd", pooled, error_pool, preferred_element_type=jnp.float32
    )
    direct = jnp.einsum("nfhwd,cd->nfhwc", error_in, w_in, preferred_element_type=jnp.float32)
    pool_grad = jnp.einsum(
        "nfhwd,cd->nfhwc", error_pool, w_pool, preferred_element_type=jnp.float32
    )
    spread_pad = jnp.pad(pool_grad, ((0, 0), (2, 2), (2, 2), (2, 2), (0, 0)))
    padded_grad = (box_sum(spread_pad) / 27.0)[:, :, 1:-1, 1:-1]
    input_grad = direct + return_input_rims(padded_grad)
    return (
        input_grad,
        (grad_in, grad_pool, grad_mid, grad_small),
        jnp.concatenate([offset_grad_a, offset_grad_b]),
    )


def reduce_grads(weight_grads):
    summed = jax.tree.map(
        lambda part: part.astype(jnp.float32), lax.psum(as_sent(weight_grads), "clip")
    )
    reduced = (
        lax.psum_scatter(
            summed[0].astype(jnp.bfloat16), "tm", scatter_dimension=1, tiled=True
        ).astype(jnp.float32),
        lax.psum_scatter(
            summed[1].astype(jnp.bfloat16), "tm", scatter_dimension=1, tiled=True
        ).astype(jnp.float32),
        lax.psum_scatter(
            summed[2].astype(jnp.bfloat16), "tm", scatter_dimension=2, tiled=True
        ).astype(jnp.float32),
        lax.psum_scatter(
            summed[3].astype(jnp.bfloat16), "tm", scatter_dimension=2, tiled=True
        ).astype(jnp.float32),
    )
    return reduced


def halve_grid(values):
    n, f, h, w, c = values.shape
    return jnp.sum(values.reshape(n, f // 2, 2, h // 2, 2, w // 2, 2, c), axis=(2, 4, 6)) * 0.125


def spread_half(grad_small_grid):
    n, f, h, w, c = grad_small_grid.shape
    expanded = jnp.broadcast_to(
        (grad_small_grid * 0.125)[:, :, None, :, None, :, None, :], (n, f, 2, h, 2, w, 2, c)
    )
    return expanded.reshape(n, 2 * f, 2 * h, 2 * w, c)


def shards(
    features,
    w_in_4f,
    w_pool_4f,
    w_mid_4f,
    w_small_4f,
    offsets_4f,
    w_in_5b,
    w_pool_5b,
    w_mid_5b,
    w_small_5b,
    offsets_5b,
    cotangent,
):
    params_first = (w_in_4f, w_pool_4f, w_mid_4f, w_small_4f, offsets_4f)
    params_second = (w_in_5b, w_pool_5b, w_mid_5b, w_small_5b, offsets_5b)
    devices_used = lax.axis_size("clip") * lax.axis_size("tm")
    count_first = float(
        features.shape[0] * features.shape[1] * features.shape[2] * features.shape[3] * devices_used
    )
    count_second = count_first / 8.0
    out_first, moments_first = block_forward(features, params_first, count_first)
    input_second = halve_grid(out_first).astype(jnp.bfloat16)
    out_second, moments_second = block_forward(input_second, params_second, count_second)
    grad_second, weights_second, offsets_grad_second = block_backward(
        input_second, params_second, moments_second, cotangent.astype(jnp.float32), count_second
    )
    reduced_second = reduce_grads(weights_second)
    grad_first, weights_first, offsets_grad_first = block_backward(
        features, params_first, moments_first, spread_half(grad_second), count_first
    )
    reduced_first = reduce_grads(weights_first)
    final_out = out_second.astype(jnp.bfloat16)
    return (
        final_out,
        grad_first,
        reduced_first[0],
        reduced_first[1],
        reduced_first[2],
        reduced_first[3],
        offsets_grad_first,
        reduced_second[0],
        reduced_second[1],
        reduced_second[2],
        reduced_second[3],
        offsets_grad_second,
    )


F32 = jnp.float32
BF16 = jnp.bfloat16
MID = 192
BOUT = 448
POOL = 128
OUTC = 832
VMEM_LIMIT = 58 * 1024 * 1024


def dot_nn(a, b):
    return lax.dot_general(a, b, (((1,), (0,)), ((), ())), preferred_element_type=F32)


def dot_nt(a, b):
    return lax.dot_general(a, b, (((1,), (1,)), ((), ())), preferred_element_type=F32)


def roll_rows(value, shift):
    rows = value.shape[0]
    shift %= rows
    return value if shift == 0 else pltpu.roll(value, shift, 0)


def eye(n):
    r = lax.broadcasted_iota(jnp.int32, (n, n), 0)
    k = lax.broadcasted_iota(jnp.int32, (n, n), 1)
    return jnp.where(r == k, 1.0, 0.0).astype(BF16)


def valid_first(rows):
    r = lax.broadcasted_iota(jnp.int32, (rows, 1), 0)
    return ((r & 255) < 224) & ((r & 15) < 14)


def valid_second(rows):
    r = lax.broadcasted_iota(jnp.int32, (rows, 1), 0)
    return ((r & 63) < 56) & ((r & 7) < 7)


def sigmoid(a):
    return 0.5 * jnp.tanh(0.5 * a) + 0.5


def act(a):
    return a * sigmoid(a)


def slope(a):
    s = sigmoid(a)
    return s + a * s * (1.0 - s)


def pack_rows(vectors):
    pieces = []
    for v in vectors:
        width = v.shape[1]
        full = -(-width // 128) * 128
        if full != width:
            v = jnp.concatenate([v, jnp.zeros((1, full - width), F32)], axis=1)
        for i in range(full // 128):
            pieces.append(v[:, i * 128 : (i + 1) * 128])
    return jnp.concatenate(pieces, axis=0)


def unpack_rows(rows, start, width):
    count = -(-width // 128)
    return jnp.concatenate([rows[start + i : start + i + 1] for i in range(count)], axis=1)[
        :, :width
    ]


def store_copies(ref, rows):
    count, height = ref.shape[0], ref.shape[1]
    if rows.shape[0] < height:
        rows = jnp.concatenate([rows, jnp.zeros((height - rows.shape[0], 128), F32)], axis=0)
    for i in range(count):
        ref[i] = rows


def local_moments(value, mask, cells):
    total = jnp.sum(jnp.where(mask, value, 0.0), axis=0, keepdims=True)
    delta = jnp.where(mask, value - total * (1.0 / cells), 0.0)
    return total, jnp.sum(delta * delta, axis=0, keepdims=True)


def joint_moments(gathered, height, cells):
    devices = gathered.shape[0]
    sums, squares = gathered[:, :height], gathered[:, height : 2 * height]
    mean = jnp.sum(sums, axis=0) * (1.0 / (cells * devices))
    apart = sums * (1.0 / cells) - mean[None]
    spread = jnp.sum(squares, axis=0) + cells * jnp.sum(apart * apart, axis=0)
    return mean, lax.rsqrt(spread * (1.0 / (cells * devices)) + EPSILON)


def halve(total, scratch, dtype):
    width = total.shape[1]
    both = total[:256] + total[256:]
    pairs = jnp.sum(both.reshape(8, 2, 16, width), axis=1).reshape(128, width)
    pieces = []
    for i in range(-(-width // 128)):
        lanes = min(128, width - i * 128)
        scratch[i, :, :lanes] = pairs[:, i * 128 : i * 128 + lanes]
        piece = scratch[i, pl.ds(0, 64, 2), :] + scratch[i, pl.ds(1, 64, 2), :]
        pieces.append(piece[:, :lanes])
    halved = jnp.concatenate(pieces, axis=1)
    return (halved * 0.125).astype(dtype)


def box_plane(value, stride):
    value = value + roll_rows(value, stride) + roll_rows(value, -stride)
    return value + roll_rows(value, 1) + roll_rows(value, -1)


def first_project(x_ref, win_ref, wpool_ref, zc_ref, zm_ref, q_ref, st_ref):
    for f in range(2):
        rows = pl.ds(f * 256, 256)
        x = x_ref[rows, :]
        z = dot_nn(x, win_ref[...])
        zc_ref[rows, :], zm_ref[rows, :] = z[:, :C0], z[:, C0:]
        q_ref[rows, :] = dot_nn(x, wpool_ref[...])
    mask = valid_first(512)
    moments = [local_moments(ref[...], mask, 392) for ref in (zc_ref, zm_ref)]
    total, squares = [jnp.concatenate([m[i] for m in moments], axis=1) for i in range(2)]
    store_copies(st_ref, pack_rows([total, squares]))


def first_hidden(
    flag_ref, st_ref, zc_ref, zm_ref, q_ref, before_ref, after_ref, win_ref, wpool_ref, wmid_ref,
    wsmall_ref, off_ref,
    zb_ref, zp_ref, st2_ref, x2_ref, mt_ref, head_ref, tail_ref, ma_ref,
    mid, um_ref, us_ref, half,
):
    mean_rows, scale_rows = joint_moments(st_ref[...], 4, 392.0)
    mean, scale = unpack_rows(mean_rows, 0, IN_OUT), unpack_rows(scale_rows, 0, IN_OUT)
    ma_ref[...] = jnp.concatenate([mean, scale], axis=0)
    off = off_ref[:, :IN_OUT]
    frame = valid_first(256)
    prev, after = flag_ref[1] > 0, flag_ref[2] > 0

    def middle(z, mask):
        return jnp.where(mask, act((z - mean[:, C0:]) * scale[:, C0:] + off[:, C0:]), 0.0)

    blank = jnp.zeros((32, MID), F32)
    for start, ref, mask in ((0, before_ref, prev), (768, after_ref, after)):
        z = jnp.concatenate([dot_nn(ref[...], win_ref[:, C0:]), blank], axis=0)
        mid[start : start + 256, :] = middle(z, frame & mask)
    mid[256:512, :] = middle(zm_ref[0:256, :], frame)
    mid[512:768, :] = middle(zm_ref[256:512, :], frame)
    for ref in (um_ref, us_ref):
        edge = jnp.zeros((16, ref.shape[1]), BF16)
        ref[0:16, :] = edge
        ref[1040:1056, :] = edge

    for f in range(4):
        rows = slice(f * 256, (f + 1) * 256)
        shifted = [roll_rows(mid[rows, :], 1 - g) for g in range(3)]
        into = slice(16 + f * 256, 16 + (f + 1) * 256)
        um_ref[into, :] = jnp.concatenate([v[:, :C1A] for v in shifted], axis=1).astype(BF16)
        us_ref[into, :] = jnp.concatenate([v[:, C1A:] for v in shifted], axis=1).astype(BF16)

    def convolve(u_ref, w_ref):
        total = None
        for a in range(3):
            for e in range(3):
                start = 16 + a * 256 + (e - 1) * 16
                term = dot_nn(u_ref[start : start + 512, :], w_ref[3 * a + e])
                total = term if total is None else total + term
        return total

    zb_ref[:, :C1B] = convolve(um_ref, wmid_ref)
    zb_ref[:, C1B:] = convolve(us_ref, wsmall_ref)

    first, last = q_ref[0:256, :], q_ref[256:512, :]
    pair = first + last
    for f, ref in ((0, before_ref), (1, after_ref)):
        beside = jnp.concatenate([dot_nn(ref[...], wpool_ref[...]), blank[:, :POOL]], axis=0)
        value = pair + beside
        value = box_plane(value, 16) * (1.0 / 27.0)
        zp_ref[f * 256 : (f + 1) * 256, :] = jnp.where(frame, value, 0.0)

    both = valid_first(512)
    total_b, squares_b = local_moments(zb_ref[...], both, 392)
    total_p, squares_p = local_moments(zp_ref[...], both, 392)
    store_copies(st2_ref, pack_rows([total_b, total_p, squares_b, squares_p]))
    for f, ref in ((0, head_ref), (1, tail_ref)):
        rows = pl.ds(f * 256, 224)
        ref[:, :BOUT] = zb_ref[rows, :].astype(BF16)
        ref[:, BOUT:] = zp_ref[rows, :].astype(BF16)
    hidden = act((zc_ref[...] - mean[:, :C0]) * scale[:, :C0] + off[:, :C0])
    x2_ref[...] = halve(jnp.where(both, hidden, 0.0), half, BF16)[:56]
    mt_ref[...] = dot_nt(eye(MID), mid[256:768, :].astype(BF16)).astype(BF16)


def first_output(st_ref, zb_ref, zp_ref, x2c_ref, off_ref, x2_ref, mb_ref, half):
    mean_rows, scale_rows = joint_moments(st_ref[...], 5, 392.0)
    both = valid_first(512)
    moments = []
    for start, width, z_ref, offset in ((0, BOUT, zb_ref, SECTION_A), (4, POOL, zp_ref, IN_OUT)):
        mean, scale = unpack_rows(mean_rows, start, width), unpack_rows(scale_rows, start, width)
        hidden = act((z_ref[...] - mean) * scale + off_ref[:, offset : offset + width])
        into = slice(C0, C0 + BOUT) if start == 0 else slice(C0 + BOUT, OUTC)
        x2_ref[:, into] = halve(jnp.where(both, hidden, 0.0), half, BF16)[:56]
        moments.append(jnp.concatenate([mean, scale], axis=0))
    x2_ref[:, :C0] = x2c_ref[...]
    mb_ref[...] = jnp.concatenate(moments, axis=1)


def second_layer(clips, frames, flag_ref, *refs):
    x_refs, cot_refs, refs = refs[:frames], refs[frames : 2 * frames], refs[2 * frames :]
    win_ref, wpool_ref, wsmall_ref, off_ref = refs[:4]
    moment_refs, far_refs, refs = refs[4:7], refs[7:11], refs[11:]
    out_ref, gin_ref, gpool_ref, gmid_hbm, gsmall_hbm, goff_ref = refs[:6]
    dn_ref, error_refs, scratch = refs[6], refs[7:13], refs[13:]
    xs, cs, za, zb, um, us, qs, eb, es, ea, et, ets, eat, da, tmid_ref, tsmall_ref = scratch[:16]
    gmid_ref, gsmall_ref, near_refs, sems = *scratch[16:18], scratch[18:-1], scratch[-1]
    loads = [
        pltpu.make_async_copy(far, near, sems.at[i])
        for i, (far, near) in enumerate(zip(far_refs, near_refs))
    ]
    loads[0].start()
    wmid_ref = near_refs[0]
    here = flag_ref[0]
    step = clips * 64
    rows = frames * step
    cells = clips * frames * 49.0
    share = 1.0 / cells
    part_mid, part_small = gmid_ref.shape[2], gsmall_ref.shape[2]
    part_in, part_pool = gin_ref.shape[0], gpool_ref.shape[0]
    mask = valid_second(step)

    tail = jnp.zeros((16, OUTC), BF16)

    def assemble(into, blocks):
        for m in range(frames):
            for c in range(clips):
                base = lax.rem(here + m, frames) * step + c * 64
                into[pl.ds(pl.multiple_of(base + 48, 16), 16), :] = tail
                into[pl.ds(pl.multiple_of(base, 64), 56), :] = blocks[m][c]

    assemble(xs, x_refs)
    for ref in (um, us, qs, ea):
        blank = jnp.zeros((step, ref.shape[1]), ref.dtype)
        ref[:step, :] = blank
        ref[step + rows :, :] = blank

    def rows_of(f):
        return slice(f * step, (f + 1) * step)

    def inner(f, shift=1):
        return slice((f + shift) * step, (f + shift + 1) * step)

    def window(a):
        return slice(a * step, a * step + rows)

    def over_frames(body, init):
        for f in range(frames):
            init = body(f, init)
        return init

    def box(f):
        value = qs[inner(f, 0), :] + qs[inner(f, 1), :] + qs[inner(f, 2), :]
        return jnp.where(mask, box_plane(value, 8) * (1.0 / 27.0), 0.0)

    za[:, :IN_OUT] = dot_nn(xs[...], win_ref[...])
    qs[window(1), :] = dot_nn(xs[...], wpool_ref[...])

    def pool_frame(f, total):
        z, p = za[rows_of(f), :IN_OUT], box(f)
        za[rows_of(f), IN_OUT:] = p
        return total + jnp.concatenate(
            [jnp.sum(z, axis=0, keepdims=True), jnp.sum(p, axis=0, keepdims=True)], axis=1
        )

    total_a = over_frames(pool_frame, jnp.zeros((1, SECTION_A), F32))
    mean_a = total_a * share

    def spread_frame(ref, mean):
        def body(f, total):
            delta = jnp.where(mask, ref[rows_of(f), :] - mean, 0.0)
            return total + jnp.sum(delta * delta, axis=0, keepdims=True)

        return body

    spread_a = over_frames(spread_frame(za, mean_a), jnp.zeros((1, SECTION_A), F32))
    scale_a = lax.rsqrt(spread_a * share + EPSILON)
    off_a, off_b = off_ref[:, :SECTION_A], off_ref[:, SECTION_A:]

    def normal_a(f, lo, hi):
        return (za[rows_of(f), lo:hi] - mean_a[:, lo:hi]) * scale_a[:, lo:hi]

    def unfold_frame(f, _):
        a = normal_a(f, C0, IN_OUT) + off_a[:, C0:IN_OUT]
        hidden = jnp.where(mask, act(a), 0.0)
        aside = [roll_rows(hidden, 1 - g) for g in range(3)]
        shifted = [roll_rows(v, 8 * (1 - e)) for e in range(3) for v in aside]
        um[inner(f), :] = jnp.concatenate([v[:, :C1A] for v in shifted], axis=1).astype(BF16)
        us[inner(f), :] = jnp.concatenate([v[:, C1A:] for v in shifted], axis=1).astype(BF16)
        return 0

    over_frames(unfold_frame, 0)
    loads[0].wait()
    for load in loads[1:]:
        load.start()

    def convolve(u_ref, w_ref):
        total = dot_nn(u_ref[window(0), :], w_ref[0])
        for a in range(1, 3):
            total = total + dot_nn(u_ref[window(a), :], w_ref[a])
        return total

    zb[:, :C1B] = convolve(um, wmid_ref)
    zb[:, C1B:] = convolve(us, wsmall_ref)
    turn_kernels(wmid_ref, tmid_ref, (1, 0, 2))
    turn_kernels(wsmall_ref, tsmall_ref, (1, 0, 2))

    def total_frame(f, total):
        return total + jnp.sum(jnp.where(mask, zb[rows_of(f), :], 0.0), axis=0, keepdims=True)

    zero_b = jnp.zeros((1, BOUT), F32)
    mean_b = over_frames(total_frame, zero_b) * share
    spread_b = over_frames(spread_frame(zb, mean_b), zero_b)
    scale_b = lax.rsqrt(spread_b * share + EPSILON)

    own = pl.ds(pl.multiple_of(here * step, 64), 64)
    hidden_a = act((za[own, :] - mean_a) * scale_a + off_a)
    hidden_b = act((zb[own, :] - mean_b) * scale_b + off_b)
    out_ref[...] = jnp.concatenate(
        [hidden_a[:, :C0], hidden_b, hidden_a[:, IN_OUT:]], axis=1
    ).astype(BF16)

    assemble(cs, cot_refs)

    def sums_b(f, carry):
        y = (zb[rows_of(f), :] - mean_b) * scale_b
        d = cs[rows_of(f), C0 : C0 + BOUT].astype(F32) * slope(y + off_b)
        zb[rows_of(f), :] = y
        da[rows_of(f), :BOUT] = d
        return (
            carry[0] + jnp.sum(d, axis=0, keepdims=True),
            carry[1] + jnp.sum(d * y, axis=0, keepdims=True),
        )

    sum_b, cross_b = over_frames(sums_b, (zero_b, zero_b))

    for ref in (eb, es):
        width = ref.shape[1] // 3
        blank = jnp.zeros((step, width), BF16)
        ref[rows - step :, width : 2 * width] = blank
        ref[:step, 2 * width :] = blank

    for f in range(frames):
        at = slice(f * step, (f + 1) * step)
        e = da[at, :BOUT] - sum_b * share - zb[at, :] * (cross_b * share)
        e = jnp.where(mask, scale_b * e, 0.0).astype(BF16)
        for i, row in enumerate((f, f - 1, f + 1)):
            if 0 <= row < frames:
                at = slice(row * step, (row + 1) * step)
                eb[at, i * C1B : (i + 1) * C1B] = e[:, :C1B]
                es[at, i * C2B : (i + 1) * C2B] = e[:, C1B:]

    def picker(count, cut, part_one, part_two, columns, edge):
        r = lax.broadcasted_iota(jnp.int32, (count, columns), 0)
        k = lax.broadcasted_iota(jnp.int32, (count, columns), 1)
        want = jnp.where(r < cut, here * part_one + r, edge + here * part_two + r - cut)
        return jnp.where(k == want, 1.0, 0.0).astype(BF16)

    pick_mid = picker(part_mid, part_mid, part_mid, 0, C1B, 0)
    pick_small = picker(part_small, part_small, part_small, 0, C2B, 0)
    et[...] = dot_nt(pick_mid, eb[:, :C1B]).astype(BF16)
    ets[...] = dot_nt(pick_small, es[:, :C2B]).astype(BF16)
    for a in range(3):
        gm = dot_nn(et[...], um[window(a), :])
        gmid_ref[9 * a : 9 * a + 9] = gm.T.reshape(9, C1A, part_mid)
        gs = dot_nn(ets[...], us[window(a), :])
        gsmall_ref[9 * a : 9 * a + 9] = gs.T.reshape(9, C2A, part_small)
    stores = [
        pltpu.make_async_copy(gmid_ref, gmid_hbm, sems.at[4]),
        pltpu.make_async_copy(gsmall_ref, gsmall_hbm, sems.at[5]),
    ]
    for store in stores:
        store.start()

    small = dot_nt(es[...], tsmall_ref[...])
    sides = [None] * 3
    for e in range(3):
        mid = dot_nt(eb[...], tmid_ref[e * 3 * C1A : (e + 1) * 3 * C1A, :])
        for g in range(3):
            k = 3 * e + g
            t = jnp.concatenate(
                [mid[:, g * C1A : (g + 1) * C1A], small[:, k * C2A : (k + 1) * C2A]], axis=1
            )
            t = roll_rows(t, 8 * (e - 1))
            sides[g] = t if e == 0 else sides[g] + t
    da[:, :MID] = roll_rows(sides[0], -1) + sides[1] + roll_rows(sides[2], 1)

    def grad_a(f, carry):
        y = normal_a(f, 0, SECTION_A)
        gain = slope(y + off_a)
        cot = cs[rows_of(f), :]
        d = jnp.concatenate(
            [cot[:, :C0].astype(F32), da[rows_of(f), :MID], cot[:, C0 + BOUT :].astype(F32)], axis=1
        )
        d = jnp.where(mask, d * gain, 0.0)
        da[rows_of(f), :] = d
        za[rows_of(f), :] = y
        return (
            carry[0] + jnp.sum(d, axis=0, keepdims=True),
            carry[1] + jnp.sum(d * y, axis=0, keepdims=True),
        )

    zero_a = jnp.zeros((1, SECTION_A), F32)
    sum_a, cross_a = over_frames(grad_a, (zero_a, zero_a))
    goff_ref[...] = jnp.concatenate([sum_a, sum_b], axis=1)

    def error_a(f, _):
        e = da[rows_of(f), :] - sum_a * share - za[rows_of(f), :] * (cross_a * share)
        e = jnp.where(mask, scale_a * e, 0.0)
        ea[inner(f), :IN_OUT] = e[:, :IN_OUT].astype(BF16)
        qs[inner(f), :] = e[:, IN_OUT:].astype(BF16).astype(F32)
        return 0

    over_frames(error_a, 0)

    def spread_pool(f, _):
        ea[inner(f), IN_OUT:] = box(f).astype(BF16)
        return 0

    over_frames(spread_pool, 0)

    near = [(here + f) * step for f in range(3)]
    near = jnp.concatenate([ea[pl.ds(pl.multiple_of(r, 64), 64), :] for r in near], axis=0)
    dx = dot_nt(near[:, :IN_OUT], win_ref[...]) + dot_nt(near[:, IN_OUT:], wpool_ref[...])
    for load in loads[1:]:
        load.wait()
    first_errors(dx[64:128], *near_refs[1:], *moment_refs, *error_refs)
    dn_ref[:64, :], dn_ref[64:, :] = dx[:64, C0:], dx[128:, C0:]
    pick_a = picker(part_in + part_pool, part_in, part_in, part_pool, SECTION_A, IN_OUT)
    eat[...] = dot_nt(pick_a, ea[window(1), :]).astype(BF16)
    gin_ref[...] = dot_nn(eat[:part_in, :], xs[...])
    gpool_ref[...] = dot_nn(eat[part_in:, :], xs[...])
    for store in stores:
        store.wait()


def second_scratch(rows, step, part):
    wide = rows + 2 * step
    return [
        ((rows, OUTC), BF16), ((rows, OUTC), BF16), ((rows, SECTION_A), F32), ((rows, BOUT), F32),
        ((wide, 9 * C1A), BF16), ((wide, 9 * C2A), BF16), ((wide, POOL), F32),
        ((rows, 3 * C1B), BF16), ((rows, 3 * C2B), BF16), ((wide, SECTION_A), BF16),
        ((part[0], rows), BF16), ((part[1], rows), BF16), ((part[2] + part[3], rows), BF16),
        ((rows, SECTION_A), F32), ((9 * C1A, 3 * C1B), BF16), ((9 * C2A, 3 * C2B), BF16),
        ((27, C1A, part[0]), F32), ((27, C2A, part[1]), F32), ((3, 9 * C1A, C1B), BF16),
        ((512, BOUT), F32),
        ((512, POOL), F32), ((512, C0), F32), pltpu.SemaphoreType.DMA((6,)),
    ]


def turn_kernels(w_ref, t_ref, order):
    width = w_ref.shape[2]
    for i, k in enumerate(order):
        t_ref[:, i * width : (i + 1) * width] = w_ref[k]


def spread_grad(d):
    r = lax.broadcasted_iota(jnp.int32, (256, 64), 0)
    k = lax.broadcasted_iota(jnp.int32, (256, 64), 1)
    spread = jnp.where(k == ((r >> 5) << 3) + ((r & 15) >> 1), 1.0, 0.0).astype(BF16)
    d = d * 0.125
    high = d.astype(BF16)
    low = (d - high.astype(F32)).astype(BF16)
    return dot_nn(spread, high) + dot_nn(spread, low)


def first_errors(
    dx, zb_ref, zp_ref, zc_ref, ma_ref, mb_ref, off_ref,
    db_ref, yb_ref, dp_ref, yp_ref, dc_ref, st_ref,
):
    g = spread_grad(dx)
    sums, crosses = [], []
    for z_ref, m_ref, lanes, part, offset, d_ref, y_ref in (
        (zb_ref, mb_ref, slice(C0, C0 + BOUT), slice(0, BOUT), SECTION_A, db_ref, yb_ref),
        (zp_ref, mb_ref, slice(C0 + BOUT, OUTC), slice(BOUT, BOUT + POOL), IN_OUT, dp_ref, yp_ref),
        (zc_ref, ma_ref, slice(0, C0), slice(0, C0), 0, dc_ref, None),
    ):
        width = part.stop - part.start
        total, cross = jnp.zeros((1, width), F32), jnp.zeros((1, width), F32)
        for f in range(2):
            rows = slice(f * 256, (f + 1) * 256)
            y = (z_ref[rows, :] - m_ref[0:1, part]) * m_ref[1:2, part]
            d = g[:, lanes] * slope(y + off_ref[:, offset : offset + width])
            d_ref[rows, :] = d.astype(BF16)
            if y_ref is not None:
                y_ref[rows, :] = y.astype(BF16)
            total = total + jnp.sum(d, axis=0, keepdims=True)
            cross = cross + jnp.sum(d * y, axis=0, keepdims=True)
        sums.append(total)
        crosses.append(cross)
    store_copies(st_ref, pack_rows(sums + crosses))


def beside_errors(dn, z_ref, mb_ref, off_ref, lanes, offset):
    z = z_ref[:, lanes].astype(F32)
    z = jnp.concatenate([z, jnp.zeros((32, z.shape[1]), F32)], axis=0)
    y = (z - mb_ref[0:1, lanes]) * mb_ref[1:2, lanes]
    return spread_grad(dn) * slope(y + off_ref[:, offset : offset + z.shape[1]]), y


def first_hidden_errors(
    cells, parts, flag_ref, st_ref, db_ref, yb_ref, dn_ref, before_ref, after_ref, mb_ref, off_ref,
    eb_ref, sum_ref, *chunk_refs,
):
    part_mid, part_small = C1B // parts, C2B // parts
    totals = jnp.sum(st_ref[...], axis=0)
    sum_ref[...] = totals
    sum_b, cross_b = unpack_rows(totals, 0, BOUT), unpack_rows(totals, 7, BOUT)
    scale_b = mb_ref[1:2, :BOUT]
    frame = valid_first(256)
    edge = jnp.zeros((16, BOUT), BF16)
    eb_ref[0:16, :] = edge
    eb_ref[1040:1056, :] = edge
    r = lax.broadcasted_iota(jnp.int32, (BOUT, part_mid + part_small), 0)
    k = lax.broadcasted_iota(jnp.int32, (BOUT, part_mid + part_small), 1)
    picks = []
    for m in range(parts):
        p = lax.rem(flag_ref[0] + m, parts)
        want = jnp.where(k < part_mid, p * part_mid + k, C1B + p * part_small + k - part_mid)
        picks.append(jnp.where(r == want, 1.0, 0.0).astype(BF16))
    for s in range(4):
        mask = frame
        if s == 0:
            mask = frame & (flag_ref[1] > 0)
            d, y = beside_errors(
                dn_ref[:64, :BOUT], before_ref, mb_ref, off_ref, slice(0, BOUT), SECTION_A
            )
        elif s == 3:
            mask = frame & (flag_ref[2] > 0)
            d, y = beside_errors(
                dn_ref[64:, :BOUT], after_ref, mb_ref, off_ref, slice(0, BOUT), SECTION_A
            )
        else:
            rows = slice((s - 1) * 256, s * 256)
            d, y = db_ref[rows, :].astype(F32), yb_ref[rows, :].astype(F32)
        e = scale_b * (d - sum_b * (1.0 / cells) - y * (cross_b * (1.0 / cells)))
        e = jnp.where(mask, e, 0.0).astype(BF16)
        eb_ref[16 + s * 256 : 16 + (s + 1) * 256, :] = e
        if s in (1, 2):
            for ref, pick in zip(chunk_refs, picks):
                ref[(s - 1) * 224 : s * 224, :] = dot_nn(e[:224], pick).astype(BF16)


def first_hidden_back(
    eb, zm_ref, ma_ref, off_ref, wmid_ref, wsmall_ref,
    dm_ref, st_ref,
):
    mids, smalls = None, None
    for a in range(3):
        for e in range(3):
            start = 16 + 256 - (a - 1) * 256 - (e - 1) * 16
            one = dot_nt(eb[start : start + 512, :C1B], wmid_ref[3 * a + e])
            two = dot_nt(eb[start : start + 512, C1B:], wsmall_ref[3 * a + e])
            mids = one if mids is None else mids + one
            smalls = two if smalls is None else smalls + two
    back = None
    for g in range(3):
        t = jnp.concatenate(
            [mids[:, g * C1A : (g + 1) * C1A], smalls[:, g * C2A : (g + 1) * C2A]], axis=1
        )
        t = roll_rows(t, g - 1)
        back = t if back is None else back + t
    y = (zm_ref[...] - ma_ref[0:1, C0:]) * ma_ref[1:2, C0:]
    d = jnp.where(valid_first(512), back * slope(y + off_ref[:, C0:IN_OUT]), 0.0)
    dm_ref[...] = d
    sums = jnp.sum(d, axis=0, keepdims=True)
    crosses = jnp.sum(d * y, axis=0, keepdims=True)
    store_copies(st_ref, pack_rows([sums, crosses]))


def first_kernel_grad(
    parts, flag_ref, *refs,
):
    errors, hidden = refs[:parts], refs[parts : 2 * parts]
    chunk_refs, (em, turned, kept) = refs[2 * parts : -3], refs[-3:]
    frames = 2 * parts
    chunks = len(chunk_refs)
    part_small = C2B // parts
    part_mid = C1B // parts
    here, clip = flag_ref[0], flag_ref[3]
    blank = jnp.zeros((16, 128), BF16)
    for m in range(parts):
        source = lax.rem(here - m + parts, parts)
        turned[:, pl.ds(pl.multiple_of(source * 512, 512), 512)] = hidden[m][...]
        for f in range(2):
            base = source * 512 + f * 256
            e = errors[m][f * 224 : f * 224 + 224, :].astype(F32)
            e = jnp.concatenate([e, jnp.zeros((224, 128 - e.shape[1]), F32)], axis=1)
            e = jnp.concatenate([e, jnp.zeros((32, 128), F32)], axis=0)
            for g in range(3):
                moved = roll_rows(e, g - 1).astype(BF16)
                lanes = [slice((3 * i + g) * 128, (3 * i + g + 1) * 128) for i in range(3)]

                def at(start, size):
                    return pl.ds(pl.multiple_of(base + start, 16), size)

                em[at(0, 240), lanes[0]] = moved[16:]
                em[at(240, 16), lanes[0]] = blank
                em[at(0, 256), lanes[1]] = moved
                em[at(0, 16), lanes[2]] = blank
                em[at(16, 240), lanes[2]] = moved[:240]
    mids, smalls = [], []
    for a in range(3):
        shift = 256 * (a - 1)
        lo, hi = max(0, shift), min(frames * 256, frames * 256 + shift)
        both = dot_nn(turned[:, lo:hi], em[lo - shift : hi - shift, :])
        for k in range(9):
            mids.append(both[:C1A, k * 128 : k * 128 + part_mid])
            smalls.append(both[C1A:, k * 128 + part_mid : k * 128 + part_mid + part_small])
    mids, smalls = jnp.concatenate(mids, axis=1), jnp.concatenate(smalls, axis=1)
    high, low = C1A // chunks, C2A // chunks
    wide = smalls.shape[1] // chunks
    blank = jnp.zeros((high - C2A, wide), F32)
    for i in range(chunks):
        tail = [smalls[i * low : (i + 1) * low, q * wide : (q + 1) * wide] for q in range(chunks)]
        tail = jnp.concatenate(tail + [blank], axis=0)
        kept[i * high : (i + 1) * high, :] = jnp.concatenate(
            [mids[i * high : (i + 1) * high], tail], axis=1
        )
    for m, ref in enumerate(chunk_refs):
        at = lax.rem(clip + m, chunks) * high
        ref[...] = kept[pl.ds(pl.multiple_of(at, 8), high), :].astype(BF16)


def first_kernel_join(flag_ref, *refs):
    chunks = len(refs) - 2
    gmid_ref, gsmall_ref = refs[chunks:]
    high, low = C1A // chunks, C2A // chunks
    part_mid, part_small = gmid_ref.shape[2], gsmall_ref.shape[2]
    for m in range(chunks):
        at = lax.rem(flag_ref[3] + m, chunks)
        value = refs[m][...].astype(F32)
        rows = pl.ds(pl.multiple_of(at * high, 8), high)
        for k in range(27):
            gmid_ref[k, rows, :] = value[:, k * part_mid : (k + 1) * part_mid]
        small = [value[q * low : (q + 1) * low, 27 * part_mid :] for q in range(chunks)]
        small = jnp.concatenate(small, axis=1)
        rows = pl.ds(pl.multiple_of(at * low, 8), low)
        for k in range(27):
            gsmall_ref[k, rows, :] = small[:, k * part_small : (k + 1) * part_small]


def first_input_errors(
    cells, parts, flag_ref, st_ref, sum_ref, dm_ref, dc_ref, dp_ref, yp_ref, dn_ref, before_ref,
    after_ref, zc_ref, zm_ref, ma_ref, mb_ref, off_ref, x_ref,
    ea, goff_ref, *refs,
):
    part_in, part_pool = IN_OUT // parts, POOL // parts
    totals = jnp.sum(st_ref[...], axis=0)
    before = sum_ref[...]
    sum_m, cross_m = unpack_rows(totals, 0, MID), unpack_rows(totals, 2, MID)
    sum_b = unpack_rows(before, 0, BOUT)
    sum_p, sum_c = unpack_rows(before, 4, POOL), unpack_rows(before, 5, C0)
    cross_p, cross_c = unpack_rows(before, 11, POOL), unpack_rows(before, 12, C0)
    goff_ref[...] = jnp.concatenate([sum_c, sum_m, sum_p, sum_b], axis=1)
    share = 1.0 / cells
    frame = valid_first(256)
    pools = []
    lanes = slice(BOUT, BOUT + POOL)
    for s in range(4):
        mask = frame
        if s == 0:
            mask = frame & (flag_ref[1] > 0)
            d, y = beside_errors(dn_ref[:64, lanes], before_ref, mb_ref, off_ref, lanes, IN_OUT)
        elif s == 3:
            mask = frame & (flag_ref[2] > 0)
            d, y = beside_errors(dn_ref[64:, lanes], after_ref, mb_ref, off_ref, lanes, IN_OUT)
        else:
            rows = slice((s - 1) * 256, s * 256)
            d, y = dp_ref[rows, :].astype(F32), yp_ref[rows, :].astype(F32)
        e = mb_ref[1:2, BOUT:] * (d - sum_p * share - y * (cross_p * share))
        pools.append(jnp.where(mask, e, 0.0).astype(BF16).astype(F32))
    for f in range(2):
        rows = slice(f * 256, (f + 1) * 256)
        value = box_plane(pools[f] + pools[f + 1] + pools[f + 2], 16) * (1.0 / 27.0)
        ea[rows, IN_OUT:] = jnp.where(frame, value, 0.0).astype(BF16)
        y = (zc_ref[rows, :] - ma_ref[0:1, :C0]) * ma_ref[1:2, :C0]
        e = dc_ref[rows, :].astype(F32) - sum_c * share - y * (cross_c * share)
        ea[rows, :C0] = jnp.where(frame, ma_ref[1:2, :C0] * e, 0.0).astype(BF16)
        y = (zm_ref[rows, :] - ma_ref[0:1, C0:]) * ma_ref[1:2, C0:]
        e = dm_ref[rows, :] - sum_m * share - y * (cross_m * share)
        ea[rows, C0:IN_OUT] = jnp.where(frame, ma_ref[1:2, C0:] * e, 0.0).astype(BF16)
    turned = dot_nt(eye(SECTION_A), ea[...]).astype(BF16)
    chunk_refs, g_ref = refs[:-1], refs[-1]
    g_ref[...] = dot_nn(turned, x_ref[...])
    for m, ref in enumerate(chunk_refs):
        p = lax.rem(flag_ref[0] + m, parts)
        rows = pl.ds(pl.multiple_of(p * part_in, 8), part_in)
        ref[:part_in] = g_ref[rows, :].astype(BF16)
        rows = pl.ds(pl.multiple_of(IN_OUT + p * part_pool, 8), part_pool)
        ref[part_in:] = g_ref[rows, :].astype(BF16)


def first_input_back(ea, win_ref, wpool_ref, dx_ref):
    dx_ref[...] = dot_nt(ea[:, :IN_OUT], win_ref[...]) + dot_nt(ea[:, IN_OUT:], wpool_ref[...])


def call(body, outs, scratch, *args, scalars=1, us=1, near=(), in_hbm=(), out_near=(), out_hbm=()):
    in_specs, placed = [], []
    for i, arg in enumerate(args):
        space = pltpu.SMEM if i < scalars else pl.ANY if i in in_hbm else pltpu.VMEM
        in_specs.append(pl.BlockSpec(memory_space=space))
        placed.append(pltpu.with_memory_space_constraint(arg, pltpu.VMEM) if i in near else arg)
    out_specs = [
        pl.BlockSpec(memory_space=pl.ANY if i in out_hbm else pltpu.VMEM) for i in range(len(outs))
    ]
    return pl.pallas_call(
        body,
        out_shape=[
            pltpu.VMEM(*out) if i in out_near else jax.ShapeDtypeStruct(*out)
            for i, out in enumerate(outs)
        ],
        in_specs=in_specs,
        out_specs=out_specs,
        scratch_shapes=[pltpu.VMEM(*s) if isinstance(s, tuple) else s for s in scratch],
        compiler_params=pltpu.CompilerParams(vmem_limit_bytes=VMEM_LIMIT),
        cost_estimate=pl.CostEstimate(
            flops=int(us * 1.1e9),
            bytes_accessed=sum(a.size * a.dtype.itemsize for a in args),
            transcendentals=0,
        ),
    )(*placed)


def exchange(copies):
    return lax.all_to_all(copies, ("clip", "tm"), 0, 0)


def neighbours(head, tail):
    size = lax.axis_size("tm")
    up = [(i, i + 1) for i in range(size - 1)]
    down = [(i + 1, i) for i in range(size - 1)]
    return lax.ppermute(tail, "tm", up), lax.ppermute(head, "tm", down)


def gather_from(value, axis, back=False):
    size = lax.axis_size(axis)
    blocks = [value]
    for m in range(1, size):
        step = -m if back else m
        blocks.append(lax.ppermute(value, axis, [((i + step) % size, i) for i in range(size)]))
    return blocks


def hand_on(chunks, axis):
    size = lax.axis_size(axis)
    blocks = [chunks[0]]
    for m in range(1, size):
        blocks.append(lax.ppermute(chunks[m], axis, [(i, (i + m) % size) for i in range(size)]))
    return blocks


def to_all(value, axis):
    size = lax.axis_size(axis)
    return lax.all_to_all(jnp.broadcast_to(value[None], (size,) + value.shape), axis, 0, 0)


def turned_to(blocks, first):
    return lax.dynamic_slice_in_dim(jnp.concatenate([blocks, blocks]), first, blocks.shape[0])


def summed(parts):
    total = parts[0].astype(F32)
    for i in range(1, len(parts)):
        total = total + parts[i].astype(F32)
    return total.astype(BF16)


def after(value, *others):
    return lax.optimization_barrier((value,) + others)[0]


def small_group(
    features, w_in_4f, w_pool_4f, w_mid_4f, w_small_4f, offsets_4f,
    w_in_5b, w_pool_5b, w_mid_5b, w_small_5b, offsets_5b, cotangent,
):
    clips, frames = lax.axis_size("clip"), lax.axis_size("tm")
    group = clips * frames
    cells = 392.0 * group
    here = lax.axis_index("tm")
    flags = jnp.stack([here, here > 0, here < frames - 1, lax.axis_index("clip")]).astype(jnp.int32)
    offsets_4f, offsets_5b = offsets_4f[None], offsets_5b[None]
    x = jnp.pad(features[0], ((0, 0), (0, 2), (0, 2), (0, 0))).reshape(512, features.shape[-1])
    cot = jnp.pad(cotangent[0, 0], ((0, 0), (0, 1), (0, 0))).reshape(56, OUTC)
    mid_4f, small_4f = w_mid_4f.reshape(9, 3 * C1A, C1B), w_small_4f.reshape(9, 3 * C2A, C2B)
    mid_5b, small_5b = w_mid_5b.reshape(3, 9 * C1A, C1B), w_small_5b.reshape(3, 9 * C2A, C2B)
    before, behind = neighbours(x[:224], x[256:480])
    z_c, z_m, q, stats = call(
        first_project,
        [((512, C0), F32), ((512, MID), F32), ((512, POOL), F32), ((group, 8, 128), F32)],
        [], x, w_in_4f, w_pool_4f, scalars=0, us=4,
    )
    cot = jnp.stack(gather_from(after(cot, q), "clip"))
    stats = exchange(stats)
    z_b, z_p, stats, x2_c, m_turned, head, tail, moments_a = call(
        first_hidden,
        [((512, BOUT), F32), ((512, POOL), F32), ((group, 16, 128), F32), ((56, C0), BF16),
         ((MID, 512), BF16),
         ((224, BOUT + POOL), BF16), ((224, BOUT + POOL), BF16), ((2, IN_OUT), F32)],
        [((1024, MID), F32), ((1056, 3 * C1A), BF16), ((1056, 3 * C2A), BF16),
         ((4, 128, 128), F32)],
        flags, stats, z_c, z_m, q, before, behind, w_in_4f, w_pool_4f, mid_4f, small_4f,
        offsets_4f, us=5, near=(1, 5, 6),
    )
    cot, stats = lax.optimization_barrier((cot, stats))
    cot = gather_from(cot, "tm")
    stats = exchange(stats)
    x2, moments_b = call(
        first_output,
        [((56, OUTC), BF16), ((2, BOUT + POOL), F32)],
        [((4, 128, 128), F32)],
        stats, z_b, z_p, x2_c, offsets_4f, scalars=0, us=3, near=(0,), out_near=(0,),
    )
    x2 = jnp.stack(gather_from(x2, "clip"))
    before, behind = neighbours(head, tail)
    m_turned = gather_from(m_turned, "tm", back=True)
    x2 = gather_from(after(x2, *cot), "tm")
    part = (C1B // frames, C2B // frames, IN_OUT // frames, POOL // frames)
    far = 2 * frames + 8
    (out, g_in_5b, g_pool_5b, g_mid_5b, g_small_5b, g_off_5b, d_near,
     d_b, y_b, d_p, y_p, d_c, stats) = call(
        functools.partial(second_layer, clips, frames),
        [((64, OUTC), BF16), ((part[2], OUTC), F32), ((part[3], OUTC), F32),
         ((27, C1A, part[0]), F32), ((27, C2A, part[1]), F32), ((1, 1024), F32),
         ((128, BOUT + POOL), F32),
         ((512, BOUT), BF16), ((512, BOUT), BF16), ((512, POOL), BF16), ((512, POOL), BF16),
         ((512, C0), BF16), ((group, 16, 128), F32)],
        second_scratch(group * 64, clips * 64, part),
        flags, *x2, *cot, w_in_5b, w_pool_5b, small_5b, offsets_5b, moments_a, moments_b,
        offsets_4f, mid_5b, z_b, z_p, z_c,
        us=35, near=range(1, 1 + 2 * frames), in_hbm=range(far, far + 4), out_hbm=(3, 4),
    )
    stats = exchange(stats)
    e_b, sums, *errors = call(
        functools.partial(first_hidden_errors, cells, frames),
        [((1056, BOUT), BF16), ((16, 128), F32)] + [((448, part[0] + part[1]), BF16)] * frames,
        [], flags, stats, d_b, y_b, d_near, before, behind, moments_b, offsets_4f, us=3, near=(1,),
        out_near=[0, *range(2, 2 + frames)],
    )
    errors = hand_on(errors, "tm")
    d_m, stats = call(
        first_hidden_back,
        [((512, MID), F32), ((group, 8, 128), F32)],
        [], e_b, z_m, moments_a, offsets_4f, mid_4f, small_4f, scalars=0, us=6, near=(0,),
    )
    stats = exchange(stats)
    wide = 27 * part[0] + 27 * part[1] // clips
    g_conv = call(
        functools.partial(first_kernel_grad, frames),
        [((C1A // clips, wide), BF16)] * clips,
        [((frames * 512, 9 * 128), BF16), ((MID, frames * 512), BF16), ((C1A, wide), F32)],
        after(flags, d_m), *errors, *m_turned, us=10, near=range(1, 1 + frames), out_near=range(clips),
    )
    stats = after(stats, *g_conv)
    g_conv = hand_on(g_conv, "clip")
    e_a, g_off, *g_a = call(
        functools.partial(first_input_errors, cells, frames),
        [((512, SECTION_A), BF16), ((1, 1024), F32)]
        + [((part[2] + part[3], features.shape[-1]), BF16)] * frames,
        [((SECTION_A, features.shape[-1]), F32)], flags, stats, sums, d_m, d_c, d_p, y_p, d_near, before, behind,
        z_c, z_m, moments_a, moments_b, offsets_4f, x, us=20, near=(1,),
        out_near=[0, *range(2, 2 + frames)],
    )
    (d_x,) = call(
        first_input_back,
        [((512, features.shape[-1]), F32)],
        [], e_a, w_in_4f, w_pool_4f, scalars=0, us=0, near=(0,),
    )
    g_a = hand_on(g_a, "tm")
    g_conv = summed(lax.optimization_barrier((*g_conv, d_x))[:clips])
    g_a = summed(lax.optimization_barrier((*g_a, g_conv))[:frames])
    g_conv = gather_from(g_conv, "clip")
    g_a = hand_on(turned_to(g_a.reshape(clips, -1, features.shape[-1]), flags[3]), "clip")
    g_a = after(summed(g_a), g_conv[1])
    g_a = jnp.stack(gather_from(g_a, "clip")).astype(F32)
    g_a = turned_to(g_a, lax.rem(clips - flags[3], clips)).reshape(part[2] + part[3], -1)
    g_mid, g_small = call(
        first_kernel_join,
        [((27, C1A, part[0]), F32), ((27, C2A, part[1]), F32)],
        [], flags, *g_conv, us=4, near=range(1, 1 + clips),
    )

    return (
        out.reshape(1, 1, 8, 8, OUTC)[:, :, :7, :7],
        d_x.reshape(1, 2, 16, 16, -1)[:, :, :14, :14],
        g_a[: part[2]].T,
        g_a[part[2] :].T,
        g_mid,
        g_small,
        g_off[0],
        g_in_5b.T,
        g_pool_5b.T,
        g_mid_5b,
        g_small_5b,
        g_off_5b[0],
    )


def solution(mesh):
    placed = (
        P(("stream", "clip"), "tm", None, None, None),
        P("stream", None),
        P("stream", None),
        P("stream", None, None),
        P("stream", None, None),
        P("stream"),
        P("stream", None),
        P("stream", None),
        P("stream", None, None),
        P("stream", None, None),
        P("stream"),
        P(("stream", "clip"), "tm", None, None, None),
    )
    group = mesh.shape["clip"] * mesh.shape["tm"]
    return jax.shard_map(
        small_group if group <= 16 else shards,
        mesh=mesh,
        in_specs=placed,
        out_specs=(
            P(("stream", "clip"), "tm", None, None, None),
            P(("stream", "clip"), "tm", None, None, None),
            P("stream", "tm"),
            P("stream", "tm"),
            P("stream", None, "tm"),
            P("stream", None, "tm"),
            P("stream"),
            P("stream", "tm"),
            P("stream", "tm"),
            P("stream", None, "tm"),
            P("stream", None, "tm"),
            P("stream"),
        ),
        check_vma=False,
    )
```

```python
import functools

import jax
import jax.numpy as jnp
from jax import lax
from jax.experimental import pallas as pl
from jax.experimental.pallas import tpu as pltpu
from jax.sharding import PartitionSpec as P

C0 = 256
C1A = 160
C1B = 320
C2A = 32
C2B = 128
IN_OUT = 448
SECTION_A = 576


EPSILON = 0.001
VOXEL_AXES = (0, 1, 2, 3)


def extended(value, sides, width):
    for axis, dim in sides:
        size, length = (lax.axis_size(axis), value.shape[dim])
        up = [(i, (i + 1) % size) for i in range(size - 1)]
        down = [(j, i) for i, j in up]
        last = lax.slice_in_dim(value, length - width, length, axis=dim)
        first = lax.slice_in_dim(value, 0, width, axis=dim)
        before = lax.ppermute(last, axis, up)
        after = lax.ppermute(first, axis, down)
        value = jnp.concatenate([before, value, after], axis=dim)
    return value


def as_sent(value):
    return jax.tree.map(lambda a: a.astype(jnp.bfloat16) if a.dtype == jnp.float32 else a, value)


def project(values, weight):
    return jnp.einsum("nfhwc,cd->nfhwd", values, weight, preferred_element_type=jnp.float32)


def pad_plane(values):
    return jnp.pad(values, ((0, 0), (0, 0), (1, 1), (1, 1), (0, 0)))


def box_sum(padded):
    summed = padded[:, :-2] + padded[:, 1:-1] + padded[:, 2:]
    summed = summed[:, :, :-2] + summed[:, :, 1:-1] + summed[:, :, 2:]
    return summed[:, :, :, :-2] + summed[:, :, :, 1:-1] + summed[:, :, :, 2:]


def unfold(padded, frames, height, width):
    slices = []
    for shift_f in range(3):
        for shift_h in range(3):
            for shift_w in range(3):
                slices.append(
                    padded[
                        :,
                        shift_f : shift_f + frames,
                        shift_h : shift_h + height,
                        shift_w : shift_w + width,
                    ]
                )
    return jnp.concatenate(slices, axis=-1)


def fold_back(patch_grad, channels):
    summed = None
    offset_index = 0
    for shift_f in range(3):
        for shift_h in range(3):
            for shift_w in range(3):
                segment = patch_grad[..., offset_index * channels : (offset_index + 1) * channels]
                placed = jnp.pad(
                    segment,
                    (
                        (0, 0),
                        (shift_f, 2 - shift_f),
                        (shift_h, 2 - shift_h),
                        (shift_w, 2 - shift_w),
                        (0, 0),
                    ),
                )
                summed = placed if summed is None else summed + placed
                offset_index += 1
    return summed


def return_input_rims(grad_padded):
    interior = grad_padded[:, 1:-1]
    rim_pair = jnp.concatenate([grad_padded[:, :1], grad_padded[:, -1:]], axis=1)
    arrived = extended(rim_pair.astype(jnp.bfloat16), (("tm", 1),), 1).astype(rim_pair.dtype)
    interior = interior.at[:, 0].add(arrived[:, 0])
    return interior.at[:, -1].add(arrived[:, 3])


def return_hidden_rims(grad_padded):
    interior = grad_padded[:, 1:-1]
    rim_pair = jnp.concatenate([grad_padded[:, :1], grad_padded[:, -1:]], axis=1)
    arrived = extended(rim_pair.astype(jnp.bfloat16), (("tm", 1),), 1).astype(rim_pair.dtype)
    interior = interior.at[:, 0].add(arrived[:, 0])
    return interior.at[:, -1].add(arrived[:, 3])


def section_first(features, w_in, w_pool):
    rimmed = extended(features, (("tm", 1),), 1)
    padded = pad_plane(rimmed).astype(jnp.float32)
    pooled = (box_sum(padded) / 27.0).astype(jnp.bfloat16)
    pre_first = jnp.concatenate([project(features, w_in), project(pooled, w_pool)], axis=-1)
    return (pre_first, pooled)


def section_second(middle, w_mid, w_small):
    rimmed = extended(middle, (("tm", 1),), 1)
    padded = pad_plane(rimmed)
    frames, height, width = (middle.shape[1], middle.shape[2], middle.shape[3])
    patch_one = unfold(padded[..., :C1A], frames, height, width)
    patch_two = unfold(padded[..., C1A:], frames, height, width)
    pre_second = jnp.concatenate(
        [
            project(patch_one, w_mid.reshape(27 * C1A, C1B)),
            project(patch_two, w_small.reshape(27 * C2A, C2B)),
        ],
        axis=-1,
    )
    return (pre_second, patch_one, patch_two)


def moments(pre_act, voxel_count):
    first_sum = lax.psum(jnp.sum(pre_act, axis=VOXEL_AXES), ("clip", "tm"))
    center = first_sum / voxel_count
    spread = lax.psum(jnp.sum(jnp.square(pre_act - center), axis=VOXEL_AXES), ("clip", "tm"))
    variance = spread / voxel_count
    return (center, variance)


def standardize(pre_act, center, variance):
    return (pre_act - center) * lax.rsqrt(variance + EPSILON)


def silu_slope(act_in):
    sigmoid_value = jax.nn.sigmoid(act_in)
    return sigmoid_value + act_in * sigmoid_value * (1.0 - sigmoid_value)


def block_forward(features, params, voxel_count):
    w_in, w_pool, w_mid, w_small, offsets = params
    pre_first, pooled = section_first(features, w_in, w_pool)
    center_a, variance_a = moments(pre_first, voxel_count)
    hidden_a = jax.nn.silu(standardize(pre_first, center_a, variance_a) + offsets[:SECTION_A])
    middle = hidden_a[..., C0:IN_OUT].astype(jnp.bfloat16)
    pre_second, patch_one, patch_two = section_second(middle, w_mid, w_small)
    center_b, variance_b = moments(pre_second, voxel_count)
    hidden_b = jax.nn.silu(standardize(pre_second, center_b, variance_b) + offsets[SECTION_A:])
    block_out = jnp.concatenate([hidden_a[..., :C0], hidden_b, hidden_a[..., IN_OUT:]], axis=-1)
    return (block_out, (center_a, variance_a, center_b, variance_b))


def norm_back(slope_grad, normed, variance, voxel_count):
    sum_grad, sum_cross = lax.psum(
        (jnp.sum(slope_grad, axis=VOXEL_AXES), jnp.sum(slope_grad * normed, axis=VOXEL_AXES)),
        ("clip", "tm"),
    )
    scaled = lax.rsqrt(variance + EPSILON) * (
        slope_grad - sum_grad / voxel_count - normed * (sum_cross / voxel_count)
    )
    return (scaled.astype(jnp.bfloat16), sum_grad)


def block_backward(features, params, moment_pair, out_grad, voxel_count):
    w_in, w_pool, w_mid, w_small, offsets = params
    center_a, variance_a, center_b, variance_b = moment_pair
    pre_first, pooled = section_first(features, w_in, w_pool)
    normed_a = standardize(pre_first, center_a, variance_a)
    act_a = normed_a + offsets[:SECTION_A]
    middle = jax.nn.silu(act_a)[..., C0:IN_OUT].astype(jnp.bfloat16)
    pre_second, patch_one, patch_two = section_second(middle, w_mid, w_small)
    normed_b = standardize(pre_second, center_b, variance_b)
    act_b = normed_b + offsets[SECTION_A:]
    grad_b = out_grad[..., C0 : C0 + C1B + C2B] * silu_slope(act_b)
    error_b, offset_grad_b = norm_back(grad_b, normed_b, variance_b, voxel_count)
    error_one = error_b[..., :C1B]
    error_two = error_b[..., C1B:]
    grad_mid = jnp.einsum(
        "nfhwk,nfhwo->ko", patch_one, error_one, preferred_element_type=jnp.float32
    ).reshape(27, C1A, C1B)
    grad_small = jnp.einsum(
        "nfhwk,nfhwo->ko", patch_two, error_two, preferred_element_type=jnp.float32
    ).reshape(27, C2A, C2B)
    back_one = fold_back(
        jnp.einsum(
            "nfhwo,ko->nfhwk",
            error_one,
            w_mid.reshape(27 * C1A, C1B),
            preferred_element_type=jnp.float32,
        ),
        C1A,
    )
    back_two = fold_back(
        jnp.einsum(
            "nfhwo,ko->nfhwk",
            error_two,
            w_small.reshape(27 * C2A, C2B),
            preferred_element_type=jnp.float32,
        ),
        C2A,
    )
    middle_grad = return_hidden_rims(
        jnp.concatenate([back_one, back_two], axis=-1)[:, :, 1:-1, 1:-1]
    )
    grad_a = jnp.concatenate(
        [out_grad[..., :C0], middle_grad, out_grad[..., C0 + C1B + C2B :]], axis=-1
    ) * silu_slope(act_a)
    error_a, offset_grad_a = norm_back(grad_a, normed_a, variance_a, voxel_count)
    error_in = error_a[..., :IN_OUT]
    error_pool = error_a[..., IN_OUT:]
    grad_in = jnp.einsum("nfhwc,nfhwd->cd", features, error_in, preferred_element_type=jnp.float32)
    grad_pool = jnp.einsum(
        "nfhwc,nfhwd->cd", pooled, error_pool, preferred_element_type=jnp.float32
    )
    direct = jnp.einsum("nfhwd,cd->nfhwc", error_in, w_in, preferred_element_type=jnp.float32)
    pool_grad = jnp.einsum(
        "nfhwd,cd->nfhwc", error_pool, w_pool, preferred_element_type=jnp.float32
    )
    spread_pad = jnp.pad(pool_grad, ((0, 0), (2, 2), (2, 2), (2, 2), (0, 0)))
    padded_grad = (box_sum(spread_pad) / 27.0)[:, :, 1:-1, 1:-1]
    input_grad = direct + return_input_rims(padded_grad)
    return (
        input_grad,
        (grad_in, grad_pool, grad_mid, grad_small),
        jnp.concatenate([offset_grad_a, offset_grad_b]),
    )


def reduce_grads(weight_grads):
    summed = jax.tree.map(
        lambda part: part.astype(jnp.float32), lax.psum(as_sent(weight_grads), "clip")
    )
    reduced = (
        lax.psum_scatter(
            summed[0].astype(jnp.bfloat16), "tm", scatter_dimension=1, tiled=True
        ).astype(jnp.float32),
        lax.psum_scatter(
            summed[1].astype(jnp.bfloat16), "tm", scatter_dimension=1, tiled=True
        ).astype(jnp.float32),
        lax.psum_scatter(
            summed[2].astype(jnp.bfloat16), "tm", scatter_dimension=2, tiled=True
        ).astype(jnp.float32),
        lax.psum_scatter(
            summed[3].astype(jnp.bfloat16), "tm", scatter_dimension=2, tiled=True
        ).astype(jnp.float32),
    )
    return reduced


def halve_grid(values):
    n, f, h, w, c = values.shape
    return jnp.sum(values.reshape(n, f // 2, 2, h // 2, 2, w // 2, 2, c), axis=(2, 4, 6)) * 0.125


def spread_half(grad_small_grid):
    n, f, h, w, c = grad_small_grid.shape
    expanded = jnp.broadcast_to(
        (grad_small_grid * 0.125)[:, :, None, :, None, :, None, :], (n, f, 2, h, 2, w, 2, c)
    )
    return expanded.reshape(n, 2 * f, 2 * h, 2 * w, c)


def shards(
    features,
    w_in_4f,
    w_pool_4f,
    w_mid_4f,
    w_small_4f,
    offsets_4f,
    w_in_5b,
    w_pool_5b,
    w_mid_5b,
    w_small_5b,
    offsets_5b,
    cotangent,
):
    params_first = (w_in_4f, w_pool_4f, w_mid_4f, w_small_4f, offsets_4f)
    params_second = (w_in_5b, w_pool_5b, w_mid_5b, w_small_5b, offsets_5b)
    devices_used = lax.axis_size("clip") * lax.axis_size("tm")
    count_first = float(
        features.shape[0] * features.shape[1] * features.shape[2] * features.shape[3] * devices_used
    )
    count_second = count_first / 8.0
    out_first, moments_first = block_forward(features, params_first, count_first)
    input_second = halve_grid(out_first).astype(jnp.bfloat16)
    out_second, moments_second = block_forward(input_second, params_second, count_second)
    grad_second, weights_second, offsets_grad_second = block_backward(
        input_second, params_second, moments_second, cotangent.astype(jnp.float32), count_second
    )
    reduced_second = reduce_grads(weights_second)
    grad_first, weights_first, offsets_grad_first = block_backward(
        features, params_first, moments_first, spread_half(grad_second), count_first
    )
    reduced_first = reduce_grads(weights_first)
    final_out = out_second.astype(jnp.bfloat16)
    return (
        final_out,
        grad_first,
        reduced_first[0],
        reduced_first[1],
        reduced_first[2],
        reduced_first[3],
        offsets_grad_first,
        reduced_second[0],
        reduced_second[1],
        reduced_second[2],
        reduced_second[3],
        offsets_grad_second,
    )


F32 = jnp.float32
BF16 = jnp.bfloat16
MID = 192
BOUT = 448
POOL = 128
OUTC = 832
VMEM_LIMIT = 58 * 1024 * 1024


def dot_nn(a, b):
    return lax.dot_general(a, b, (((1,), (0,)), ((), ())), preferred_element_type=F32)


def dot_nt(a, b):
    return lax.dot_general(a, b, (((1,), (1,)), ((), ())), preferred_element_type=F32)


def dot_tn(a, b):
    return lax.dot_general(a, b, (((0,), (0,)), ((), ())), preferred_element_type=F32)


def roll_rows(value, shift):
    rows = value.shape[0]
    shift %= rows
    return value if shift == 0 else pltpu.roll(value, shift, 0)


def eye(n):
    r = lax.broadcasted_iota(jnp.int32, (n, n), 0)
    k = lax.broadcasted_iota(jnp.int32, (n, n), 1)
    return jnp.where(r == k, 1.0, 0.0).astype(BF16)


def valid_first(rows):
    r = lax.broadcasted_iota(jnp.int32, (rows, 1), 0)
    return ((r & 255) < 224) & ((r & 15) < 14)


def valid_second(rows):
    r = lax.broadcasted_iota(jnp.int32, (rows, 1), 0)
    return ((r & 63) < 56) & ((r & 7) < 7)


def sigmoid(a):
    return 0.5 * jnp.tanh(0.5 * a) + 0.5


def act(a):
    return a * sigmoid(a)


def slope(a):
    s = sigmoid(a)
    return s + a * s * (1.0 - s)


def pack_rows(vectors):
    pieces = []
    for v in vectors:
        width = v.shape[1]
        full = -(-width // 128) * 128
        if full != width:
            v = jnp.concatenate([v, jnp.zeros((1, full - width), F32)], axis=1)
        for i in range(full // 128):
            pieces.append(v[:, i * 128 : (i + 1) * 128])
    return jnp.concatenate(pieces, axis=0)


def unpack_rows(rows, start, width):
    count = -(-width // 128)
    return jnp.concatenate([rows[start + i : start + i + 1] for i in range(count)], axis=1)[
        :, :width
    ]


def store_copies(ref, rows):
    count, height = ref.shape[0], ref.shape[1]
    if rows.shape[0] < height:
        rows = jnp.concatenate([rows, jnp.zeros((height - rows.shape[0], 128), F32)], axis=0)
    for i in range(count):
        ref[i] = rows


def local_moments(value, mask, cells):
    total = jnp.sum(jnp.where(mask, value, 0.0), axis=0, keepdims=True)
    delta = jnp.where(mask, value - total * (1.0 / cells), 0.0)
    return total, jnp.sum(delta * delta, axis=0, keepdims=True)


def joint_moments(gathered, height, cells):
    devices = gathered.shape[0]
    sums, squares = gathered[:, :height], gathered[:, height : 2 * height]
    mean = jnp.sum(sums, axis=0) * (1.0 / (cells * devices))
    apart = sums * (1.0 / cells) - mean[None]
    spread = jnp.sum(squares, axis=0) + cells * jnp.sum(apart * apart, axis=0)
    return mean, lax.rsqrt(spread * (1.0 / (cells * devices)) + EPSILON)


def halve(total, scratch, dtype):
    width = total.shape[1]
    both = total[:256] + total[256:]
    pairs = jnp.sum(both.reshape(8, 2, 16, width), axis=1).reshape(128, width)
    pieces = []
    for i in range(-(-width // 128)):
        lanes = min(128, width - i * 128)
        scratch[i, :, :lanes] = pairs[:, i * 128 : i * 128 + lanes]
        piece = scratch[i, pl.ds(0, 64, 2), :] + scratch[i, pl.ds(1, 64, 2), :]
        pieces.append(piece[:, :lanes])
    halved = jnp.concatenate(pieces, axis=1)
    return (halved * 0.125).astype(dtype)


def box_plane(value, stride):
    value = value + roll_rows(value, stride) + roll_rows(value, -stride)
    return value + roll_rows(value, 1) + roll_rows(value, -1)


def first_project(x_ref, win_ref, wpool_ref, zc_ref, zm_ref, q_ref, st_ref):
    for f in range(2):
        rows = pl.ds(f * 256, 256)
        x = x_ref[rows, :]
        z = dot_nn(x, win_ref[...])
        zc_ref[rows, :], zm_ref[rows, :] = z[:, :C0], z[:, C0:]
        q_ref[rows, :] = dot_nn(x, wpool_ref[...])
    mask = valid_first(512)
    moments = [local_moments(ref[...], mask, 392) for ref in (zc_ref, zm_ref)]
    total, squares = [jnp.concatenate([m[i] for m in moments], axis=1) for i in range(2)]
    store_copies(st_ref, pack_rows([total, squares]))


def first_hidden(
    flag_ref, st_ref, zc_ref, zm_ref, q_ref, before_ref, after_ref, win_ref, wpool_ref, wmid_ref,
    wsmall_ref, off_ref,
    zb_ref, zp_ref, st2_ref, x2_ref, mt_ref, head_ref, tail_ref, ma_ref,
    mid, um_ref, us_ref, half,
):
    mean_rows, scale_rows = joint_moments(st_ref[...], 4, 392.0)
    mean, scale = unpack_rows(mean_rows, 0, IN_OUT), unpack_rows(scale_rows, 0, IN_OUT)
    ma_ref[...] = jnp.concatenate([mean, scale], axis=0)
    off = off_ref[:, :IN_OUT]
    frame = valid_first(256)
    prev, after = flag_ref[1] > 0, flag_ref[2] > 0

    def middle(z, mask):
        return jnp.where(mask, act((z - mean[:, C0:]) * scale[:, C0:] + off[:, C0:]), 0.0)

    blank = jnp.zeros((32, MID), F32)
    for start, ref, mask in ((0, before_ref, prev), (768, after_ref, after)):
        z = jnp.concatenate([dot_nn(ref[...], win_ref[:, C0:]), blank], axis=0)
        mid[start : start + 256, :] = middle(z, frame & mask)
    mid[256:512, :] = middle(zm_ref[0:256, :], frame)
    mid[512:768, :] = middle(zm_ref[256:512, :], frame)
    for ref in (um_ref, us_ref):
        edge = jnp.zeros((16, ref.shape[1]), BF16)
        ref[0:16, :] = edge
        ref[1040:1056, :] = edge

    for f in range(4):
        rows = slice(f * 256, (f + 1) * 256)
        shifted = [roll_rows(mid[rows, :], 1 - g) for g in range(3)]
        into = slice(16 + f * 256, 16 + (f + 1) * 256)
        um_ref[into, :] = jnp.concatenate([v[:, :C1A] for v in shifted], axis=1).astype(BF16)
        us_ref[into, :] = jnp.concatenate([v[:, C1A:] for v in shifted], axis=1).astype(BF16)

    def convolve(u_ref, w_ref):
        total = None
        for a in range(3):
            for e in range(3):
                start = 16 + a * 256 + (e - 1) * 16
                term = dot_nn(u_ref[start : start + 512, :], w_ref[3 * a + e])
                total = term if total is None else total + term
        return total

    zb_ref[:, :C1B] = convolve(um_ref, wmid_ref)
    zb_ref[:, C1B:] = convolve(us_ref, wsmall_ref)

    first, last = q_ref[0:256, :], q_ref[256:512, :]
    pair = first + last
    for f, ref in ((0, before_ref), (1, after_ref)):
        beside = jnp.concatenate([dot_nn(ref[...], wpool_ref[...]), blank[:, :POOL]], axis=0)
        value = pair + beside
        value = box_plane(value, 16) * (1.0 / 27.0)
        zp_ref[f * 256 : (f + 1) * 256, :] = jnp.where(frame, value, 0.0)

    both = valid_first(512)
    total_b, squares_b = local_moments(zb_ref[...], both, 392)
    total_p, squares_p = local_moments(zp_ref[...], both, 392)
    store_copies(st2_ref, pack_rows([total_b, total_p, squares_b, squares_p]))
    for f, ref in ((0, head_ref), (1, tail_ref)):
        rows = pl.ds(f * 256, 224)
        ref[:, :BOUT] = zb_ref[rows, :].astype(BF16)
        ref[:, BOUT:] = zp_ref[rows, :].astype(BF16)
    hidden = act((zc_ref[...] - mean[:, :C0]) * scale[:, :C0] + off[:, :C0])
    x2_ref[...] = halve(jnp.where(both, hidden, 0.0), half, BF16)[:56]
    mt_ref[...] = dot_nt(eye(MID), mid[256:768, :].astype(BF16)).astype(BF16)


def first_output(st_ref, zb_ref, zp_ref, x2c_ref, off_ref, x2_ref, mb_ref, half):
    mean_rows, scale_rows = joint_moments(st_ref[...], 5, 392.0)
    both = valid_first(512)
    moments = []
    for start, width, z_ref, offset in ((0, BOUT, zb_ref, SECTION_A), (4, POOL, zp_ref, IN_OUT)):
        mean, scale = unpack_rows(mean_rows, start, width), unpack_rows(scale_rows, start, width)
        hidden = act((z_ref[...] - mean) * scale + off_ref[:, offset : offset + width])
        into = slice(C0, C0 + BOUT) if start == 0 else slice(C0 + BOUT, OUTC)
        x2_ref[:, into] = halve(jnp.where(both, hidden, 0.0), half, BF16)[:56]
        moments.append(jnp.concatenate([mean, scale], axis=0))
    x2_ref[:, :C0] = x2c_ref[...]
    mb_ref[...] = jnp.concatenate(moments, axis=1)


def second_layer(clips, frames, flag_ref, *refs):
    x_refs, cot_refs, refs = refs[:frames], refs[frames : 2 * frames], refs[2 * frames :]
    win_ref, wpool_ref, wsmall_ref, off_ref = refs[:4]
    moment_refs, wide_refs, refs = refs[4:7], refs[7:11], refs[11:]
    out_ref, gin_ref, gpool_ref, gmid_hbm, gsmall_hbm, goff_ref = refs[:6]
    dn_ref, error_refs, scratch = refs[6], refs[7:13], refs[13:]
    xs, cs, za, zb, um, us, qs, eb, es, ea, et, ets, eat, da, tmid_ref, tsmall_ref = scratch[:16]
    gmid_ref, gsmall_ref, sems = *scratch[16:18], scratch[-1]
    wmid_ref = wide_refs[0]
    here = flag_ref[0]
    step = clips * 64
    rows = frames * step
    cells = clips * frames * 49.0
    share = 1.0 / cells
    part_mid, part_small = gmid_ref.shape[2], gsmall_ref.shape[2]
    part_in, part_pool = gin_ref.shape[0], gpool_ref.shape[0]
    mask = valid_second(step)

    tail = jnp.zeros((16, OUTC), BF16)

    def assemble(into, blocks):
        for m in range(frames):
            for c in range(clips):
                base = lax.rem(here + m, frames) * step + c * 64
                into[pl.ds(pl.multiple_of(base + 48, 16), 16), :] = tail
                into[pl.ds(pl.multiple_of(base, 64), 56), :] = blocks[m][c]

    assemble(xs, x_refs)
    for ref in (um, us, qs, ea):
        blank = jnp.zeros((step, ref.shape[1]), ref.dtype)
        ref[:step, :] = blank
        ref[step + rows :, :] = blank

    def rows_of(f):
        return slice(f * step, (f + 1) * step)

    def inner(f, shift=1):
        return slice((f + shift) * step, (f + shift + 1) * step)

    def window(a):
        return slice(a * step, a * step + rows)

    def over_frames(body, init):
        for f in range(frames):
            init = body(f, init)
        return init

    def box(f):
        value = qs[inner(f, 0), :] + qs[inner(f, 1), :] + qs[inner(f, 2), :]
        return jnp.where(mask, box_plane(value, 8) * (1.0 / 27.0), 0.0)

    za[:, :IN_OUT] = dot_nn(xs[...], win_ref[...])
    qs[window(1), :] = dot_nn(xs[...], wpool_ref[...])

    def pool_frame(f, total):
        z, p = za[rows_of(f), :IN_OUT], box(f)
        za[rows_of(f), IN_OUT:] = p
        return total + jnp.concatenate(
            [jnp.sum(z, axis=0, keepdims=True), jnp.sum(p, axis=0, keepdims=True)], axis=1
        )

    total_a = over_frames(pool_frame, jnp.zeros((1, SECTION_A), F32))
    mean_a = total_a * share

    def spread_frame(ref, mean):
        def body(f, total):
            delta = jnp.where(mask, ref[rows_of(f), :] - mean, 0.0)
            return total + jnp.sum(delta * delta, axis=0, keepdims=True)

        return body

    spread_a = over_frames(spread_frame(za, mean_a), jnp.zeros((1, SECTION_A), F32))
    scale_a = lax.rsqrt(spread_a * share + EPSILON)
    off_a, off_b = off_ref[:, :SECTION_A], off_ref[:, SECTION_A:]

    def normal_a(f, lo, hi):
        return (za[rows_of(f), lo:hi] - mean_a[:, lo:hi]) * scale_a[:, lo:hi]

    def unfold_frame(f, _):
        a = normal_a(f, C0, IN_OUT) + off_a[:, C0:IN_OUT]
        hidden = jnp.where(mask, act(a), 0.0)
        aside = [roll_rows(hidden, 1 - g) for g in range(3)]
        shifted = [roll_rows(v, 8 * (1 - e)) for e in range(3) for v in aside]
        um[inner(f), :] = jnp.concatenate([v[:, :C1A] for v in shifted], axis=1).astype(BF16)
        us[inner(f), :] = jnp.concatenate([v[:, C1A:] for v in shifted], axis=1).astype(BF16)
        return 0

    over_frames(unfold_frame, 0)

    def convolve(u_ref, w_ref):
        total = dot_nn(u_ref[window(0), :], w_ref[0])
        for a in range(1, 3):
            total = total + dot_nn(u_ref[window(a), :], w_ref[a])
        return total

    zb[:, :C1B] = convolve(um, wmid_ref)
    zb[:, C1B:] = convolve(us, wsmall_ref)
    turn_kernels(wmid_ref, tmid_ref, (1, 0, 2))
    turn_kernels(wsmall_ref, tsmall_ref, (1, 0, 2))

    def total_frame(f, total):
        return total + jnp.sum(jnp.where(mask, zb[rows_of(f), :], 0.0), axis=0, keepdims=True)

    zero_b = jnp.zeros((1, BOUT), F32)
    mean_b = over_frames(total_frame, zero_b) * share
    spread_b = over_frames(spread_frame(zb, mean_b), zero_b)
    scale_b = lax.rsqrt(spread_b * share + EPSILON)

    own = pl.ds(pl.multiple_of(here * step, 64), 64)
    hidden_a = act((za[own, :] - mean_a) * scale_a + off_a)
    hidden_b = act((zb[own, :] - mean_b) * scale_b + off_b)
    out_ref[...] = jnp.concatenate(
        [hidden_a[:, :C0], hidden_b, hidden_a[:, IN_OUT:]], axis=1
    ).astype(BF16)

    assemble(cs, cot_refs)

    def sums_b(f, carry):
        y = (zb[rows_of(f), :] - mean_b) * scale_b
        d = cs[rows_of(f), C0 : C0 + BOUT].astype(F32) * slope(y + off_b)
        zb[rows_of(f), :] = y
        da[rows_of(f), :BOUT] = d
        return (
            carry[0] + jnp.sum(d, axis=0, keepdims=True),
            carry[1] + jnp.sum(d * y, axis=0, keepdims=True),
        )

    sum_b, cross_b = over_frames(sums_b, (zero_b, zero_b))

    for ref in (eb, es):
        width = ref.shape[1] // 3
        blank = jnp.zeros((step, width), BF16)
        ref[rows - step :, width : 2 * width] = blank
        ref[:step, 2 * width :] = blank

    for f in range(frames):
        at = slice(f * step, (f + 1) * step)
        e = da[at, :BOUT] - sum_b * share - zb[at, :] * (cross_b * share)
        e = jnp.where(mask, scale_b * e, 0.0).astype(BF16)
        for i, row in enumerate((f, f - 1, f + 1)):
            if 0 <= row < frames:
                at = slice(row * step, (row + 1) * step)
                eb[at, i * C1B : (i + 1) * C1B] = e[:, :C1B]
                es[at, i * C2B : (i + 1) * C2B] = e[:, C1B:]

    def picker(count, cut, part_one, part_two, columns, edge):
        r = lax.broadcasted_iota(jnp.int32, (count, columns), 0)
        k = lax.broadcasted_iota(jnp.int32, (count, columns), 1)
        want = jnp.where(r < cut, here * part_one + r, edge + here * part_two + r - cut)
        return jnp.where(k == want, 1.0, 0.0).astype(BF16)

    pick_mid = picker(part_mid, part_mid, part_mid, 0, C1B, 0)
    pick_small = picker(part_small, part_small, part_small, 0, C2B, 0)
    et[...] = dot_nt(pick_mid, eb[:, :C1B]).astype(BF16)
    ets[...] = dot_nt(pick_small, es[:, :C2B]).astype(BF16)
    for a in range(3):
        gm = dot_nn(et[...], um[window(a), :])
        gmid_ref[9 * a : 9 * a + 9] = gm.T.reshape(9, C1A, part_mid)
        gs = dot_nn(ets[...], us[window(a), :])
        gsmall_ref[9 * a : 9 * a + 9] = gs.T.reshape(9, C2A, part_small)
    stores = [
        pltpu.make_async_copy(gmid_ref, gmid_hbm, sems.at[0]),
        pltpu.make_async_copy(gsmall_ref, gsmall_hbm, sems.at[1]),
    ]
    for store in stores:
        store.start()

    small = dot_nt(es[...], tsmall_ref[...])
    sides = [None] * 3
    for e in range(3):
        mid = dot_nt(eb[...], tmid_ref[e * 3 * C1A : (e + 1) * 3 * C1A, :])
        for g in range(3):
            k = 3 * e + g
            t = jnp.concatenate(
                [mid[:, g * C1A : (g + 1) * C1A], small[:, k * C2A : (k + 1) * C2A]], axis=1
            )
            t = roll_rows(t, 8 * (e - 1))
            sides[g] = t if e == 0 else sides[g] + t
    da[:, :MID] = roll_rows(sides[0], -1) + sides[1] + roll_rows(sides[2], 1)

    def grad_a(f, carry):
        y = normal_a(f, 0, SECTION_A)
        gain = slope(y + off_a)
        cot = cs[rows_of(f), :]
        d = jnp.concatenate(
            [cot[:, :C0].astype(F32), da[rows_of(f), :MID], cot[:, C0 + BOUT :].astype(F32)], axis=1
        )
        d = jnp.where(mask, d * gain, 0.0)
        da[rows_of(f), :] = d
        za[rows_of(f), :] = y
        return (
            carry[0] + jnp.sum(d, axis=0, keepdims=True),
            carry[1] + jnp.sum(d * y, axis=0, keepdims=True),
        )

    zero_a = jnp.zeros((1, SECTION_A), F32)
    sum_a, cross_a = over_frames(grad_a, (zero_a, zero_a))
    goff_ref[...] = jnp.concatenate([sum_a, sum_b], axis=1)

    def error_a(f, _):
        e = da[rows_of(f), :] - sum_a * share - za[rows_of(f), :] * (cross_a * share)
        e = jnp.where(mask, scale_a * e, 0.0)
        ea[inner(f), :IN_OUT] = e[:, :IN_OUT].astype(BF16)
        qs[inner(f), :] = e[:, IN_OUT:].astype(BF16).astype(F32)
        return 0

    over_frames(error_a, 0)

    def spread_pool(f, _):
        ea[inner(f), IN_OUT:] = box(f).astype(BF16)
        return 0

    over_frames(spread_pool, 0)

    near = [(here + f) * step for f in range(3)]
    near = jnp.concatenate([ea[pl.ds(pl.multiple_of(r, 64), 64), :] for r in near], axis=0)
    dx = dot_nt(near[:, :IN_OUT], win_ref[...]) + dot_nt(near[:, IN_OUT:], wpool_ref[...])
    first_errors(dx[64:128], *wide_refs[1:], *moment_refs, *error_refs)
    dn_ref[:64, :], dn_ref[64:, :] = dx[:64, C0:], dx[128:, C0:]
    pick_a = picker(part_in + part_pool, part_in, part_in, part_pool, SECTION_A, IN_OUT)
    eat[...] = dot_nt(pick_a, ea[window(1), :]).astype(BF16)
    gin_ref[...] = dot_nn(eat[:part_in, :], xs[...])
    gpool_ref[...] = dot_nn(eat[part_in:, :], xs[...])
    for store in stores:
        store.wait()


def second_scratch(rows, step, part):
    wide = rows + 2 * step
    return [
        ((rows, OUTC), BF16), ((rows, OUTC), BF16), ((rows, SECTION_A), F32), ((rows, BOUT), F32),
        ((wide, 9 * C1A), BF16), ((wide, 9 * C2A), BF16), ((wide, POOL), F32),
        ((rows, 3 * C1B), BF16), ((rows, 3 * C2B), BF16), ((wide, SECTION_A), BF16),
        ((part[0], rows), BF16), ((part[1], rows), BF16), ((part[2] + part[3], rows), BF16),
        ((rows, SECTION_A), F32), ((9 * C1A, 3 * C1B), BF16), ((9 * C2A, 3 * C2B), BF16),
        ((27, C1A, part[0]), F32), ((27, C2A, part[1]), F32), pltpu.SemaphoreType.DMA((2,)),
    ]


def turn_kernels(w_ref, t_ref, order):
    width = w_ref.shape[2]
    for i, k in enumerate(order):
        t_ref[:, i * width : (i + 1) * width] = w_ref[k]


def spread_grad(d):
    r = lax.broadcasted_iota(jnp.int32, (256, 64), 0)
    k = lax.broadcasted_iota(jnp.int32, (256, 64), 1)
    spread = jnp.where(k == ((r >> 5) << 3) + ((r & 15) >> 1), 1.0, 0.0).astype(BF16)
    d = d * 0.125
    high = d.astype(BF16)
    low = (d - high.astype(F32)).astype(BF16)
    return dot_nn(spread, high) + dot_nn(spread, low)


def first_errors(
    dx, zb_ref, zp_ref, zc_ref, ma_ref, mb_ref, off_ref,
    db_ref, yb_ref, dp_ref, yp_ref, dc_ref, st_ref,
):
    g = spread_grad(dx)
    sums, crosses = [], []
    for z_ref, m_ref, lanes, part, offset, d_ref, y_ref in (
        (zb_ref, mb_ref, slice(C0, C0 + BOUT), slice(0, BOUT), SECTION_A, db_ref, yb_ref),
        (zp_ref, mb_ref, slice(C0 + BOUT, OUTC), slice(BOUT, BOUT + POOL), IN_OUT, dp_ref, yp_ref),
        (zc_ref, ma_ref, slice(0, C0), slice(0, C0), 0, dc_ref, None),
    ):
        width = part.stop - part.start
        total, cross = jnp.zeros((1, width), F32), jnp.zeros((1, width), F32)
        for f in range(2):
            rows = slice(f * 256, (f + 1) * 256)
            y = (z_ref[rows, :] - m_ref[0:1, part]) * m_ref[1:2, part]
            d = g[:, lanes] * slope(y + off_ref[:, offset : offset + width])
            d_ref[rows, :] = d.astype(BF16)
            if y_ref is not None:
                y_ref[rows, :] = y.astype(BF16)
            total = total + jnp.sum(d, axis=0, keepdims=True)
            cross = cross + jnp.sum(d * y, axis=0, keepdims=True)
        sums.append(total)
        crosses.append(cross)
    store_copies(st_ref, pack_rows(sums + crosses))


def beside_errors(dn, z_ref, mb_ref, off_ref, lanes, offset):
    z = z_ref[:, lanes].astype(F32)
    z = jnp.concatenate([z, jnp.zeros((32, z.shape[1]), F32)], axis=0)
    y = (z - mb_ref[0:1, lanes]) * mb_ref[1:2, lanes]
    return spread_grad(dn) * slope(y + off_ref[:, offset : offset + z.shape[1]]), y


def first_hidden_errors(
    cells, parts, flag_ref, st_ref, db_ref, yb_ref, dn_ref, before_ref, after_ref, mb_ref, off_ref,
    eb_ref, sum_ref, *chunk_refs,
):
    part_mid, part_small = C1B // parts, C2B // parts
    totals = jnp.sum(st_ref[...], axis=0)
    sum_ref[...] = totals
    sum_b, cross_b = unpack_rows(totals, 0, BOUT), unpack_rows(totals, 7, BOUT)
    scale_b = mb_ref[1:2, :BOUT]
    frame = valid_first(256)
    edge = jnp.zeros((16, BOUT), BF16)
    eb_ref[0:16, :] = edge
    eb_ref[1040:1056, :] = edge
    r = lax.broadcasted_iota(jnp.int32, (BOUT, part_mid + part_small), 0)
    k = lax.broadcasted_iota(jnp.int32, (BOUT, part_mid + part_small), 1)
    picks = []
    for m in range(parts):
        p = lax.rem(flag_ref[0] + m, parts)
        want = jnp.where(k < part_mid, p * part_mid + k, C1B + p * part_small + k - part_mid)
        picks.append(jnp.where(r == want, 1.0, 0.0).astype(BF16))
    for s in range(4):
        mask = frame
        if s == 0:
            mask = frame & (flag_ref[1] > 0)
            d, y = beside_errors(
                dn_ref[:64, :BOUT], before_ref, mb_ref, off_ref, slice(0, BOUT), SECTION_A
            )
        elif s == 3:
            mask = frame & (flag_ref[2] > 0)
            d, y = beside_errors(
                dn_ref[64:, :BOUT], after_ref, mb_ref, off_ref, slice(0, BOUT), SECTION_A
            )
        else:
            rows = slice((s - 1) * 256, s * 256)
            d, y = db_ref[rows, :].astype(F32), yb_ref[rows, :].astype(F32)
        e = scale_b * (d - sum_b * (1.0 / cells) - y * (cross_b * (1.0 / cells)))
        e = jnp.where(mask, e, 0.0).astype(BF16)
        eb_ref[16 + s * 256 : 16 + (s + 1) * 256, :] = e
        if s in (1, 2):
            for ref, pick in zip(chunk_refs, picks):
                ref[(s - 1) * 224 : s * 224, :] = dot_nn(e[:224], pick).astype(BF16)


def first_hidden_back(
    eb, zm_ref, ma_ref, off_ref, wmid_ref, wsmall_ref,
    dm_ref, st_ref,
):
    mids, smalls = None, None
    for a in range(3):
        for e in range(3):
            start = 16 + 256 - (a - 1) * 256 - (e - 1) * 16
            one = dot_nt(eb[start : start + 512, :C1B], wmid_ref[3 * a + e])
            two = dot_nt(eb[start : start + 512, C1B:], wsmall_ref[3 * a + e])
            mids = one if mids is None else mids + one
            smalls = two if smalls is None else smalls + two
    back = None
    for g in range(3):
        t = jnp.concatenate(
            [mids[:, g * C1A : (g + 1) * C1A], smalls[:, g * C2A : (g + 1) * C2A]], axis=1
        )
        t = roll_rows(t, g - 1)
        back = t if back is None else back + t
    y = (zm_ref[...] - ma_ref[0:1, C0:]) * ma_ref[1:2, C0:]
    d = jnp.where(valid_first(512), back * slope(y + off_ref[:, C0:IN_OUT]), 0.0)
    dm_ref[...] = d
    sums = jnp.sum(d, axis=0, keepdims=True)
    crosses = jnp.sum(d * y, axis=0, keepdims=True)
    store_copies(st_ref, pack_rows([sums, crosses]))


def first_kernel_grad(
    parts, flag_ref, *refs,
):
    errors, hidden = refs[:parts], refs[parts : 2 * parts]
    chunk_refs, (em, turned, kept) = refs[2 * parts : -3], refs[-3:]
    frames = 2 * parts
    chunks = len(chunk_refs)
    part_small = C2B // parts
    part_mid = C1B // parts
    here, clip = flag_ref[0], flag_ref[3]
    blank = jnp.zeros((16, 128), BF16)
    for m in range(parts):
        source = lax.rem(here - m + parts, parts)
        turned[:, pl.ds(pl.multiple_of(source * 512, 512), 512)] = hidden[m][...]
        for f in range(2):
            base = source * 512 + f * 256
            e = errors[m][f * 224 : f * 224 + 224, :].astype(F32)
            e = jnp.concatenate([e, jnp.zeros((224, 128 - e.shape[1]), F32)], axis=1)
            e = jnp.concatenate([e, jnp.zeros((32, 128), F32)], axis=0)
            for g in range(3):
                moved = roll_rows(e, g - 1).astype(BF16)
                lanes = [slice((3 * i + g) * 128, (3 * i + g + 1) * 128) for i in range(3)]

                def at(start, size):
                    return pl.ds(pl.multiple_of(base + start, 16), size)

                em[at(0, 240), lanes[0]] = moved[16:]
                em[at(240, 16), lanes[0]] = blank
                em[at(0, 256), lanes[1]] = moved
                em[at(0, 16), lanes[2]] = blank
                em[at(16, 240), lanes[2]] = moved[:240]
    mids, smalls = [], []
    for a in range(3):
        shift = 256 * (a - 1)
        lo, hi = max(0, shift), min(frames * 256, frames * 256 + shift)
        both = dot_nn(turned[:, lo:hi], em[lo - shift : hi - shift, :])
        for k in range(9):
            mids.append(both[:C1A, k * 128 : k * 128 + part_mid])
            smalls.append(both[C1A:, k * 128 + part_mid : k * 128 + part_mid + part_small])
    mids, smalls = jnp.concatenate(mids, axis=1), jnp.concatenate(smalls, axis=1)
    high, low = C1A // chunks, C2A // chunks
    wide = smalls.shape[1] // chunks
    blank = jnp.zeros((high - C2A, wide), F32)
    for i in range(chunks):
        tail = [smalls[i * low : (i + 1) * low, q * wide : (q + 1) * wide] for q in range(chunks)]
        tail = jnp.concatenate(tail + [blank], axis=0)
        kept[i * high : (i + 1) * high, :] = jnp.concatenate(
            [mids[i * high : (i + 1) * high], tail], axis=1
        )
    for m, ref in enumerate(chunk_refs):
        at = lax.rem(clip + m, chunks) * high
        ref[...] = kept[pl.ds(pl.multiple_of(at, 8), high), :].astype(BF16)


def first_kernel_join(flag_ref, *refs):
    chunks = len(refs) - 2
    gmid_ref, gsmall_ref = refs[chunks:]
    high, low = C1A // chunks, C2A // chunks
    part_mid, part_small = gmid_ref.shape[2], gsmall_ref.shape[2]
    for m in range(chunks):
        at = lax.rem(flag_ref[3] + m, chunks)
        value = refs[m][...].astype(F32)
        rows = pl.ds(pl.multiple_of(at * high, 8), high)
        for k in range(27):
            gmid_ref[k, rows, :] = value[:, k * part_mid : (k + 1) * part_mid]
        small = [value[q * low : (q + 1) * low, 27 * part_mid :] for q in range(chunks)]
        small = jnp.concatenate(small, axis=1)
        rows = pl.ds(pl.multiple_of(at * low, 8), low)
        for k in range(27):
            gsmall_ref[k, rows, :] = small[:, k * part_small : (k + 1) * part_small]


def first_input_errors(
    cells, parts, flag_ref, st_ref, sum_ref, dm_ref, dc_ref, dp_ref, yp_ref, dn_ref, before_ref,
    after_ref, zc_ref, zm_ref, ma_ref, mb_ref, off_ref, x_ref,
    ea, goff_ref, *refs,
):
    part_in, part_pool = IN_OUT // parts, POOL // parts
    totals = jnp.sum(st_ref[...], axis=0)
    before = sum_ref[...]
    sum_m, cross_m = unpack_rows(totals, 0, MID), unpack_rows(totals, 2, MID)
    sum_b = unpack_rows(before, 0, BOUT)
    sum_p, sum_c = unpack_rows(before, 4, POOL), unpack_rows(before, 5, C0)
    cross_p, cross_c = unpack_rows(before, 11, POOL), unpack_rows(before, 12, C0)
    goff_ref[...] = jnp.concatenate([sum_c, sum_m, sum_p, sum_b], axis=1)
    share = 1.0 / cells
    frame = valid_first(256)
    pools = []
    lanes = slice(BOUT, BOUT + POOL)
    for s in range(4):
        mask = frame
        if s == 0:
            mask = frame & (flag_ref[1] > 0)
            d, y = beside_errors(dn_ref[:64, lanes], before_ref, mb_ref, off_ref, lanes, IN_OUT)
        elif s == 3:
            mask = frame & (flag_ref[2] > 0)
            d, y = beside_errors(dn_ref[64:, lanes], after_ref, mb_ref, off_ref, lanes, IN_OUT)
        else:
            rows = slice((s - 1) * 256, s * 256)
            d, y = dp_ref[rows, :].astype(F32), yp_ref[rows, :].astype(F32)
        e = mb_ref[1:2, BOUT:] * (d - sum_p * share - y * (cross_p * share))
        pools.append(jnp.where(mask, e, 0.0).astype(BF16).astype(F32))
    for f in range(2):
        rows = slice(f * 256, (f + 1) * 256)
        value = box_plane(pools[f] + pools[f + 1] + pools[f + 2], 16) * (1.0 / 27.0)
        ea[rows, IN_OUT:] = jnp.where(frame, value, 0.0).astype(BF16)
        y = (zc_ref[rows, :] - ma_ref[0:1, :C0]) * ma_ref[1:2, :C0]
        e = dc_ref[rows, :].astype(F32) - sum_c * share - y * (cross_c * share)
        ea[rows, :C0] = jnp.where(frame, ma_ref[1:2, :C0] * e, 0.0).astype(BF16)
        y = (zm_ref[rows, :] - ma_ref[0:1, C0:]) * ma_ref[1:2, C0:]
        e = dm_ref[rows, :] - sum_m * share - y * (cross_m * share)
        ea[rows, C0:IN_OUT] = jnp.where(frame, ma_ref[1:2, C0:] * e, 0.0).astype(BF16)
    chunk_refs, g_ref = refs[:-1], refs[-1]
    g_ref[...] = dot_tn(ea[...], x_ref[...])
    for m, ref in enumerate(chunk_refs):
        p = lax.rem(flag_ref[0] + m, parts)
        rows = pl.ds(pl.multiple_of(p * part_in, 8), part_in)
        ref[:part_in] = g_ref[rows, :].astype(BF16)
        rows = pl.ds(pl.multiple_of(IN_OUT + p * part_pool, 8), part_pool)
        ref[part_in:] = g_ref[rows, :].astype(BF16)


def first_input_back(ea, win_ref, wpool_ref, dx_ref):
    dx_ref[...] = dot_nt(ea[:, :IN_OUT], win_ref[...]) + dot_nt(ea[:, IN_OUT:], wpool_ref[...])


def call(body, outs, scratch, *args, scalars=1, us=1, near=(), out_near=(), out_hbm=()):
    in_specs, placed = [], []
    for i, arg in enumerate(args):
        space = pltpu.SMEM if i < scalars else pltpu.VMEM
        in_specs.append(pl.BlockSpec(memory_space=space))
        placed.append(pltpu.with_memory_space_constraint(arg, pltpu.VMEM) if i in near else arg)
    out_specs = [
        pl.BlockSpec(memory_space=pl.ANY if i in out_hbm else pltpu.VMEM) for i in range(len(outs))
    ]
    return pl.pallas_call(
        body,
        out_shape=[
            pltpu.VMEM(*out) if i in out_near else jax.ShapeDtypeStruct(*out)
            for i, out in enumerate(outs)
        ],
        in_specs=in_specs,
        out_specs=out_specs,
        scratch_shapes=[pltpu.VMEM(*s) if isinstance(s, tuple) else s for s in scratch],
        compiler_params=pltpu.CompilerParams(vmem_limit_bytes=VMEM_LIMIT),
        cost_estimate=pl.CostEstimate(
            flops=int(us * 1.1e9),
            bytes_accessed=sum(a.size * a.dtype.itemsize for a in args),
            transcendentals=0,
        ),
    )(*placed)


def exchange(copies):
    return lax.all_to_all(copies, ("clip", "tm"), 0, 0)


def neighbours(head, tail):
    size = lax.axis_size("tm")
    up = [(i, i + 1) for i in range(size - 1)]
    down = [(i + 1, i) for i in range(size - 1)]
    return lax.ppermute(tail, "tm", up), lax.ppermute(head, "tm", down)


def gather_from(value, axis, back=False):
    size = lax.axis_size(axis)
    blocks = [value]
    for m in range(1, size):
        step = -m if back else m
        blocks.append(lax.ppermute(value, axis, [((i + step) % size, i) for i in range(size)]))
    return blocks


def hand_on(chunks, axis):
    size = lax.axis_size(axis)
    blocks = [chunks[0]]
    for m in range(1, size):
        blocks.append(lax.ppermute(chunks[m], axis, [(i, (i + m) % size) for i in range(size)]))
    return blocks


def to_all(value, axis):
    size = lax.axis_size(axis)
    return lax.all_to_all(jnp.broadcast_to(value[None], (size,) + value.shape), axis, 0, 0)


def turned_to(blocks, first):
    return lax.dynamic_slice_in_dim(jnp.concatenate([blocks, blocks]), first, blocks.shape[0])


def summed(parts):
    total = parts[0].astype(F32)
    for i in range(1, len(parts)):
        total = total + parts[i].astype(F32)
    return total.astype(BF16)


def after(value, *others):
    return lax.optimization_barrier((value,) + others)[0]


def small_group(
    features, w_in_4f, w_pool_4f, w_mid_4f, w_small_4f, offsets_4f,
    w_in_5b, w_pool_5b, w_mid_5b, w_small_5b, offsets_5b, cotangent,
):
    clips, frames = lax.axis_size("clip"), lax.axis_size("tm")
    group = clips * frames
    cells = 392.0 * group
    here = lax.axis_index("tm")
    flags = jnp.stack([here, here > 0, here < frames - 1, lax.axis_index("clip")]).astype(jnp.int32)
    offsets_4f, offsets_5b = offsets_4f[None], offsets_5b[None]
    x = jnp.pad(features[0], ((0, 0), (0, 2), (0, 2), (0, 0))).reshape(512, features.shape[-1])
    cot = jnp.pad(cotangent[0, 0], ((0, 0), (0, 1), (0, 0))).reshape(56, OUTC)
    mid_4f, small_4f = w_mid_4f.reshape(9, 3 * C1A, C1B), w_small_4f.reshape(9, 3 * C2A, C2B)
    mid_5b, small_5b = w_mid_5b.reshape(3, 9 * C1A, C1B), w_small_5b.reshape(3, 9 * C2A, C2B)
    before, behind = neighbours(x[:224], x[256:480])
    z_c, z_m, q, stats = call(
        first_project,
        [((512, C0), F32), ((512, MID), F32), ((512, POOL), F32), ((group, 8, 128), F32)],
        [], x, w_in_4f, w_pool_4f, scalars=0, us=4,
    )
    cot = gather_from(after(cot, q), "clip")
    stats = exchange(stats)
    z_b, z_p, stats, x2_c, m_turned, head, tail, moments_a = call(
        first_hidden,
        [((512, BOUT), F32), ((512, POOL), F32), ((group, 16, 128), F32), ((56, C0), BF16),
         ((MID, 512), BF16),
         ((224, BOUT + POOL), BF16), ((224, BOUT + POOL), BF16), ((2, IN_OUT), F32)],
        [((1024, MID), F32), ((1056, 3 * C1A), BF16), ((1056, 3 * C2A), BF16),
         ((4, 128, 128), F32)],
        flags, stats, z_c, z_m, q, before, behind, w_in_4f, w_pool_4f, mid_4f, small_4f,
        offsets_4f, us=20, near=(1, 5, 6),
    )
    *cot, stats = lax.optimization_barrier((*cot, stats))
    cot = gather_from(jnp.stack(cot), "tm")
    stats = exchange(stats)
    x2, moments_b = call(
        first_output,
        [((56, OUTC), BF16), ((2, BOUT + POOL), F32)],
        [((4, 128, 128), F32)],
        stats, z_b, z_p, x2_c, offsets_4f, scalars=0, us=3, near=(0,), out_near=(0,),
    )
    x2 = jnp.stack(gather_from(x2, "clip"))
    before, behind = neighbours(head, tail)
    m_turned = gather_from(m_turned, "tm", back=True)
    x2 = gather_from(after(x2, *cot), "tm")
    part = (C1B // frames, C2B // frames, IN_OUT // frames, POOL // frames)
    (out, g_in_5b, g_pool_5b, g_mid_5b, g_small_5b, g_off_5b, d_near,
     d_b, y_b, d_p, y_p, d_c, stats) = call(
        functools.partial(second_layer, clips, frames),
        [((64, OUTC), BF16), ((part[2], OUTC), F32), ((part[3], OUTC), F32),
         ((27, C1A, part[0]), F32), ((27, C2A, part[1]), F32), ((1, 1024), F32),
         ((128, BOUT + POOL), F32),
         ((512, BOUT), BF16), ((512, BOUT), BF16), ((512, POOL), BF16), ((512, POOL), BF16),
         ((512, C0), BF16), ((group, 16, 128), F32)],
        second_scratch(group * 64, clips * 64, part),
        flags, *x2, *cot, w_in_5b, w_pool_5b, small_5b, offsets_5b, moments_a, moments_b,
        offsets_4f, mid_5b, z_b, z_p, z_c,
        us=35, near=range(1, 1 + 2 * frames), out_hbm=(3, 4),
    )
    stats = exchange(stats)
    e_b, sums, *errors = call(
        functools.partial(first_hidden_errors, cells, frames),
        [((1056, BOUT), BF16), ((16, 128), F32)] + [((448, part[0] + part[1]), BF16)] * frames,
        [], flags, stats, d_b, y_b, d_near, before, behind, moments_b, offsets_4f, us=3, near=(1,),
        out_near=[0, *range(2, 2 + frames)],
    )
    errors = hand_on(errors, "tm")
    d_m, stats = call(
        first_hidden_back,
        [((512, MID), F32), ((group, 8, 128), F32)],
        [], e_b, z_m, moments_a, offsets_4f, mid_4f, small_4f, scalars=0, us=6, near=(0,),
    )
    stats = exchange(stats)
    wide = 27 * part[0] + 27 * part[1] // clips
    g_conv = call(
        functools.partial(first_kernel_grad, frames),
        [((C1A // clips, wide), BF16)] * clips,
        [((frames * 512, 9 * 128), BF16), ((MID, frames * 512), BF16), ((C1A, wide), F32)],
        after(flags, d_m), *errors, *m_turned, us=10, near=range(1, 1 + frames), out_near=range(clips),
    )
    stats = after(stats, *g_conv)
    g_conv = hand_on(g_conv, "clip")
    e_a, g_off, *g_a = call(
        functools.partial(first_input_errors, cells, frames),
        [((512, SECTION_A), BF16), ((1, 1024), F32)]
        + [((part[2] + part[3], features.shape[-1]), BF16)] * frames,
        [((SECTION_A, features.shape[-1]), F32)], flags, stats, sums, d_m, d_c, d_p, y_p, d_near, before, behind,
        z_c, z_m, moments_a, moments_b, offsets_4f, x, us=20, near=(1,),
        out_near=[0, *range(2, 2 + frames)],
    )
    (d_x,) = call(
        first_input_back,
        [((512, features.shape[-1]), F32)],
        [], after(e_a, g_conv[1]), w_in_4f, w_pool_4f, scalars=0, us=0, near=(0,),
    )
    g_a = hand_on(g_a, "tm")
    g_conv = summed(lax.optimization_barrier((*g_conv, d_x))[:clips])
    g_a = summed(lax.optimization_barrier((*g_a, g_conv))[:frames])
    g_conv = gather_from(g_conv, "clip")
    g_a = hand_on(turned_to(g_a.reshape(clips, -1, features.shape[-1]), flags[3]), "clip")
    g_a = after(summed(g_a), g_conv[1])
    g_a = jnp.stack(gather_from(g_a, "clip")).astype(F32)
    g_a = turned_to(g_a, lax.rem(clips - flags[3], clips)).reshape(part[2] + part[3], -1)
    g_mid, g_small = call(
        first_kernel_join,
        [((27, C1A, part[0]), F32), ((27, C2A, part[1]), F32)],
        [], flags, *g_conv, us=4, near=range(1, 1 + clips),
    )

    return (
        out.reshape(1, 1, 8, 8, OUTC)[:, :, :7, :7],
        d_x.reshape(1, 2, 16, 16, -1)[:, :, :14, :14],
        g_a[: part[2]].T,
        g_a[part[2] :].T,
        g_mid,
        g_small,
        g_off[0],
        g_in_5b.T,
        g_pool_5b.T,
        g_mid_5b,
        g_small_5b,
        g_off_5b[0],
    )


def solution(mesh):
    placed = (
        P(("stream", "clip"), "tm", None, None, None),
        P("stream", None),
        P("stream", None),
        P("stream", None, None),
        P("stream", None, None),
        P("stream"),
        P("stream", None),
        P("stream", None),
        P("stream", None, None),
        P("stream", None, None),
        P("stream"),
        P(("stream", "clip"), "tm", None, None, None),
    )
    group = mesh.shape["clip"] * mesh.shape["tm"]
    return jax.shard_map(
        small_group if group <= 16 else shards,
        mesh=mesh,
        in_specs=placed,
        out_specs=(
            P(("stream", "clip"), "tm", None, None, None),
            P(("stream", "clip"), "tm", None, None, None),
            P("stream", "tm"),
            P("stream", "tm"),
            P("stream", None, "tm"),
            P("stream", None, "tm"),
            P("stream"),
            P("stream", "tm"),
            P("stream", "tm"),
            P("stream", None, "tm"),
            P("stream", None, "tm"),
            P("stream"),
        ),
        check_vma=False,
    )
```

```python
import functools

import jax
import jax.numpy as jnp
from jax import lax
from jax.experimental import pallas as pl
from jax.experimental.pallas import tpu as pltpu
from jax.sharding import PartitionSpec as P

C0 = 256
C1A = 160
C1B = 320
C2A = 32
C2B = 128
IN_OUT = 448
SECTION_A = 576


EPSILON = 0.001
VOXEL_AXES = (0, 1, 2, 3)


def extended(value, sides, width):
    for axis, dim in sides:
        size, length = (lax.axis_size(axis), value.shape[dim])
        up = [(i, (i + 1) % size) for i in range(size - 1)]
        down = [(j, i) for i, j in up]
        last = lax.slice_in_dim(value, length - width, length, axis=dim)
        first = lax.slice_in_dim(value, 0, width, axis=dim)
        before = lax.ppermute(last, axis, up)
        after = lax.ppermute(first, axis, down)
        value = jnp.concatenate([before, value, after], axis=dim)
    return value


def as_sent(value):
    return jax.tree.map(lambda a: a.astype(jnp.bfloat16) if a.dtype == jnp.float32 else a, value)


def project(values, weight):
    return jnp.einsum("nfhwc,cd->nfhwd", values, weight, preferred_element_type=jnp.float32)


def pad_plane(values):
    return jnp.pad(values, ((0, 0), (0, 0), (1, 1), (1, 1), (0, 0)))


def box_sum(padded):
    summed = padded[:, :-2] + padded[:, 1:-1] + padded[:, 2:]
    summed = summed[:, :, :-2] + summed[:, :, 1:-1] + summed[:, :, 2:]
    return summed[:, :, :, :-2] + summed[:, :, :, 1:-1] + summed[:, :, :, 2:]


def unfold(padded, frames, height, width):
    slices = []
    for shift_f in range(3):
        for shift_h in range(3):
            for shift_w in range(3):
                slices.append(
                    padded[
                        :,
                        shift_f : shift_f + frames,
                        shift_h : shift_h + height,
                        shift_w : shift_w + width,
                    ]
                )
    return jnp.concatenate(slices, axis=-1)


def fold_back(patch_grad, channels):
    summed = None
    offset_index = 0
    for shift_f in range(3):
        for shift_h in range(3):
            for shift_w in range(3):
                segment = patch_grad[..., offset_index * channels : (offset_index + 1) * channels]
                placed = jnp.pad(
                    segment,
                    (
                        (0, 0),
                        (shift_f, 2 - shift_f),
                        (shift_h, 2 - shift_h),
                        (shift_w, 2 - shift_w),
                        (0, 0),
                    ),
                )
                summed = placed if summed is None else summed + placed
                offset_index += 1
    return summed


def return_input_rims(grad_padded):
    interior = grad_padded[:, 1:-1]
    rim_pair = jnp.concatenate([grad_padded[:, :1], grad_padded[:, -1:]], axis=1)
    arrived = extended(rim_pair.astype(jnp.bfloat16), (("tm", 1),), 1).astype(rim_pair.dtype)
    interior = interior.at[:, 0].add(arrived[:, 0])
    return interior.at[:, -1].add(arrived[:, 3])


def return_hidden_rims(grad_padded):
    interior = grad_padded[:, 1:-1]
    rim_pair = jnp.concatenate([grad_padded[:, :1], grad_padded[:, -1:]], axis=1)
    arrived = extended(rim_pair.astype(jnp.bfloat16), (("tm", 1),), 1).astype(rim_pair.dtype)
    interior = interior.at[:, 0].add(arrived[:, 0])
    return interior.at[:, -1].add(arrived[:, 3])


def section_first(features, w_in, w_pool):
    rimmed = extended(features, (("tm", 1),), 1)
    padded = pad_plane(rimmed).astype(jnp.float32)
    pooled = (box_sum(padded) / 27.0).astype(jnp.bfloat16)
    pre_first = jnp.concatenate([project(features, w_in), project(pooled, w_pool)], axis=-1)
    return (pre_first, pooled)


def section_second(middle, w_mid, w_small):
    rimmed = extended(middle, (("tm", 1),), 1)
    padded = pad_plane(rimmed)
    frames, height, width = (middle.shape[1], middle.shape[2], middle.shape[3])
    patch_one = unfold(padded[..., :C1A], frames, height, width)
    patch_two = unfold(padded[..., C1A:], frames, height, width)
    pre_second = jnp.concatenate(
        [
            project(patch_one, w_mid.reshape(27 * C1A, C1B)),
            project(patch_two, w_small.reshape(27 * C2A, C2B)),
        ],
        axis=-1,
    )
    return (pre_second, patch_one, patch_two)


def moments(pre_act, voxel_count):
    first_sum = lax.psum(jnp.sum(pre_act, axis=VOXEL_AXES), ("clip", "tm"))
    center = first_sum / voxel_count
    spread = lax.psum(jnp.sum(jnp.square(pre_act - center), axis=VOXEL_AXES), ("clip", "tm"))
    variance = spread / voxel_count
    return (center, variance)


def standardize(pre_act, center, variance):
    return (pre_act - center) * lax.rsqrt(variance + EPSILON)


def silu_slope(act_in):
    sigmoid_value = jax.nn.sigmoid(act_in)
    return sigmoid_value + act_in * sigmoid_value * (1.0 - sigmoid_value)


def block_forward(features, params, voxel_count):
    w_in, w_pool, w_mid, w_small, offsets = params
    pre_first, pooled = section_first(features, w_in, w_pool)
    center_a, variance_a = moments(pre_first, voxel_count)
    hidden_a = jax.nn.silu(standardize(pre_first, center_a, variance_a) + offsets[:SECTION_A])
    middle = hidden_a[..., C0:IN_OUT].astype(jnp.bfloat16)
    pre_second, patch_one, patch_two = section_second(middle, w_mid, w_small)
    center_b, variance_b = moments(pre_second, voxel_count)
    hidden_b = jax.nn.silu(standardize(pre_second, center_b, variance_b) + offsets[SECTION_A:])
    block_out = jnp.concatenate([hidden_a[..., :C0], hidden_b, hidden_a[..., IN_OUT:]], axis=-1)
    return (block_out, (center_a, variance_a, center_b, variance_b))


def norm_back(slope_grad, normed, variance, voxel_count):
    sum_grad, sum_cross = lax.psum(
        (jnp.sum(slope_grad, axis=VOXEL_AXES), jnp.sum(slope_grad * normed, axis=VOXEL_AXES)),
        ("clip", "tm"),
    )
    scaled = lax.rsqrt(variance + EPSILON) * (
        slope_grad - sum_grad / voxel_count - normed * (sum_cross / voxel_count)
    )
    return (scaled.astype(jnp.bfloat16), sum_grad)


def block_backward(features, params, moment_pair, out_grad, voxel_count):
    w_in, w_pool, w_mid, w_small, offsets = params
    center_a, variance_a, center_b, variance_b = moment_pair
    pre_first, pooled = section_first(features, w_in, w_pool)
    normed_a = standardize(pre_first, center_a, variance_a)
    act_a = normed_a + offsets[:SECTION_A]
    middle = jax.nn.silu(act_a)[..., C0:IN_OUT].astype(jnp.bfloat16)
    pre_second, patch_one, patch_two = section_second(middle, w_mid, w_small)
    normed_b = standardize(pre_second, center_b, variance_b)
    act_b = normed_b + offsets[SECTION_A:]
    grad_b = out_grad[..., C0 : C0 + C1B + C2B] * silu_slope(act_b)
    error_b, offset_grad_b = norm_back(grad_b, normed_b, variance_b, voxel_count)
    error_one = error_b[..., :C1B]
    error_two = error_b[..., C1B:]
    grad_mid = jnp.einsum(
        "nfhwk,nfhwo->ko", patch_one, error_one, preferred_element_type=jnp.float32
    ).reshape(27, C1A, C1B)
    grad_small = jnp.einsum(
        "nfhwk,nfhwo->ko", patch_two, error_two, preferred_element_type=jnp.float32
    ).reshape(27, C2A, C2B)
    back_one = fold_back(
        jnp.einsum(
            "nfhwo,ko->nfhwk",
            error_one,
            w_mid.reshape(27 * C1A, C1B),
            preferred_element_type=jnp.float32,
        ),
        C1A,
    )
    back_two = fold_back(
        jnp.einsum(
            "nfhwo,ko->nfhwk",
            error_two,
            w_small.reshape(27 * C2A, C2B),
            preferred_element_type=jnp.float32,
        ),
        C2A,
    )
    middle_grad = return_hidden_rims(
        jnp.concatenate([back_one, back_two], axis=-1)[:, :, 1:-1, 1:-1]
    )
    grad_a = jnp.concatenate(
        [out_grad[..., :C0], middle_grad, out_grad[..., C0 + C1B + C2B :]], axis=-1
    ) * silu_slope(act_a)
    error_a, offset_grad_a = norm_back(grad_a, normed_a, variance_a, voxel_count)
    error_in = error_a[..., :IN_OUT]
    error_pool = error_a[..., IN_OUT:]
    grad_in = jnp.einsum("nfhwc,nfhwd->cd", features, error_in, preferred_element_type=jnp.float32)
    grad_pool = jnp.einsum(
        "nfhwc,nfhwd->cd", pooled, error_pool, preferred_element_type=jnp.float32
    )
    direct = jnp.einsum("nfhwd,cd->nfhwc", error_in, w_in, preferred_element_type=jnp.float32)
    pool_grad = jnp.einsum(
        "nfhwd,cd->nfhwc", error_pool, w_pool, preferred_element_type=jnp.float32
    )
    spread_pad = jnp.pad(pool_grad, ((0, 0), (2, 2), (2, 2), (2, 2), (0, 0)))
    padded_grad = (box_sum(spread_pad) / 27.0)[:, :, 1:-1, 1:-1]
    input_grad = direct + return_input_rims(padded_grad)
    return (
        input_grad,
        (grad_in, grad_pool, grad_mid, grad_small),
        jnp.concatenate([offset_grad_a, offset_grad_b]),
    )


def reduce_grads(weight_grads):
    summed = jax.tree.map(
        lambda part: part.astype(jnp.float32), lax.psum(as_sent(weight_grads), "clip")
    )
    reduced = (
        lax.psum_scatter(
            summed[0].astype(jnp.bfloat16), "tm", scatter_dimension=1, tiled=True
        ).astype(jnp.float32),
        lax.psum_scatter(
            summed[1].astype(jnp.bfloat16), "tm", scatter_dimension=1, tiled=True
        ).astype(jnp.float32),
        lax.psum_scatter(
            summed[2].astype(jnp.bfloat16), "tm", scatter_dimension=2, tiled=True
        ).astype(jnp.float32),
        lax.psum_scatter(
            summed[3].astype(jnp.bfloat16), "tm", scatter_dimension=2, tiled=True
        ).astype(jnp.float32),
    )
    return reduced


def halve_grid(values):
    n, f, h, w, c = values.shape
    return jnp.sum(values.reshape(n, f // 2, 2, h // 2, 2, w // 2, 2, c), axis=(2, 4, 6)) * 0.125


def spread_half(grad_small_grid):
    n, f, h, w, c = grad_small_grid.shape
    expanded = jnp.broadcast_to(
        (grad_small_grid * 0.125)[:, :, None, :, None, :, None, :], (n, f, 2, h, 2, w, 2, c)
    )
    return expanded.reshape(n, 2 * f, 2 * h, 2 * w, c)


def shards(
    features,
    w_in_4f,
    w_pool_4f,
    w_mid_4f,
    w_small_4f,
    offsets_4f,
    w_in_5b,
    w_pool_5b,
    w_mid_5b,
    w_small_5b,
    offsets_5b,
    cotangent,
):
    params_first = (w_in_4f, w_pool_4f, w_mid_4f, w_small_4f, offsets_4f)
    params_second = (w_in_5b, w_pool_5b, w_mid_5b, w_small_5b, offsets_5b)
    devices_used = lax.axis_size("clip") * lax.axis_size("tm")
    count_first = float(
        features.shape[0] * features.shape[1] * features.shape[2] * features.shape[3] * devices_used
    )
    count_second = count_first / 8.0
    out_first, moments_first = block_forward(features, params_first, count_first)
    input_second = halve_grid(out_first).astype(jnp.bfloat16)
    out_second, moments_second = block_forward(input_second, params_second, count_second)
    grad_second, weights_second, offsets_grad_second = block_backward(
        input_second, params_second, moments_second, cotangent.astype(jnp.float32), count_second
    )
    reduced_second = reduce_grads(weights_second)
    grad_first, weights_first, offsets_grad_first = block_backward(
        features, params_first, moments_first, spread_half(grad_second), count_first
    )
    reduced_first = reduce_grads(weights_first)
    final_out = out_second.astype(jnp.bfloat16)
    return (
        final_out,
        grad_first,
        reduced_first[0],
        reduced_first[1],
        reduced_first[2],
        reduced_first[3],
        offsets_grad_first,
        reduced_second[0],
        reduced_second[1],
        reduced_second[2],
        reduced_second[3],
        offsets_grad_second,
    )


F32 = jnp.float32
BF16 = jnp.bfloat16
MID = 192
BOUT = 448
POOL = 128
OUTC = 832
VMEM_LIMIT = 58 * 1024 * 1024


def dot_nn(a, b):
    return lax.dot_general(a, b, (((1,), (0,)), ((), ())), preferred_element_type=F32)


def dot_nt(a, b):
    return lax.dot_general(a, b, (((1,), (1,)), ((), ())), preferred_element_type=F32)


def dot_tn(a, b):
    return lax.dot_general(a, b, (((0,), (0,)), ((), ())), preferred_element_type=F32)


def roll_rows(value, shift):
    rows = value.shape[0]
    shift %= rows
    return value if shift == 0 else pltpu.roll(value, shift, 0)


def eye(n):
    r = lax.broadcasted_iota(jnp.int32, (n, n), 0)
    k = lax.broadcasted_iota(jnp.int32, (n, n), 1)
    return jnp.where(r == k, 1.0, 0.0).astype(BF16)


def valid_first(rows):
    r = lax.broadcasted_iota(jnp.int32, (rows, 1), 0)
    return ((r & 255) < 224) & ((r & 15) < 14)


def valid_second(rows):
    r = lax.broadcasted_iota(jnp.int32, (rows, 1), 0)
    return ((r & 63) < 56) & ((r & 7) < 7)


def sigmoid(a):
    return 0.5 * jnp.tanh(0.5 * a) + 0.5


def act(a):
    return a * sigmoid(a)


def slope(a):
    s = sigmoid(a)
    return s + a * s * (1.0 - s)


def pack_rows(vectors):
    pieces = []
    for v in vectors:
        width = v.shape[1]
        full = -(-width // 128) * 128
        if full != width:
            v = jnp.concatenate([v, jnp.zeros((1, full - width), F32)], axis=1)
        for i in range(full // 128):
            pieces.append(v[:, i * 128 : (i + 1) * 128])
    return jnp.concatenate(pieces, axis=0)


def unpack_rows(rows, start, width):
    count = -(-width // 128)
    return jnp.concatenate([rows[start + i : start + i + 1] for i in range(count)], axis=1)[
        :, :width
    ]


def store_copies(ref, rows):
    count, height = ref.shape[0], ref.shape[1]
    if rows.shape[0] < height:
        rows = jnp.concatenate([rows, jnp.zeros((height - rows.shape[0], 128), F32)], axis=0)
    for i in range(count):
        ref[i] = rows


def local_moments(value, mask, cells):
    total = jnp.sum(jnp.where(mask, value, 0.0), axis=0, keepdims=True)
    delta = jnp.where(mask, value - total * (1.0 / cells), 0.0)
    return total, jnp.sum(delta * delta, axis=0, keepdims=True)


def joint_moments(gathered, height, cells):
    devices = gathered.shape[0]
    sums, squares = gathered[:, :height], gathered[:, height : 2 * height]
    mean = jnp.sum(sums, axis=0) * (1.0 / (cells * devices))
    apart = sums * (1.0 / cells) - mean[None]
    spread = jnp.sum(squares, axis=0) + cells * jnp.sum(apart * apart, axis=0)
    return mean, lax.rsqrt(spread * (1.0 / (cells * devices)) + EPSILON)


def halve(total, scratch, dtype):
    width = total.shape[1]
    both = total[:256] + total[256:]
    pairs = jnp.sum(both.reshape(8, 2, 16, width), axis=1).reshape(128, width)
    pieces = []
    for i in range(-(-width // 128)):
        lanes = min(128, width - i * 128)
        scratch[i, :, :lanes] = pairs[:, i * 128 : i * 128 + lanes]
        piece = scratch[i, pl.ds(0, 64, 2), :] + scratch[i, pl.ds(1, 64, 2), :]
        pieces.append(piece[:, :lanes])
    halved = jnp.concatenate(pieces, axis=1)
    return (halved * 0.125).astype(dtype)


def box_plane(value, stride):
    value = value + roll_rows(value, stride) + roll_rows(value, -stride)
    return value + roll_rows(value, 1) + roll_rows(value, -1)


def first_project(x_ref, win_ref, wpool_ref, zc_ref, zm_ref, q_ref, st_ref):
    for f in range(2):
        rows = pl.ds(f * 256, 256)
        x = x_ref[rows, :]
        z = dot_nn(x, win_ref[...])
        zc_ref[rows, :], zm_ref[rows, :] = z[:, :C0], z[:, C0:]
        q_ref[rows, :] = dot_nn(x, wpool_ref[...])
    mask = valid_first(512)
    moments = [local_moments(ref[...], mask, 392) for ref in (zc_ref, zm_ref)]
    total, squares = [jnp.concatenate([m[i] for m in moments], axis=1) for i in range(2)]
    store_copies(st_ref, pack_rows([total, squares]))


def first_hidden(
    flag_ref, st_ref, zc_ref, zm_ref, q_ref, before_ref, after_ref, win_ref, wpool_ref, wmid_ref,
    wsmall_ref, off_ref,
    zb_ref, zp_ref, st2_ref, x2_ref, mt_ref, head_ref, tail_ref, ma_ref,
    mid, um_ref, us_ref, half,
):
    mean_rows, scale_rows = joint_moments(st_ref[...], 4, 392.0)
    mean, scale = unpack_rows(mean_rows, 0, IN_OUT), unpack_rows(scale_rows, 0, IN_OUT)
    ma_ref[...] = jnp.concatenate([mean, scale], axis=0)
    off = off_ref[:, :IN_OUT]
    frame = valid_first(256)
    prev, after = flag_ref[1] > 0, flag_ref[2] > 0

    def middle(z, mask):
        return jnp.where(mask, act((z - mean[:, C0:]) * scale[:, C0:] + off[:, C0:]), 0.0)

    blank = jnp.zeros((32, MID), F32)
    for start, ref, mask in ((0, before_ref, prev), (768, after_ref, after)):
        z = jnp.concatenate([dot_nn(ref[...], win_ref[:, C0:]), blank], axis=0)
        mid[start : start + 256, :] = middle(z, frame & mask)
    mid[256:512, :] = middle(zm_ref[0:256, :], frame)
    mid[512:768, :] = middle(zm_ref[256:512, :], frame)
    for ref in (um_ref, us_ref):
        edge = jnp.zeros((16, ref.shape[1]), BF16)
        ref[0:16, :] = edge
        ref[1040:1056, :] = edge

    for f in range(4):
        rows = slice(f * 256, (f + 1) * 256)
        shifted = [roll_rows(mid[rows, :], 1 - g) for g in range(3)]
        into = slice(16 + f * 256, 16 + (f + 1) * 256)
        um_ref[into, :] = jnp.concatenate([v[:, :C1A] for v in shifted], axis=1).astype(BF16)
        us_ref[into, :] = jnp.concatenate([v[:, C1A:] for v in shifted], axis=1).astype(BF16)

    def convolve(u_ref, w_ref):
        total = None
        for a in range(3):
            for e in range(3):
                start = 16 + a * 256 + (e - 1) * 16
                term = dot_nn(u_ref[start : start + 512, :], w_ref[3 * a + e])
                total = term if total is None else total + term
        return total

    zb_ref[:, :C1B] = convolve(um_ref, wmid_ref)
    zb_ref[:, C1B:] = convolve(us_ref, wsmall_ref)

    first, last = q_ref[0:256, :], q_ref[256:512, :]
    pair = first + last
    for f, ref in ((0, before_ref), (1, after_ref)):
        beside = jnp.concatenate([dot_nn(ref[...], wpool_ref[...]), blank[:, :POOL]], axis=0)
        value = pair + beside
        value = box_plane(value, 16) * (1.0 / 27.0)
        zp_ref[f * 256 : (f + 1) * 256, :] = jnp.where(frame, value, 0.0)

    both = valid_first(512)
    total_b, squares_b = local_moments(zb_ref[...], both, 392)
    total_p, squares_p = local_moments(zp_ref[...], both, 392)
    store_copies(st2_ref, pack_rows([total_b, total_p, squares_b, squares_p]))
    middle_z = jnp.concatenate([total_b, total_p], axis=1) * (1.0 / 392.0)
    high = middle_z.astype(BF16).astype(F32)
    means = jnp.concatenate([high, middle_z - high, jnp.zeros((14, BOUT + POOL), F32)], axis=0)
    for f, ref in ((0, head_ref), (1, tail_ref)):
        rows = pl.ds(f * 256, 224)
        ref[:224, :BOUT] = (zb_ref[rows, :] - middle_z[:, :BOUT]).astype(BF16)
        ref[:224, BOUT:] = (zp_ref[rows, :] - middle_z[:, BOUT:]).astype(BF16)
        ref[224:, :] = means.astype(BF16)
    hidden = act((zc_ref[...] - mean[:, :C0]) * scale[:, :C0] + off[:, :C0])
    x2_ref[...] = halve(jnp.where(both, hidden, 0.0), half, BF16)[:56]
    mt_ref[...] = dot_nt(eye(MID), mid[256:768, :].astype(BF16)).astype(BF16)


def first_output(st_ref, zb_ref, zp_ref, x2c_ref, off_ref, x2_ref, mb_ref, half):
    mean_rows, scale_rows = joint_moments(st_ref[...], 5, 392.0)
    both = valid_first(512)
    moments = []
    for start, width, z_ref, offset in ((0, BOUT, zb_ref, SECTION_A), (4, POOL, zp_ref, IN_OUT)):
        mean, scale = unpack_rows(mean_rows, start, width), unpack_rows(scale_rows, start, width)
        hidden = act((z_ref[...] - mean) * scale + off_ref[:, offset : offset + width])
        into = slice(C0, C0 + BOUT) if start == 0 else slice(C0 + BOUT, OUTC)
        x2_ref[:, into] = halve(jnp.where(both, hidden, 0.0), half, BF16)[:56]
        moments.append(jnp.concatenate([mean, scale], axis=0))
    x2_ref[:, :C0] = x2c_ref[...]
    mb_ref[...] = jnp.concatenate(moments, axis=1)


def second_layer(clips, frames, flag_ref, *refs):
    x_refs, cot_refs, refs = refs[:frames], refs[frames : 2 * frames], refs[2 * frames :]
    win_ref, wpool_ref, wsmall_ref, off_ref = refs[:4]
    moment_refs, wide_refs, refs = refs[4:7], refs[7:11], refs[11:]
    out_ref, gin_ref, gpool_ref, gmid_hbm, gsmall_hbm, goff_ref = refs[:6]
    dn_ref, error_refs, scratch = refs[6], refs[7:13], refs[13:]
    xs, cs, za, zb, um, us, qs, eb, es, ea, et, ets, eat, da, tmid_ref, tsmall_ref = scratch[:16]
    gmid_ref, gsmall_ref, sems = *scratch[16:18], scratch[-1]
    wmid_ref = wide_refs[0]
    here = flag_ref[0]
    step = clips * 64
    rows = frames * step
    cells = clips * frames * 49.0
    share = 1.0 / cells
    part_mid, part_small = gmid_ref.shape[2], gsmall_ref.shape[2]
    part_in, part_pool = gin_ref.shape[0], gpool_ref.shape[0]
    mask = valid_second(step)

    tail = jnp.zeros((16, OUTC), BF16)

    def assemble(into, blocks):
        for m in range(frames):
            for c in range(clips):
                base = lax.rem(here + m, frames) * step + c * 64
                into[pl.ds(pl.multiple_of(base + 48, 16), 16), :] = tail
                into[pl.ds(pl.multiple_of(base, 64), 56), :] = blocks[m][c]

    assemble(xs, x_refs)
    for ref in (um, us, qs, ea):
        blank = jnp.zeros((step, ref.shape[1]), ref.dtype)
        ref[:step, :] = blank
        ref[step + rows :, :] = blank

    def rows_of(f):
        return slice(f * step, (f + 1) * step)

    def inner(f, shift=1):
        return slice((f + shift) * step, (f + shift + 1) * step)

    def window(a):
        return slice(a * step, a * step + rows)

    def over_frames(body, init):
        for f in range(frames):
            init = body(f, init)
        return init

    def box(f):
        value = qs[inner(f, 0), :] + qs[inner(f, 1), :] + qs[inner(f, 2), :]
        return jnp.where(mask, box_plane(value, 8) * (1.0 / 27.0), 0.0)

    za[:, :IN_OUT] = dot_nn(xs[...], win_ref[...])
    qs[window(1), :] = dot_nn(xs[...], wpool_ref[...])

    def pool_frame(f, total):
        z, p = za[rows_of(f), :IN_OUT], box(f)
        za[rows_of(f), IN_OUT:] = p
        return total + jnp.concatenate(
            [jnp.sum(z, axis=0, keepdims=True), jnp.sum(p, axis=0, keepdims=True)], axis=1
        )

    total_a = over_frames(pool_frame, jnp.zeros((1, SECTION_A), F32))
    mean_a = total_a * share

    def spread_frame(ref, mean):
        def body(f, total):
            delta = jnp.where(mask, ref[rows_of(f), :] - mean, 0.0)
            return total + jnp.sum(delta * delta, axis=0, keepdims=True)

        return body

    spread_a = over_frames(spread_frame(za, mean_a), jnp.zeros((1, SECTION_A), F32))
    scale_a = lax.rsqrt(spread_a * share + EPSILON)
    off_a, off_b = off_ref[:, :SECTION_A], off_ref[:, SECTION_A:]

    def normal_a(f, lo, hi):
        return (za[rows_of(f), lo:hi] - mean_a[:, lo:hi]) * scale_a[:, lo:hi]

    def unfold_frame(f, _):
        a = normal_a(f, C0, IN_OUT) + off_a[:, C0:IN_OUT]
        hidden = jnp.where(mask, act(a), 0.0)
        aside = [roll_rows(hidden, 1 - g) for g in range(3)]
        shifted = [roll_rows(v, 8 * (1 - e)) for e in range(3) for v in aside]
        um[inner(f), :] = jnp.concatenate([v[:, :C1A] for v in shifted], axis=1).astype(BF16)
        us[inner(f), :] = jnp.concatenate([v[:, C1A:] for v in shifted], axis=1).astype(BF16)
        return 0

    over_frames(unfold_frame, 0)

    def convolve(u_ref, w_ref):
        total = dot_nn(u_ref[window(0), :], w_ref[0])
        for a in range(1, 3):
            total = total + dot_nn(u_ref[window(a), :], w_ref[a])
        return total

    zb[:, :C1B] = convolve(um, wmid_ref)
    zb[:, C1B:] = convolve(us, wsmall_ref)
    turn_kernels(wmid_ref, tmid_ref, (1, 0, 2))
    turn_kernels(wsmall_ref, tsmall_ref, (1, 0, 2))

    def total_frame(f, total):
        return total + jnp.sum(jnp.where(mask, zb[rows_of(f), :], 0.0), axis=0, keepdims=True)

    zero_b = jnp.zeros((1, BOUT), F32)
    mean_b = over_frames(total_frame, zero_b) * share
    spread_b = over_frames(spread_frame(zb, mean_b), zero_b)
    scale_b = lax.rsqrt(spread_b * share + EPSILON)

    own = pl.ds(pl.multiple_of(here * step, 64), 64)
    hidden_a = act((za[own, :] - mean_a) * scale_a + off_a)
    hidden_b = act((zb[own, :] - mean_b) * scale_b + off_b)
    out_ref[...] = jnp.concatenate(
        [hidden_a[:, :C0], hidden_b, hidden_a[:, IN_OUT:]], axis=1
    ).astype(BF16)

    assemble(cs, cot_refs)

    def sums_b(f, carry):
        y = (zb[rows_of(f), :] - mean_b) * scale_b
        d = cs[rows_of(f), C0 : C0 + BOUT].astype(F32) * slope(y + off_b)
        zb[rows_of(f), :] = y
        da[rows_of(f), :BOUT] = d
        return (
            carry[0] + jnp.sum(d, axis=0, keepdims=True),
            carry[1] + jnp.sum(d * y, axis=0, keepdims=True),
        )

    sum_b, cross_b = over_frames(sums_b, (zero_b, zero_b))

    for ref in (eb, es):
        width = ref.shape[1] // 3
        blank = jnp.zeros((step, width), BF16)
        ref[rows - step :, width : 2 * width] = blank
        ref[:step, 2 * width :] = blank

    for f in range(frames):
        at = slice(f * step, (f + 1) * step)
        e = da[at, :BOUT] - sum_b * share - zb[at, :] * (cross_b * share)
        e = jnp.where(mask, scale_b * e, 0.0).astype(BF16)
        for i, row in enumerate((f, f - 1, f + 1)):
            if 0 <= row < frames:
                at = slice(row * step, (row + 1) * step)
                eb[at, i * C1B : (i + 1) * C1B] = e[:, :C1B]
                es[at, i * C2B : (i + 1) * C2B] = e[:, C1B:]

    def picker(count, cut, part_one, part_two, columns, edge):
        r = lax.broadcasted_iota(jnp.int32, (count, columns), 0)
        k = lax.broadcasted_iota(jnp.int32, (count, columns), 1)
        want = jnp.where(r < cut, here * part_one + r, edge + here * part_two + r - cut)
        return jnp.where(k == want, 1.0, 0.0).astype(BF16)

    pick_mid = picker(part_mid, part_mid, part_mid, 0, C1B, 0)
    pick_small = picker(part_small, part_small, part_small, 0, C2B, 0)
    et[...] = dot_nt(pick_mid, eb[:, :C1B]).astype(BF16)
    ets[...] = dot_nt(pick_small, es[:, :C2B]).astype(BF16)
    for a in range(3):
        gm = dot_nn(et[...], um[window(a), :])
        gmid_ref[9 * a : 9 * a + 9] = gm.T.reshape(9, C1A, part_mid)
        gs = dot_nn(ets[...], us[window(a), :])
        gsmall_ref[9 * a : 9 * a + 9] = gs.T.reshape(9, C2A, part_small)
    stores = [
        pltpu.make_async_copy(gmid_ref, gmid_hbm, sems.at[0]),
        pltpu.make_async_copy(gsmall_ref, gsmall_hbm, sems.at[1]),
    ]
    for store in stores:
        store.start()

    small = dot_nt(es[...], tsmall_ref[...])
    sides = [None] * 3
    for e in range(3):
        mid = dot_nt(eb[...], tmid_ref[e * 3 * C1A : (e + 1) * 3 * C1A, :])
        for g in range(3):
            k = 3 * e + g
            t = jnp.concatenate(
                [mid[:, g * C1A : (g + 1) * C1A], small[:, k * C2A : (k + 1) * C2A]], axis=1
            )
            t = roll_rows(t, 8 * (e - 1))
            sides[g] = t if e == 0 else sides[g] + t
    da[:, :MID] = roll_rows(sides[0], -1) + sides[1] + roll_rows(sides[2], 1)

    def grad_a(f, carry):
        y = normal_a(f, 0, SECTION_A)
        gain = slope(y + off_a)
        cot = cs[rows_of(f), :]
        d = jnp.concatenate(
            [cot[:, :C0].astype(F32), da[rows_of(f), :MID], cot[:, C0 + BOUT :].astype(F32)], axis=1
        )
        d = jnp.where(mask, d * gain, 0.0)
        da[rows_of(f), :] = d
        za[rows_of(f), :] = y
        return (
            carry[0] + jnp.sum(d, axis=0, keepdims=True),
            carry[1] + jnp.sum(d * y, axis=0, keepdims=True),
        )

    zero_a = jnp.zeros((1, SECTION_A), F32)
    sum_a, cross_a = over_frames(grad_a, (zero_a, zero_a))
    goff_ref[...] = jnp.concatenate([sum_a, sum_b], axis=1)

    def error_a(f, _):
        e = da[rows_of(f), :] - sum_a * share - za[rows_of(f), :] * (cross_a * share)
        e = jnp.where(mask, scale_a * e, 0.0)
        ea[inner(f), :IN_OUT] = e[:, :IN_OUT].astype(BF16)
        qs[inner(f), :] = e[:, IN_OUT:].astype(BF16).astype(F32)
        return 0

    over_frames(error_a, 0)

    def spread_pool(f, _):
        ea[inner(f), IN_OUT:] = box(f).astype(BF16)
        return 0

    over_frames(spread_pool, 0)

    near = [(here + f) * step for f in range(3)]
    near = jnp.concatenate([ea[pl.ds(pl.multiple_of(r, 64), 64), :] for r in near], axis=0)
    dx = dot_nt(near[:, :IN_OUT], win_ref[...]) + dot_nt(near[:, IN_OUT:], wpool_ref[...])
    first_errors(dx[64:128], *wide_refs[1:], *moment_refs, *error_refs)
    dn_ref[:64, :], dn_ref[64:, :] = dx[:64, C0:], dx[128:, C0:]
    pick_a = picker(part_in + part_pool, part_in, part_in, part_pool, SECTION_A, IN_OUT)
    eat[...] = dot_nt(pick_a, ea[window(1), :]).astype(BF16)
    gin_ref[...] = dot_nn(eat[:part_in, :], xs[...])
    gpool_ref[...] = dot_nn(eat[part_in:, :], xs[...])
    for store in stores:
        store.wait()


def second_scratch(rows, step, part):
    wide = rows + 2 * step
    return [
        ((rows, OUTC), BF16), ((rows, OUTC), BF16), ((rows, SECTION_A), F32), ((rows, BOUT), F32),
        ((wide, 9 * C1A), BF16), ((wide, 9 * C2A), BF16), ((wide, POOL), F32),
        ((rows, 3 * C1B), BF16), ((rows, 3 * C2B), BF16), ((wide, SECTION_A), BF16),
        ((part[0], rows), BF16), ((part[1], rows), BF16), ((part[2] + part[3], rows), BF16),
        ((rows, SECTION_A), F32), ((9 * C1A, 3 * C1B), BF16), ((9 * C2A, 3 * C2B), BF16),
        ((27, C1A, part[0]), F32), ((27, C2A, part[1]), F32), pltpu.SemaphoreType.DMA((2,)),
    ]


def turn_kernels(w_ref, t_ref, order):
    width = w_ref.shape[2]
    for i, k in enumerate(order):
        t_ref[:, i * width : (i + 1) * width] = w_ref[k]


def spread_grad(d):
    r = lax.broadcasted_iota(jnp.int32, (256, 64), 0)
    k = lax.broadcasted_iota(jnp.int32, (256, 64), 1)
    spread = jnp.where(k == ((r >> 5) << 3) + ((r & 15) >> 1), 1.0, 0.0).astype(BF16)
    d = d * 0.125
    high = d.astype(BF16)
    low = (d - high.astype(F32)).astype(BF16)
    return dot_nn(spread, high) + dot_nn(spread, low)


def first_errors(
    dx, zb_ref, zp_ref, zc_ref, ma_ref, mb_ref, off_ref,
    db_ref, yb_ref, dp_ref, yp_ref, dc_ref, st_ref,
):
    g = spread_grad(dx)
    sums, crosses = [], []
    for z_ref, m_ref, lanes, part, offset, d_ref, y_ref in (
        (zb_ref, mb_ref, slice(C0, C0 + BOUT), slice(0, BOUT), SECTION_A, db_ref, yb_ref),
        (zp_ref, mb_ref, slice(C0 + BOUT, OUTC), slice(BOUT, BOUT + POOL), IN_OUT, dp_ref, yp_ref),
        (zc_ref, ma_ref, slice(0, C0), slice(0, C0), 0, dc_ref, None),
    ):
        width = part.stop - part.start
        total, cross = jnp.zeros((1, width), F32), jnp.zeros((1, width), F32)
        for f in range(2):
            rows = slice(f * 256, (f + 1) * 256)
            y = (z_ref[rows, :] - m_ref[0:1, part]) * m_ref[1:2, part]
            d = g[:, lanes] * slope(y + off_ref[:, offset : offset + width])
            d_ref[rows, :] = d.astype(BF16)
            if y_ref is not None:
                y_ref[rows, :] = y.astype(BF16)
            total = total + jnp.sum(d, axis=0, keepdims=True)
            cross = cross + jnp.sum(d * y, axis=0, keepdims=True)
        sums.append(total)
        crosses.append(cross)
    store_copies(st_ref, pack_rows(sums + crosses))


def beside_errors(dn, z_ref, mb_ref, off_ref, lanes, offset):
    means = z_ref[224:, lanes].astype(F32)
    z = z_ref[:224, lanes].astype(F32) + (means[0:1] + means[1:2])
    z = jnp.concatenate([z, jnp.zeros((32, z.shape[1]), F32)], axis=0)
    y = (z - mb_ref[0:1, lanes]) * mb_ref[1:2, lanes]
    return spread_grad(dn) * slope(y + off_ref[:, offset : offset + z.shape[1]]), y


def first_hidden_errors(
    cells, parts, flag_ref, st_ref, db_ref, yb_ref, dn_ref, before_ref, after_ref, mb_ref, off_ref,
    eb_ref, sum_ref, *chunk_refs,
):
    part_mid, part_small = C1B // parts, C2B // parts
    totals = jnp.sum(st_ref[...], axis=0)
    sum_ref[...] = totals
    sum_b, cross_b = unpack_rows(totals, 0, BOUT), unpack_rows(totals, 7, BOUT)
    scale_b = mb_ref[1:2, :BOUT]
    frame = valid_first(256)
    edge = jnp.zeros((16, BOUT), BF16)
    eb_ref[0:16, :] = edge
    eb_ref[1040:1056, :] = edge
    r = lax.broadcasted_iota(jnp.int32, (BOUT, part_mid + part_small), 0)
    k = lax.broadcasted_iota(jnp.int32, (BOUT, part_mid + part_small), 1)
    picks = []
    for m in range(parts):
        p = lax.rem(flag_ref[0] + m, parts)
        want = jnp.where(k < part_mid, p * part_mid + k, C1B + p * part_small + k - part_mid)
        picks.append(jnp.where(r == want, 1.0, 0.0).astype(BF16))
    for s in range(4):
        mask = frame
        if s == 0:
            mask = frame & (flag_ref[1] > 0)
            d, y = beside_errors(
                dn_ref[:64, :BOUT], before_ref, mb_ref, off_ref, slice(0, BOUT), SECTION_A
            )
        elif s == 3:
            mask = frame & (flag_ref[2] > 0)
            d, y = beside_errors(
                dn_ref[64:, :BOUT], after_ref, mb_ref, off_ref, slice(0, BOUT), SECTION_A
            )
        else:
            rows = slice((s - 1) * 256, s * 256)
            d, y = db_ref[rows, :].astype(F32), yb_ref[rows, :].astype(F32)
        e = scale_b * (d - sum_b * (1.0 / cells) - y * (cross_b * (1.0 / cells)))
        e = jnp.where(mask, e, 0.0).astype(BF16)
        eb_ref[16 + s * 256 : 16 + (s + 1) * 256, :] = e
        if s in (1, 2):
            for ref, pick in zip(chunk_refs, picks):
                ref[(s - 1) * 224 : s * 224, :] = dot_nn(e[:224], pick).astype(BF16)


def first_hidden_back(
    eb, zm_ref, ma_ref, off_ref, wmid_ref, wsmall_ref,
    dm_ref, st_ref,
):
    mids, smalls = None, None
    for a in range(3):
        for e in range(3):
            start = 16 + 256 - (a - 1) * 256 - (e - 1) * 16
            one = dot_nt(eb[start : start + 512, :C1B], wmid_ref[3 * a + e])
            two = dot_nt(eb[start : start + 512, C1B:], wsmall_ref[3 * a + e])
            mids = one if mids is None else mids + one
            smalls = two if smalls is None else smalls + two
    back = None
    for g in range(3):
        t = jnp.concatenate(
            [mids[:, g * C1A : (g + 1) * C1A], smalls[:, g * C2A : (g + 1) * C2A]], axis=1
        )
        t = roll_rows(t, g - 1)
        back = t if back is None else back + t
    y = (zm_ref[...] - ma_ref[0:1, C0:]) * ma_ref[1:2, C0:]
    d = jnp.where(valid_first(512), back * slope(y + off_ref[:, C0:IN_OUT]), 0.0)
    dm_ref[...] = d
    sums = jnp.sum(d, axis=0, keepdims=True)
    crosses = jnp.sum(d * y, axis=0, keepdims=True)
    store_copies(st_ref, pack_rows([sums, crosses]))


def first_kernel_grad(
    parts, flag_ref, *refs,
):
    errors, hidden = refs[:parts], refs[parts : 2 * parts]
    chunk_refs, (em, turned, kept) = refs[2 * parts : -3], refs[-3:]
    frames = 2 * parts
    chunks = len(chunk_refs)
    part_small = C2B // parts
    part_mid = C1B // parts
    here, clip = flag_ref[0], flag_ref[3]
    blank = jnp.zeros((16, 128), BF16)
    for m in range(parts):
        source = lax.rem(here - m + parts, parts)
        turned[:, pl.ds(pl.multiple_of(source * 512, 512), 512)] = hidden[m][...]
        for f in range(2):
            base = source * 512 + f * 256
            e = errors[m][f * 224 : f * 224 + 224, :].astype(F32)
            e = jnp.concatenate([e, jnp.zeros((224, 128 - e.shape[1]), F32)], axis=1)
            e = jnp.concatenate([e, jnp.zeros((32, 128), F32)], axis=0)
            for g in range(3):
                moved = roll_rows(e, g - 1).astype(BF16)
                lanes = [slice((3 * i + g) * 128, (3 * i + g + 1) * 128) for i in range(3)]

                def at(start, size):
                    return pl.ds(pl.multiple_of(base + start, 16), size)

                em[at(0, 240), lanes[0]] = moved[16:]
                em[at(240, 16), lanes[0]] = blank
                em[at(0, 256), lanes[1]] = moved
                em[at(0, 16), lanes[2]] = blank
                em[at(16, 240), lanes[2]] = moved[:240]
    mids, smalls = [], []
    for a in range(3):
        shift = 256 * (a - 1)
        lo, hi = max(0, shift), min(frames * 256, frames * 256 + shift)
        both = dot_nn(turned[:, lo:hi], em[lo - shift : hi - shift, :])
        for k in range(9):
            mids.append(both[:C1A, k * 128 : k * 128 + part_mid])
            smalls.append(both[C1A:, k * 128 + part_mid : k * 128 + part_mid + part_small])
    mids, smalls = jnp.concatenate(mids, axis=1), jnp.concatenate(smalls, axis=1)
    high, low = C1A // chunks, C2A // chunks
    wide = smalls.shape[1] // chunks
    blank = jnp.zeros((high - C2A, wide), F32)
    for i in range(chunks):
        tail = [smalls[i * low : (i + 1) * low, q * wide : (q + 1) * wide] for q in range(chunks)]
        tail = jnp.concatenate(tail + [blank], axis=0)
        kept[i * high : (i + 1) * high, :] = jnp.concatenate(
            [mids[i * high : (i + 1) * high], tail], axis=1
        )
    for m, ref in enumerate(chunk_refs):
        at = lax.rem(clip + m, chunks) * high
        ref[...] = kept[pl.ds(pl.multiple_of(at, 8), high), :].astype(BF16)


def first_kernel_join(flag_ref, *refs):
    chunks = len(refs) - 2
    gmid_ref, gsmall_ref = refs[chunks:]
    high, low = C1A // chunks, C2A // chunks
    part_mid, part_small = gmid_ref.shape[2], gsmall_ref.shape[2]
    for m in range(chunks):
        at = lax.rem(flag_ref[3] + m, chunks)
        value = refs[m][...].astype(F32)
        rows = pl.ds(pl.multiple_of(at * high, 8), high)
        for k in range(27):
            gmid_ref[k, rows, :] = value[:, k * part_mid : (k + 1) * part_mid]
        small = [value[q * low : (q + 1) * low, 27 * part_mid :] for q in range(chunks)]
        small = jnp.concatenate(small, axis=1)
        rows = pl.ds(pl.multiple_of(at * low, 8), low)
        for k in range(27):
            gsmall_ref[k, rows, :] = small[:, k * part_small : (k + 1) * part_small]


def first_input_errors(
    cells, parts, flag_ref, st_ref, sum_ref, dm_ref, dc_ref, dp_ref, yp_ref, dn_ref, before_ref,
    after_ref, zc_ref, zm_ref, ma_ref, mb_ref, off_ref, x_ref,
    ea, goff_ref, *refs,
):
    part_in, part_pool = IN_OUT // parts, POOL // parts
    totals = jnp.sum(st_ref[...], axis=0)
    before = sum_ref[...]
    sum_m, cross_m = unpack_rows(totals, 0, MID), unpack_rows(totals, 2, MID)
    sum_b = unpack_rows(before, 0, BOUT)
    sum_p, sum_c = unpack_rows(before, 4, POOL), unpack_rows(before, 5, C0)
    cross_p, cross_c = unpack_rows(before, 11, POOL), unpack_rows(before, 12, C0)
    goff_ref[...] = jnp.concatenate([sum_c, sum_m, sum_p, sum_b], axis=1)
    share = 1.0 / cells
    frame = valid_first(256)
    pools = []
    lanes = slice(BOUT, BOUT + POOL)
    for s in range(4):
        mask = frame
        if s == 0:
            mask = frame & (flag_ref[1] > 0)
            d, y = beside_errors(dn_ref[:64, lanes], before_ref, mb_ref, off_ref, lanes, IN_OUT)
        elif s == 3:
            mask = frame & (flag_ref[2] > 0)
            d, y = beside_errors(dn_ref[64:, lanes], after_ref, mb_ref, off_ref, lanes, IN_OUT)
        else:
            rows = slice((s - 1) * 256, s * 256)
            d, y = dp_ref[rows, :].astype(F32), yp_ref[rows, :].astype(F32)
        e = mb_ref[1:2, BOUT:] * (d - sum_p * share - y * (cross_p * share))
        pools.append(jnp.where(mask, e, 0.0).astype(BF16).astype(F32))
    for f in range(2):
        rows = slice(f * 256, (f + 1) * 256)
        value = box_plane(pools[f] + pools[f + 1] + pools[f + 2], 16) * (1.0 / 27.0)
        ea[rows, IN_OUT:] = jnp.where(frame, value, 0.0).astype(BF16)
        y = (zc_ref[rows, :] - ma_ref[0:1, :C0]) * ma_ref[1:2, :C0]
        e = dc_ref[rows, :].astype(F32) - sum_c * share - y * (cross_c * share)
        ea[rows, :C0] = jnp.where(frame, ma_ref[1:2, :C0] * e, 0.0).astype(BF16)
        y = (zm_ref[rows, :] - ma_ref[0:1, C0:]) * ma_ref[1:2, C0:]
        e = dm_ref[rows, :] - sum_m * share - y * (cross_m * share)
        ea[rows, C0:IN_OUT] = jnp.where(frame, ma_ref[1:2, C0:] * e, 0.0).astype(BF16)
    chunk_refs, g_ref = refs[:-1], refs[-1]
    g_ref[...] = dot_tn(ea[...], x_ref[...])
    for m, ref in enumerate(chunk_refs):
        p = lax.rem(flag_ref[0] + m, parts)
        rows = pl.ds(pl.multiple_of(p * part_in, 8), part_in)
        ref[:part_in] = g_ref[rows, :].astype(BF16)
        rows = pl.ds(pl.multiple_of(IN_OUT + p * part_pool, 8), part_pool)
        ref[part_in:] = g_ref[rows, :].astype(BF16)


def first_input_back(ea, win_ref, wpool_ref, dx_ref):
    dx_ref[...] = dot_nt(ea[:, :IN_OUT], win_ref[...]) + dot_nt(ea[:, IN_OUT:], wpool_ref[...])


def call(body, outs, scratch, *args, scalars=1, us=1, near=(), out_near=(), out_hbm=()):
    in_specs, placed = [], []
    for i, arg in enumerate(args):
        space = pltpu.SMEM if i < scalars else pltpu.VMEM
        in_specs.append(pl.BlockSpec(memory_space=space))
        placed.append(pltpu.with_memory_space_constraint(arg, pltpu.VMEM) if i in near else arg)
    out_specs = [
        pl.BlockSpec(memory_space=pl.ANY if i in out_hbm else pltpu.VMEM) for i in range(len(outs))
    ]
    return pl.pallas_call(
        body,
        out_shape=[
            pltpu.VMEM(*out) if i in out_near else jax.ShapeDtypeStruct(*out)
            for i, out in enumerate(outs)
        ],
        in_specs=in_specs,
        out_specs=out_specs,
        scratch_shapes=[pltpu.VMEM(*s) if isinstance(s, tuple) else s for s in scratch],
        compiler_params=pltpu.CompilerParams(vmem_limit_bytes=VMEM_LIMIT),
        cost_estimate=pl.CostEstimate(
            flops=int(us * 1.1e9),
            bytes_accessed=sum(a.size * a.dtype.itemsize for a in args),
            transcendentals=0,
        ),
    )(*placed)


def exchange(copies):
    return lax.all_to_all(copies, ("clip", "tm"), 0, 0)


def neighbours(head, tail):
    size = lax.axis_size("tm")
    up = [(i, i + 1) for i in range(size - 1)]
    down = [(i + 1, i) for i in range(size - 1)]
    return lax.ppermute(tail, "tm", up), lax.ppermute(head, "tm", down)


def gather_from(value, axis, back=False):
    size = lax.axis_size(axis)
    blocks = [value]
    for m in range(1, size):
        step = -m if back else m
        blocks.append(lax.ppermute(value, axis, [((i + step) % size, i) for i in range(size)]))
    return blocks


def hand_on(chunks, axis):
    size = lax.axis_size(axis)
    blocks = [chunks[0]]
    for m in range(1, size):
        blocks.append(lax.ppermute(chunks[m], axis, [(i, (i + m) % size) for i in range(size)]))
    return blocks


def to_all(value, axis):
    size = lax.axis_size(axis)
    return lax.all_to_all(jnp.broadcast_to(value[None], (size,) + value.shape), axis, 0, 0)


def turned_to(blocks, first):
    return lax.dynamic_slice_in_dim(jnp.concatenate([blocks, blocks]), first, blocks.shape[0])


def summed(parts):
    total = parts[0].astype(F32)
    for i in range(1, len(parts)):
        total = total + parts[i].astype(F32)
    return total.astype(BF16)


def after(value, *others):
    return lax.optimization_barrier((value,) + others)[0]


def small_group(
    features, w_in_4f, w_pool_4f, w_mid_4f, w_small_4f, offsets_4f,
    w_in_5b, w_pool_5b, w_mid_5b, w_small_5b, offsets_5b, cotangent,
):
    clips, frames = lax.axis_size("clip"), lax.axis_size("tm")
    group = clips * frames
    cells = 392.0 * group
    here = lax.axis_index("tm")
    flags = jnp.stack([here, here > 0, here < frames - 1, lax.axis_index("clip")]).astype(jnp.int32)
    offsets_4f, offsets_5b = offsets_4f[None], offsets_5b[None]
    x = jnp.pad(features[0], ((0, 0), (0, 2), (0, 2), (0, 0))).reshape(512, features.shape[-1])
    cot = jnp.pad(cotangent[0, 0], ((0, 0), (0, 1), (0, 0))).reshape(56, OUTC)
    mid_4f, small_4f = w_mid_4f.reshape(9, 3 * C1A, C1B), w_small_4f.reshape(9, 3 * C2A, C2B)
    mid_5b, small_5b = w_mid_5b.reshape(3, 9 * C1A, C1B), w_small_5b.reshape(3, 9 * C2A, C2B)
    before, behind = neighbours(x[:224], x[256:480])
    z_c, z_m, q, stats = call(
        first_project,
        [((512, C0), F32), ((512, MID), F32), ((512, POOL), F32), ((group, 8, 128), F32)],
        [], x, w_in_4f, w_pool_4f, scalars=0, us=4,
    )
    cot = gather_from(after(cot, q), "clip")
    stats = exchange(stats)
    z_b, z_p, stats, x2_c, m_turned, head, tail, moments_a = call(
        first_hidden,
        [((512, BOUT), F32), ((512, POOL), F32), ((group, 16, 128), F32), ((56, C0), BF16),
         ((MID, 512), BF16),
         ((240, BOUT + POOL), BF16), ((240, BOUT + POOL), BF16), ((2, IN_OUT), F32)],
        [((1024, MID), F32), ((1056, 3 * C1A), BF16), ((1056, 3 * C2A), BF16),
         ((4, 128, 128), F32)],
        flags, stats, z_c, z_m, q, before, behind, w_in_4f, w_pool_4f, mid_4f, small_4f,
        offsets_4f, us=20, near=(1, 5, 6),
    )
    *cot, stats = lax.optimization_barrier((*cot, stats))
    cot = gather_from(jnp.stack(cot), "tm")
    stats = exchange(stats)
    x2, moments_b = call(
        first_output,
        [((56, OUTC), BF16), ((2, BOUT + POOL), F32)],
        [((4, 128, 128), F32)],
        stats, z_b, z_p, x2_c, offsets_4f, scalars=0, us=3, near=(0,), out_near=(0,),
    )
    x2 = jnp.stack(gather_from(x2, "clip"))
    before, behind = neighbours(head, tail)
    m_turned = gather_from(m_turned, "tm", back=True)
    x2 = gather_from(after(x2, *cot), "tm")
    part = (C1B // frames, C2B // frames, IN_OUT // frames, POOL // frames)
    (out, g_in_5b, g_pool_5b, g_mid_5b, g_small_5b, g_off_5b, d_near,
     d_b, y_b, d_p, y_p, d_c, stats) = call(
        functools.partial(second_layer, clips, frames),
        [((64, OUTC), BF16), ((part[2], OUTC), F32), ((part[3], OUTC), F32),
         ((27, C1A, part[0]), F32), ((27, C2A, part[1]), F32), ((1, 1024), F32),
         ((128, BOUT + POOL), F32),
         ((512, BOUT), BF16), ((512, BOUT), BF16), ((512, POOL), BF16), ((512, POOL), BF16),
         ((512, C0), BF16), ((group, 16, 128), F32)],
        second_scratch(group * 64, clips * 64, part),
        flags, *x2, *cot, w_in_5b, w_pool_5b, small_5b, offsets_5b, moments_a, moments_b,
        offsets_4f, mid_5b, z_b, z_p, z_c,
        us=35, near=range(1, 1 + 2 * frames), out_hbm=(3, 4),
    )
    stats = exchange(stats)
    e_b, sums, *errors = call(
        functools.partial(first_hidden_errors, cells, frames),
        [((1056, BOUT), BF16), ((16, 128), F32)] + [((448, part[0] + part[1]), BF16)] * frames,
        [], flags, stats, d_b, y_b, d_near, before, behind, moments_b, offsets_4f, us=3, near=(1,),
        out_near=[0, *range(2, 2 + frames)],
    )
    errors = hand_on(errors, "tm")
    d_m, stats = call(
        first_hidden_back,
        [((512, MID), F32), ((group, 8, 128), F32)],
        [], e_b, z_m, moments_a, offsets_4f, mid_4f, small_4f, scalars=0, us=6, near=(0,),
    )
    stats = exchange(stats)
    wide = 27 * part[0] + 27 * part[1] // clips
    g_conv = call(
        functools.partial(first_kernel_grad, frames),
        [((C1A // clips, wide), BF16)] * clips,
        [((frames * 512, 9 * 128), BF16), ((MID, frames * 512), BF16), ((C1A, wide), F32)],
        after(flags, d_m), *errors, *m_turned, us=10, near=range(1, 1 + frames), out_near=range(clips),
    )
    stats = after(stats, *g_conv)
    g_conv = hand_on(g_conv, "clip")
    e_a, g_off, *g_a = call(
        functools.partial(first_input_errors, cells, frames),
        [((512, SECTION_A), BF16), ((1, 1024), F32)]
        + [((part[2] + part[3], features.shape[-1]), BF16)] * frames,
        [((SECTION_A, features.shape[-1]), F32)], flags, stats, sums, d_m, d_c, d_p, y_p, d_near, before, behind,
        z_c, z_m, moments_a, moments_b, offsets_4f, x, us=20, near=(1,),
        out_near=[0, *range(2, 2 + frames)],
    )
    (d_x,) = call(
        first_input_back,
        [((512, features.shape[-1]), F32)],
        [], after(e_a, g_conv[1]), w_in_4f, w_pool_4f, scalars=0, us=0, near=(0,),
    )
    g_a = hand_on(g_a, "tm")
    g_conv = summed(lax.optimization_barrier((*g_conv, d_x))[:clips])
    g_a = summed(lax.optimization_barrier((*g_a, g_conv))[:frames])
    g_conv = gather_from(g_conv, "clip")
    g_a = hand_on(turned_to(g_a.reshape(clips, -1, features.shape[-1]), flags[3]), "clip")
    g_a = after(summed(g_a), g_conv[1])
    g_a = jnp.stack(gather_from(g_a, "clip")).astype(F32)
    g_a = turned_to(g_a, lax.rem(clips - flags[3], clips)).reshape(part[2] + part[3], -1)
    g_mid, g_small = call(
        first_kernel_join,
        [((27, C1A, part[0]), F32), ((27, C2A, part[1]), F32)],
        [], flags, *g_conv, us=4, near=range(1, 1 + clips),
    )

    return (
        out.reshape(1, 1, 8, 8, OUTC)[:, :, :7, :7],
        d_x.reshape(1, 2, 16, 16, -1)[:, :, :14, :14],
        g_a[: part[2]].T,
        g_a[part[2] :].T,
        g_mid,
        g_small,
        g_off[0],
        g_in_5b.T,
        g_pool_5b.T,
        g_mid_5b,
        g_small_5b,
        g_off_5b[0],
    )


def solution(mesh):
    placed = (
        P(("stream", "clip"), "tm", None, None, None),
        P("stream", None),
        P("stream", None),
        P("stream", None, None),
        P("stream", None, None),
        P("stream"),
        P("stream", None),
        P("stream", None),
        P("stream", None, None),
        P("stream", None, None),
        P("stream"),
        P(("stream", "clip"), "tm", None, None, None),
    )
    group = mesh.shape["clip"] * mesh.shape["tm"]
    return jax.shard_map(
        small_group if group <= 16 else shards,
        mesh=mesh,
        in_specs=placed,
        out_specs=(
            P(("stream", "clip"), "tm", None, None, None),
            P(("stream", "clip"), "tm", None, None, None),
            P("stream", "tm"),
            P("stream", "tm"),
            P("stream", None, "tm"),
            P("stream", None, "tm"),
            P("stream"),
            P("stream", "tm"),
            P("stream", "tm"),
            P("stream", None, "tm"),
            P("stream", None, "tm"),
            P("stream"),
        ),
        check_vma=False,
    )
```

```python
import functools

import jax
import jax.numpy as jnp
from jax import lax
from jax.experimental import pallas as pl
from jax.experimental.pallas import tpu as pltpu
from jax.sharding import PartitionSpec as P

C0 = 256
C1A = 160
C1B = 320
C2A = 32
C2B = 128
IN_OUT = 448
SECTION_A = 576


EPSILON = 0.001
VOXEL_AXES = (0, 1, 2, 3)


def extended(value, sides, width):
    for axis, dim in sides:
        size, length = (lax.axis_size(axis), value.shape[dim])
        up = [(i, (i + 1) % size) for i in range(size - 1)]
        down = [(j, i) for i, j in up]
        last = lax.slice_in_dim(value, length - width, length, axis=dim)
        first = lax.slice_in_dim(value, 0, width, axis=dim)
        before = lax.ppermute(last, axis, up)
        after = lax.ppermute(first, axis, down)
        value = jnp.concatenate([before, value, after], axis=dim)
    return value


def as_sent(value):
    return jax.tree.map(lambda a: a.astype(jnp.bfloat16) if a.dtype == jnp.float32 else a, value)


def project(values, weight):
    return jnp.einsum("nfhwc,cd->nfhwd", values, weight, preferred_element_type=jnp.float32)


def pad_plane(values):
    return jnp.pad(values, ((0, 0), (0, 0), (1, 1), (1, 1), (0, 0)))


def box_sum(padded):
    summed = padded[:, :-2] + padded[:, 1:-1] + padded[:, 2:]
    summed = summed[:, :, :-2] + summed[:, :, 1:-1] + summed[:, :, 2:]
    return summed[:, :, :, :-2] + summed[:, :, :, 1:-1] + summed[:, :, :, 2:]


def unfold(padded, frames, height, width):
    slices = []
    for shift_f in range(3):
        for shift_h in range(3):
            for shift_w in range(3):
                slices.append(
                    padded[
                        :,
                        shift_f : shift_f + frames,
                        shift_h : shift_h + height,
                        shift_w : shift_w + width,
                    ]
                )
    return jnp.concatenate(slices, axis=-1)


def fold_back(patch_grad, channels):
    summed = None
    offset_index = 0
    for shift_f in range(3):
        for shift_h in range(3):
            for shift_w in range(3):
                segment = patch_grad[..., offset_index * channels : (offset_index + 1) * channels]
                placed = jnp.pad(
                    segment,
                    (
                        (0, 0),
                        (shift_f, 2 - shift_f),
                        (shift_h, 2 - shift_h),
                        (shift_w, 2 - shift_w),
                        (0, 0),
                    ),
                )
                summed = placed if summed is None else summed + placed
                offset_index += 1
    return summed


def return_input_rims(grad_padded):
    interior = grad_padded[:, 1:-1]
    rim_pair = jnp.concatenate([grad_padded[:, :1], grad_padded[:, -1:]], axis=1)
    arrived = extended(rim_pair.astype(jnp.bfloat16), (("tm", 1),), 1).astype(rim_pair.dtype)
    interior = interior.at[:, 0].add(arrived[:, 0])
    return interior.at[:, -1].add(arrived[:, 3])


def return_hidden_rims(grad_padded):
    interior = grad_padded[:, 1:-1]
    rim_pair = jnp.concatenate([grad_padded[:, :1], grad_padded[:, -1:]], axis=1)
    arrived = extended(rim_pair.astype(jnp.bfloat16), (("tm", 1),), 1).astype(rim_pair.dtype)
    interior = interior.at[:, 0].add(arrived[:, 0])
    return interior.at[:, -1].add(arrived[:, 3])


def section_first(features, w_in, w_pool):
    rimmed = extended(features, (("tm", 1),), 1)
    padded = pad_plane(rimmed).astype(jnp.float32)
    pooled = (box_sum(padded) / 27.0).astype(jnp.bfloat16)
    pre_first = jnp.concatenate([project(features, w_in), project(pooled, w_pool)], axis=-1)
    return (pre_first, pooled)


def section_second(middle, w_mid, w_small):
    rimmed = extended(middle, (("tm", 1),), 1)
    padded = pad_plane(rimmed)
    frames, height, width = (middle.shape[1], middle.shape[2], middle.shape[3])
    patch_one = unfold(padded[..., :C1A], frames, height, width)
    patch_two = unfold(padded[..., C1A:], frames, height, width)
    pre_second = jnp.concatenate(
        [
            project(patch_one, w_mid.reshape(27 * C1A, C1B)),
            project(patch_two, w_small.reshape(27 * C2A, C2B)),
        ],
        axis=-1,
    )
    return (pre_second, patch_one, patch_two)


def moments(pre_act, voxel_count):
    first_sum = lax.psum(jnp.sum(pre_act, axis=VOXEL_AXES), ("clip", "tm"))
    center = first_sum / voxel_count
    spread = lax.psum(jnp.sum(jnp.square(pre_act - center), axis=VOXEL_AXES), ("clip", "tm"))
    variance = spread / voxel_count
    return (center, variance)


def standardize(pre_act, center, variance):
    return (pre_act - center) * lax.rsqrt(variance + EPSILON)


def silu_slope(act_in):
    sigmoid_value = jax.nn.sigmoid(act_in)
    return sigmoid_value + act_in * sigmoid_value * (1.0 - sigmoid_value)


def block_forward(features, params, voxel_count):
    w_in, w_pool, w_mid, w_small, offsets = params
    pre_first, pooled = section_first(features, w_in, w_pool)
    center_a, variance_a = moments(pre_first, voxel_count)
    hidden_a = jax.nn.silu(standardize(pre_first, center_a, variance_a) + offsets[:SECTION_A])
    middle = hidden_a[..., C0:IN_OUT].astype(jnp.bfloat16)
    pre_second, patch_one, patch_two = section_second(middle, w_mid, w_small)
    center_b, variance_b = moments(pre_second, voxel_count)
    hidden_b = jax.nn.silu(standardize(pre_second, center_b, variance_b) + offsets[SECTION_A:])
    block_out = jnp.concatenate([hidden_a[..., :C0], hidden_b, hidden_a[..., IN_OUT:]], axis=-1)
    return (block_out, (center_a, variance_a, center_b, variance_b))


def norm_back(slope_grad, normed, variance, voxel_count):
    sum_grad, sum_cross = lax.psum(
        (jnp.sum(slope_grad, axis=VOXEL_AXES), jnp.sum(slope_grad * normed, axis=VOXEL_AXES)),
        ("clip", "tm"),
    )
    scaled = lax.rsqrt(variance + EPSILON) * (
        slope_grad - sum_grad / voxel_count - normed * (sum_cross / voxel_count)
    )
    return (scaled.astype(jnp.bfloat16), sum_grad)


def block_backward(features, params, moment_pair, out_grad, voxel_count):
    w_in, w_pool, w_mid, w_small, offsets = params
    center_a, variance_a, center_b, variance_b = moment_pair
    pre_first, pooled = section_first(features, w_in, w_pool)
    normed_a = standardize(pre_first, center_a, variance_a)
    act_a = normed_a + offsets[:SECTION_A]
    middle = jax.nn.silu(act_a)[..., C0:IN_OUT].astype(jnp.bfloat16)
    pre_second, patch_one, patch_two = section_second(middle, w_mid, w_small)
    normed_b = standardize(pre_second, center_b, variance_b)
    act_b = normed_b + offsets[SECTION_A:]
    grad_b = out_grad[..., C0 : C0 + C1B + C2B] * silu_slope(act_b)
    error_b, offset_grad_b = norm_back(grad_b, normed_b, variance_b, voxel_count)
    error_one = error_b[..., :C1B]
    error_two = error_b[..., C1B:]
    grad_mid = jnp.einsum(
        "nfhwk,nfhwo->ko", patch_one, error_one, preferred_element_type=jnp.float32
    ).reshape(27, C1A, C1B)
    grad_small = jnp.einsum(
        "nfhwk,nfhwo->ko", patch_two, error_two, preferred_element_type=jnp.float32
    ).reshape(27, C2A, C2B)
    back_one = fold_back(
        jnp.einsum(
            "nfhwo,ko->nfhwk",
            error_one,
            w_mid.reshape(27 * C1A, C1B),
            preferred_element_type=jnp.float32,
        ),
        C1A,
    )
    back_two = fold_back(
        jnp.einsum(
            "nfhwo,ko->nfhwk",
            error_two,
            w_small.reshape(27 * C2A, C2B),
            preferred_element_type=jnp.float32,
        ),
        C2A,
    )
    middle_grad = return_hidden_rims(
        jnp.concatenate([back_one, back_two], axis=-1)[:, :, 1:-1, 1:-1]
    )
    grad_a = jnp.concatenate(
        [out_grad[..., :C0], middle_grad, out_grad[..., C0 + C1B + C2B :]], axis=-1
    ) * silu_slope(act_a)
    error_a, offset_grad_a = norm_back(grad_a, normed_a, variance_a, voxel_count)
    error_in = error_a[..., :IN_OUT]
    error_pool = error_a[..., IN_OUT:]
    grad_in = jnp.einsum("nfhwc,nfhwd->cd", features, error_in, preferred_element_type=jnp.float32)
    grad_pool = jnp.einsum(
        "nfhwc,nfhwd->cd", pooled, error_pool, preferred_element_type=jnp.float32
    )
    direct = jnp.einsum("nfhwd,cd->nfhwc", error_in, w_in, preferred_element_type=jnp.float32)
    pool_grad = jnp.einsum(
        "nfhwd,cd->nfhwc", error_pool, w_pool, preferred_element_type=jnp.float32
    )
    spread_pad = jnp.pad(pool_grad, ((0, 0), (2, 2), (2, 2), (2, 2), (0, 0)))
    padded_grad = (box_sum(spread_pad) / 27.0)[:, :, 1:-1, 1:-1]
    input_grad = direct + return_input_rims(padded_grad)
    return (
        input_grad,
        (grad_in, grad_pool, grad_mid, grad_small),
        jnp.concatenate([offset_grad_a, offset_grad_b]),
    )


def reduce_grads(weight_grads):
    summed = jax.tree.map(
        lambda part: part.astype(jnp.float32), lax.psum(as_sent(weight_grads), "clip")
    )
    reduced = (
        lax.psum_scatter(
            summed[0].astype(jnp.bfloat16), "tm", scatter_dimension=1, tiled=True
        ).astype(jnp.float32),
        lax.psum_scatter(
            summed[1].astype(jnp.bfloat16), "tm", scatter_dimension=1, tiled=True
        ).astype(jnp.float32),
        lax.psum_scatter(
            summed[2].astype(jnp.bfloat16), "tm", scatter_dimension=2, tiled=True
        ).astype(jnp.float32),
        lax.psum_scatter(
            summed[3].astype(jnp.bfloat16), "tm", scatter_dimension=2, tiled=True
        ).astype(jnp.float32),
    )
    return reduced


def halve_grid(values):
    n, f, h, w, c = values.shape
    return jnp.sum(values.reshape(n, f // 2, 2, h // 2, 2, w // 2, 2, c), axis=(2, 4, 6)) * 0.125


def spread_half(grad_small_grid):
    n, f, h, w, c = grad_small_grid.shape
    expanded = jnp.broadcast_to(
        (grad_small_grid * 0.125)[:, :, None, :, None, :, None, :], (n, f, 2, h, 2, w, 2, c)
    )
    return expanded.reshape(n, 2 * f, 2 * h, 2 * w, c)


def shards(
    features,
    w_in_4f,
    w_pool_4f,
    w_mid_4f,
    w_small_4f,
    offsets_4f,
    w_in_5b,
    w_pool_5b,
    w_mid_5b,
    w_small_5b,
    offsets_5b,
    cotangent,
):
    params_first = (w_in_4f, w_pool_4f, w_mid_4f, w_small_4f, offsets_4f)
    params_second = (w_in_5b, w_pool_5b, w_mid_5b, w_small_5b, offsets_5b)
    devices_used = lax.axis_size("clip") * lax.axis_size("tm")
    count_first = float(
        features.shape[0] * features.shape[1] * features.shape[2] * features.shape[3] * devices_used
    )
    count_second = count_first / 8.0
    out_first, moments_first = block_forward(features, params_first, count_first)
    input_second = halve_grid(out_first).astype(jnp.bfloat16)
    out_second, moments_second = block_forward(input_second, params_second, count_second)
    grad_second, weights_second, offsets_grad_second = block_backward(
        input_second, params_second, moments_second, cotangent.astype(jnp.float32), count_second
    )
    reduced_second = reduce_grads(weights_second)
    grad_first, weights_first, offsets_grad_first = block_backward(
        features, params_first, moments_first, spread_half(grad_second), count_first
    )
    reduced_first = reduce_grads(weights_first)
    final_out = out_second.astype(jnp.bfloat16)
    return (
        final_out,
        grad_first,
        reduced_first[0],
        reduced_first[1],
        reduced_first[2],
        reduced_first[3],
        offsets_grad_first,
        reduced_second[0],
        reduced_second[1],
        reduced_second[2],
        reduced_second[3],
        offsets_grad_second,
    )


F32 = jnp.float32
BF16 = jnp.bfloat16
MID = 192
BOUT = 448
POOL = 128
OUTC = 832
VMEM_LIMIT = 58 * 1024 * 1024


def dot_nn(a, b):
    return lax.dot_general(a, b, (((1,), (0,)), ((), ())), preferred_element_type=F32)


def dot_nt(a, b):
    return lax.dot_general(a, b, (((1,), (1,)), ((), ())), preferred_element_type=F32)


def dot_tn(a, b):
    return lax.dot_general(a, b, (((0,), (0,)), ((), ())), preferred_element_type=F32)


def roll_rows(value, shift):
    rows = value.shape[0]
    shift %= rows
    return value if shift == 0 else pltpu.roll(value, shift, 0)


def eye(n):
    r = lax.broadcasted_iota(jnp.int32, (n, n), 0)
    k = lax.broadcasted_iota(jnp.int32, (n, n), 1)
    return jnp.where(r == k, 1.0, 0.0).astype(BF16)


def valid_first(rows):
    r = lax.broadcasted_iota(jnp.int32, (rows, 1), 0)
    return ((r & 255) < 224) & ((r & 15) < 14)


def valid_second(rows):
    r = lax.broadcasted_iota(jnp.int32, (rows, 1), 0)
    return ((r & 63) < 56) & ((r & 7) < 7)


def sigmoid(a):
    return 0.5 * jnp.tanh(0.5 * a) + 0.5


def act(a):
    return a * sigmoid(a)


def slope(a):
    s = sigmoid(a)
    return s + a * s * (1.0 - s)


def pack_rows(vectors):
    pieces = []
    for v in vectors:
        width = v.shape[1]
        full = -(-width // 128) * 128
        if full != width:
            v = jnp.concatenate([v, jnp.zeros((1, full - width), F32)], axis=1)
        for i in range(full // 128):
            pieces.append(v[:, i * 128 : (i + 1) * 128])
    return jnp.concatenate(pieces, axis=0)


def unpack_rows(rows, start, width):
    count = -(-width // 128)
    return jnp.concatenate([rows[start + i : start + i + 1] for i in range(count)], axis=1)[
        :, :width
    ]


def store_copies(ref, rows):
    count, height = ref.shape[0], ref.shape[1]
    if rows.shape[0] < height:
        rows = jnp.concatenate([rows, jnp.zeros((height - rows.shape[0], 128), F32)], axis=0)
    for i in range(count):
        ref[i] = rows


def local_moments(value, mask, cells):
    total = jnp.sum(jnp.where(mask, value, 0.0), axis=0, keepdims=True)
    delta = jnp.where(mask, value - total * (1.0 / cells), 0.0)
    return total, jnp.sum(delta * delta, axis=0, keepdims=True)


def joint_moments(gathered, height, cells):
    devices = gathered.shape[0]
    sums, squares = gathered[:, :height], gathered[:, height : 2 * height]
    mean = jnp.sum(sums, axis=0) * (1.0 / (cells * devices))
    apart = sums * (1.0 / cells) - mean[None]
    spread = jnp.sum(squares, axis=0) + cells * jnp.sum(apart * apart, axis=0)
    return mean, lax.rsqrt(spread * (1.0 / (cells * devices)) + EPSILON)


def halve(total, scratch, dtype):
    width = total.shape[1]
    both = total[:256] + total[256:]
    pairs = jnp.sum(both.reshape(8, 2, 16, width), axis=1).reshape(128, width)
    pieces = []
    for i in range(-(-width // 128)):
        lanes = min(128, width - i * 128)
        scratch[i, :, :lanes] = pairs[:, i * 128 : i * 128 + lanes]
        piece = scratch[i, pl.ds(0, 64, 2), :] + scratch[i, pl.ds(1, 64, 2), :]
        pieces.append(piece[:, :lanes])
    halved = jnp.concatenate(pieces, axis=1)
    return (halved * 0.125).astype(dtype)


def box_plane(value, stride):
    value = value + roll_rows(value, stride) + roll_rows(value, -stride)
    return value + roll_rows(value, 1) + roll_rows(value, -1)


def first_project(x_ref, win_ref, wpool_ref, zc_ref, zm_ref, q_ref, st_ref):
    for f in range(2):
        rows = pl.ds(f * 256, 256)
        x = x_ref[rows, :]
        z = dot_nn(x, win_ref[...])
        zc_ref[rows, :], zm_ref[rows, :] = z[:, :C0], z[:, C0:]
        q_ref[rows, :] = dot_nn(x, wpool_ref[...])
    mask = valid_first(512)
    moments = [local_moments(ref[...], mask, 392) for ref in (zc_ref, zm_ref)]
    total, squares = [jnp.concatenate([m[i] for m in moments], axis=1) for i in range(2)]
    store_copies(st_ref, pack_rows([total, squares]))


def first_hidden(
    flag_ref, st_ref, zc_ref, zm_ref, q_ref, before_ref, after_ref, win_ref, wpool_ref, wmid_ref,
    wsmall_ref, off_ref,
    zb_ref, zp_ref, st2_ref, x2_ref, mt_ref, head_ref, tail_ref, ma_ref,
    mid, um_ref, us_ref, half,
):
    mean_rows, scale_rows = joint_moments(st_ref[...], 4, 392.0)
    mean, scale = unpack_rows(mean_rows, 0, IN_OUT), unpack_rows(scale_rows, 0, IN_OUT)
    ma_ref[...] = jnp.concatenate([mean, scale], axis=0)
    off = off_ref[:, :IN_OUT]
    frame = valid_first(256)
    prev, after = flag_ref[1] > 0, flag_ref[2] > 0

    def middle(z, mask):
        return jnp.where(mask, act((z - mean[:, C0:]) * scale[:, C0:] + off[:, C0:]), 0.0)

    blank = jnp.zeros((32, MID), F32)
    for start, ref, mask in ((0, before_ref, prev), (768, after_ref, after)):
        z = jnp.concatenate([dot_nn(ref[...], win_ref[:, C0:]), blank], axis=0)
        mid[start : start + 256, :] = middle(z, frame & mask)
    mid[256:512, :] = middle(zm_ref[0:256, :], frame)
    mid[512:768, :] = middle(zm_ref[256:512, :], frame)
    for ref in (um_ref, us_ref):
        edge = jnp.zeros((16, ref.shape[1]), BF16)
        ref[0:16, :] = edge
        ref[1040:1056, :] = edge

    for f in range(4):
        rows = slice(f * 256, (f + 1) * 256)
        shifted = [roll_rows(mid[rows, :], 1 - g) for g in range(3)]
        into = slice(16 + f * 256, 16 + (f + 1) * 256)
        um_ref[into, :] = jnp.concatenate([v[:, :C1A] for v in shifted], axis=1).astype(BF16)
        us_ref[into, :] = jnp.concatenate([v[:, C1A:] for v in shifted], axis=1).astype(BF16)

    def convolve(u_ref, w_ref):
        total = None
        for a in range(3):
            for e in range(3):
                start = 16 + a * 256 + (e - 1) * 16
                term = dot_nn(u_ref[start : start + 512, :], w_ref[3 * a + e])
                total = term if total is None else total + term
        return total

    zb_ref[:, :C1B] = convolve(um_ref, wmid_ref)
    zb_ref[:, C1B:] = convolve(us_ref, wsmall_ref)

    first, last = q_ref[0:256, :], q_ref[256:512, :]
    pair = first + last
    for f, ref in ((0, before_ref), (1, after_ref)):
        beside = jnp.concatenate([dot_nn(ref[...], wpool_ref[...]), blank[:, :POOL]], axis=0)
        value = pair + beside
        value = box_plane(value, 16) * (1.0 / 27.0)
        zp_ref[f * 256 : (f + 1) * 256, :] = jnp.where(frame, value, 0.0)

    both = valid_first(512)
    total_b, squares_b = local_moments(zb_ref[...], both, 392)
    total_p, squares_p = local_moments(zp_ref[...], both, 392)
    store_copies(st2_ref, pack_rows([total_b, total_p, squares_b, squares_p]))
    middle_z = jnp.concatenate([total_b, total_p], axis=1) * (1.0 / 392.0)
    high = middle_z.astype(BF16).astype(F32)
    means = jnp.concatenate([high, middle_z - high, jnp.zeros((14, BOUT + POOL), F32)], axis=0)
    for f, ref in ((0, head_ref), (1, tail_ref)):
        rows = pl.ds(f * 256, 224)
        ref[:224, :BOUT] = (zb_ref[rows, :] - middle_z[:, :BOUT]).astype(BF16)
        ref[:224, BOUT:] = (zp_ref[rows, :] - middle_z[:, BOUT:]).astype(BF16)
        ref[224:, :] = means.astype(BF16)
    hidden = act((zc_ref[...] - mean[:, :C0]) * scale[:, :C0] + off[:, :C0])
    x2_ref[...] = halve(jnp.where(both, hidden, 0.0), half, BF16)[:56]
    mt_ref[...] = dot_nt(eye(MID), mid[256:768, :].astype(BF16)).astype(BF16)


def first_output(st_ref, zb_ref, zp_ref, x2c_ref, off_ref, x2_ref, mb_ref, half):
    mean_rows, scale_rows = joint_moments(st_ref[...], 5, 392.0)
    both = valid_first(512)
    moments = []
    for start, width, z_ref, offset in ((0, BOUT, zb_ref, SECTION_A), (4, POOL, zp_ref, IN_OUT)):
        mean, scale = unpack_rows(mean_rows, start, width), unpack_rows(scale_rows, start, width)
        hidden = act((z_ref[...] - mean) * scale + off_ref[:, offset : offset + width])
        into = slice(C0, C0 + BOUT) if start == 0 else slice(C0 + BOUT, OUTC)
        x2_ref[:, into] = halve(jnp.where(both, hidden, 0.0), half, BF16)[:56]
        moments.append(jnp.concatenate([mean, scale], axis=0))
    x2_ref[:, :C0] = x2c_ref[...]
    mb_ref[...] = jnp.concatenate(moments, axis=1)


def second_layer(clips, frames, flag_ref, *refs):
    x_refs, cot_refs, refs = refs[:frames], refs[frames : 2 * frames], refs[2 * frames :]
    win_ref, wpool_ref, wsmall_ref, off_ref = refs[:4]
    moment_refs, wide_refs, refs = refs[4:7], refs[7:11], refs[11:]
    out_ref, gin_ref, gpool_ref, gmid_hbm, gsmall_hbm, goff_ref = refs[:6]
    dn_ref, error_refs, scratch = refs[6], refs[7:13], refs[13:]
    xs, cs, za, zb, um, us, qs, eb, es, ea, et, ets, eat, da, tmid_ref, tsmall_ref = scratch[:16]
    gmid_ref, gsmall_ref, sems = *scratch[16:18], scratch[-1]
    wmid_ref = wide_refs[0]
    here = flag_ref[0]
    step = clips * 64
    rows = frames * step
    cells = clips * frames * 49.0
    share = 1.0 / cells
    part_mid, part_small = gmid_ref.shape[2], gsmall_ref.shape[2]
    part_in, part_pool = gin_ref.shape[0], gpool_ref.shape[0]
    mask = valid_second(step)

    tail = jnp.zeros((16, OUTC), BF16)

    def assemble(into, blocks):
        for m in range(frames):
            for c in range(clips):
                base = lax.rem(here + m, frames) * step + c * 64
                into[pl.ds(pl.multiple_of(base + 48, 16), 16), :] = tail
                into[pl.ds(pl.multiple_of(base, 64), 56), :] = blocks[m][c]

    assemble(xs, x_refs)
    for ref in (um, us, qs, ea):
        blank = jnp.zeros((step, ref.shape[1]), ref.dtype)
        ref[:step, :] = blank
        ref[step + rows :, :] = blank

    def rows_of(f):
        return slice(f * step, (f + 1) * step)

    def inner(f, shift=1):
        return slice((f + shift) * step, (f + shift + 1) * step)

    def window(a):
        return slice(a * step, a * step + rows)

    def over_frames(body, init):
        for f in range(frames):
            init = body(f, init)
        return init

    def box(f):
        value = qs[inner(f, 0), :] + qs[inner(f, 1), :] + qs[inner(f, 2), :]
        return jnp.where(mask, box_plane(value, 8) * (1.0 / 27.0), 0.0)

    za[:, :IN_OUT] = dot_nn(xs[...], win_ref[...])
    qs[window(1), :] = dot_nn(xs[...], wpool_ref[...])

    def pool_frame(f, total):
        z, p = za[rows_of(f), :IN_OUT], box(f)
        za[rows_of(f), IN_OUT:] = p
        return total + jnp.concatenate(
            [jnp.sum(z, axis=0, keepdims=True), jnp.sum(p, axis=0, keepdims=True)], axis=1
        )

    total_a = over_frames(pool_frame, jnp.zeros((1, SECTION_A), F32))
    mean_a = total_a * share

    def spread_frame(ref, mean):
        def body(f, total):
            delta = jnp.where(mask, ref[rows_of(f), :] - mean, 0.0)
            return total + jnp.sum(delta * delta, axis=0, keepdims=True)

        return body

    spread_a = over_frames(spread_frame(za, mean_a), jnp.zeros((1, SECTION_A), F32))
    scale_a = lax.rsqrt(spread_a * share + EPSILON)
    off_a, off_b = off_ref[:, :SECTION_A], off_ref[:, SECTION_A:]

    def normal_a(f, lo, hi):
        return (za[rows_of(f), lo:hi] - mean_a[:, lo:hi]) * scale_a[:, lo:hi]

    def unfold_frame(f, _):
        a = normal_a(f, C0, IN_OUT) + off_a[:, C0:IN_OUT]
        hidden = jnp.where(mask, act(a), 0.0)
        aside = [roll_rows(hidden, 1 - g) for g in range(3)]
        shifted = [roll_rows(v, 8 * (1 - e)) for e in range(3) for v in aside]
        um[inner(f), :] = jnp.concatenate([v[:, :C1A] for v in shifted], axis=1).astype(BF16)
        us[inner(f), :] = jnp.concatenate([v[:, C1A:] for v in shifted], axis=1).astype(BF16)
        return 0

    over_frames(unfold_frame, 0)

    def convolve(u_ref, w_ref):
        total = dot_nn(u_ref[window(0), :], w_ref[0])
        for a in range(1, 3):
            total = total + dot_nn(u_ref[window(a), :], w_ref[a])
        return total

    zb[:, :C1B] = convolve(um, wmid_ref)
    zb[:, C1B:] = convolve(us, wsmall_ref)
    turn_kernels(wmid_ref, tmid_ref, (1, 0, 2))
    turn_kernels(wsmall_ref, tsmall_ref, (1, 0, 2))

    def total_frame(f, total):
        return total + jnp.sum(jnp.where(mask, zb[rows_of(f), :], 0.0), axis=0, keepdims=True)

    zero_b = jnp.zeros((1, BOUT), F32)
    mean_b = over_frames(total_frame, zero_b) * share
    spread_b = over_frames(spread_frame(zb, mean_b), zero_b)
    scale_b = lax.rsqrt(spread_b * share + EPSILON)

    own = pl.ds(pl.multiple_of(here * step, 64), 64)
    hidden_a = act((za[own, :] - mean_a) * scale_a + off_a)
    hidden_b = act((zb[own, :] - mean_b) * scale_b + off_b)
    out_ref[...] = jnp.concatenate(
        [hidden_a[:, :C0], hidden_b, hidden_a[:, IN_OUT:]], axis=1
    ).astype(BF16)

    assemble(cs, cot_refs)

    def sums_b(f, carry):
        y = (zb[rows_of(f), :] - mean_b) * scale_b
        d = cs[rows_of(f), C0 : C0 + BOUT].astype(F32) * slope(y + off_b)
        zb[rows_of(f), :] = y
        da[rows_of(f), :BOUT] = d
        return (
            carry[0] + jnp.sum(d, axis=0, keepdims=True),
            carry[1] + jnp.sum(d * y, axis=0, keepdims=True),
        )

    sum_b, cross_b = over_frames(sums_b, (zero_b, zero_b))

    for ref in (eb, es):
        width = ref.shape[1] // 3
        blank = jnp.zeros((step, width), BF16)
        ref[rows - step :, width : 2 * width] = blank
        ref[:step, 2 * width :] = blank

    for f in range(frames):
        at = slice(f * step, (f + 1) * step)
        e = da[at, :BOUT] - sum_b * share - zb[at, :] * (cross_b * share)
        e = jnp.where(mask, scale_b * e, 0.0).astype(BF16)
        for i, row in enumerate((f, f - 1, f + 1)):
            if 0 <= row < frames:
                at = slice(row * step, (row + 1) * step)
                eb[at, i * C1B : (i + 1) * C1B] = e[:, :C1B]
                es[at, i * C2B : (i + 1) * C2B] = e[:, C1B:]

    def picker(count, cut, part_one, part_two, columns, edge):
        r = lax.broadcasted_iota(jnp.int32, (count, columns), 0)
        k = lax.broadcasted_iota(jnp.int32, (count, columns), 1)
        want = jnp.where(r < cut, here * part_one + r, edge + here * part_two + r - cut)
        return jnp.where(k == want, 1.0, 0.0).astype(BF16)

    pick_mid = picker(part_mid, part_mid, part_mid, 0, C1B, 0)
    pick_small = picker(part_small, part_small, part_small, 0, C2B, 0)
    et[...] = dot_nt(pick_mid, eb[:, :C1B]).astype(BF16)
    ets[...] = dot_nt(pick_small, es[:, :C2B]).astype(BF16)
    for a in range(3):
        gm = dot_nn(et[...], um[window(a), :])
        gmid_ref[9 * a : 9 * a + 9] = gm.T.reshape(9, C1A, part_mid)
        gs = dot_nn(ets[...], us[window(a), :])
        gsmall_ref[9 * a : 9 * a + 9] = gs.T.reshape(9, C2A, part_small)
    stores = [
        pltpu.make_async_copy(gmid_ref, gmid_hbm, sems.at[0]),
        pltpu.make_async_copy(gsmall_ref, gsmall_hbm, sems.at[1]),
    ]
    for store in stores:
        store.start()

    small = dot_nt(es[...], tsmall_ref[...])
    sides = [None] * 3
    for e in range(3):
        mid = dot_nt(eb[...], tmid_ref[e * 3 * C1A : (e + 1) * 3 * C1A, :])
        for g in range(3):
            k = 3 * e + g
            t = jnp.concatenate(
                [mid[:, g * C1A : (g + 1) * C1A], small[:, k * C2A : (k + 1) * C2A]], axis=1
            )
            t = roll_rows(t, 8 * (e - 1))
            sides[g] = t if e == 0 else sides[g] + t
    da[:, :MID] = roll_rows(sides[0], -1) + sides[1] + roll_rows(sides[2], 1)

    def grad_a(f, carry):
        y = normal_a(f, 0, SECTION_A)
        gain = slope(y + off_a)
        cot = cs[rows_of(f), :]
        d = jnp.concatenate(
            [cot[:, :C0].astype(F32), da[rows_of(f), :MID], cot[:, C0 + BOUT :].astype(F32)], axis=1
        )
        d = jnp.where(mask, d * gain, 0.0)
        da[rows_of(f), :] = d
        za[rows_of(f), :] = y
        return (
            carry[0] + jnp.sum(d, axis=0, keepdims=True),
            carry[1] + jnp.sum(d * y, axis=0, keepdims=True),
        )

    zero_a = jnp.zeros((1, SECTION_A), F32)
    sum_a, cross_a = over_frames(grad_a, (zero_a, zero_a))
    goff_ref[...] = jnp.concatenate([sum_a, sum_b], axis=1)

    def error_a(f, _):
        e = da[rows_of(f), :] - sum_a * share - za[rows_of(f), :] * (cross_a * share)
        e = jnp.where(mask, scale_a * e, 0.0)
        ea[inner(f), :IN_OUT] = e[:, :IN_OUT].astype(BF16)
        qs[inner(f), :] = e[:, IN_OUT:].astype(BF16).astype(F32)
        return 0

    over_frames(error_a, 0)

    def spread_pool(f, _):
        ea[inner(f), IN_OUT:] = box(f).astype(BF16)
        return 0

    over_frames(spread_pool, 0)

    near = [(here + f) * step for f in range(3)]
    near = jnp.concatenate([ea[pl.ds(pl.multiple_of(r, 64), 64), :] for r in near], axis=0)
    dx = dot_nt(near[:, :IN_OUT], win_ref[...]) + dot_nt(near[:, IN_OUT:], wpool_ref[...])
    first_errors(dx[64:128], *wide_refs[1:], *moment_refs, *error_refs)
    dn_ref[:64, :], dn_ref[64:, :] = dx[:64, C0:], dx[128:, C0:]
    pick_a = picker(part_in + part_pool, part_in, part_in, part_pool, SECTION_A, IN_OUT)
    eat[...] = dot_nt(pick_a, ea[window(1), :]).astype(BF16)
    gin_ref[...] = dot_nn(eat[:part_in, :], xs[...])
    gpool_ref[...] = dot_nn(eat[part_in:, :], xs[...])
    for store in stores:
        store.wait()


def second_scratch(rows, step, part):
    wide = rows + 2 * step
    return [
        ((rows, OUTC), BF16), ((rows, OUTC), BF16), ((rows, SECTION_A), F32), ((rows, BOUT), F32),
        ((wide, 9 * C1A), BF16), ((wide, 9 * C2A), BF16), ((wide, POOL), F32),
        ((rows, 3 * C1B), BF16), ((rows, 3 * C2B), BF16), ((wide, SECTION_A), BF16),
        ((part[0], rows), BF16), ((part[1], rows), BF16), ((part[2] + part[3], rows), BF16),
        ((rows, SECTION_A), F32), ((9 * C1A, 3 * C1B), BF16), ((9 * C2A, 3 * C2B), BF16),
        ((27, C1A, part[0]), F32), ((27, C2A, part[1]), F32), pltpu.SemaphoreType.DMA((2,)),
    ]


def turn_kernels(w_ref, t_ref, order):
    width = w_ref.shape[2]
    for i, k in enumerate(order):
        t_ref[:, i * width : (i + 1) * width] = w_ref[k]


def spread_grad(d):
    r = lax.broadcasted_iota(jnp.int32, (256, 64), 0)
    k = lax.broadcasted_iota(jnp.int32, (256, 64), 1)
    spread = jnp.where(k == ((r >> 5) << 3) + ((r & 15) >> 1), 1.0, 0.0).astype(BF16)
    d = d * 0.125
    high = d.astype(BF16)
    low = (d - high.astype(F32)).astype(BF16)
    return dot_nn(spread, high) + dot_nn(spread, low)


def first_errors(
    dx, zb_ref, zp_ref, zc_ref, ma_ref, mb_ref, off_ref,
    db_ref, yb_ref, dp_ref, yp_ref, dc_ref, st_ref,
):
    g = spread_grad(dx)
    sums, crosses = [], []
    for z_ref, m_ref, lanes, part, offset, d_ref, y_ref in (
        (zb_ref, mb_ref, slice(C0, C0 + BOUT), slice(0, BOUT), SECTION_A, db_ref, yb_ref),
        (zp_ref, mb_ref, slice(C0 + BOUT, OUTC), slice(BOUT, BOUT + POOL), IN_OUT, dp_ref, yp_ref),
        (zc_ref, ma_ref, slice(0, C0), slice(0, C0), 0, dc_ref, None),
    ):
        width = part.stop - part.start
        total, cross = jnp.zeros((1, width), F32), jnp.zeros((1, width), F32)
        for f in range(2):
            rows = slice(f * 256, (f + 1) * 256)
            y = (z_ref[rows, :] - m_ref[0:1, part]) * m_ref[1:2, part]
            d = g[:, lanes] * slope(y + off_ref[:, offset : offset + width])
            d_ref[rows, :] = d.astype(BF16)
            if y_ref is not None:
                y_ref[rows, :] = y.astype(BF16)
            total = total + jnp.sum(d, axis=0, keepdims=True)
            cross = cross + jnp.sum(d * y, axis=0, keepdims=True)
        sums.append(total)
        crosses.append(cross)
    store_copies(st_ref, pack_rows(sums + crosses))


def beside_errors(dn, z_ref, mb_ref, off_ref, lanes, offset):
    means = z_ref[224:, lanes].astype(F32)
    z = z_ref[:224, lanes].astype(F32) + (means[0:1] + means[1:2])
    z = jnp.concatenate([z, jnp.zeros((32, z.shape[1]), F32)], axis=0)
    y = (z - mb_ref[0:1, lanes]) * mb_ref[1:2, lanes]
    return spread_grad(dn) * slope(y + off_ref[:, offset : offset + z.shape[1]]), y


def first_beside(dn_ref, before_ref, after_ref, mb_ref, off_ref, db_ref, yb_ref, dp_ref, yp_ref):
    lanes = slice(BOUT, BOUT + POOL)
    for f, ref in ((0, before_ref), (1, after_ref)):
        rows, near = slice(f * 256, (f + 1) * 256), slice(f * 64, (f + 1) * 64)
        d, y = beside_errors(dn_ref[near, :BOUT], ref, mb_ref, off_ref, slice(0, BOUT), SECTION_A)
        db_ref[rows, :], yb_ref[rows, :] = d.astype(BF16), y.astype(BF16)
        d, y = beside_errors(dn_ref[near, lanes], ref, mb_ref, off_ref, lanes, IN_OUT)
        dp_ref[rows, :], yp_ref[rows, :] = d.astype(BF16), y.astype(BF16)


def first_hidden_errors(
    cells, parts, flag_ref, st_ref, db_ref, yb_ref, dbn_ref, ybn_ref, mb_ref,
    eb_ref, sum_ref, *chunk_refs,
):
    part_mid, part_small = C1B // parts, C2B // parts
    totals = jnp.sum(st_ref[...], axis=0)
    sum_ref[...] = totals
    sum_b, cross_b = unpack_rows(totals, 0, BOUT), unpack_rows(totals, 7, BOUT)
    scale_b = mb_ref[1:2, :BOUT]
    frame = valid_first(256)
    edge = jnp.zeros((16, BOUT), BF16)
    eb_ref[0:16, :] = edge
    eb_ref[1040:1056, :] = edge
    r = lax.broadcasted_iota(jnp.int32, (BOUT, part_mid + part_small), 0)
    k = lax.broadcasted_iota(jnp.int32, (BOUT, part_mid + part_small), 1)
    picks = []
    for m in range(parts):
        p = lax.rem(flag_ref[0] + m, parts)
        want = jnp.where(k < part_mid, p * part_mid + k, C1B + p * part_small + k - part_mid)
        picks.append(jnp.where(r == want, 1.0, 0.0).astype(BF16))
    for s in range(4):
        mask = frame
        if s == 0:
            mask = frame & (flag_ref[1] > 0)
            d, y = dbn_ref[:256, :].astype(F32), ybn_ref[:256, :].astype(F32)
        elif s == 3:
            mask = frame & (flag_ref[2] > 0)
            d, y = dbn_ref[256:, :].astype(F32), ybn_ref[256:, :].astype(F32)
        else:
            rows = slice((s - 1) * 256, s * 256)
            d, y = db_ref[rows, :].astype(F32), yb_ref[rows, :].astype(F32)
        e = scale_b * (d - sum_b * (1.0 / cells) - y * (cross_b * (1.0 / cells)))
        e = jnp.where(mask, e, 0.0).astype(BF16)
        eb_ref[16 + s * 256 : 16 + (s + 1) * 256, :] = e
        if s in (1, 2):
            for ref, pick in zip(chunk_refs, picks):
                ref[(s - 1) * 224 : s * 224, :] = dot_nn(e[:224], pick).astype(BF16)


def first_hidden_back(
    eb, zm_ref, ma_ref, off_ref, wmid_ref, wsmall_ref,
    dm_ref, st_ref,
):
    mids, smalls = None, None
    for a in range(3):
        for e in range(3):
            start = 16 + 256 - (a - 1) * 256 - (e - 1) * 16
            one = dot_nt(eb[start : start + 512, :C1B], wmid_ref[3 * a + e])
            two = dot_nt(eb[start : start + 512, C1B:], wsmall_ref[3 * a + e])
            mids = one if mids is None else mids + one
            smalls = two if smalls is None else smalls + two
    back = None
    for g in range(3):
        t = jnp.concatenate(
            [mids[:, g * C1A : (g + 1) * C1A], smalls[:, g * C2A : (g + 1) * C2A]], axis=1
        )
        t = roll_rows(t, g - 1)
        back = t if back is None else back + t
    y = (zm_ref[...] - ma_ref[0:1, C0:]) * ma_ref[1:2, C0:]
    d = jnp.where(valid_first(512), back * slope(y + off_ref[:, C0:IN_OUT]), 0.0)
    dm_ref[...] = d
    sums = jnp.sum(d, axis=0, keepdims=True)
    crosses = jnp.sum(d * y, axis=0, keepdims=True)
    store_copies(st_ref, pack_rows([sums, crosses]))


def first_kernel_grad(
    parts, flag_ref, *refs,
):
    errors, hidden = refs[:parts], refs[parts : 2 * parts]
    chunk_refs, (em, turned, kept) = refs[2 * parts : -3], refs[-3:]
    frames = 2 * parts
    chunks = len(chunk_refs)
    part_small = C2B // parts
    part_mid = C1B // parts
    here, clip = flag_ref[0], flag_ref[3]
    blank = jnp.zeros((16, 128), BF16)
    for m in range(parts):
        source = lax.rem(here - m + parts, parts)
        turned[:, pl.ds(pl.multiple_of(source * 512, 512), 512)] = hidden[m][...]
        for f in range(2):
            base = source * 512 + f * 256
            e = errors[m][f * 224 : f * 224 + 224, :].astype(F32)
            e = jnp.concatenate([e, jnp.zeros((224, 128 - e.shape[1]), F32)], axis=1)
            e = jnp.concatenate([e, jnp.zeros((32, 128), F32)], axis=0)
            for g in range(3):
                moved = roll_rows(e, g - 1).astype(BF16)
                lanes = [slice((3 * i + g) * 128, (3 * i + g + 1) * 128) for i in range(3)]

                def at(start, size):
                    return pl.ds(pl.multiple_of(base + start, 16), size)

                em[at(0, 240), lanes[0]] = moved[16:]
                em[at(240, 16), lanes[0]] = blank
                em[at(0, 256), lanes[1]] = moved
                em[at(0, 16), lanes[2]] = blank
                em[at(16, 240), lanes[2]] = moved[:240]
    mids, smalls = [], []
    for a in range(3):
        shift = 256 * (a - 1)
        lo, hi = max(0, shift), min(frames * 256, frames * 256 + shift)
        both = dot_nn(turned[:, lo:hi], em[lo - shift : hi - shift, :])
        for k in range(9):
            mids.append(both[:C1A, k * 128 : k * 128 + part_mid])
            smalls.append(both[C1A:, k * 128 + part_mid : k * 128 + part_mid + part_small])
    mids, smalls = jnp.concatenate(mids, axis=1), jnp.concatenate(smalls, axis=1)
    high, low = C1A // chunks, C2A // chunks
    wide = smalls.shape[1] // chunks
    blank = jnp.zeros((high - C2A, wide), F32)
    for i in range(chunks):
        tail = [smalls[i * low : (i + 1) * low, q * wide : (q + 1) * wide] for q in range(chunks)]
        tail = jnp.concatenate(tail + [blank], axis=0)
        kept[i * high : (i + 1) * high, :] = jnp.concatenate(
            [mids[i * high : (i + 1) * high], tail], axis=1
        )
    for m, ref in enumerate(chunk_refs):
        at = lax.rem(clip + m, chunks) * high
        ref[...] = kept[pl.ds(pl.multiple_of(at, 8), high), :].astype(BF16)


def first_kernel_join(flag_ref, *refs):
    chunks = len(refs) - 2
    gmid_ref, gsmall_ref = refs[chunks:]
    high, low = C1A // chunks, C2A // chunks
    part_mid, part_small = gmid_ref.shape[2], gsmall_ref.shape[2]
    for m in range(chunks):
        at = lax.rem(flag_ref[3] + m, chunks)
        value = refs[m][...].astype(F32)
        rows = pl.ds(pl.multiple_of(at * high, 8), high)
        for k in range(27):
            gmid_ref[k, rows, :] = value[:, k * part_mid : (k + 1) * part_mid]
        small = [value[q * low : (q + 1) * low, 27 * part_mid :] for q in range(chunks)]
        small = jnp.concatenate(small, axis=1)
        rows = pl.ds(pl.multiple_of(at * low, 8), low)
        for k in range(27):
            gsmall_ref[k, rows, :] = small[:, k * part_small : (k + 1) * part_small]


def first_input_errors(
    cells, parts, flag_ref, st_ref, sum_ref, dm_ref, dc_ref, dp_ref, yp_ref, dpn_ref, ypn_ref,
    zc_ref, zm_ref, ma_ref, mb_ref, x_ref,
    ea, goff_ref, *refs,
):
    part_in, part_pool = IN_OUT // parts, POOL // parts
    totals = jnp.sum(st_ref[...], axis=0)
    before = sum_ref[...]
    sum_m, cross_m = unpack_rows(totals, 0, MID), unpack_rows(totals, 2, MID)
    sum_b = unpack_rows(before, 0, BOUT)
    sum_p, sum_c = unpack_rows(before, 4, POOL), unpack_rows(before, 5, C0)
    cross_p, cross_c = unpack_rows(before, 11, POOL), unpack_rows(before, 12, C0)
    goff_ref[...] = jnp.concatenate([sum_c, sum_m, sum_p, sum_b], axis=1)
    share = 1.0 / cells
    frame = valid_first(256)
    pools = []
    for s in range(4):
        mask = frame
        if s == 0:
            mask = frame & (flag_ref[1] > 0)
            d, y = dpn_ref[:256, :].astype(F32), ypn_ref[:256, :].astype(F32)
        elif s == 3:
            mask = frame & (flag_ref[2] > 0)
            d, y = dpn_ref[256:, :].astype(F32), ypn_ref[256:, :].astype(F32)
        else:
            rows = slice((s - 1) * 256, s * 256)
            d, y = dp_ref[rows, :].astype(F32), yp_ref[rows, :].astype(F32)
        e = mb_ref[1:2, BOUT:] * (d - sum_p * share - y * (cross_p * share))
        pools.append(jnp.where(mask, e, 0.0).astype(BF16).astype(F32))
    for f in range(2):
        rows = slice(f * 256, (f + 1) * 256)
        value = box_plane(pools[f] + pools[f + 1] + pools[f + 2], 16) * (1.0 / 27.0)
        ea[rows, IN_OUT:] = jnp.where(frame, value, 0.0).astype(BF16)
        y = (zc_ref[rows, :] - ma_ref[0:1, :C0]) * ma_ref[1:2, :C0]
        e = dc_ref[rows, :].astype(F32) - sum_c * share - y * (cross_c * share)
        ea[rows, :C0] = jnp.where(frame, ma_ref[1:2, :C0] * e, 0.0).astype(BF16)
        y = (zm_ref[rows, :] - ma_ref[0:1, C0:]) * ma_ref[1:2, C0:]
        e = dm_ref[rows, :] - sum_m * share - y * (cross_m * share)
        ea[rows, C0:IN_OUT] = jnp.where(frame, ma_ref[1:2, C0:] * e, 0.0).astype(BF16)
    chunk_refs, g_ref = refs[:-1], refs[-1]
    g_ref[...] = dot_tn(ea[...], x_ref[...])
    for m, ref in enumerate(chunk_refs):
        p = lax.rem(flag_ref[0] + m, parts)
        rows = pl.ds(pl.multiple_of(p * part_in, 8), part_in)
        ref[:part_in] = g_ref[rows, :].astype(BF16)
        rows = pl.ds(pl.multiple_of(IN_OUT + p * part_pool, 8), part_pool)
        ref[part_in:] = g_ref[rows, :].astype(BF16)


def first_input_back(ea, win_ref, wpool_ref, dx_ref):
    dx_ref[...] = dot_nt(ea[:, :IN_OUT], win_ref[...]) + dot_nt(ea[:, IN_OUT:], wpool_ref[...])


def call(body, outs, scratch, *args, scalars=1, us=1, near=(), out_near=(), out_hbm=()):
    in_specs, placed = [], []
    for i, arg in enumerate(args):
        space = pltpu.SMEM if i < scalars else pltpu.VMEM
        in_specs.append(pl.BlockSpec(memory_space=space))
        placed.append(pltpu.with_memory_space_constraint(arg, pltpu.VMEM) if i in near else arg)
    out_specs = [
        pl.BlockSpec(memory_space=pl.ANY if i in out_hbm else pltpu.VMEM) for i in range(len(outs))
    ]
    return pl.pallas_call(
        body,
        out_shape=[
            pltpu.VMEM(*out) if i in out_near else jax.ShapeDtypeStruct(*out)
            for i, out in enumerate(outs)
        ],
        in_specs=in_specs,
        out_specs=out_specs,
        scratch_shapes=[pltpu.VMEM(*s) if isinstance(s, tuple) else s for s in scratch],
        compiler_params=pltpu.CompilerParams(vmem_limit_bytes=VMEM_LIMIT),
        cost_estimate=pl.CostEstimate(
            flops=int(us * 1.1e9),
            bytes_accessed=sum(a.size * a.dtype.itemsize for a in args),
            transcendentals=0,
        ),
    )(*placed)


def exchange(copies):
    return lax.all_to_all(copies, ("clip", "tm"), 0, 0)


def neighbours(head, tail):
    size = lax.axis_size("tm")
    up = [(i, i + 1) for i in range(size - 1)]
    down = [(i + 1, i) for i in range(size - 1)]
    return lax.ppermute(tail, "tm", up), lax.ppermute(head, "tm", down)


def gather_from(value, axis, back=False):
    size = lax.axis_size(axis)
    blocks = [value]
    for m in range(1, size):
        step = -m if back else m
        blocks.append(lax.ppermute(value, axis, [((i + step) % size, i) for i in range(size)]))
    return blocks


def hand_on(chunks, axis):
    size = lax.axis_size(axis)
    blocks = [chunks[0]]
    for m in range(1, size):
        blocks.append(lax.ppermute(chunks[m], axis, [(i, (i + m) % size) for i in range(size)]))
    return blocks


def to_all(value, axis):
    size = lax.axis_size(axis)
    return lax.all_to_all(jnp.broadcast_to(value[None], (size,) + value.shape), axis, 0, 0)


def turned_to(blocks, first):
    return lax.dynamic_slice_in_dim(jnp.concatenate([blocks, blocks]), first, blocks.shape[0])


def summed(parts):
    total = parts[0].astype(F32)
    for i in range(1, len(parts)):
        total = total + parts[i].astype(F32)
    return total.astype(BF16)


def after(value, *others):
    return lax.optimization_barrier((value,) + others)[0]


def small_group(
    features, w_in_4f, w_pool_4f, w_mid_4f, w_small_4f, offsets_4f,
    w_in_5b, w_pool_5b, w_mid_5b, w_small_5b, offsets_5b, cotangent,
):
    clips, frames = lax.axis_size("clip"), lax.axis_size("tm")
    group = clips * frames
    cells = 392.0 * group
    here = lax.axis_index("tm")
    flags = jnp.stack([here, here > 0, here < frames - 1, lax.axis_index("clip")]).astype(jnp.int32)
    offsets_4f, offsets_5b = offsets_4f[None], offsets_5b[None]
    x = jnp.pad(features[0], ((0, 0), (0, 2), (0, 2), (0, 0))).reshape(512, features.shape[-1])
    cot = jnp.pad(cotangent[0, 0], ((0, 0), (0, 1), (0, 0))).reshape(56, OUTC)
    mid_4f, small_4f = w_mid_4f.reshape(9, 3 * C1A, C1B), w_small_4f.reshape(9, 3 * C2A, C2B)
    mid_5b, small_5b = w_mid_5b.reshape(3, 9 * C1A, C1B), w_small_5b.reshape(3, 9 * C2A, C2B)
    before, behind = neighbours(x[:224], x[256:480])
    z_c, z_m, q, stats = call(
        first_project,
        [((512, C0), F32), ((512, MID), F32), ((512, POOL), F32), ((group, 8, 128), F32)],
        [], x, w_in_4f, w_pool_4f, scalars=0, us=4,
    )
    cot = gather_from(after(cot, q), "clip")
    stats = exchange(stats)
    z_b, z_p, stats, x2_c, m_turned, head, tail, moments_a = call(
        first_hidden,
        [((512, BOUT), F32), ((512, POOL), F32), ((group, 16, 128), F32), ((56, C0), BF16),
         ((MID, 512), BF16),
         ((240, BOUT + POOL), BF16), ((240, BOUT + POOL), BF16), ((2, IN_OUT), F32)],
        [((1024, MID), F32), ((1056, 3 * C1A), BF16), ((1056, 3 * C2A), BF16),
         ((4, 128, 128), F32)],
        flags, stats, z_c, z_m, q, before, behind, w_in_4f, w_pool_4f, mid_4f, small_4f,
        offsets_4f, us=20, near=(1, 5, 6),
    )
    *cot, stats = lax.optimization_barrier((*cot, stats))
    cot = gather_from(jnp.stack(cot), "tm")
    stats = exchange(stats)
    x2, moments_b = call(
        first_output,
        [((56, OUTC), BF16), ((2, BOUT + POOL), F32)],
        [((4, 128, 128), F32)],
        stats, z_b, z_p, x2_c, offsets_4f, scalars=0, us=3, near=(0,), out_near=(0,),
    )
    x2 = jnp.stack(gather_from(x2, "clip"))
    before, behind = neighbours(head, tail)
    m_turned = gather_from(m_turned, "tm", back=True)
    x2 = gather_from(after(x2, *cot), "tm")
    part = (C1B // frames, C2B // frames, IN_OUT // frames, POOL // frames)
    (out, g_in_5b, g_pool_5b, g_mid_5b, g_small_5b, g_off_5b, d_near,
     d_b, y_b, d_p, y_p, d_c, stats) = call(
        functools.partial(second_layer, clips, frames),
        [((64, OUTC), BF16), ((part[2], OUTC), F32), ((part[3], OUTC), F32),
         ((27, C1A, part[0]), F32), ((27, C2A, part[1]), F32), ((1, 1024), F32),
         ((128, BOUT + POOL), F32),
         ((512, BOUT), BF16), ((512, BOUT), BF16), ((512, POOL), BF16), ((512, POOL), BF16),
         ((512, C0), BF16), ((group, 16, 128), F32)],
        second_scratch(group * 64, clips * 64, part),
        flags, *x2, *cot, w_in_5b, w_pool_5b, small_5b, offsets_5b, moments_a, moments_b,
        offsets_4f, mid_5b, z_b, z_p, z_c,
        us=35, near=range(1, 1 + 2 * frames), out_hbm=(3, 4),
    )
    stats = exchange(stats)
    d_bn, y_bn, d_pn, y_pn = call(
        first_beside,
        [((512, BOUT), BF16), ((512, BOUT), BF16), ((512, POOL), BF16), ((512, POOL), BF16)],
        [], d_near, before, behind, moments_b, offsets_4f, scalars=0, us=10,
    )
    e_b, sums, *errors = call(
        functools.partial(first_hidden_errors, cells, frames),
        [((1056, BOUT), BF16), ((16, 128), F32)] + [((448, part[0] + part[1]), BF16)] * frames,
        [], flags, stats, d_b, y_b, d_bn, y_bn, moments_b, us=3, near=(1,),
        out_near=[0, *range(2, 2 + frames)],
    )
    errors = hand_on(errors, "tm")
    d_m, stats = call(
        first_hidden_back,
        [((512, MID), F32), ((group, 8, 128), F32)],
        [], e_b, z_m, moments_a, offsets_4f, mid_4f, small_4f, scalars=0, us=6, near=(0,),
    )
    stats = exchange(stats)
    wide = 27 * part[0] + 27 * part[1] // clips
    g_conv = call(
        functools.partial(first_kernel_grad, frames),
        [((C1A // clips, wide), BF16)] * clips,
        [((frames * 512, 9 * 128), BF16), ((MID, frames * 512), BF16), ((C1A, wide), F32)],
        after(flags, d_m), *errors, *m_turned, us=10, near=range(1, 1 + frames), out_near=range(clips),
    )
    stats = after(stats, *g_conv)
    g_conv = hand_on(g_conv, "clip")
    e_a, g_off, *g_a = call(
        functools.partial(first_input_errors, cells, frames),
        [((512, SECTION_A), BF16), ((1, 1024), F32)]
        + [((part[2] + part[3], features.shape[-1]), BF16)] * frames,
        [((SECTION_A, features.shape[-1]), F32)], flags, stats, sums, d_m, d_c, d_p, y_p, d_pn, y_pn,
        z_c, z_m, moments_a, moments_b, x, us=20, near=(1,),
        out_near=[0, *range(2, 2 + frames)],
    )
    (d_x,) = call(
        first_input_back,
        [((512, features.shape[-1]), F32)],
        [], after(e_a, g_conv[1]), w_in_4f, w_pool_4f, scalars=0, us=0, near=(0,),
    )
    g_a = hand_on(g_a, "tm")
    g_conv = summed(lax.optimization_barrier((*g_conv, d_x))[:clips])
    g_a = summed(lax.optimization_barrier((*g_a, g_conv))[:frames])
    g_conv = gather_from(g_conv, "clip")
    g_a = hand_on(turned_to(g_a.reshape(clips, -1, features.shape[-1]), flags[3]), "clip")
    g_a = after(summed(g_a), g_conv[1])
    g_a = jnp.stack(gather_from(g_a, "clip")).astype(F32)
    g_a = turned_to(g_a, lax.rem(clips - flags[3], clips)).reshape(part[2] + part[3], -1)
    g_mid, g_small = call(
        first_kernel_join,
        [((27, C1A, part[0]), F32), ((27, C2A, part[1]), F32)],
        [], flags, *g_conv, us=4, near=range(1, 1 + clips),
    )

    return (
        out.reshape(1, 1, 8, 8, OUTC)[:, :, :7, :7],
        d_x.reshape(1, 2, 16, 16, -1)[:, :, :14, :14],
        g_a[: part[2]].T,
        g_a[part[2] :].T,
        g_mid,
        g_small,
        g_off[0],
        g_in_5b.T,
        g_pool_5b.T,
        g_mid_5b,
        g_small_5b,
        g_off_5b[0],
    )


def solution(mesh):
    placed = (
        P(("stream", "clip"), "tm", None, None, None),
        P("stream", None),
        P("stream", None),
        P("stream", None, None),
        P("stream", None, None),
        P("stream"),
        P("stream", None),
        P("stream", None),
        P("stream", None, None),
        P("stream", None, None),
        P("stream"),
        P(("stream", "clip"), "tm", None, None, None),
    )
    group = mesh.shape["clip"] * mesh.shape["tm"]
    return jax.shard_map(
        small_group if group <= 16 else shards,
        mesh=mesh,
        in_specs=placed,
        out_specs=(
            P(("stream", "clip"), "tm", None, None, None),
            P(("stream", "clip"), "tm", None, None, None),
            P("stream", "tm"),
            P("stream", "tm"),
            P("stream", None, "tm"),
            P("stream", None, "tm"),
            P("stream"),
            P("stream", "tm"),
            P("stream", "tm"),
            P("stream", None, "tm"),
            P("stream", None, "tm"),
            P("stream"),
        ),
        check_vma=False,
    )
```
